32 devices in a mesh: dp: 2 (over x), blk: 16 (over z, y, core).
Axes of the slice: x: 2, y: 2, z: 4, core: 2. Of those that a mesh axis runs over, the one named last changes fastest.
Arguments:
- tokens: bfloat16 [2, 16, 128, 1024], P('dp', 'blk'), may hold values from -6 to 6
- cotangent: bfloat16 [2, 16, 128, 1024], P('dp', 'blk'), may hold values from -6 to 6
- lengths: int32 [2, 2], P('dp'), may hold values from 1 to 1536, as said below
- w_query: bfloat16 [1024, 1024], replicated, may hold values from -0.1875 to 0.1875
- w_key: bfloat16 [1024, 1024], replicated, may hold values from -0.1875 to 0.1875
- w_value: bfloat16 [1024, 1024], replicated, may hold values from -0.1875 to 0.1875
- w_out: bfloat16 [1024, 1024], replicated, may hold values from -0.1875 to 0.1875
- w_up: bfloat16 [1024, 4096], replicated, may hold values from -0.1875 to 0.1875
- w_gate: bfloat16 [1024, 4096], replicated, may hold values from -0.1875 to 0.1875
- w_down: bfloat16 [4096, 1024], replicated, may hold values from -0.09375 to 0.09375
- s_qk: float32 [1024], replicated, may hold values from 0.8 to 1.6
- s_up: float32 [4096], replicated, may hold values from 0.5 to 2
- s_gate: float32 [4096], replicated, may hold values from 0.5 to 2
- alpha_attn: float32 [1024], replicated, may hold values from 0.1 to 0.8
- alpha_mlp: float32 [1024], replicated, may hold values from 0.1 to 0.8
Outputs:
- output: bfloat16 [2, 16, 128, 1024], P('dp', 'blk')
- input_grad: float32 [2, 16, 128, 1024], P('dp', 'blk')
- grad_query: float32 [1024, 1024], P(('dp', 'blk'))
- grad_key: float32 [1024, 1024], P(('dp', 'blk'))
- grad_value: float32 [1024, 1024], P(('dp', 'blk'))
- grad_out: float32 [1024, 1024], P(('dp', 'blk'))
- grad_up: float32 [1024, 4096], P(('dp', 'blk'))
- grad_gate: float32 [1024, 4096], P(('dp', 'blk'))
- grad_down: float32 [4096, 1024], P(('dp', 'blk'))
- grad_qk_scale: float32 [1024], P(('dp', 'blk'))
- grad_up_scale: float32 [4096], P(('dp', 'blk'))
- grad_gate_scale: float32 [4096], P(('dp', 'blk'))
- grad_alpha_attn: float32 [1024], P(('dp', 'blk'))
- grad_alpha_mlp: float32 [1024], P(('dp', 'blk'))
- mean_alpha: float32 [], replicated
The draws below stay inside these ranges and needn't reach their ends.
Inputs may be any that keep to these rules, and one draw needn't show every extreme that they name: In each row the lengths sum to 2048, and the first or the last of them is more than half of that sum; in every draw some row's long document has the largest length.
All inputs are finite; a program needn't handle non-finite values.
Results may differ from the reference program's by a relative error of at most 0.025.
Values may be sent and summed in bfloat16 or wider, within the bound.
A program may use at most 640 MiB of HBM per device.

```python
import math
from functools import partial
import jax
import jax.numpy as jnp
from jax import lax

D = 1024
HEADS = 16
HEAD_DIM = 64
FF = 4096
TOK_DEV = 128
NDOC = 2
N_DP = 2
N_BLK = 16


def draw_lengths(key, part):
    key = jax.random.fold_in(key, 17)
    total_len = TOK_DEV * N_BLK
    first_key, second_key, third_key = jax.random.split(key, 3)
    extra_len = jax.random.randint(first_key, (N_DP,), 1, total_len // 4 + 1)
    extra_len = extra_len.at[0].set(total_len // 4)
    long_len = total_len // 2 + extra_len
    rest_len = total_len - long_len
    shares = jax.random.randint(second_key, (N_DP, NDOC - 1), 1, 5)
    running = jnp.cumsum(shares, axis=1, dtype=jnp.int32)
    bounds = rest_len[:, None] * running // running[:, -1:]
    pieces = jnp.diff(bounds, axis=1, prepend=jnp.zeros((N_DP, 1), jnp.int32))
    at_front = jax.random.randint(third_key, (N_DP, 1), 0, 2)
    long_first = jnp.concatenate([long_len[:, None], pieces], axis=1)
    long_last = jnp.concatenate([pieces, long_len[:, None]], axis=1)
    return jnp.where(at_front == 1, long_first, long_last).astype(jnp.int32)


def raised(array, own_key, source, target, blocks, factor):
    owner, partner = [(jnp.arange(array.shape[dim]) // (array.shape[dim] // blocks)).reshape([-1 if axis == dim else 1 for axis in range(array.ndim)]) for dim in (source, target)]
    chosen = jax.random.permutation(own_key, blocks)[partner]
    strong = (owner == chosen) | (owner == (partner + blocks // 2) % blocks)
    return jnp.where(strong, factor * array, array)


def block_scale(rng, dims, cuts, low, largest):
    level, own = 1.0, jax.random.fold_in(rng, 6)
    for position, blocks in cuts:
        heights = jnp.exp(jax.random.uniform(jax.random.fold_in(own, position), (blocks,), jnp.float32, low / len(cuts), largest / len(cuts)))
        level = level * jnp.repeat(heights, dims[position] // blocks).reshape([-1 if axis == position else 1 for axis in range(len(dims))])
    return level


def gaussian(own_key, dims, spread, most, shards=(), held_as=jnp.bfloat16):
    gain = block_scale(own_key, dims, shards, -0.22, 0.18) if shards else 1.0
    drawn = jax.random.normal(own_key, dims, jnp.float32) * spread * gain
    return jnp.minimum(jnp.maximum(drawn, -most), most).astype(held_as)


def bell_draw_with(own_key, shape, scale, bound, shards, heavy, kind=jnp.bfloat16):
    array = scale * jax.random.normal(own_key, shape, jnp.float32)
    if shards:
        array = array * block_scale(own_key, shape, shards, -0.22, 0.18)
    return jnp.clip(raised(array, jax.random.fold_in(own_key, 3), *heavy), -bound, bound).astype(kind)


def setup_inputs(seed: int = 0) -> dict:
    key_of = jax.random.split(jax.random.key(seed), 16)
    tokens = bell_draw_with(key_of[0], (N_DP, N_BLK, TOK_DEV, D), 1.0, 6.0, ((0, 2), (1, 16)), (1, 3, 16, 2.0))
    cotangent = gaussian(key_of[1], (N_DP, N_BLK, TOK_DEV, D), 1.0, 6.0, ((0, 2), (1, 16)))
    lengths = draw_lengths(jax.random.fold_in(key_of[15], 71), 0)
    w_query = gaussian(key_of[3], (D, D), D ** -0.5, 0.1875)
    w_key = gaussian(key_of[4], (D, D), D ** -0.5, 0.1875)
    w_value = gaussian(key_of[5], (D, D), D ** -0.5, 0.1875)
    w_out = gaussian(key_of[6], (D, D), D ** -0.5, 0.1875)
    w_up = gaussian(key_of[7], (D, FF), D ** -0.5, 0.1875)
    w_gate = gaussian(key_of[8], (D, FF), D ** -0.5, 0.1875)
    w_down = gaussian(key_of[9], (FF, D), FF ** -0.5, 0.09375)
    s_qk = jnp.clip(jnp.exp(jax.random.uniform(key_of[10], (D,), jnp.float32, math.log(0.8), math.log(1.6))), 0.8, 1.6)
    s_up = jnp.clip(jnp.exp(jax.random.uniform(key_of[11], (FF,), jnp.float32, math.log(0.5), math.log(2.0))), 0.5, 2.0)
    s_gate = jnp.clip(jnp.exp(jax.random.uniform(key_of[12], (FF,), jnp.float32, math.log(0.5), math.log(2.0))), 0.5, 2.0)
    alpha_attn = jnp.clip(jnp.exp(jax.random.uniform(key_of[13], (D,), jnp.float32, math.log(0.1), math.log(0.8))), 0.1, 0.8)
    alpha_mlp = jnp.clip(jnp.exp(jax.random.uniform(key_of[14], (D,), jnp.float32, math.log(0.1), math.log(0.8))), 0.1, 0.8)
    return {"tokens": tokens, "cotangent": cotangent, "lengths": lengths, "w_query": w_query, "w_key": w_key, "w_value": w_value, "w_out": w_out, "w_up": w_up, "w_gate": w_gate, "w_down": w_down, "s_qk": s_qk, "s_up": s_up, "s_gate": s_gate, "alpha_attn": alpha_attn, "alpha_mlp": alpha_mlp}


@jax.custom_vjp
def low(v):
    return lax.optimization_barrier(v.astype(jnp.bfloat16)).astype(jnp.float32)

@jax.custom_vjp
def low_back(v):
    return v

def low_keep(v):
    return (low(v), None)

def low_pass(kept, grad):
    return (grad,)

def back_keep(v):
    return (v, None)

def back_low(kept, grad):
    return (low(grad),)
low.defvjp(low_keep, low_pass)
low_back.defvjp(back_keep, back_low)

def product(left_matrix, right_matrix):
    return jnp.dot(left_matrix, right_matrix, precision=lax.Precision.HIGHEST, preferred_element_type=jnp.float32)

def rms_norm(vector):
    return vector * lax.rsqrt(lax.optimization_barrier(jnp.mean(vector * vector, axis=-1, keepdims=True)) + 1e-06)

def head_norm(vector):
    shaped = vector.reshape(vector.shape[0], HEADS, HEAD_DIM)
    return rms_norm(shaped).reshape(vector.shape)

def silu_smooth(vector):
    return vector / (1.0 + jnp.exp(-vector))

def stream_order(blocks):
    half_rows = blocks.shape[1] // 2
    lower_half = blocks[:, :half_rows].reshape(-1, blocks.shape[2])
    upper_half = blocks[::-1, half_rows:].reshape(-1, blocks.shape[2])
    return jnp.concatenate([lower_half, upper_half], axis=0)

def device_order(stream):
    middle_row = stream.shape[0] // 2
    lower_half = stream[:middle_row].reshape(N_BLK, -1, stream.shape[1])
    upper_half = stream[middle_row:].reshape(N_BLK, -1, stream.shape[1])[::-1]
    return jnp.concatenate([lower_half, upper_half], axis=1)

def attend_block(key_heads, value_heads, key_pos, key_doc, block_data):
    query_block, query_pos, query_doc = block_data
    scores = low_back(jnp.einsum('qhd,khd->hqk', query_block, key_heads, precision=lax.Precision.HIGHEST) * HEAD_DIM ** (-0.5))
    allowed = (key_pos[None, :] <= query_pos[:, None]) & (key_doc[None, :] == query_doc[:, None])
    scores = jnp.where(allowed[None], scores, -1e+30)
    row_peaks = lax.optimization_barrier(jnp.max(scores, axis=2, keepdims=True))
    weights = jnp.exp(scores - row_peaks)
    weights = weights / lax.optimization_barrier(jnp.sum(weights, axis=2, keepdims=True))
    return jnp.einsum('hqk,khd->qhd', low(weights), value_heads, precision=lax.Precision.HIGHEST)

def layer_forward(params, hidden, documents):
    w_query, w_key, w_value, w_out, w_up, w_gate, w_down, s_qk, s_up, s_gate, alpha_attn, alpha_mlp = params
    length = hidden.shape[0]
    query_raw = low_back(product(hidden, w_query))
    key_raw = low_back(product(hidden, w_key))
    value_raw = low(low_back(product(hidden, w_value)))
    queries = low(head_norm(query_raw) * s_qk)
    key_rows = low(head_norm(key_raw) * s_qk)
    positions = jnp.arange(length, dtype=jnp.int32)
    block_rows = 256
    blocks = length // block_rows
    split_queries = (queries.reshape(blocks, block_rows, HEADS, HEAD_DIM), positions.reshape(blocks, block_rows), documents.reshape(blocks, block_rows))
    attend = jax.checkpoint(partial(attend_block, key_rows.reshape(length, HEADS, HEAD_DIM), value_raw.reshape(length, HEADS, HEAD_DIM), positions, documents))
    attended = lax.map(attend, split_queries).reshape(length, D)
    attended = low(low_back(attended))
    branch = low_back(product(attended, w_out))
    middle = rms_norm(hidden + alpha_attn * (rms_norm(branch) - hidden))
    middle_low = low(middle)
    up_raw = low_back(product(middle_low, w_up))
    gate_raw = low_back(product(middle_low, w_gate))
    inner_act = low(up_raw * s_up * silu_smooth(gate_raw * s_gate))
    mlp_raw = low_back(product(inner_act, w_down))
    return rms_norm(middle + alpha_mlp * (rms_norm(mlp_raw) - middle))

def reference(tokens, cotangent, lengths, w_query, w_key, w_value, w_out, w_up, w_gate, w_down, s_qk, s_up, s_gate, alpha_attn, alpha_mlp):
    params = tuple((argument.astype(jnp.float32) for argument in (w_query, w_key, w_value, w_out, w_up, w_gate, w_down, s_qk, s_up, s_gate, alpha_attn, alpha_mlp)))

    def one_group(grad_sums, group_data):
        hidden, grad_output, group_lengths = group_data
        stream = stream_order(hidden.astype(jnp.float32))
        doc_ends = jnp.cumsum(group_lengths, dtype=jnp.int32)
        positions = jnp.arange(stream.shape[0], dtype=jnp.int32)
        documents = lax.optimization_barrier(jnp.sum((positions[:, None] >= doc_ends[None, :]).astype(jnp.int32), axis=1, dtype=jnp.int32))
        result, pullback = jax.vjp(lambda weights, inputs: layer_forward(weights, inputs, documents), params, stream)
        grad_params, grad_inputs = pullback(stream_order(grad_output.astype(jnp.float32)))
        grad_sums = jax.tree.map(lambda running_sum, new_term: running_sum + new_term, grad_sums, grad_params)
        return (grad_sums, (device_order(result).astype(jnp.bfloat16), device_order(grad_inputs)))
    zero_sums = jax.tree.map(jnp.zeros_like, params)
    grad_sums, (output, input_grad) = lax.scan(one_group, zero_sums, (tokens, cotangent, lengths))
    mean_alpha = 0.5 * (jnp.mean(params[10]) + jnp.mean(params[11]))
    return (output, input_grad, grad_sums[0], grad_sums[1], grad_sums[2], grad_sums[3], grad_sums[4], grad_sums[5], grad_sums[6], grad_sums[7], grad_sums[8], grad_sums[9], grad_sums[10], grad_sums[11], mean_alpha)
```

```python
import functools
import math

import jax
import jax.numpy as jnp
from jax import lax
from jax.experimental import pallas as pl
from jax.experimental.pallas import tpu as pltpu
from jax.sharding import PartitionSpec as P

HEAD_DIM = 64


def rms_norm(vector):
    return vector * lax.rsqrt(jnp.mean(vector * vector, axis=-1, keepdims=True) + 1e-06)


def head_norm(vector, head_count):
    shaped = vector.reshape(vector.shape[0], head_count, -1)
    return rms_norm(shaped).reshape(vector.shape)


def silu_smooth(vector):
    return vector / (1.0 + jnp.exp(-vector))


def residual_mix(inputs, branch, alphas):
    return rms_norm(inputs + alphas * (rms_norm(branch) - inputs))


def gated_inner(up_raw, gate_raw, s_up, s_gate):
    return up_raw * s_up * silu_smooth(gate_raw * s_gate)


def stream_positions(row_index, tok_rows, members):
    half_rows = tok_rows // 2
    device = row_index // tok_rows
    within = row_index % tok_rows
    block_id = jnp.where(within < half_rows, device, 2 * members - 1 - device)
    return block_id * half_rows + within % half_rows


def doc_index(positions, doc_ends):
    return jnp.sum(
        (positions[:, None] >= doc_ends[None, :]).astype(jnp.int32), axis=1, dtype=jnp.int32
    )


def allowed_pairs(query_pos, query_doc, key_pos, key_doc):
    return (key_pos[None, :] <= query_pos[:, None]) & (key_doc[None, :] == query_doc[:, None])


def take_rows(matrix, first_row, row_count):
    return lax.dynamic_slice_in_dim(matrix, first_row, row_count, 0)


def fold_half(running, query_heads, key_heads, value_heads, allowed, score_scale):

    def absorb(carried):
        best_score, total_sum, accumulated = carried
        scores = (
            jnp.einsum("qhd,khd->hqk", query_heads, key_heads, preferred_element_type=jnp.float32)
            * score_scale
        )
        scores = jnp.where(allowed[None], scores, -1e30)
        new_best = jnp.maximum(best_score, jnp.max(scores, axis=2))
        weights = jnp.where(allowed[None], jnp.exp(scores - new_best[:, :, None]), 0.0)
        fade_factor = jnp.exp(best_score - new_best)
        total_sum = jnp.sum(weights, axis=2)
        accumulated = accumulated * fade_factor.T[:, :, None] + jnp.einsum(
            "hqk,khd->qhd",
            weights.astype(jnp.bfloat16),
            value_heads,
            preferred_element_type=jnp.float32,
        )
        return (new_best, total_sum, accumulated)

    return lax.cond(jnp.any(allowed), absorb, lambda carried: carried, running)


def pair_terms(query_side, key_heads, value_heads, allowed, score_scale):
    query_heads, grad_heads, log_total, delta_rows = (
        query_side[0],
        query_side[1],
        query_side[2],
        query_side[3],
    )
    scores = (
        jnp.einsum("qhd,khd->hqk", query_heads, key_heads, preferred_element_type=jnp.float32)
        * score_scale
    )
    scores = jnp.where(allowed[None], scores, -1e30)
    weights = jnp.exp(scores - log_total[:, :, None])
    grad_weights = jnp.einsum(
        "qhd,khd->hqk", grad_heads, value_heads, preferred_element_type=jnp.float32
    )
    grad_scores = (weights * (grad_weights - delta_rows[:, :, None])).astype(jnp.bfloat16)
    return (weights.astype(jnp.bfloat16), grad_scores)


def query_term(query_side, key_heads, value_heads, allowed, score_scale):
    weights, grad_scores = pair_terms(query_side, key_heads, value_heads, allowed, score_scale)
    return score_scale * jnp.einsum(
        "hqk,khd->qhd", grad_scores, key_heads, preferred_element_type=jnp.float32
    )


def key_term(query_side, key_heads, value_heads, allowed, score_scale):
    weights, grad_scores = pair_terms(query_side, key_heads, value_heads, allowed, score_scale)
    grad_keys = score_scale * jnp.einsum(
        "hqk,qhd->khd", grad_scores, query_side[0], preferred_element_type=jnp.float32
    )
    grad_values = jnp.einsum(
        "hqk,qhd->khd", weights, query_side[1], preferred_element_type=jnp.float32
    )
    return (grad_keys, grad_values)


def on_device_general(
    tokens,
    cotangent,
    lengths,
    w_query,
    w_key,
    w_value,
    w_out,
    w_up,
    w_gate,
    w_down,
    s_qk,
    s_up,
    s_gate,
    alpha_attn,
    alpha_mlp,
):
    model_width = w_query.shape[0]
    head_count = model_width // HEAD_DIM
    score_scale = 1.0 / math.sqrt(HEAD_DIM)
    tok_rows = tokens.shape[2]
    half_rows = tok_rows // 2
    members = lax.axis_size("blk")
    position = lax.axis_index("blk")
    doc_ends = jnp.cumsum(lengths[0], dtype=jnp.int32)
    hidden = tokens[0, 0]
    hidden_f = hidden.astype(jnp.float32)

    def key_info(first_row, row_count):
        key_pos = stream_positions(
            first_row + jnp.arange(row_count, dtype=jnp.int32), tok_rows, members
        )
        return (key_pos, doc_index(key_pos, doc_ends))

    def heads_of(matrix):
        return matrix.reshape(matrix.shape[0], head_count, HEAD_DIM)

    def scaled_norm(raw_rows, gain_vector):
        return head_norm(raw_rows, head_count) * gain_vector

    own_pos, own_doc = key_info(position * tok_rows, tok_rows)
    query_raw = jnp.dot(hidden, w_query, preferred_element_type=jnp.float32)
    key_raw = jnp.dot(hidden, w_key, preferred_element_type=jnp.float32)
    value_raw = jnp.dot(hidden, w_value, preferred_element_type=jnp.float32)
    queries = scaled_norm(query_raw, s_qk).astype(jnp.bfloat16)
    key_rows = scaled_norm(key_raw, s_qk).astype(jnp.bfloat16)
    value_rows = value_raw.astype(jnp.bfloat16)
    query_heads = heads_of(queries)

    def empty_state():
        return (
            jnp.full((head_count, half_rows), -1e30, jnp.float32),
            jnp.zeros((head_count, half_rows), jnp.float32),
            jnp.zeros((half_rows, head_count, HEAD_DIM), jnp.float32),
        )

    running = (empty_state(), empty_state())
    key_part = lax.all_gather(key_rows, "blk", axis=0, tiled=True)
    value_part = lax.all_gather(value_rows, "blk", axis=0, tiled=True)
    key_pos, key_doc = key_info(jnp.int32(0), key_part.shape[0])
    updated = []
    for part_index in range(2):
        rows_here = slice(part_index * half_rows, (part_index + 1) * half_rows)
        allowed = allowed_pairs(own_pos[rows_here], own_doc[rows_here], key_pos, key_doc)
        updated.append(
            fold_half(
                running[part_index],
                query_heads[rows_here],
                heads_of(key_part),
                heads_of(value_part),
                allowed,
                score_scale,
            )
        )
    folded = (updated[0], updated[1])
    best_score = jnp.concatenate([folded[0][0], folded[1][0]], axis=1)
    total_sum = jnp.concatenate([folded[0][1], folded[1][1]], axis=1)
    accumulated = jnp.concatenate([folded[0][2], folded[1][2]], axis=0)
    attended = accumulated / total_sum.T[:, :, None]
    log_total = best_score + jnp.log(total_sum)
    attended_low = attended.reshape(tok_rows, model_width).astype(jnp.bfloat16)
    branch = jnp.dot(attended_low, w_out, preferred_element_type=jnp.float32)
    middle = residual_mix(hidden_f, branch, alpha_attn)
    middle_low = middle.astype(jnp.bfloat16)
    up_raw = jnp.dot(middle_low, w_up, preferred_element_type=jnp.float32)
    gate_raw = jnp.dot(middle_low, w_gate, preferred_element_type=jnp.float32)
    inner_low = gated_inner(up_raw, gate_raw, s_up, s_gate).astype(jnp.bfloat16)
    mlp_raw = jnp.dot(inner_low, w_down, preferred_element_type=jnp.float32)
    result = residual_mix(middle, mlp_raw, alpha_mlp)
    mixed_out, pull_out = jax.vjp(residual_mix, middle, mlp_raw, alpha_mlp)
    grad_middle, grad_mlp, grad_alpha_mlp = pull_out(cotangent[0, 0].astype(jnp.float32))
    grad_mlp_low = grad_mlp.astype(jnp.bfloat16)
    grad_w_down = jnp.dot(inner_low.T, grad_mlp_low, preferred_element_type=jnp.float32)
    grad_inner = jnp.dot(grad_mlp_low, w_down.T, preferred_element_type=jnp.float32)
    inner_out, pull_inner = jax.vjp(gated_inner, up_raw, gate_raw, s_up, s_gate)
    grad_up_raw, grad_gate_raw, grad_s_up, grad_s_gate = pull_inner(grad_inner)
    up_low = grad_up_raw.astype(jnp.bfloat16)
    gate_low = grad_gate_raw.astype(jnp.bfloat16)
    grad_w_up = jnp.dot(middle_low.T, up_low, preferred_element_type=jnp.float32)
    grad_w_gate = jnp.dot(middle_low.T, gate_low, preferred_element_type=jnp.float32)
    grad_middle = (
        grad_middle
        + jnp.dot(up_low, w_up.T, preferred_element_type=jnp.float32)
        + jnp.dot(gate_low, w_gate.T, preferred_element_type=jnp.float32)
    )
    attn_out, pull_attn = jax.vjp(residual_mix, hidden_f, branch, alpha_attn)
    grad_hidden, grad_branch, grad_alpha_attn = pull_attn(grad_middle)
    branch_low = grad_branch.astype(jnp.bfloat16)
    grad_w_out = jnp.dot(attended_low.T, branch_low, preferred_element_type=jnp.float32)
    grad_att_low = jnp.dot(branch_low, w_out.T, preferred_element_type=jnp.float32).astype(
        jnp.bfloat16
    )
    grad_heads = heads_of(grad_att_low)
    delta_rows = jnp.sum(grad_heads.astype(jnp.float32) * attended, axis=2).T

    def local_side(part_index):
        rows_here = slice(part_index * half_rows, (part_index + 1) * half_rows)
        return (
            query_heads[rows_here],
            grad_heads[rows_here],
            log_total[:, rows_here],
            delta_rows[:, rows_here],
            own_pos[rows_here],
            own_doc[rows_here],
        )

    local_parts = (local_side(0), local_side(1))
    whole_keys, whole_values = (
        lax.all_gather(key_rows, "blk", axis=0, tiled=True),
        lax.all_gather(value_rows, "blk", axis=0, tiled=True),
    )

    def query_step(grad_parts, shard_index):
        first_row = shard_index * tok_rows
        key_part = heads_of(take_rows(whole_keys, first_row, tok_rows))
        value_part = heads_of(take_rows(whole_values, first_row, tok_rows))
        key_pos, key_doc = key_info(first_row, tok_rows)
        updated = []
        for part_index in range(2):
            query_side = local_parts[part_index]
            allowed = allowed_pairs(query_side[4], query_side[5], key_pos, key_doc)

            def add_term(grad_now):
                return grad_now + query_term(query_side, key_part, value_part, allowed, score_scale)

            updated.append(
                lax.cond(
                    jnp.any(allowed), add_term, lambda grad_now: grad_now, grad_parts[part_index]
                )
            )
        return ((updated[0], updated[1]), None)

    zero_part = jnp.zeros((half_rows, head_count, HEAD_DIM), jnp.float32)
    grad_parts, unused_out = lax.scan(
        query_step, (zero_part, zero_part), jnp.arange(members, dtype=jnp.int32)
    )
    grad_queries = jnp.concatenate(grad_parts, axis=0).reshape(tok_rows, model_width)
    first_row = jnp.int32(0)
    row_count = lax.axis_size("blk") * tok_rows
    key_part = heads_of(take_rows(whole_keys, first_row, row_count))
    value_part = heads_of(take_rows(whole_values, first_row, row_count))
    key_pos, key_doc = key_info(first_row, row_count)
    zero_keys = jnp.zeros((row_count, head_count, HEAD_DIM), jnp.float32)
    totals = (zero_keys, zero_keys)
    for part_index in range(2):
        query_side = local_parts[part_index]
        allowed = allowed_pairs(query_side[4], query_side[5], key_pos, key_doc)

        def add_terms(grad_now):
            grad_keys, grad_values = key_term(
                query_side, key_part, value_part, allowed, score_scale
            )
            return (grad_now[0] + grad_keys, grad_now[1] + grad_values)

        totals = lax.cond(jnp.any(allowed), add_terms, lambda grad_now: grad_now, totals)
    key_value_grads = lax.psum_scatter(
        jnp.concatenate(
            [totals[0].reshape(row_count, model_width), totals[1].reshape(row_count, model_width)],
            axis=1,
        ),
        "blk",
        scatter_dimension=0,
        tiled=True,
    )
    grad_keys = key_value_grads[:, :model_width]
    grad_values = key_value_grads[:, model_width:]
    query_out, pull_query = jax.vjp(scaled_norm, query_raw, s_qk)
    grad_query_raw, grad_qk_first = pull_query(grad_queries)
    key_out, pull_key = jax.vjp(scaled_norm, key_raw, s_qk)
    grad_key_raw, grad_qk_second = pull_key(grad_keys)
    grad_s_qk = grad_qk_first + grad_qk_second
    query_low = grad_query_raw.astype(jnp.bfloat16)
    key_low = grad_key_raw.astype(jnp.bfloat16)
    value_low = grad_values.astype(jnp.bfloat16)
    grad_w_query = jnp.dot(hidden.T, query_low, preferred_element_type=jnp.float32)
    grad_w_key = jnp.dot(hidden.T, key_low, preferred_element_type=jnp.float32)
    grad_w_value = jnp.dot(hidden.T, value_low, preferred_element_type=jnp.float32)
    input_grad = (
        grad_hidden
        + jnp.dot(query_low, w_query.T, preferred_element_type=jnp.float32)
        + jnp.dot(key_low, w_key.T, preferred_element_type=jnp.float32)
        + jnp.dot(value_low, w_value.T, preferred_element_type=jnp.float32)
    )
    summed = (
        lax.psum_scatter(grad_w_query, ("dp", "blk"), scatter_dimension=0, tiled=True),
        lax.psum_scatter(grad_w_key, ("dp", "blk"), scatter_dimension=0, tiled=True),
        lax.psum_scatter(grad_w_value, ("dp", "blk"), scatter_dimension=0, tiled=True),
        lax.psum_scatter(grad_w_out, ("dp", "blk"), scatter_dimension=0, tiled=True),
        lax.psum_scatter(grad_w_up, ("dp", "blk"), scatter_dimension=0, tiled=True),
        lax.psum_scatter(grad_w_gate, ("dp", "blk"), scatter_dimension=0, tiled=True),
        lax.psum_scatter(grad_w_down, ("dp", "blk"), scatter_dimension=0, tiled=True),
        lax.psum_scatter(grad_s_qk, ("dp", "blk"), scatter_dimension=0, tiled=True),
        lax.psum_scatter(grad_s_up, ("dp", "blk"), scatter_dimension=0, tiled=True),
        lax.psum_scatter(grad_s_gate, ("dp", "blk"), scatter_dimension=0, tiled=True),
        lax.psum_scatter(grad_alpha_attn, ("dp", "blk"), scatter_dimension=0, tiled=True),
        lax.psum_scatter(grad_alpha_mlp, ("dp", "blk"), scatter_dimension=0, tiled=True),
    )
    mean_alpha = 0.5 * (jnp.mean(alpha_attn) + jnp.mean(alpha_mlp))
    output = result.astype(jnp.bfloat16)[None, None]
    return (
        output,
        input_grad[None, None],
        summed[0],
        summed[1],
        summed[2],
        summed[3],
        summed[4],
        summed[5],
        summed[6],
        summed[7],
        summed[8],
        summed[9],
        summed[10],
        summed[11],
        mean_alpha,
    )


MESH = pl.DeviceIdType.MESH
VMEM_SPEC = pl.BlockSpec(memory_space=pltpu.VMEM)
VMEM_LIMIT = 56 << 20
GROUP = 16


def here():
    return lax.axis_index("dp"), lax.axis_index("blk")


def greet(partners):
    barrier = pltpu.get_barrier_semaphore()
    for partner in partners:
        pl.semaphore_signal(barrier, inc=1, device_id=partner, device_id_type=MESH)
    pl.semaphore_wait(barrier, len(partners))


def remote(src, dst, send_sem, recv_sem, device):
    return pltpu.make_async_remote_copy(
        src_ref=src,
        dst_ref=dst,
        send_sem=send_sem,
        recv_sem=recv_sem,
        device_id=device,
        device_id_type=MESH,
    )


class Gather:
    CLASSES = 15

    def __init__(self, own, out, send, recv):
        self.own, self.out, self.send, self.recv = own, out, send, recv
        dp, b = here()
        self.z, self.y, self.c = b // 4, (b // 2) % 2, b % 2
        self.up = (dp, self.block(1, 0))
        self.down = (dp, self.block(3, 0))
        self.side = (dp, self.block(0, 1))
        self.sib = (dp, b + 1 - 2 * self.c)
        self.b = b

    def block(self, dz, dy):
        return (((self.z + dz) % 4) * 2 + (self.y + dy) % 2) * 2 + self.c

    def slot(self, block, half):
        return 2 * GROUP - 1 - block if half else block

    def copy(self, block, kind, half, device, own=False):
        place = self.slot(block, half)
        source = self.own.at[half] if own else self.out.at[place]
        index = 2 * kind + half
        return remote(source, self.out.at[place], self.send.at[index], self.recv.at[index], device)

    def partners(self):
        return [self.up, self.down, self.side, self.sib]

    KINDS = {
        0: (0, 1, (0, 1)),
        1: (3, 0, (0, 1)),
        2: (1, 0, (0, 1)),
        3: (3, 1, (0, 1)),
        4: (1, 1, (0, 1)),
        5: (2, 0, (0, 1)),
        6: (2, 1, (0, 1)),
    }

    def start(self):
        for half in (0, 1):
            self.copy(self.b, 1, half, self.up, True).start()
            self.copy(self.b, 2, half, self.down, True).start()
            self.copy(self.b, 0, half, self.side, True).start()
        for half in (0, 1):
            self.copy(self.b, 7, half, self.sib, True).start()
        for half in (0, 1):
            self.out[self.slot(self.b, half)] = self.own[half]

    def arrive(self, kind):
        dz, dy, halves = self.KINDS[kind]
        block = self.block(dz, dy)
        for half in halves:
            self.copy(block, kind, half, self.sib).wait_recv()
            if kind == 0:
                self.copy(block, 3, half, self.up).start()
                self.copy(block, 4, half, self.down).start()
            if kind == 1 and half == 0:
                self.copy(block, 5, half, self.up).start()
            if kind == 2 and half == 1:
                self.copy(block, 5, half, self.down).start()
            if kind == 5:
                self.copy(block, 6, half, self.side).start()
            self.copy(block, 8 + kind, half, self.sib).start()

    def first(self):
        for kind in (0, 1, 2):
            self.arrive(kind)

    def second(self):
        for kind in (5, 3, 4):
            self.arrive(kind)

    def last(self):
        self.arrive(6)
        for kind in range(7):
            dz, dy, halves = self.KINDS[kind]
            other = self.block(dz, dy) + 1 - 2 * self.c
            for half in halves:
                self.copy(other, 8 + kind, half, self.sib).wait_recv()
        for half in (0, 1):
            self.copy(self.b + 1 - 2 * self.c, 7, half, self.sib).wait_recv()
        for kind in range(self.CLASSES):
            for half in (0, 1):
                self.copy(self.b, kind, half, self.sib).wait_send()


def gather_kernel(own, out, send, recv):
    gather = Gather(own, out, send, recv)
    greet(gather.partners())
    gather.start()
    gather.first()
    gather.second()
    gather.last()


def comm_params(collective_id):
    return pltpu.CompilerParams(
        collective_id=collective_id, has_side_effects=True, vmem_limit_bytes=VMEM_LIMIT
    )


def all_gather_group(rows, collective_id):
    tok_rows, width = rows.shape
    gathered = pl.pallas_call(
        gather_kernel,
        out_shape=jax.ShapeDtypeStruct((2 * GROUP, tok_rows // 2, width), rows.dtype),
        in_specs=[VMEM_SPEC],
        out_specs=VMEM_SPEC,
        scratch_shapes=[
            pltpu.SemaphoreType.DMA((2 * Gather.CLASSES,)),
            pltpu.SemaphoreType.DMA((2 * Gather.CLASSES,)),
        ],
        compiler_params=comm_params(collective_id),
        name="gather_group",
    )(rows.reshape(2, tok_rows // 2, width))
    return gathered.reshape(GROUP * tok_rows, width)


def swap_group_kernel(blocks, out, send, recv):
    dp, b = here()
    greet([(dp, (b + step) % GROUP) for step in range(1, GROUP)])
    copies = []
    for step in range(1, GROUP):
        target = (b + step) % GROUP
        copies.append(
            remote(blocks.at[target], out.at[b], send.at[step], recv.at[step], (dp, target))
        )
        copies[-1].start()
    out[b] = blocks[b]
    for copy in copies:
        copy.wait()


def swap_group(blocks, collective_id):
    return pl.pallas_call(
        swap_group_kernel,
        out_shape=jax.ShapeDtypeStruct(blocks.shape, blocks.dtype),
        in_specs=[VMEM_SPEC],
        out_specs=VMEM_SPEC,
        scratch_shapes=[
            pltpu.SemaphoreType.DMA((GROUP,)),
            pltpu.SemaphoreType.DMA((GROUP,)),
        ],
        compiler_params=comm_params(collective_id),
        name="swap_group",
    )(blocks)


def swap_dp_kernel(count, *refs):
    blocks, outs, send, recv = refs[:count], refs[count : 2 * count], refs[-2], refs[-1]
    dp, b = here()
    greet([(1 - dp, b)])
    copies = [
        remote(blocks[i], outs[i], send.at[i], recv.at[i], (1 - dp, b)) for i in range(count)
    ]
    for copy in copies:
        copy.start()
    for copy in copies:
        copy.wait()


def swap_dp(blocks, collective_id):
    count = len(blocks)
    return pl.pallas_call(
        functools.partial(swap_dp_kernel, count),
        out_shape=[jax.ShapeDtypeStruct(block.shape, block.dtype) for block in blocks],
        in_specs=[VMEM_SPEC] * count,
        out_specs=[VMEM_SPEC] * count,
        scratch_shapes=[
            pltpu.SemaphoreType.DMA((count,)),
            pltpu.SemaphoreType.DMA((count,)),
        ],
        compiler_params=comm_params(collective_id),
        name="swap_dp",
    )(*blocks)


def swap_all_kernel(blocks, out, send, recv):
    dp, b = here()
    me = dp * GROUP + b
    total = 2 * GROUP
    targets = [(me + step) % total for step in range(1, total)]
    greet([(target // GROUP, target % GROUP) for target in targets])
    copies = []
    for step, target in enumerate(targets):
        copies.append(
            remote(
                blocks.at[target],
                out.at[me],
                send.at[step],
                recv.at[step],
                (target // GROUP, target % GROUP),
            )
        )
        copies[-1].start()
    out[me] = blocks[me]
    for copy in copies:
        copy.wait()


def swap_all(blocks, collective_id):
    return pl.pallas_call(
        swap_all_kernel,
        out_shape=jax.ShapeDtypeStruct(blocks.shape, blocks.dtype),
        in_specs=[VMEM_SPEC],
        out_specs=VMEM_SPEC,
        scratch_shapes=[
            pltpu.SemaphoreType.DMA((2 * GROUP,)),
            pltpu.SemaphoreType.DMA((2 * GROUP,)),
        ],
        compiler_params=comm_params(collective_id),
        name="swap_all",
    )(blocks)


ATT = 256


def dot_nt(left, right):
    return lax.dot_general(left, right, (((1,), (1,)), ((), ())), preferred_element_type=jnp.float32)


def dot_tn(left, right):
    return lax.dot_general(left, right, (((0,), (0,)), ((), ())), preferred_element_type=jnp.float32)


def dot_nn(left, right):
    return jnp.dot(left, right, preferred_element_type=jnp.float32)


def attend_kernel(first_ref, q_ref, k_ref, v_ref, start_ref, o_ref, l_ref):
    length = q_ref.shape[0]
    for query_block in range(length // ATT):
        rows = pl.ds(query_block * ATT, ATT)
        queries = q_ref[rows, :]
        doc_start = start_ref[rows, :]
        query_pos = query_block * ATT + lax.broadcasted_iota(jnp.int32, (ATT, ATT), 0)
        key_lane = lax.broadcasted_iota(jnp.int32, (ATT, ATT), 1)

        def step(key_block, total):
            base = pl.multiple_of(key_block * ATT, ATT)
            keys = k_ref[pl.ds(base, ATT), :]
            values = v_ref[pl.ds(base, ATT), :]
            key_pos = base + key_lane
            allowed = (key_pos <= query_pos) & (key_pos >= doc_start)
            weights = jnp.where(allowed, jnp.exp(dot_nt(queries, keys)), 0.0)
            return total + dot_nn(weights.astype(jnp.bfloat16), values)

        total = lax.fori_loop(
            first_ref[query_block], query_block + 1, step, jnp.zeros((ATT, 128), jnp.float32)
        )
        row_sum = total[:, HEAD_DIM : HEAD_DIM + 1]
        o_ref[rows, :] = total[:, :HEAD_DIM] / row_sum
        l_ref[rows, :] = jnp.log(row_sum)


def attend_grad_kernel(last_ref, q_ref, k_ref, v_ref, g_ref, start_ref, dq_ref, dk_ref, dv_ref):
    length = q_ref.shape[0]
    dq_ref[...] = jnp.zeros_like(dq_ref)
    key_row = lax.broadcasted_iota(jnp.int32, (ATT, ATT), 0)
    query_lane = lax.broadcasted_iota(jnp.int32, (ATT, ATT), 1)
    for key_block in range(length // ATT):
        rows = pl.ds(key_block * ATT, ATT)
        keys = k_ref[rows, :]
        values = v_ref[rows, :]
        key_pos = key_block * ATT + key_row

        def step(query_block, carried):
            dk, dv = carried
            base = pl.multiple_of(query_block * ATT, ATT)
            queries = q_ref[pl.ds(base, ATT), :]
            grads = g_ref[pl.ds(base, ATT), :]
            doc_start = start_ref[pl.ds(query_block, 1), :]
            allowed = (key_pos <= base + query_lane) & (key_pos >= doc_start)
            weights = jnp.where(allowed, jnp.exp(dot_nt(keys, queries)), 0.0)
            slopes = (weights * dot_nt(values, grads)).astype(jnp.bfloat16)
            dv = dv + dot_nn(weights.astype(jnp.bfloat16), grads)
            dk = dk + dot_nn(slopes, queries)
            dq_ref[pl.ds(base, ATT), :] += dot_tn(slopes, keys)
            return dk, dv

        zero = jnp.zeros((ATT, 128), jnp.float32)
        dk, dv = lax.fori_loop(key_block, last_ref[key_block], step, (zero, zero))
        dk_ref[rows, :] = dk
        dv_ref[rows, :] = dv


SMEM_SPEC = pl.BlockSpec(memory_space=pltpu.SMEM)


def split_three(column):
    high = column.astype(jnp.bfloat16)
    rest = column - high.astype(jnp.float32)
    mid = rest.astype(jnp.bfloat16)
    low = (rest - mid.astype(jnp.float32)).astype(jnp.bfloat16)
    return [high, mid, low]


def widened(matrix, columns):
    joined = jnp.concatenate([matrix] + columns, axis=1)
    return jnp.pad(joined, ((0, 0), (0, 128 - joined.shape[1])))


def pack_stream(stream):
    half = stream.shape[0] // 2
    lower = stream[:half].reshape(GROUP, half // GROUP, -1)
    upper = stream[half:].reshape(GROUP, half // GROUP, -1)[::-1]
    return jnp.concatenate([lower, upper], axis=2)


def unpack_rows(blocks):
    width = blocks.shape[2] // 2
    return jnp.concatenate(
        [blocks[:, :, :width].transpose(1, 0, 2), blocks[:, :, width:].transpose(1, 0, 2)], axis=0
    )


def pack_rows(rows):
    half = rows.shape[0] // 2
    return jnp.concatenate(
        [
            rows[:half].reshape(half, GROUP, -1).transpose(1, 0, 2),
            rows[half:].reshape(half, GROUP, -1).transpose(1, 0, 2),
        ],
        axis=2,
    )


def unpack_stream(blocks):
    width = blocks.shape[2] // 2
    lower = blocks[:, :, :width].reshape(-1, width)
    upper = blocks[::-1, :, width:].reshape(-1, width)
    return jnp.concatenate([lower, upper], axis=0)


def on_device_heads(
    tokens,
    cotangent,
    lengths,
    w_query,
    w_key,
    w_value,
    w_out,
    w_up,
    w_gate,
    w_down,
    s_qk,
    s_up,
    s_gate,
    alpha_attn,
    alpha_mlp,
):
    low = jnp.bfloat16
    model_width = w_query.shape[0]
    tok_rows = tokens.shape[2]
    length = GROUP * tok_rows
    dp, b = here()
    score_scale = 1.0 / math.sqrt(HEAD_DIM)
    hidden = tokens[0, 0]
    hidden_f = hidden.astype(jnp.float32)
    positions = jnp.arange(length, dtype=jnp.int32)
    doc_ends = jnp.cumsum(lengths[0], dtype=jnp.int32)
    doc_starts = doc_ends - lengths[0]
    document = doc_index(positions, doc_ends)
    member = document[:, None] == jnp.arange(lengths.shape[1], dtype=jnp.int32)[None]
    start_of = jnp.sum(jnp.where(member, doc_starts[None], 0), axis=1, dtype=jnp.int32)
    end_of = jnp.sum(jnp.where(member, doc_ends[None], 0), axis=1, dtype=jnp.int32)
    blocks = length // ATT
    first_block = start_of[::ATT] // ATT
    last_block = (end_of[ATT - 1 :: ATT] + ATT - 1) // ATT

    hidden_all = all_gather_group(hidden, 0)
    head_col = b * HEAD_DIM

    def head_slice(weight):
        return lax.dynamic_slice_in_dim(weight, head_col, HEAD_DIM, 1)

    gain = lax.dynamic_slice_in_dim(s_qk, head_col, HEAD_DIM, 0)
    w_head = jnp.concatenate([head_slice(w_query), head_slice(w_key), head_slice(w_value)], axis=1)
    raw = dot_nn(hidden_all, w_head)
    query_raw, key_raw, value_raw = (
        raw[:, :HEAD_DIM],
        raw[:, HEAD_DIM : 2 * HEAD_DIM],
        raw[:, 2 * HEAD_DIM :],
    )

    def scaled_norm(raw_rows, gain_vector):
        return rms_norm(raw_rows) * gain_vector

    queries = scaled_norm(query_raw, gain).astype(low)
    keys = scaled_norm(key_raw, gain).astype(low)
    values = value_raw.astype(low)
    scaled_queries = queries * jnp.asarray(score_scale, low)
    ones = jnp.ones((length, 1), low)
    attended_head, log_total = pl.pallas_call(
        attend_kernel,
        out_shape=[
            jax.ShapeDtypeStruct((length, HEAD_DIM), jnp.float32),
            jax.ShapeDtypeStruct((length, 1), jnp.float32),
        ],
        in_specs=[SMEM_SPEC] + [VMEM_SPEC] * 4,
        out_specs=[VMEM_SPEC] * 2,
        compiler_params=pltpu.CompilerParams(vmem_limit_bytes=VMEM_LIMIT),
        name="attend",
    )(first_block, scaled_queries, keys, widened(values, [ones]), start_of[:, None])
    attended_head_low = attended_head.astype(low)

    attended_low = unpack_rows(swap_group(pack_stream(attended_head_low), 1)).reshape(
        tok_rows, model_width
    )
    branch = dot_nn(attended_low, w_out)
    middle, pull_attn = jax.vjp(residual_mix, hidden_f, branch, alpha_attn)
    middle_low = middle.astype(low)
    up_raw = dot_nn(middle_low, w_up)
    gate_raw = dot_nn(middle_low, w_gate)
    inner_low = gated_inner(up_raw, gate_raw, s_up, s_gate).astype(low)
    mlp_raw = dot_nn(inner_low, w_down)
    result, pull_out = jax.vjp(residual_mix, middle, mlp_raw, alpha_mlp)
    grad_middle, grad_mlp, grad_alpha_mlp = pull_out(cotangent[0, 0].astype(jnp.float32))
    grad_mlp_low = grad_mlp.astype(low)
    grad_inner = dot_nt(grad_mlp_low, w_down)
    _, pull_inner = jax.vjp(lambda u, g: gated_inner(u, g, s_up, s_gate), up_raw, gate_raw)
    grad_up_raw, grad_gate_raw = pull_inner(grad_inner)
    grad_middle = (
        grad_middle
        + dot_nt(grad_up_raw.astype(low), w_up)
        + dot_nt(grad_gate_raw.astype(low), w_gate)
    )
    grad_hidden, grad_branch, grad_alpha_attn = pull_attn(grad_middle)
    branch_low = grad_branch.astype(low)
    grad_att_low = dot_nt(branch_low, w_out).astype(low)

    grad_head = unpack_stream(swap_group(pack_rows(grad_att_low), 2))
    delta = jnp.sum(grad_head.astype(jnp.float32) * attended_head, axis=1, keepdims=True)
    minus = [-ones] * 3
    dq, dk, dv = pl.pallas_call(
        attend_grad_kernel,
        out_shape=[jax.ShapeDtypeStruct((length, 128), jnp.float32)] * 3,
        in_specs=[SMEM_SPEC] + [VMEM_SPEC] * 5,
        out_specs=[VMEM_SPEC] * 3,
        compiler_params=pltpu.CompilerParams(vmem_limit_bytes=VMEM_LIMIT),
        name="attend_grad",
    )(
        last_block,
        widened(scaled_queries, split_three(log_total)),
        widened(keys, minus),
        widened(values, minus),
        widened(grad_head, split_three(delta)),
        start_of.reshape(blocks, ATT),
    )
    grad_queries = dq[:, :HEAD_DIM] * score_scale
    grad_keys = dk[:, :HEAD_DIM]
    grad_values = dv[:, :HEAD_DIM]
    _, pull_query = jax.vjp(scaled_norm, query_raw, gain)
    grad_query_raw, grad_qk_first = pull_query(grad_queries)
    _, pull_key = jax.vjp(scaled_norm, key_raw, gain)
    grad_key_raw, grad_qk_second = pull_key(grad_keys)
    grad_s_qk = grad_qk_first + grad_qk_second
    raw_low = jnp.concatenate([grad_query_raw, grad_key_raw, grad_values], axis=1).astype(low)
    home = swap_group(pack_stream(raw_low), 3)
    home = unpack_rows(home)

    def home_part(index):
        return home[:, :, index * HEAD_DIM : (index + 1) * HEAD_DIM].reshape(tok_rows, model_width)

    input_grad = (
        grad_hidden
        + dot_nt(home_part(0), w_query)
        + dot_nt(home_part(1), w_key)
        + dot_nt(home_part(2), w_value)
    )

    middle_all = all_gather_group(middle_low, 4)
    mlp_all = all_gather_group(grad_mlp_low, 5)
    branch_all = all_gather_group(branch_low, 6)
    ff_part = w_up.shape[1] // (2 * GROUP)
    ff_half = w_up.shape[1] // 2

    def ff_slice(array, axis):
        return jnp.concatenate(
            [
                lax.dynamic_slice_in_dim(array, b * ff_part, ff_part, axis),
                lax.dynamic_slice_in_dim(array, ff_half + b * ff_part, ff_part, axis),
            ],
            axis=axis,
        )

    up_part = dot_nn(middle_all, ff_slice(w_up, 1))
    gate_part = dot_nn(middle_all, ff_slice(w_gate, 1))
    inner_grad_part = dot_nt(mlp_all, ff_slice(w_down, 0))
    inner_part, pull_part = jax.vjp(
        gated_inner, up_part, gate_part, ff_slice(s_up, 0), ff_slice(s_gate, 0)
    )
    g_up, g_gate, g_s_up, g_s_gate = pull_part(inner_grad_part)
    part_down = dot_tn(inner_part.astype(low), mlp_all)
    part_up = dot_tn(middle_all, g_up.astype(low))
    part_gate = dot_tn(middle_all, g_gate.astype(low))
    part_qkv = dot_tn(hidden_all, raw_low)
    part_out = dot_tn(attended_head_low, branch_all)

    part_wide = jnp.concatenate(
        [part_up, part_gate, part_qkv, jnp.zeros((model_width, 64), jnp.float32)], axis=1
    )
    half_width = model_width // 2

    def mine(array, size, axis=0):
        return lax.dynamic_slice_in_dim(array, dp * size, size, axis)

    def other(array, size, axis=0):
        return lax.dynamic_slice_in_dim(array, (1 - dp) * size, size, axis)

    got_wide, got_down, got_out = swap_dp(
        [other(part_wide, half_width).astype(low), other(part_down, ff_part).astype(low), part_out.astype(low)],
        7,
    )
    grad_down = mine(part_down, ff_part) + got_down
    wide = (mine(part_wide, half_width) + got_wide).astype(low)
    out_rows = part_out + got_out
    wide = wide.reshape(GROUP, half_width // GROUP, -1)
    got = swap_group(wide, 8)
    grad_up = jnp.concatenate(
        [got[:, :, i * ff_part : (i + 1) * ff_part].transpose(1, 0, 2).reshape(-1, ff_half) for i in (0, 1)],
        axis=1,
    ).astype(jnp.float32)
    grad_gate = jnp.concatenate(
        [got[:, :, i * ff_part : (i + 1) * ff_part].transpose(1, 0, 2).reshape(-1, ff_half) for i in (2, 3)],
        axis=1,
    ).astype(jnp.float32)
    base = 4 * ff_part
    grad_query, grad_key, grad_value = (
        got[:, :, base + i * HEAD_DIM : base + (i + 1) * HEAD_DIM]
        .transpose(1, 0, 2)
        .reshape(-1, model_width)
        .astype(jnp.float32)
        for i in range(3)
    )
    out_all = lax.all_gather(out_rows, "blk", axis=0, tiled=True)
    rows_out = model_width // (2 * GROUP)
    grad_out = lax.dynamic_slice_in_dim(out_all, (dp * GROUP + b) * rows_out, rows_out, 0)

    def vector_rows(vector):
        rows = vector.reshape(2 * GROUP, -1)
        return jnp.pad(rows, ((0, 0), (0, 128 - rows.shape[1])))

    def placed(part, total):
        full = jnp.zeros((total,), jnp.float32)
        return full, part

    s_full = jnp.zeros((model_width,), jnp.float32)
    s_full = lax.dynamic_update_slice_in_dim(s_full, grad_s_qk, head_col, 0)

    def ff_full(part):
        full = jnp.zeros((w_up.shape[1],), jnp.float32)
        full = lax.dynamic_update_slice_in_dim(full, part[:ff_part], b * ff_part, 0)
        return lax.dynamic_update_slice_in_dim(full, part[ff_part:], ff_half + b * ff_part, 0)

    small = jnp.stack(
        [
            vector_rows(s_full),
            vector_rows(ff_full(g_s_up)),
            vector_rows(ff_full(g_s_gate)),
            vector_rows(grad_alpha_attn),
            vector_rows(grad_alpha_mlp),
        ],
        axis=1,
    )
    small = jnp.pad(small, ((0, 0), (0, 3), (0, 0)))
    small = jnp.sum(swap_all(small, 9), axis=0)
    mean_alpha = 0.5 * (jnp.mean(alpha_attn) + jnp.mean(alpha_mlp))
    return (
        result.astype(low)[None, None],
        input_grad[None, None],
        grad_query,
        grad_key,
        grad_value,
        grad_out,
        grad_up,
        grad_gate,
        grad_down,
        small[0, :rows_out],
        small[1],
        small[2],
        small[3, :rows_out],
        small[4, :rows_out],
        mean_alpha,
    )


def on_device(*arrays):
    head_count = arrays[3].shape[0] // HEAD_DIM
    tok_rows = arrays[0].shape[2]
    fits = lax.axis_size("blk") == head_count == 16 and lax.axis_size("dp") == 2
    if fits and tok_rows == 128:
        return on_device_heads(*arrays)
    return on_device_general(*arrays)


def solution(mesh):
    in_specs = (
        P("dp", "blk", None, None),
        P("dp", "blk", None, None),
        P("dp", None),
        P(),
        P(),
        P(),
        P(),
        P(),
        P(),
        P(),
        P(),
        P(),
        P(),
        P(),
        P(),
    )
    out_specs = (
        P("dp", "blk", None, None),
        P("dp", "blk", None, None),
        P(("dp", "blk"), None),
        P(("dp", "blk"), None),
        P(("dp", "blk"), None),
        P(("dp", "blk"), None),
        P(("dp", "blk"), None),
        P(("dp", "blk"), None),
        P(("dp", "blk"), None),
        P(("dp", "blk")),
        P(("dp", "blk")),
        P(("dp", "blk")),
        P(("dp", "blk")),
        P(("dp", "blk")),
        P(),
    )
    return jax.shard_map(
        on_device, mesh=mesh, in_specs=in_specs, out_specs=out_specs, check_vma=False
    )
```

```python
import functools
import math

import jax
import jax.numpy as jnp
from jax import lax
from jax.experimental import pallas as pl
from jax.experimental.pallas import tpu as pltpu
from jax.sharding import PartitionSpec as P

HEAD_DIM = 64


def rms_norm(vector):
    return vector * lax.rsqrt(jnp.mean(vector * vector, axis=-1, keepdims=True) + 1e-06)


def head_norm(vector, head_count):
    shaped = vector.reshape(vector.shape[0], head_count, -1)
    return rms_norm(shaped).reshape(vector.shape)


def silu_smooth(vector):
    return vector / (1.0 + jnp.exp(-vector))


def residual_mix(inputs, branch, alphas):
    return rms_norm(inputs + alphas * (rms_norm(branch) - inputs))


def gated_inner(up_raw, gate_raw, s_up, s_gate):
    return up_raw * s_up * silu_smooth(gate_raw * s_gate)


def stream_positions(row_index, tok_rows, members):
    half_rows = tok_rows // 2
    device = row_index // tok_rows
    within = row_index % tok_rows
    block_id = jnp.where(within < half_rows, device, 2 * members - 1 - device)
    return block_id * half_rows + within % half_rows


def doc_index(positions, doc_ends):
    return jnp.sum(
        (positions[:, None] >= doc_ends[None, :]).astype(jnp.int32), axis=1, dtype=jnp.int32
    )


def allowed_pairs(query_pos, query_doc, key_pos, key_doc):
    return (key_pos[None, :] <= query_pos[:, None]) & (key_doc[None, :] == query_doc[:, None])


def take_rows(matrix, first_row, row_count):
    return lax.dynamic_slice_in_dim(matrix, first_row, row_count, 0)


def fold_half(running, query_heads, key_heads, value_heads, allowed, score_scale):

    def absorb(carried):
        best_score, total_sum, accumulated = carried
        scores = (
            jnp.einsum("qhd,khd->hqk", query_heads, key_heads, preferred_element_type=jnp.float32)
            * score_scale
        )
        scores = jnp.where(allowed[None], scores, -1e30)
        new_best = jnp.maximum(best_score, jnp.max(scores, axis=2))
        weights = jnp.where(allowed[None], jnp.exp(scores - new_best[:, :, None]), 0.0)
        fade_factor = jnp.exp(best_score - new_best)
        total_sum = jnp.sum(weights, axis=2)
        accumulated = accumulated * fade_factor.T[:, :, None] + jnp.einsum(
            "hqk,khd->qhd",
            weights.astype(jnp.bfloat16),
            value_heads,
            preferred_element_type=jnp.float32,
        )
        return (new_best, total_sum, accumulated)

    return lax.cond(jnp.any(allowed), absorb, lambda carried: carried, running)


def pair_terms(query_side, key_heads, value_heads, allowed, score_scale):
    query_heads, grad_heads, log_total, delta_rows = (
        query_side[0],
        query_side[1],
        query_side[2],
        query_side[3],
    )
    scores = (
        jnp.einsum("qhd,khd->hqk", query_heads, key_heads, preferred_element_type=jnp.float32)
        * score_scale
    )
    scores = jnp.where(allowed[None], scores, -1e30)
    weights = jnp.exp(scores - log_total[:, :, None])
    grad_weights = jnp.einsum(
        "qhd,khd->hqk", grad_heads, value_heads, preferred_element_type=jnp.float32
    )
    grad_scores = (weights * (grad_weights - delta_rows[:, :, None])).astype(jnp.bfloat16)
    return (weights.astype(jnp.bfloat16), grad_scores)


def query_term(query_side, key_heads, value_heads, allowed, score_scale):
    weights, grad_scores = pair_terms(query_side, key_heads, value_heads, allowed, score_scale)
    return score_scale * jnp.einsum(
        "hqk,khd->qhd", grad_scores, key_heads, preferred_element_type=jnp.float32
    )


def key_term(query_side, key_heads, value_heads, allowed, score_scale):
    weights, grad_scores = pair_terms(query_side, key_heads, value_heads, allowed, score_scale)
    grad_keys = score_scale * jnp.einsum(
        "hqk,qhd->khd", grad_scores, query_side[0], preferred_element_type=jnp.float32
    )
    grad_values = jnp.einsum(
        "hqk,qhd->khd", weights, query_side[1], preferred_element_type=jnp.float32
    )
    return (grad_keys, grad_values)


def on_device_general(
    tokens,
    cotangent,
    lengths,
    w_query,
    w_key,
    w_value,
    w_out,
    w_up,
    w_gate,
    w_down,
    s_qk,
    s_up,
    s_gate,
    alpha_attn,
    alpha_mlp,
):
    model_width = w_query.shape[0]
    head_count = model_width // HEAD_DIM
    score_scale = 1.0 / math.sqrt(HEAD_DIM)
    tok_rows = tokens.shape[2]
    half_rows = tok_rows // 2
    members = lax.axis_size("blk")
    position = lax.axis_index("blk")
    doc_ends = jnp.cumsum(lengths[0], dtype=jnp.int32)
    hidden = tokens[0, 0]
    hidden_f = hidden.astype(jnp.float32)

    def key_info(first_row, row_count):
        key_pos = stream_positions(
            first_row + jnp.arange(row_count, dtype=jnp.int32), tok_rows, members
        )
        return (key_pos, doc_index(key_pos, doc_ends))

    def heads_of(matrix):
        return matrix.reshape(matrix.shape[0], head_count, HEAD_DIM)

    def scaled_norm(raw_rows, gain_vector):
        return head_norm(raw_rows, head_count) * gain_vector

    own_pos, own_doc = key_info(position * tok_rows, tok_rows)
    query_raw = jnp.dot(hidden, w_query, preferred_element_type=jnp.float32)
    key_raw = jnp.dot(hidden, w_key, preferred_element_type=jnp.float32)
    value_raw = jnp.dot(hidden, w_value, preferred_element_type=jnp.float32)
    queries = scaled_norm(query_raw, s_qk).astype(jnp.bfloat16)
    key_rows = scaled_norm(key_raw, s_qk).astype(jnp.bfloat16)
    value_rows = value_raw.astype(jnp.bfloat16)
    query_heads = heads_of(queries)

    def empty_state():
        return (
            jnp.full((head_count, half_rows), -1e30, jnp.float32),
            jnp.zeros((head_count, half_rows), jnp.float32),
            jnp.zeros((half_rows, head_count, HEAD_DIM), jnp.float32),
        )

    running = (empty_state(), empty_state())
    key_part = lax.all_gather(key_rows, "blk", axis=0, tiled=True)
    value_part = lax.all_gather(value_rows, "blk", axis=0, tiled=True)
    key_pos, key_doc = key_info(jnp.int32(0), key_part.shape[0])
    updated = []
    for part_index in range(2):
        rows_here = slice(part_index * half_rows, (part_index + 1) * half_rows)
        allowed = allowed_pairs(own_pos[rows_here], own_doc[rows_here], key_pos, key_doc)
        updated.append(
            fold_half(
                running[part_index],
                query_heads[rows_here],
                heads_of(key_part),
                heads_of(value_part),
                allowed,
                score_scale,
            )
        )
    folded = (updated[0], updated[1])
    best_score = jnp.concatenate([folded[0][0], folded[1][0]], axis=1)
    total_sum = jnp.concatenate([folded[0][1], folded[1][1]], axis=1)
    accumulated = jnp.concatenate([folded[0][2], folded[1][2]], axis=0)
    attended = accumulated / total_sum.T[:, :, None]
    log_total = best_score + jnp.log(total_sum)
    attended_low = attended.reshape(tok_rows, model_width).astype(jnp.bfloat16)
    branch = jnp.dot(attended_low, w_out, preferred_element_type=jnp.float32)
    middle = residual_mix(hidden_f, branch, alpha_attn)
    middle_low = middle.astype(jnp.bfloat16)
    up_raw = jnp.dot(middle_low, w_up, preferred_element_type=jnp.float32)
    gate_raw = jnp.dot(middle_low, w_gate, preferred_element_type=jnp.float32)
    inner_low = gated_inner(up_raw, gate_raw, s_up, s_gate).astype(jnp.bfloat16)
    mlp_raw = jnp.dot(inner_low, w_down, preferred_element_type=jnp.float32)
    result = residual_mix(middle, mlp_raw, alpha_mlp)
    mixed_out, pull_out = jax.vjp(residual_mix, middle, mlp_raw, alpha_mlp)
    grad_middle, grad_mlp, grad_alpha_mlp = pull_out(cotangent[0, 0].astype(jnp.float32))
    grad_mlp_low = grad_mlp.astype(jnp.bfloat16)
    grad_w_down = jnp.dot(inner_low.T, grad_mlp_low, preferred_element_type=jnp.float32)
    grad_inner = jnp.dot(grad_mlp_low, w_down.T, preferred_element_type=jnp.float32)
    inner_out, pull_inner = jax.vjp(gated_inner, up_raw, gate_raw, s_up, s_gate)
    grad_up_raw, grad_gate_raw, grad_s_up, grad_s_gate = pull_inner(grad_inner)
    up_low = grad_up_raw.astype(jnp.bfloat16)
    gate_low = grad_gate_raw.astype(jnp.bfloat16)
    grad_w_up = jnp.dot(middle_low.T, up_low, preferred_element_type=jnp.float32)
    grad_w_gate = jnp.dot(middle_low.T, gate_low, preferred_element_type=jnp.float32)
    grad_middle = (
        grad_middle
        + jnp.dot(up_low, w_up.T, preferred_element_type=jnp.float32)
        + jnp.dot(gate_low, w_gate.T, preferred_element_type=jnp.float32)
    )
    attn_out, pull_attn = jax.vjp(residual_mix, hidden_f, branch, alpha_attn)
    grad_hidden, grad_branch, grad_alpha_attn = pull_attn(grad_middle)
    branch_low = grad_branch.astype(jnp.bfloat16)
    grad_w_out = jnp.dot(attended_low.T, branch_low, preferred_element_type=jnp.float32)
    grad_att_low = jnp.dot(branch_low, w_out.T, preferred_element_type=jnp.float32).astype(
        jnp.bfloat16
    )
    grad_heads = heads_of(grad_att_low)
    delta_rows = jnp.sum(grad_heads.astype(jnp.float32) * attended, axis=2).T

    def local_side(part_index):
        rows_here = slice(part_index * half_rows, (part_index + 1) * half_rows)
        return (
            query_heads[rows_here],
            grad_heads[rows_here],
            log_total[:, rows_here],
            delta_rows[:, rows_here],
            own_pos[rows_here],
            own_doc[rows_here],
        )

    local_parts = (local_side(0), local_side(1))
    whole_keys, whole_values = (
        lax.all_gather(key_rows, "blk", axis=0, tiled=True),
        lax.all_gather(value_rows, "blk", axis=0, tiled=True),
    )

    def query_step(grad_parts, shard_index):
        first_row = shard_index * tok_rows
        key_part = heads_of(take_rows(whole_keys, first_row, tok_rows))
        value_part = heads_of(take_rows(whole_values, first_row, tok_rows))
        key_pos, key_doc = key_info(first_row, tok_rows)
        updated = []
        for part_index in range(2):
            query_side = local_parts[part_index]
            allowed = allowed_pairs(query_side[4], query_side[5], key_pos, key_doc)

            def add_term(grad_now):
                return grad_now + query_term(query_side, key_part, value_part, allowed, score_scale)

            updated.append(
                lax.cond(
                    jnp.any(allowed), add_term, lambda grad_now: grad_now, grad_parts[part_index]
                )
            )
        return ((updated[0], updated[1]), None)

    zero_part = jnp.zeros((half_rows, head_count, HEAD_DIM), jnp.float32)
    grad_parts, unused_out = lax.scan(
        query_step, (zero_part, zero_part), jnp.arange(members, dtype=jnp.int32)
    )
    grad_queries = jnp.concatenate(grad_parts, axis=0).reshape(tok_rows, model_width)
    first_row = jnp.int32(0)
    row_count = lax.axis_size("blk") * tok_rows
    key_part = heads_of(take_rows(whole_keys, first_row, row_count))
    value_part = heads_of(take_rows(whole_values, first_row, row_count))
    key_pos, key_doc = key_info(first_row, row_count)
    zero_keys = jnp.zeros((row_count, head_count, HEAD_DIM), jnp.float32)
    totals = (zero_keys, zero_keys)
    for part_index in range(2):
        query_side = local_parts[part_index]
        allowed = allowed_pairs(query_side[4], query_side[5], key_pos, key_doc)

        def add_terms(grad_now):
            grad_keys, grad_values = key_term(
                query_side, key_part, value_part, allowed, score_scale
            )
            return (grad_now[0] + grad_keys, grad_now[1] + grad_values)

        totals = lax.cond(jnp.any(allowed), add_terms, lambda grad_now: grad_now, totals)
    key_value_grads = lax.psum_scatter(
        jnp.concatenate(
            [totals[0].reshape(row_count, model_width), totals[1].reshape(row_count, model_width)],
            axis=1,
        ),
        "blk",
        scatter_dimension=0,
        tiled=True,
    )
    grad_keys = key_value_grads[:, :model_width]
    grad_values = key_value_grads[:, model_width:]
    query_out, pull_query = jax.vjp(scaled_norm, query_raw, s_qk)
    grad_query_raw, grad_qk_first = pull_query(grad_queries)
    key_out, pull_key = jax.vjp(scaled_norm, key_raw, s_qk)
    grad_key_raw, grad_qk_second = pull_key(grad_keys)
    grad_s_qk = grad_qk_first + grad_qk_second
    query_low = grad_query_raw.astype(jnp.bfloat16)
    key_low = grad_key_raw.astype(jnp.bfloat16)
    value_low = grad_values.astype(jnp.bfloat16)
    grad_w_query = jnp.dot(hidden.T, query_low, preferred_element_type=jnp.float32)
    grad_w_key = jnp.dot(hidden.T, key_low, preferred_element_type=jnp.float32)
    grad_w_value = jnp.dot(hidden.T, value_low, preferred_element_type=jnp.float32)
    input_grad = (
        grad_hidden
        + jnp.dot(query_low, w_query.T, preferred_element_type=jnp.float32)
        + jnp.dot(key_low, w_key.T, preferred_element_type=jnp.float32)
        + jnp.dot(value_low, w_value.T, preferred_element_type=jnp.float32)
    )
    summed = (
        lax.psum_scatter(grad_w_query, ("dp", "blk"), scatter_dimension=0, tiled=True),
        lax.psum_scatter(grad_w_key, ("dp", "blk"), scatter_dimension=0, tiled=True),
        lax.psum_scatter(grad_w_value, ("dp", "blk"), scatter_dimension=0, tiled=True),
        lax.psum_scatter(grad_w_out, ("dp", "blk"), scatter_dimension=0, tiled=True),
        lax.psum_scatter(grad_w_up, ("dp", "blk"), scatter_dimension=0, tiled=True),
        lax.psum_scatter(grad_w_gate, ("dp", "blk"), scatter_dimension=0, tiled=True),
        lax.psum_scatter(grad_w_down, ("dp", "blk"), scatter_dimension=0, tiled=True),
        lax.psum_scatter(grad_s_qk, ("dp", "blk"), scatter_dimension=0, tiled=True),
        lax.psum_scatter(grad_s_up, ("dp", "blk"), scatter_dimension=0, tiled=True),
        lax.psum_scatter(grad_s_gate, ("dp", "blk"), scatter_dimension=0, tiled=True),
        lax.psum_scatter(grad_alpha_attn, ("dp", "blk"), scatter_dimension=0, tiled=True),
        lax.psum_scatter(grad_alpha_mlp, ("dp", "blk"), scatter_dimension=0, tiled=True),
    )
    mean_alpha = 0.5 * (jnp.mean(alpha_attn) + jnp.mean(alpha_mlp))
    output = result.astype(jnp.bfloat16)[None, None]
    return (
        output,
        input_grad[None, None],
        summed[0],
        summed[1],
        summed[2],
        summed[3],
        summed[4],
        summed[5],
        summed[6],
        summed[7],
        summed[8],
        summed[9],
        summed[10],
        summed[11],
        mean_alpha,
    )


MESH = pl.DeviceIdType.MESH
VMEM_SPEC = pl.BlockSpec(memory_space=pltpu.VMEM)
VMEM_LIMIT = 56 << 20
GROUP = 16


def here():
    return lax.axis_index("dp"), lax.axis_index("blk")


def greet(partners):
    barrier = pltpu.get_barrier_semaphore()
    for partner in partners:
        pl.semaphore_signal(barrier, inc=1, device_id=partner, device_id_type=MESH)
    pl.semaphore_wait(barrier, len(partners))


def remote(src, dst, send_sem, recv_sem, device):
    return pltpu.make_async_remote_copy(
        src_ref=src,
        dst_ref=dst,
        send_sem=send_sem,
        recv_sem=recv_sem,
        device_id=device,
        device_id_type=MESH,
    )


class Gather:
    SEMAPHORES = 40

    def __init__(self, own, out, send, recv):
        self.own, self.out, self.send, self.recv = own, out, send, recv
        dp, b = here()
        self.dp, self.b = dp, b
        self.z, self.y, self.c = b // 4, (b // 2) % 2, b % 2
        self.up = (dp, (b + 4) % GROUP)
        self.down = (dp, (b + 12) % GROUP)
        self.side = (dp, b + 2 - 4 * self.y)
        self.sib = (dp, b + 1 - 2 * self.c)

    def partners(self):
        return [self.up, self.down, self.side, self.sib]

    def copy(self, z, y, c, kind, half, device, own=False):
        block = z * 4 + y * 2 + c
        place = 2 * GROUP - 1 - block if half else block
        source = self.own.at[half] if own else self.out.at[place]
        index = 2 * kind + half
        return remote(source, self.out.at[place], self.send.at[index], self.recv.at[index], device)

    def along(self, z, half, device, own=False, back=False):
        return self.copy(z, self.y, self.c, z + (16 if back else 0), half, device, own)

    def across(self, z, y, half, own=False):
        return self.copy(z, y, self.c, 4 + z, half, self.side, own)

    def to_sib(self, z, y, c, half, own=False):
        return self.copy(z, y, c, 8 + 2 * z + y, half, self.sib, own)

    def start(self):
        z, y = self.z, self.y
        for half in (0, 1):

            @pl.when(z < 3)
            def _():
                self.along(z, half, self.up, True).start()

            @pl.when(z > 0)
            def _():
                self.along(z, half, self.down, True, True).start()

            self.across(z, y, half, True).start()
        for half in (0, 1):
            self.to_sib(z, y, self.c, half, True).start()
        for half in (0, 1):
            place = 2 * GROUP - 1 - self.b if half else self.b
            self.out[place] = self.own[half]

    def line(self, distance):
        for half in (0, 1):
            low, high = self.z - distance, self.z + distance

            @pl.when(low >= 0)
            def _():
                self.along(low, half, self.sib).wait_recv()

                @pl.when(self.z < 3)
                def _():
                    self.along(low, half, self.up).start()

                self.across(low, self.y, half).start()
                self.to_sib(low, self.y, self.c, half).start()

            @pl.when(high <= 3)
            def _():
                self.along(high, half, self.sib, False, True).wait_recv()

                @pl.when(self.z > 0)
                def _():
                    self.along(high, half, self.down, False, True).start()

                self.across(high, self.y, half).start()
                self.to_sib(high, self.y, self.c, half).start()

    def sides(self, distance):
        def one(z, half):
            self.across(z, 1 - self.y, half).wait_recv()
            self.to_sib(z, 1 - self.y, self.c, half).start()

        for half in (0, 1):
            if distance == 0:
                one(self.z, half)
            else:

                @pl.when(self.z - distance >= 0)
                def _():
                    one(self.z - distance, half)

                @pl.when(self.z + distance <= 3)
                def _():
                    one(self.z + distance, half)

    def finish(self):
        for half in (0, 1):
            for z in range(4):
                for y in (0, 1):
                    self.to_sib(z, y, 1 - self.c, half).wait_recv()
                    self.to_sib(z, y, self.c, half).wait_send()
                self.across(z, self.y, half).wait_send()

                @pl.when((self.z >= z) & (self.z < 3))
                def _():
                    self.along(z, half, self.up).wait_send()

                @pl.when((self.z <= z) & (self.z > 0))
                def _():
                    self.along(z, half, self.down, False, True).wait_send()


def gather_scratch():
    return [pltpu.SemaphoreType.DMA((Gather.SEMAPHORES,)) for _ in range(2)]


def gather_kernel(own, out, send, recv):
    gather = Gather(own, out, send, recv)
    greet(gather.partners())
    gather.start()
    gather.line(1)
    gather.sides(0)
    gather.line(2)
    gather.sides(1)
    gather.line(3)
    gather.sides(2)
    gather.sides(3)
    gather.finish()


def comm_params(collective_id):
    return pltpu.CompilerParams(
        collective_id=collective_id, has_side_effects=True, vmem_limit_bytes=VMEM_LIMIT
    )


def all_gather_group(rows, collective_id):
    tok_rows, width = rows.shape
    gathered = pl.pallas_call(
        gather_kernel,
        out_shape=jax.ShapeDtypeStruct((2 * GROUP, tok_rows // 2, width), rows.dtype),
        in_specs=[VMEM_SPEC],
        out_specs=VMEM_SPEC,
        scratch_shapes=gather_scratch(),
        compiler_params=comm_params(collective_id),
        name="gather_group",
    )(rows.reshape(2, tok_rows // 2, width))
    return gathered.reshape(GROUP * tok_rows, width)


def swap_group_kernel(blocks, out, send, recv):
    dp, b = here()
    greet([(dp, (b + step) % GROUP) for step in range(1, GROUP)])
    copies = []
    for step in range(1, GROUP):
        target = (b + step) % GROUP
        copies.append(
            remote(blocks.at[target], out.at[b], send.at[step], recv.at[step], (dp, target))
        )
        copies[-1].start()
    out[b] = blocks[b]
    for copy in copies:
        copy.wait()


def swap_group(blocks, collective_id):
    return pl.pallas_call(
        swap_group_kernel,
        out_shape=jax.ShapeDtypeStruct(blocks.shape, blocks.dtype),
        in_specs=[VMEM_SPEC],
        out_specs=VMEM_SPEC,
        scratch_shapes=[
            pltpu.SemaphoreType.DMA((GROUP,)),
            pltpu.SemaphoreType.DMA((GROUP,)),
        ],
        compiler_params=comm_params(collective_id),
        name="swap_group",
    )(blocks)


def swap_dp_kernel(count, *refs):
    blocks, outs, send, recv = refs[:count], refs[count : 2 * count], refs[-2], refs[-1]
    dp, b = here()
    greet([(1 - dp, b)])
    copies = [
        remote(blocks[i], outs[i], send.at[i], recv.at[i], (1 - dp, b)) for i in range(count)
    ]
    for copy in copies:
        copy.start()
    for copy in copies:
        copy.wait()


def swap_dp(blocks, collective_id):
    count = len(blocks)
    return pl.pallas_call(
        functools.partial(swap_dp_kernel, count),
        out_shape=[jax.ShapeDtypeStruct(block.shape, block.dtype) for block in blocks],
        in_specs=[VMEM_SPEC] * count,
        out_specs=[VMEM_SPEC] * count,
        scratch_shapes=[
            pltpu.SemaphoreType.DMA((count,)),
            pltpu.SemaphoreType.DMA((count,)),
        ],
        compiler_params=comm_params(collective_id),
        name="swap_dp",
    )(*blocks)


def swap_all_kernel(blocks, out, send, recv):
    dp, b = here()
    me = dp * GROUP + b
    total = 2 * GROUP
    targets = [(me + step) % total for step in range(1, total)]
    greet([(target // GROUP, target % GROUP) for target in targets])
    copies = []
    for step, target in enumerate(targets):
        copies.append(
            remote(
                blocks.at[target],
                out.at[me],
                send.at[step],
                recv.at[step],
                (target // GROUP, target % GROUP),
            )
        )
        copies[-1].start()
    out[me] = blocks[me]
    for copy in copies:
        copy.wait()


def swap_all(blocks, collective_id):
    return pl.pallas_call(
        swap_all_kernel,
        out_shape=jax.ShapeDtypeStruct(blocks.shape, blocks.dtype),
        in_specs=[VMEM_SPEC],
        out_specs=VMEM_SPEC,
        scratch_shapes=[
            pltpu.SemaphoreType.DMA((2 * GROUP,)),
            pltpu.SemaphoreType.DMA((2 * GROUP,)),
        ],
        compiler_params=comm_params(collective_id),
        name="swap_all",
    )(blocks)


ATT = 256


def dot_nt(left, right):
    return lax.dot_general(left, right, (((1,), (1,)), ((), ())), preferred_element_type=jnp.float32)


def dot_tn(left, right):
    return lax.dot_general(left, right, (((0,), (0,)), ((), ())), preferred_element_type=jnp.float32)


def dot_nn(left, right):
    return jnp.dot(left, right, preferred_element_type=jnp.float32)


def attend_kernel(first_ref, q_ref, k_ref, v_ref, start_ref, o_ref, l_ref):
    length = q_ref.shape[0]
    for query_block in range(length // ATT):
        rows = pl.ds(query_block * ATT, ATT)
        queries = q_ref[rows, :]
        doc_start = start_ref[rows, :]
        query_pos = query_block * ATT + lax.broadcasted_iota(jnp.int32, (ATT, ATT), 0)
        key_lane = lax.broadcasted_iota(jnp.int32, (ATT, ATT), 1)

        def step(key_block, total):
            base = pl.multiple_of(key_block * ATT, ATT)
            keys = k_ref[pl.ds(base, ATT), :]
            values = v_ref[pl.ds(base, ATT), :]
            key_pos = base + key_lane
            allowed = (key_pos <= query_pos) & (key_pos >= doc_start)
            weights = jnp.where(allowed, jnp.exp(dot_nt(queries, keys)), 0.0)
            return total + dot_nn(weights.astype(jnp.bfloat16), values)

        total = lax.fori_loop(
            first_ref[query_block], query_block + 1, step, jnp.zeros((ATT, 128), jnp.float32)
        )
        row_sum = total[:, HEAD_DIM : HEAD_DIM + 1]
        o_ref[rows, :] = total[:, :HEAD_DIM] / row_sum
        l_ref[rows, :] = jnp.log(row_sum)


def attend_grad_kernel(last_ref, q_ref, k_ref, v_ref, g_ref, start_ref, dq_ref, dk_ref, dv_ref):
    length = q_ref.shape[0]
    dq_ref[...] = jnp.zeros_like(dq_ref)
    key_row = lax.broadcasted_iota(jnp.int32, (ATT, ATT), 0)
    query_lane = lax.broadcasted_iota(jnp.int32, (ATT, ATT), 1)
    for key_block in range(length // ATT):
        rows = pl.ds(key_block * ATT, ATT)
        keys = k_ref[rows, :]
        values = v_ref[rows, :]
        key_pos = key_block * ATT + key_row

        def step(query_block, carried):
            dk, dv = carried
            base = pl.multiple_of(query_block * ATT, ATT)
            queries = q_ref[pl.ds(base, ATT), :]
            grads = g_ref[pl.ds(base, ATT), :]
            doc_start = start_ref[pl.ds(query_block, 1), :]
            allowed = (key_pos <= base + query_lane) & (key_pos >= doc_start)
            weights = jnp.where(allowed, jnp.exp(dot_nt(keys, queries)), 0.0)
            slopes = (weights * dot_nt(values, grads)).astype(jnp.bfloat16)
            dv = dv + dot_nn(weights.astype(jnp.bfloat16), grads)
            dk = dk + dot_nn(slopes, queries)
            dq_ref[pl.ds(base, ATT), :] += dot_tn(slopes, keys)
            return dk, dv

        zero = jnp.zeros((ATT, 128), jnp.float32)
        dk, dv = lax.fori_loop(key_block, last_ref[key_block], step, (zero, zero))
        dk_ref[rows, :] = dk
        dv_ref[rows, :] = dv


FF_STEP = 512


def mean_last(array):
    return jnp.mean(array, axis=-1, keepdims=True)


def rms_scale(array):
    return lax.rsqrt(mean_last(array * array) + 1e-06)


def rms_pull(grad, normed, scale):
    return scale * (grad - normed * mean_last(grad * normed))


def half_lanes(shape):
    return lax.broadcasted_iota(jnp.int32, shape, 1) < HEAD_DIM


class Swap:
    def __init__(self, blocks, out, send, recv):
        self.blocks, self.out = blocks, out
        dp, self.b = here()
        self.copies = []
        for step in range(1, GROUP):
            target = (self.b + step) % GROUP
            self.copies.append(
                remote(blocks.at[target], out.at[self.b], send.at[step], recv.at[step], (dp, target))
            )
        self.partners = [(dp, (self.b + step) % GROUP) for step in range(1, GROUP)]

    def start(self):
        for copy in self.copies:
            copy.start()
        self.out[self.b] = self.blocks[self.b]

    def wait(self):
        for copy in self.copies:
            copy.wait()


def middle_kernel(
    o_ref,
    hidden_ref,
    cot_ref,
    w_out_hbm,
    w_up_hbm,
    w_gate_hbm,
    w_down_hbm,
    s_up_ref,
    s_gate_ref,
    alpha_attn_ref,
    alpha_mlp_ref,
    result_ref,
    g_res_ref,
    grad_head_ref,
    mid_all_ref,
    g_mlp_ref,
    att_ref,
    g_branch_ref,
    g_alpha_attn_ref,
    g_alpha_mlp_ref,
    w_out,
    w_up,
    w_gate,
    w_down,
    up_raw,
    gate_raw,
    mid_own,
    o_in,
    g_send,
    acc,
    load_sem,
    swap_sems,
    back_sems,
    ag_send,
    ag_recv,
):
    low = jnp.bfloat16
    loads = [
        pltpu.make_async_copy(source, target, load_sem.at[i])
        for i, (source, target) in enumerate(
            [(w_out_hbm, w_out), (w_up_hbm, w_up), (w_gate_hbm, w_gate), (w_down_hbm, w_down)]
        )
    ]
    for load in loads:
        load.start()
    swap = Swap(o_ref, o_in, swap_sems.at[0], swap_sems.at[1])
    gather = Gather(mid_own, mid_all_ref, ag_send, ag_recv)
    greet(swap.partners)
    swap.start()
    swap.wait()
    rows = hidden_ref.shape[0]
    half = rows // 2
    first = half_lanes((half, 128))
    for pair in range(GROUP // 2):
        even = o_in[2 * pair].astype(jnp.float32)
        odd = o_in[2 * pair + 1].astype(jnp.float32)
        lanes = pl.ds(pair * 128, 128)
        att_ref[:half, lanes] = jnp.where(first, even, pltpu.roll(odd, HEAD_DIM, 1)).astype(low)
        att_ref[half:, lanes] = jnp.where(first, pltpu.roll(even, HEAD_DIM, 1), odd).astype(low)
    hidden = hidden_ref[...].astype(jnp.float32)
    alpha_attn = alpha_attn_ref[...]
    alpha_mlp = alpha_mlp_ref[...]
    loads[0].wait()
    branch = dot_nn(att_ref[...], w_out[...])
    branch_scale = rms_scale(branch)
    branch_normed = branch * branch_scale
    mixed = hidden + alpha_attn * (branch_normed - hidden)
    middle_scale = rms_scale(mixed)
    middle = mixed * middle_scale
    middle_low = middle.astype(low)
    mid_own[0] = middle_low[:half]
    mid_own[1] = middle_low[half:]
    gather.start()

    for load in loads[1:]:
        load.wait()
    steps = w_up.shape[1] // FF_STEP
    acc[...] = jnp.zeros_like(acc)

    def forward(step, carry):
        cols = pl.ds(pl.multiple_of(step * FF_STEP, FF_STEP), FF_STEP)
        up = dot_nn(middle_low, w_up[:, cols])
        gate = dot_nn(middle_low, w_gate[:, cols])
        up_raw[:, cols] = up
        gate_raw[:, cols] = gate
        scaled = gate * s_gate_ref[:, cols]
        inner = up * s_up_ref[:, cols] * (scaled / (1.0 + jnp.exp(-scaled)))
        acc[...] += dot_nn(inner.astype(low), w_down[cols, :])
        return carry

    lax.fori_loop(0, steps, forward, 0)
    gather.line(1)
    gather.sides(0)
    mlp = acc[...]
    mlp_scale = rms_scale(mlp)
    mlp_normed = mlp * mlp_scale
    mixed_out = middle + alpha_mlp * (mlp_normed - middle)
    out_scale = rms_scale(mixed_out)
    result = mixed_out * out_scale
    result_ref[...] = result.astype(low)
    g_mixed = rms_pull(cot_ref[...].astype(jnp.float32), result, out_scale)
    g_alpha_mlp_ref[...] = jnp.sum(g_mixed * (mlp_normed - middle), axis=0, keepdims=True)
    g_mlp = rms_pull(g_mixed * alpha_mlp, mlp_normed, mlp_scale).astype(low)
    g_mlp_ref[...] = g_mlp
    acc[...] = g_mixed * (1.0 - alpha_mlp)

    def backward(step, carry):
        cols = pl.ds(pl.multiple_of(step * FF_STEP, FF_STEP), FF_STEP)
        g_inner = dot_nt(g_mlp, w_down[cols, :])
        s_up = s_up_ref[:, cols]
        s_gate = s_gate_ref[:, cols]
        scaled = gate_raw[:, cols] * s_gate
        sigmoid = 1.0 / (1.0 + jnp.exp(-scaled))
        g_up = g_inner * (scaled * sigmoid) * s_up
        slope = sigmoid * (1.0 + scaled * (1.0 - sigmoid))
        g_gate = g_inner * (up_raw[:, cols] * s_up) * slope * s_gate
        acc[...] += dot_nt(g_up.astype(low), w_up[:, cols]) + dot_nt(
            g_gate.astype(low), w_gate[:, cols]
        )
        return carry

    lax.fori_loop(0, steps // 2, backward, 0)
    gather.line(2)
    gather.sides(1)
    lax.fori_loop(steps // 2, steps, backward, 0)
    g_pre = rms_pull(acc[...], middle, middle_scale)
    g_res_ref[...] = g_pre * (1.0 - alpha_attn)
    g_alpha_attn_ref[...] = jnp.sum(g_pre * (branch_normed - hidden), axis=0, keepdims=True)
    g_branch = rms_pull(g_pre * alpha_attn, branch_normed, branch_scale).astype(low)
    g_branch_ref[...] = g_branch
    g_att = dot_nt(g_branch, w_out[...]).astype(low).astype(jnp.float32)
    for pair in range(GROUP // 2):
        lower = g_att[:half, pair * 128 : (pair + 1) * 128]
        upper = g_att[half:, pair * 128 : (pair + 1) * 128]
        g_send[2 * pair] = jnp.where(first, lower, pltpu.roll(upper, HEAD_DIM, 1)).astype(low)
        g_send[2 * pair + 1] = jnp.where(first, pltpu.roll(lower, HEAD_DIM, 1), upper).astype(low)
    back = Swap(g_send, grad_head_ref, back_sems.at[0], back_sems.at[1])
    back.start()
    gather.line(3)
    gather.sides(2)
    gather.sides(3)
    gather.finish()
    back.wait()


ANY_SPEC = pl.BlockSpec(memory_space=pl.ANY)


def middle_block(packed, hidden, cot, w_out, w_up, w_gate, w_down, s_up, s_gate, alpha_attn, alpha_mlp):
    rows, width = hidden.shape
    ff = w_up.shape[1]
    low, f32 = jnp.bfloat16, jnp.float32
    shape = jax.ShapeDtypeStruct
    return pl.pallas_call(
        middle_kernel,
        out_shape=[
            shape((rows, width), low),
            shape((rows, width), f32),
            shape(packed.shape, low),
            shape((2 * GROUP, rows // 2, width), low),
            shape((rows, width), low),
            shape((rows, width), low),
            shape((rows, width), low),
            shape((1, width), f32),
            shape((1, width), f32),
        ],
        in_specs=[VMEM_SPEC] * 3 + [ANY_SPEC] * 4 + [VMEM_SPEC] * 4,
        out_specs=[VMEM_SPEC] * 9,
        scratch_shapes=[
            pltpu.VMEM(w_out.shape, low),
            pltpu.VMEM(w_up.shape, low),
            pltpu.VMEM(w_gate.shape, low),
            pltpu.VMEM(w_down.shape, low),
            pltpu.VMEM((rows, ff), f32),
            pltpu.VMEM((rows, ff), f32),
            pltpu.VMEM((2, rows // 2, width), low),
            pltpu.VMEM(packed.shape, low),
            pltpu.VMEM(packed.shape, low),
            pltpu.VMEM((rows, width), f32),
            pltpu.SemaphoreType.DMA((4,)),
            pltpu.SemaphoreType.DMA((2, GROUP)),
            pltpu.SemaphoreType.DMA((2, GROUP)),
        ]
        + gather_scratch(),
        compiler_params=comm_params(1),
        name="middle_block",
    )(
        packed,
        hidden,
        cot,
        w_out,
        w_up,
        w_gate,
        w_down,
        s_up[None],
        s_gate[None],
        alpha_attn[None],
        alpha_mlp[None],
    )


SMEM_SPEC = pl.BlockSpec(memory_space=pltpu.SMEM)


def split_three(column):
    high = lax.reduce_precision(column, 8, 7)
    rest = column - high
    mid = lax.reduce_precision(rest, 8, 7)
    return [part.astype(jnp.bfloat16) for part in (high, mid, rest - mid)]


def widened(matrix, columns):
    joined = jnp.concatenate([matrix] + columns, axis=1)
    return jnp.pad(joined, ((0, 0), (0, 128 - joined.shape[1])))


def pack_stream(stream):
    half = stream.shape[0] // 2
    lower = stream[:half].reshape(GROUP, half // GROUP, -1)
    upper = stream[half:].reshape(GROUP, half // GROUP, -1)[::-1]
    return jnp.concatenate([lower, upper], axis=2)


def unpack_rows(blocks):
    width = blocks.shape[2] // 2
    return jnp.concatenate(
        [blocks[:, :, :width].transpose(1, 0, 2), blocks[:, :, width:].transpose(1, 0, 2)], axis=0
    )


def pack_rows(rows):
    half = rows.shape[0] // 2
    return jnp.concatenate(
        [
            rows[:half].reshape(half, GROUP, -1).transpose(1, 0, 2),
            rows[half:].reshape(half, GROUP, -1).transpose(1, 0, 2),
        ],
        axis=2,
    )


def unpack_stream(blocks):
    width = blocks.shape[2] // 2
    lower = blocks[:, :, :width].reshape(-1, width)
    upper = blocks[::-1, :, width:].reshape(-1, width)
    return jnp.concatenate([lower, upper], axis=0)


def on_device_heads(
    tokens,
    cotangent,
    lengths,
    w_query,
    w_key,
    w_value,
    w_out,
    w_up,
    w_gate,
    w_down,
    s_qk,
    s_up,
    s_gate,
    alpha_attn,
    alpha_mlp,
):
    low = jnp.bfloat16
    model_width = w_query.shape[0]
    tok_rows = tokens.shape[2]
    length = GROUP * tok_rows
    dp, b = here()
    score_scale = 1.0 / math.sqrt(HEAD_DIM)
    hidden = tokens[0, 0]
    hidden_f = hidden.astype(jnp.float32)
    positions = jnp.arange(length, dtype=jnp.int32)
    doc_ends = jnp.cumsum(lengths[0], dtype=jnp.int32)
    doc_starts = doc_ends - lengths[0]
    document = doc_index(positions, doc_ends)
    member = document[:, None] == jnp.arange(lengths.shape[1], dtype=jnp.int32)[None]
    start_of = jnp.sum(jnp.where(member, doc_starts[None], 0), axis=1, dtype=jnp.int32)
    end_of = jnp.sum(jnp.where(member, doc_ends[None], 0), axis=1, dtype=jnp.int32)
    blocks = length // ATT
    first_block = start_of[::ATT] // ATT
    last_block = (end_of[ATT - 1 :: ATT] + ATT - 1) // ATT

    hidden_all = all_gather_group(hidden, 0)
    head_col = b * HEAD_DIM

    def head_slice(weight):
        return lax.dynamic_slice_in_dim(weight, head_col, HEAD_DIM, 1)

    gain = lax.dynamic_slice_in_dim(s_qk, head_col, HEAD_DIM, 0)
    w_head = jnp.concatenate([head_slice(w_query), head_slice(w_key), head_slice(w_value)], axis=1)
    raw = dot_nn(hidden_all, w_head)
    query_raw, key_raw, value_raw = (
        raw[:, :HEAD_DIM],
        raw[:, HEAD_DIM : 2 * HEAD_DIM],
        raw[:, 2 * HEAD_DIM :],
    )

    def scaled_norm(raw_rows, gain_vector):
        return rms_norm(raw_rows) * gain_vector

    queries = scaled_norm(query_raw, gain).astype(low)
    keys = scaled_norm(key_raw, gain).astype(low)
    values = value_raw.astype(low)
    scaled_queries = queries * jnp.asarray(score_scale, low)
    ones = jnp.ones((length, 1), low)
    attended_head, log_total = pl.pallas_call(
        attend_kernel,
        out_shape=[
            jax.ShapeDtypeStruct((length, HEAD_DIM), jnp.float32),
            jax.ShapeDtypeStruct((length, 1), jnp.float32),
        ],
        in_specs=[SMEM_SPEC] + [VMEM_SPEC] * 4,
        out_specs=[VMEM_SPEC] * 2,
        compiler_params=pltpu.CompilerParams(vmem_limit_bytes=VMEM_LIMIT),
        name="attend",
    )(first_block, scaled_queries, keys, widened(values, [ones]), start_of[:, None])
    attended_head_low = attended_head.astype(low)

    (
        result,
        grad_hidden,
        grad_packed,
        middle_all,
        grad_mlp_low,
        attended_low,
        branch_low,
        grad_alpha_attn,
        grad_alpha_mlp,
    ) = middle_block(
        pack_stream(attended_head_low),
        hidden,
        cotangent[0, 0],
        w_out,
        w_up,
        w_gate,
        w_down,
        s_up,
        s_gate,
        alpha_attn,
        alpha_mlp,
    )
    middle_all = middle_all.reshape(length, model_width)

    grad_head = unpack_stream(grad_packed)
    delta = jnp.sum(grad_head.astype(jnp.float32) * attended_head, axis=1, keepdims=True)
    minus = [-ones] * 3
    dq, dk, dv = pl.pallas_call(
        attend_grad_kernel,
        out_shape=[jax.ShapeDtypeStruct((length, 128), jnp.float32)] * 3,
        in_specs=[SMEM_SPEC] + [VMEM_SPEC] * 5,
        out_specs=[VMEM_SPEC] * 3,
        compiler_params=pltpu.CompilerParams(vmem_limit_bytes=VMEM_LIMIT),
        name="attend_grad",
    )(
        last_block,
        widened(scaled_queries, split_three(log_total)),
        widened(keys, minus),
        widened(values, minus),
        widened(grad_head, split_three(delta)),
        start_of.reshape(blocks, ATT),
    )
    grad_queries = dq[:, :HEAD_DIM] * score_scale
    grad_keys = dk[:, :HEAD_DIM]
    grad_values = dv[:, :HEAD_DIM]
    _, pull_query = jax.vjp(scaled_norm, query_raw, gain)
    grad_query_raw, grad_qk_first = pull_query(grad_queries)
    _, pull_key = jax.vjp(scaled_norm, key_raw, gain)
    grad_key_raw, grad_qk_second = pull_key(grad_keys)
    grad_s_qk = grad_qk_first + grad_qk_second
    raw_low = jnp.concatenate([grad_query_raw, grad_key_raw, grad_values], axis=1).astype(low)
    home = swap_group(pack_stream(raw_low), 3)
    home = unpack_rows(home)

    def home_part(index):
        return home[:, :, index * HEAD_DIM : (index + 1) * HEAD_DIM].reshape(tok_rows, model_width)

    input_grad = (
        grad_hidden
        + dot_nt(home_part(0), w_query)
        + dot_nt(home_part(1), w_key)
        + dot_nt(home_part(2), w_value)
    )

    mlp_all = all_gather_group(grad_mlp_low, 5)
    ff_part = w_up.shape[1] // (2 * GROUP)
    ff_half = w_up.shape[1] // 2

    def ff_slice(array, axis):
        return jnp.concatenate(
            [
                lax.dynamic_slice_in_dim(array, b * ff_part, ff_part, axis),
                lax.dynamic_slice_in_dim(array, ff_half + b * ff_part, ff_part, axis),
            ],
            axis=axis,
        )

    up_part = dot_nn(middle_all, ff_slice(w_up, 1))
    gate_part = dot_nn(middle_all, ff_slice(w_gate, 1))
    inner_grad_part = dot_nt(mlp_all, ff_slice(w_down, 0))
    inner_part, pull_part = jax.vjp(
        gated_inner, up_part, gate_part, ff_slice(s_up, 0), ff_slice(s_gate, 0)
    )
    g_up, g_gate, g_s_up, g_s_gate = pull_part(inner_grad_part)
    part_down = dot_tn(inner_part.astype(low), mlp_all)
    part_up = dot_tn(middle_all, g_up.astype(low))
    part_gate = dot_tn(middle_all, g_gate.astype(low))
    part_qkv = dot_tn(hidden_all, raw_low)
    part_out = dot_tn(attended_low, branch_low)

    part_wide = jnp.concatenate(
        [part_up, part_gate, part_qkv, jnp.zeros((model_width, 64), jnp.float32)], axis=1
    )
    half_width = model_width // 2

    def mine(array, size, axis=0):
        return lax.dynamic_slice_in_dim(array, dp * size, size, axis)

    def other(array, size, axis=0):
        return lax.dynamic_slice_in_dim(array, (1 - dp) * size, size, axis)

    got_wide, got_down = swap_dp(
        [other(part_wide, half_width).astype(low), other(part_down, ff_part).astype(low)], 7
    )
    grad_down = mine(part_down, ff_part) + got_down
    wide = (mine(part_wide, half_width) + got_wide).astype(low)
    wide = wide.reshape(GROUP, half_width // GROUP, -1)
    got = swap_group(wide, 8)
    grad_up = jnp.concatenate(
        [got[:, :, i * ff_part : (i + 1) * ff_part].transpose(1, 0, 2).reshape(-1, ff_half) for i in (0, 1)],
        axis=1,
    ).astype(jnp.float32)
    grad_gate = jnp.concatenate(
        [got[:, :, i * ff_part : (i + 1) * ff_part].transpose(1, 0, 2).reshape(-1, ff_half) for i in (2, 3)],
        axis=1,
    ).astype(jnp.float32)
    base = 4 * ff_part
    grad_query, grad_key, grad_value = (
        got[:, :, base + i * HEAD_DIM : base + (i + 1) * HEAD_DIM]
        .transpose(1, 0, 2)
        .reshape(-1, model_width)
        .astype(jnp.float32)
        for i in range(3)
    )
    rows_out = model_width // (2 * GROUP)
    grad_out = lax.psum_scatter(part_out, ("dp", "blk"), scatter_dimension=0, tiled=True)

    def vector_rows(vector):
        rows = vector.reshape(2 * GROUP, -1)
        return jnp.pad(rows, ((0, 0), (0, 128 - rows.shape[1])))

    s_full = jnp.zeros((model_width,), jnp.float32)
    s_full = lax.dynamic_update_slice_in_dim(s_full, grad_s_qk, head_col, 0)

    def ff_full(part):
        full = jnp.zeros((w_up.shape[1],), jnp.float32)
        full = lax.dynamic_update_slice_in_dim(full, part[:ff_part], b * ff_part, 0)
        return lax.dynamic_update_slice_in_dim(full, part[ff_part:], ff_half + b * ff_part, 0)

    small = jnp.stack(
        [
            vector_rows(s_full),
            vector_rows(ff_full(g_s_up)),
            vector_rows(ff_full(g_s_gate)),
            vector_rows(grad_alpha_attn[0]),
            vector_rows(grad_alpha_mlp[0]),
        ],
        axis=1,
    )
    small = jnp.pad(small, ((0, 0), (0, 3), (0, 0)))
    small = jnp.sum(swap_all(small, 9), axis=0)
    mean_alpha = 0.5 * (jnp.mean(alpha_attn) + jnp.mean(alpha_mlp))
    return (
        result[None, None],
        input_grad[None, None],
        grad_query,
        grad_key,
        grad_value,
        grad_out,
        grad_up,
        grad_gate,
        grad_down,
        small[0, :rows_out],
        small[1],
        small[2],
        small[3, :rows_out],
        small[4, :rows_out],
        mean_alpha,
    )


def on_device(*arrays):
    head_count = arrays[3].shape[0] // HEAD_DIM
    tok_rows = arrays[0].shape[2]
    fits = lax.axis_size("blk") == head_count == 16 and lax.axis_size("dp") == 2
    if fits and tok_rows == 128:
        return on_device_heads(*arrays)
    return on_device_general(*arrays)


def solution(mesh):
    in_specs = (
        P("dp", "blk", None, None),
        P("dp", "blk", None, None),
        P("dp", None),
        P(),
        P(),
        P(),
        P(),
        P(),
        P(),
        P(),
        P(),
        P(),
        P(),
        P(),
        P(),
    )
    out_specs = (
        P("dp", "blk", None, None),
        P("dp", "blk", None, None),
        P(("dp", "blk"), None),
        P(("dp", "blk"), None),
        P(("dp", "blk"), None),
        P(("dp", "blk"), None),
        P(("dp", "blk"), None),
        P(("dp", "blk"), None),
        P(("dp", "blk"), None),
        P(("dp", "blk")),
        P(("dp", "blk")),
        P(("dp", "blk")),
        P(("dp", "blk")),
        P(("dp", "blk")),
        P(),
    )
    return jax.shard_map(
        on_device, mesh=mesh, in_specs=in_specs, out_specs=out_specs, check_vma=False
    )
```

```python
import functools
import math

import jax
import jax.numpy as jnp
from jax import lax
from jax.experimental import pallas as pl
from jax.experimental.pallas import tpu as pltpu
from jax.sharding import PartitionSpec as P

HEAD_DIM = 64


def rms_norm(vector):
    return vector * lax.rsqrt(jnp.mean(vector * vector, axis=-1, keepdims=True) + 1e-06)


def head_norm(vector, head_count):
    shaped = vector.reshape(vector.shape[0], head_count, -1)
    return rms_norm(shaped).reshape(vector.shape)


def silu_smooth(vector):
    return vector / (1.0 + jnp.exp(-vector))


def residual_mix(inputs, branch, alphas):
    return rms_norm(inputs + alphas * (rms_norm(branch) - inputs))


def gated_inner(up_raw, gate_raw, s_up, s_gate):
    return up_raw * s_up * silu_smooth(gate_raw * s_gate)


def stream_positions(row_index, tok_rows, members):
    half_rows = tok_rows // 2
    device = row_index // tok_rows
    within = row_index % tok_rows
    block_id = jnp.where(within < half_rows, device, 2 * members - 1 - device)
    return block_id * half_rows + within % half_rows


def doc_index(positions, doc_ends):
    return jnp.sum(
        (positions[:, None] >= doc_ends[None, :]).astype(jnp.int32), axis=1, dtype=jnp.int32
    )


def allowed_pairs(query_pos, query_doc, key_pos, key_doc):
    return (key_pos[None, :] <= query_pos[:, None]) & (key_doc[None, :] == query_doc[:, None])


def take_rows(matrix, first_row, row_count):
    return lax.dynamic_slice_in_dim(matrix, first_row, row_count, 0)


def fold_half(running, query_heads, key_heads, value_heads, allowed, score_scale):

    def absorb(carried):
        best_score, total_sum, accumulated = carried
        scores = (
            jnp.einsum("qhd,khd->hqk", query_heads, key_heads, preferred_element_type=jnp.float32)
            * score_scale
        )
        scores = jnp.where(allowed[None], scores, -1e30)
        new_best = jnp.maximum(best_score, jnp.max(scores, axis=2))
        weights = jnp.where(allowed[None], jnp.exp(scores - new_best[:, :, None]), 0.0)
        fade_factor = jnp.exp(best_score - new_best)
        total_sum = jnp.sum(weights, axis=2)
        accumulated = accumulated * fade_factor.T[:, :, None] + jnp.einsum(
            "hqk,khd->qhd",
            weights.astype(jnp.bfloat16),
            value_heads,
            preferred_element_type=jnp.float32,
        )
        return (new_best, total_sum, accumulated)

    return lax.cond(jnp.any(allowed), absorb, lambda carried: carried, running)


def pair_terms(query_side, key_heads, value_heads, allowed, score_scale):
    query_heads, grad_heads, log_total, delta_rows = (
        query_side[0],
        query_side[1],
        query_side[2],
        query_side[3],
    )
    scores = (
        jnp.einsum("qhd,khd->hqk", query_heads, key_heads, preferred_element_type=jnp.float32)
        * score_scale
    )
    scores = jnp.where(allowed[None], scores, -1e30)
    weights = jnp.exp(scores - log_total[:, :, None])
    grad_weights = jnp.einsum(
        "qhd,khd->hqk", grad_heads, value_heads, preferred_element_type=jnp.float32
    )
    grad_scores = (weights * (grad_weights - delta_rows[:, :, None])).astype(jnp.bfloat16)
    return (weights.astype(jnp.bfloat16), grad_scores)


def query_term(query_side, key_heads, value_heads, allowed, score_scale):
    weights, grad_scores = pair_terms(query_side, key_heads, value_heads, allowed, score_scale)
    return score_scale * jnp.einsum(
        "hqk,khd->qhd", grad_scores, key_heads, preferred_element_type=jnp.float32
    )


def key_term(query_side, key_heads, value_heads, allowed, score_scale):
    weights, grad_scores = pair_terms(query_side, key_heads, value_heads, allowed, score_scale)
    grad_keys = score_scale * jnp.einsum(
        "hqk,qhd->khd", grad_scores, query_side[0], preferred_element_type=jnp.float32
    )
    grad_values = jnp.einsum(
        "hqk,qhd->khd", weights, query_side[1], preferred_element_type=jnp.float32
    )
    return (grad_keys, grad_values)


def on_device_general(
    tokens,
    cotangent,
    lengths,
    w_query,
    w_key,
    w_value,
    w_out,
    w_up,
    w_gate,
    w_down,
    s_qk,
    s_up,
    s_gate,
    alpha_attn,
    alpha_mlp,
):
    model_width = w_query.shape[0]
    head_count = model_width // HEAD_DIM
    score_scale = 1.0 / math.sqrt(HEAD_DIM)
    tok_rows = tokens.shape[2]
    half_rows = tok_rows // 2
    members = lax.axis_size("blk")
    position = lax.axis_index("blk")
    doc_ends = jnp.cumsum(lengths[0], dtype=jnp.int32)
    hidden = tokens[0, 0]
    hidden_f = hidden.astype(jnp.float32)

    def key_info(first_row, row_count):
        key_pos = stream_positions(
            first_row + jnp.arange(row_count, dtype=jnp.int32), tok_rows, members
        )
        return (key_pos, doc_index(key_pos, doc_ends))

    def heads_of(matrix):
        return matrix.reshape(matrix.shape[0], head_count, HEAD_DIM)

    def scaled_norm(raw_rows, gain_vector):
        return head_norm(raw_rows, head_count) * gain_vector

    own_pos, own_doc = key_info(position * tok_rows, tok_rows)
    query_raw = jnp.dot(hidden, w_query, preferred_element_type=jnp.float32)
    key_raw = jnp.dot(hidden, w_key, preferred_element_type=jnp.float32)
    value_raw = jnp.dot(hidden, w_value, preferred_element_type=jnp.float32)
    queries = scaled_norm(query_raw, s_qk).astype(jnp.bfloat16)
    key_rows = scaled_norm(key_raw, s_qk).astype(jnp.bfloat16)
    value_rows = value_raw.astype(jnp.bfloat16)
    query_heads = heads_of(queries)

    def empty_state():
        return (
            jnp.full((head_count, half_rows), -1e30, jnp.float32),
            jnp.zeros((head_count, half_rows), jnp.float32),
            jnp.zeros((half_rows, head_count, HEAD_DIM), jnp.float32),
        )

    running = (empty_state(), empty_state())
    key_part = lax.all_gather(key_rows, "blk", axis=0, tiled=True)
    value_part = lax.all_gather(value_rows, "blk", axis=0, tiled=True)
    key_pos, key_doc = key_info(jnp.int32(0), key_part.shape[0])
    updated = []
    for part_index in range(2):
        rows_here = slice(part_index * half_rows, (part_index + 1) * half_rows)
        allowed = allowed_pairs(own_pos[rows_here], own_doc[rows_here], key_pos, key_doc)
        updated.append(
            fold_half(
                running[part_index],
                query_heads[rows_here],
                heads_of(key_part),
                heads_of(value_part),
                allowed,
                score_scale,
            )
        )
    folded = (updated[0], updated[1])
    best_score = jnp.concatenate([folded[0][0], folded[1][0]], axis=1)
    total_sum = jnp.concatenate([folded[0][1], folded[1][1]], axis=1)
    accumulated = jnp.concatenate([folded[0][2], folded[1][2]], axis=0)
    attended = accumulated / total_sum.T[:, :, None]
    log_total = best_score + jnp.log(total_sum)
    attended_low = attended.reshape(tok_rows, model_width).astype(jnp.bfloat16)
    branch = jnp.dot(attended_low, w_out, preferred_element_type=jnp.float32)
    middle = residual_mix(hidden_f, branch, alpha_attn)
    middle_low = middle.astype(jnp.bfloat16)
    up_raw = jnp.dot(middle_low, w_up, preferred_element_type=jnp.float32)
    gate_raw = jnp.dot(middle_low, w_gate, preferred_element_type=jnp.float32)
    inner_low = gated_inner(up_raw, gate_raw, s_up, s_gate).astype(jnp.bfloat16)
    mlp_raw = jnp.dot(inner_low, w_down, preferred_element_type=jnp.float32)
    result = residual_mix(middle, mlp_raw, alpha_mlp)
    mixed_out, pull_out = jax.vjp(residual_mix, middle, mlp_raw, alpha_mlp)
    grad_middle, grad_mlp, grad_alpha_mlp = pull_out(cotangent[0, 0].astype(jnp.float32))
    grad_mlp_low = grad_mlp.astype(jnp.bfloat16)
    grad_w_down = jnp.dot(inner_low.T, grad_mlp_low, preferred_element_type=jnp.float32)
    grad_inner = jnp.dot(grad_mlp_low, w_down.T, preferred_element_type=jnp.float32)
    inner_out, pull_inner = jax.vjp(gated_inner, up_raw, gate_raw, s_up, s_gate)
    grad_up_raw, grad_gate_raw, grad_s_up, grad_s_gate = pull_inner(grad_inner)
    up_low = grad_up_raw.astype(jnp.bfloat16)
    gate_low = grad_gate_raw.astype(jnp.bfloat16)
    grad_w_up = jnp.dot(middle_low.T, up_low, preferred_element_type=jnp.float32)
    grad_w_gate = jnp.dot(middle_low.T, gate_low, preferred_element_type=jnp.float32)
    grad_middle = (
        grad_middle
        + jnp.dot(up_low, w_up.T, preferred_element_type=jnp.float32)
        + jnp.dot(gate_low, w_gate.T, preferred_element_type=jnp.float32)
    )
    attn_out, pull_attn = jax.vjp(residual_mix, hidden_f, branch, alpha_attn)
    grad_hidden, grad_branch, grad_alpha_attn = pull_attn(grad_middle)
    branch_low = grad_branch.astype(jnp.bfloat16)
    grad_w_out = jnp.dot(attended_low.T, branch_low, preferred_element_type=jnp.float32)
    grad_att_low = jnp.dot(branch_low, w_out.T, preferred_element_type=jnp.float32).astype(
        jnp.bfloat16
    )
    grad_heads = heads_of(grad_att_low)
    delta_rows = jnp.sum(grad_heads.astype(jnp.float32) * attended, axis=2).T

    def local_side(part_index):
        rows_here = slice(part_index * half_rows, (part_index + 1) * half_rows)
        return (
            query_heads[rows_here],
            grad_heads[rows_here],
            log_total[:, rows_here],
            delta_rows[:, rows_here],
            own_pos[rows_here],
            own_doc[rows_here],
        )

    local_parts = (local_side(0), local_side(1))
    whole_keys, whole_values = (
        lax.all_gather(key_rows, "blk", axis=0, tiled=True),
        lax.all_gather(value_rows, "blk", axis=0, tiled=True),
    )

    def query_step(grad_parts, shard_index):
        first_row = shard_index * tok_rows
        key_part = heads_of(take_rows(whole_keys, first_row, tok_rows))
        value_part = heads_of(take_rows(whole_values, first_row, tok_rows))
        key_pos, key_doc = key_info(first_row, tok_rows)
        updated = []
        for part_index in range(2):
            query_side = local_parts[part_index]
            allowed = allowed_pairs(query_side[4], query_side[5], key_pos, key_doc)

            def add_term(grad_now):
                return grad_now + query_term(query_side, key_part, value_part, allowed, score_scale)

            updated.append(
                lax.cond(
                    jnp.any(allowed), add_term, lambda grad_now: grad_now, grad_parts[part_index]
                )
            )
        return ((updated[0], updated[1]), None)

    zero_part = jnp.zeros((half_rows, head_count, HEAD_DIM), jnp.float32)
    grad_parts, unused_out = lax.scan(
        query_step, (zero_part, zero_part), jnp.arange(members, dtype=jnp.int32)
    )
    grad_queries = jnp.concatenate(grad_parts, axis=0).reshape(tok_rows, model_width)
    first_row = jnp.int32(0)
    row_count = lax.axis_size("blk") * tok_rows
    key_part = heads_of(take_rows(whole_keys, first_row, row_count))
    value_part = heads_of(take_rows(whole_values, first_row, row_count))
    key_pos, key_doc = key_info(first_row, row_count)
    zero_keys = jnp.zeros((row_count, head_count, HEAD_DIM), jnp.float32)
    totals = (zero_keys, zero_keys)
    for part_index in range(2):
        query_side = local_parts[part_index]
        allowed = allowed_pairs(query_side[4], query_side[5], key_pos, key_doc)

        def add_terms(grad_now):
            grad_keys, grad_values = key_term(
                query_side, key_part, value_part, allowed, score_scale
            )
            return (grad_now[0] + grad_keys, grad_now[1] + grad_values)

        totals = lax.cond(jnp.any(allowed), add_terms, lambda grad_now: grad_now, totals)
    key_value_grads = lax.psum_scatter(
        jnp.concatenate(
            [totals[0].reshape(row_count, model_width), totals[1].reshape(row_count, model_width)],
            axis=1,
        ),
        "blk",
        scatter_dimension=0,
        tiled=True,
    )
    grad_keys = key_value_grads[:, :model_width]
    grad_values = key_value_grads[:, model_width:]
    query_out, pull_query = jax.vjp(scaled_norm, query_raw, s_qk)
    grad_query_raw, grad_qk_first = pull_query(grad_queries)
    key_out, pull_key = jax.vjp(scaled_norm, key_raw, s_qk)
    grad_key_raw, grad_qk_second = pull_key(grad_keys)
    grad_s_qk = grad_qk_first + grad_qk_second
    query_low = grad_query_raw.astype(jnp.bfloat16)
    key_low = grad_key_raw.astype(jnp.bfloat16)
    value_low = grad_values.astype(jnp.bfloat16)
    grad_w_query = jnp.dot(hidden.T, query_low, preferred_element_type=jnp.float32)
    grad_w_key = jnp.dot(hidden.T, key_low, preferred_element_type=jnp.float32)
    grad_w_value = jnp.dot(hidden.T, value_low, preferred_element_type=jnp.float32)
    input_grad = (
        grad_hidden
        + jnp.dot(query_low, w_query.T, preferred_element_type=jnp.float32)
        + jnp.dot(key_low, w_key.T, preferred_element_type=jnp.float32)
        + jnp.dot(value_low, w_value.T, preferred_element_type=jnp.float32)
    )
    summed = (
        lax.psum_scatter(grad_w_query, ("dp", "blk"), scatter_dimension=0, tiled=True),
        lax.psum_scatter(grad_w_key, ("dp", "blk"), scatter_dimension=0, tiled=True),
        lax.psum_scatter(grad_w_value, ("dp", "blk"), scatter_dimension=0, tiled=True),
        lax.psum_scatter(grad_w_out, ("dp", "blk"), scatter_dimension=0, tiled=True),
        lax.psum_scatter(grad_w_up, ("dp", "blk"), scatter_dimension=0, tiled=True),
        lax.psum_scatter(grad_w_gate, ("dp", "blk"), scatter_dimension=0, tiled=True),
        lax.psum_scatter(grad_w_down, ("dp", "blk"), scatter_dimension=0, tiled=True),
        lax.psum_scatter(grad_s_qk, ("dp", "blk"), scatter_dimension=0, tiled=True),
        lax.psum_scatter(grad_s_up, ("dp", "blk"), scatter_dimension=0, tiled=True),
        lax.psum_scatter(grad_s_gate, ("dp", "blk"), scatter_dimension=0, tiled=True),
        lax.psum_scatter(grad_alpha_attn, ("dp", "blk"), scatter_dimension=0, tiled=True),
        lax.psum_scatter(grad_alpha_mlp, ("dp", "blk"), scatter_dimension=0, tiled=True),
    )
    mean_alpha = 0.5 * (jnp.mean(alpha_attn) + jnp.mean(alpha_mlp))
    output = result.astype(jnp.bfloat16)[None, None]
    return (
        output,
        input_grad[None, None],
        summed[0],
        summed[1],
        summed[2],
        summed[3],
        summed[4],
        summed[5],
        summed[6],
        summed[7],
        summed[8],
        summed[9],
        summed[10],
        summed[11],
        mean_alpha,
    )


MESH = pl.DeviceIdType.MESH
VMEM_SPEC = pl.BlockSpec(memory_space=pltpu.VMEM)
VMEM_LIMIT = 56 << 20
GROUP = 16


def here():
    return lax.axis_index("dp"), lax.axis_index("blk")


def greet(partners):
    barrier = pltpu.get_barrier_semaphore()
    for partner in partners:
        pl.semaphore_signal(barrier, inc=1, device_id=partner, device_id_type=MESH)
    pl.semaphore_wait(barrier, len(partners))


def remote(src, dst, send_sem, recv_sem, device):
    return pltpu.make_async_remote_copy(
        src_ref=src,
        dst_ref=dst,
        send_sem=send_sem,
        recv_sem=recv_sem,
        device_id=device,
        device_id_type=MESH,
    )


class Gather:
    SEMAPHORES = 40

    def __init__(self, own, out, send, recv):
        self.own, self.out, self.send, self.recv = own, out, send, recv
        dp, b = here()
        self.dp, self.b = dp, b
        self.z, self.y, self.c = b // 4, (b // 2) % 2, b % 2
        self.up = (dp, (b + 4) % GROUP)
        self.down = (dp, (b + 12) % GROUP)
        self.side = (dp, b + 2 - 4 * self.y)
        self.sib = (dp, b + 1 - 2 * self.c)

    def partners(self):
        return [self.up, self.down, self.side, self.sib]

    def copy(self, z, y, c, kind, half, device, own=False):
        block = z * 4 + y * 2 + c
        place = 2 * GROUP - 1 - block if half else block
        source = self.own.at[half] if own else self.out.at[place]
        index = 2 * kind + half
        return remote(source, self.out.at[place], self.send.at[index], self.recv.at[index], device)

    def along(self, z, half, device, own=False, back=False):
        return self.copy(z, self.y, self.c, z + (16 if back else 0), half, device, own)

    def across(self, z, y, half, own=False):
        return self.copy(z, y, self.c, 4 + z, half, self.side, own)

    def to_sib(self, z, y, c, half, own=False):
        return self.copy(z, y, c, 8 + 2 * z + y, half, self.sib, own)

    def start(self):
        z, y = self.z, self.y
        for half in (0, 1):

            @pl.when(z < 3)
            def _():
                self.along(z, half, self.up, True).start()

            @pl.when(z > 0)
            def _():
                self.along(z, half, self.down, True, True).start()

            self.across(z, y, half, True).start()
        for half in (0, 1):
            self.to_sib(z, y, self.c, half, True).start()
        for half in (0, 1):
            place = 2 * GROUP - 1 - self.b if half else self.b
            self.out[place] = self.own[half]

    def line(self, distance):
        for half in (0, 1):
            low, high = self.z - distance, self.z + distance

            @pl.when(low >= 0)
            def _():
                self.along(low, half, self.sib).wait_recv()

                @pl.when(self.z < 3)
                def _():
                    self.along(low, half, self.up).start()

                self.across(low, self.y, half).start()
                self.to_sib(low, self.y, self.c, half).start()

            @pl.when(high <= 3)
            def _():
                self.along(high, half, self.sib, False, True).wait_recv()

                @pl.when(self.z > 0)
                def _():
                    self.along(high, half, self.down, False, True).start()

                self.across(high, self.y, half).start()
                self.to_sib(high, self.y, self.c, half).start()

    def sides(self, distance):
        def one(z, half):
            self.across(z, 1 - self.y, half).wait_recv()
            self.to_sib(z, 1 - self.y, self.c, half).start()

        for half in (0, 1):
            if distance == 0:
                one(self.z, half)
            else:

                @pl.when(self.z - distance >= 0)
                def _():
                    one(self.z - distance, half)

                @pl.when(self.z + distance <= 3)
                def _():
                    one(self.z + distance, half)

    def from_sib(self, distance):
        def one(z):
            for half in (0, 1):
                for y in (0, 1):
                    self.to_sib(z, y, 1 - self.c, half).wait_recv()

        if distance == 0:
            one(self.z)
        else:

            @pl.when(self.z - distance >= 0)
            def _():
                one(self.z - distance)

            @pl.when(self.z + distance <= 3)
            def _():
                one(self.z + distance)

    def drain(self):
        for half in (0, 1):
            for z in range(4):
                for y in (0, 1):
                    self.to_sib(z, y, self.c, half).wait_send()
                self.across(z, self.y, half).wait_send()

                @pl.when((self.z >= z) & (self.z < 3))
                def _():
                    self.along(z, half, self.up).wait_send()

                @pl.when((self.z <= z) & (self.z > 0))
                def _():
                    self.along(z, half, self.down, False, True).wait_send()

    def finish(self):
        for distance in range(4):
            self.from_sib(distance)
        self.drain()


def gather_scratch():
    return [pltpu.SemaphoreType.DMA((Gather.SEMAPHORES,)) for _ in range(2)]


def comm_params(collective_id):
    return pltpu.CompilerParams(
        collective_id=collective_id, has_side_effects=True, vmem_limit_bytes=VMEM_LIMIT
    )


def dot_nt(left, right):
    return lax.dot_general(left, right, (((1,), (1,)), ((), ())), preferred_element_type=jnp.float32)


def dot_tn(left, right):
    return lax.dot_general(left, right, (((0,), (0,)), ((), ())), preferred_element_type=jnp.float32)


def dot_nn(left, right):
    return jnp.dot(left, right, preferred_element_type=jnp.float32)


FF_STEP = 512


def mean_last(array):
    return jnp.mean(array, axis=-1, keepdims=True)


def rms_scale(array):
    return lax.rsqrt(mean_last(array * array) + 1e-06)


def rms_pull(grad, normed, scale):
    return scale * (grad - normed * mean_last(grad * normed))


def half_lanes(shape):
    return lax.broadcasted_iota(jnp.int32, shape, 1) < HEAD_DIM


class Swap:
    def __init__(self, blocks, out, send, recv, own=True):
        self.blocks, self.out, self.own = blocks, out, own
        dp, self.b = here()
        self.copies = []
        for step in range(1, GROUP):
            target = (self.b + step) % GROUP
            self.copies.append(
                remote(
                    blocks.at[target] if own else blocks,
                    out.at[self.b],
                    send.at[step],
                    recv.at[step],
                    (dp, target),
                )
            )
        self.partners = [(dp, (self.b + step) % GROUP) for step in range(1, GROUP)]

    def start(self):
        for copy in self.copies:
            copy.start()
        if self.own:
            self.out[self.b] = self.blocks[self.b]

    def wait(self):
        for copy in self.copies:
            copy.wait()


def middle_kernel(
    o_ref,
    hidden_ref,
    cot_ref,
    w_out_hbm,
    w_up_hbm,
    w_gate_hbm,
    w_down_hbm,
    s_up_ref,
    s_gate_ref,
    alpha_attn_ref,
    alpha_mlp_ref,
    result_ref,
    g_res_ref,
    grad_head_ref,
    mid_all_ref,
    g_mlp_ref,
    att_ref,
    g_branch_ref,
    g_alpha_attn_ref,
    g_alpha_mlp_ref,
    w_out,
    w_up,
    w_gate,
    w_down,
    up_raw,
    gate_raw,
    mid_own,
    o_in,
    g_send,
    acc,
    load_sem,
    swap_sems,
    back_sems,
    ag_send,
    ag_recv,
):
    low = jnp.bfloat16
    loads = [
        pltpu.make_async_copy(source, target, load_sem.at[i])
        for i, (source, target) in enumerate(
            [(w_out_hbm, w_out), (w_up_hbm, w_up), (w_gate_hbm, w_gate), (w_down_hbm, w_down)]
        )
    ]
    for load in loads:
        load.start()
    swap = Swap(o_ref, o_in, swap_sems.at[0], swap_sems.at[1])
    gather = Gather(mid_own, mid_all_ref, ag_send, ag_recv)
    greet(swap.partners)
    swap.start()
    swap.wait()
    rows = hidden_ref.shape[0]
    half = rows // 2
    first = half_lanes((half, 128))
    for pair in range(GROUP // 2):
        even = o_in[2 * pair].astype(jnp.float32)
        odd = o_in[2 * pair + 1].astype(jnp.float32)
        lanes = pl.ds(pair * 128, 128)
        att_ref[:half, lanes] = jnp.where(first, even, pltpu.roll(odd, HEAD_DIM, 1)).astype(low)
        att_ref[half:, lanes] = jnp.where(first, pltpu.roll(even, HEAD_DIM, 1), odd).astype(low)
    hidden = hidden_ref[...].astype(jnp.float32)
    alpha_attn = alpha_attn_ref[...]
    alpha_mlp = alpha_mlp_ref[...]
    loads[0].wait()
    branch = dot_nn(att_ref[...], w_out[...])
    branch_scale = rms_scale(branch)
    branch_normed = branch * branch_scale
    mixed = hidden + alpha_attn * (branch_normed - hidden)
    middle_scale = rms_scale(mixed)
    middle = mixed * middle_scale
    middle_low = middle.astype(low)
    mid_own[0] = middle_low[:half]
    mid_own[1] = middle_low[half:]
    gather.start()

    for load in loads[1:]:
        load.wait()
    steps = w_up.shape[1] // FF_STEP
    acc[...] = jnp.zeros_like(acc)

    def forward(step, carry):
        cols = pl.ds(pl.multiple_of(step * FF_STEP, FF_STEP), FF_STEP)
        up = dot_nn(middle_low, w_up[:, cols])
        gate = dot_nn(middle_low, w_gate[:, cols])
        up_raw[:, cols] = up
        gate_raw[:, cols] = gate
        scaled = gate * s_gate_ref[:, cols]
        inner = up * s_up_ref[:, cols] * (scaled / (1.0 + jnp.exp(-scaled)))
        acc[...] += dot_nn(inner.astype(low), w_down[cols, :])
        return carry

    lax.fori_loop(0, steps, forward, 0)
    gather.line(1)
    gather.sides(0)
    mlp = acc[...]
    mlp_scale = rms_scale(mlp)
    mlp_normed = mlp * mlp_scale
    mixed_out = middle + alpha_mlp * (mlp_normed - middle)
    out_scale = rms_scale(mixed_out)
    result = mixed_out * out_scale
    result_ref[...] = result.astype(low)
    g_mixed = rms_pull(cot_ref[...].astype(jnp.float32), result, out_scale)
    g_alpha_mlp_ref[...] = jnp.sum(g_mixed * (mlp_normed - middle), axis=0, keepdims=True)
    g_mlp = rms_pull(g_mixed * alpha_mlp, mlp_normed, mlp_scale).astype(low)
    g_mlp_ref[...] = g_mlp
    acc[...] = g_mixed * (1.0 - alpha_mlp)

    def backward(step, carry):
        cols = pl.ds(pl.multiple_of(step * FF_STEP, FF_STEP), FF_STEP)
        g_inner = dot_nt(g_mlp, w_down[cols, :])
        s_up = s_up_ref[:, cols]
        s_gate = s_gate_ref[:, cols]
        scaled = gate_raw[:, cols] * s_gate
        sigmoid = 1.0 / (1.0 + jnp.exp(-scaled))
        g_up = g_inner * (scaled * sigmoid) * s_up
        slope = sigmoid * (1.0 + scaled * (1.0 - sigmoid))
        g_gate = g_inner * (up_raw[:, cols] * s_up) * slope * s_gate
        acc[...] += dot_nt(g_up.astype(low), w_up[:, cols]) + dot_nt(
            g_gate.astype(low), w_gate[:, cols]
        )
        return carry

    lax.fori_loop(0, steps // 2, backward, 0)
    gather.line(2)
    gather.sides(1)
    lax.fori_loop(steps // 2, steps, backward, 0)
    g_pre = rms_pull(acc[...], middle, middle_scale)
    g_res_ref[...] = g_pre * (1.0 - alpha_attn)
    g_alpha_attn_ref[...] = jnp.sum(g_pre * (branch_normed - hidden), axis=0, keepdims=True)
    g_branch = rms_pull(g_pre * alpha_attn, branch_normed, branch_scale).astype(low)
    g_branch_ref[...] = g_branch
    g_att = dot_nt(g_branch, w_out[...]).astype(low).astype(jnp.float32)
    for pair in range(GROUP // 2):
        lower = g_att[:half, pair * 128 : (pair + 1) * 128]
        upper = g_att[half:, pair * 128 : (pair + 1) * 128]
        g_send[2 * pair] = jnp.where(first, lower, pltpu.roll(upper, HEAD_DIM, 1)).astype(low)
        g_send[2 * pair + 1] = jnp.where(first, pltpu.roll(lower, HEAD_DIM, 1), upper).astype(low)
    back = Swap(g_send, grad_head_ref, back_sems.at[0], back_sems.at[1])
    back.start()
    gather.line(3)
    gather.sides(2)
    gather.sides(3)
    gather.finish()
    back.wait()


ANY_SPEC = pl.BlockSpec(memory_space=pl.ANY)


def middle_block(packed, hidden, cot, w_out, w_up, w_gate, w_down, s_up, s_gate, alpha_attn, alpha_mlp):
    rows, width = hidden.shape
    ff = w_up.shape[1]
    low, f32 = jnp.bfloat16, jnp.float32
    shape = jax.ShapeDtypeStruct
    return pl.pallas_call(
        middle_kernel,
        out_shape=[
            shape((rows, width), low),
            shape((rows, width), f32),
            shape(packed.shape, low),
            shape((2 * GROUP, rows // 2, width), low),
            shape((rows, width), low),
            shape((rows, width), low),
            shape((rows, width), low),
            shape((1, width), f32),
            shape((1, width), f32),
        ],
        in_specs=[VMEM_SPEC] * 3 + [ANY_SPEC] * 4 + [VMEM_SPEC] * 4,
        out_specs=[VMEM_SPEC] * 9,
        scratch_shapes=[
            pltpu.VMEM(w_out.shape, low),
            pltpu.VMEM(w_up.shape, low),
            pltpu.VMEM(w_gate.shape, low),
            pltpu.VMEM(w_down.shape, low),
            pltpu.VMEM((rows, ff), f32),
            pltpu.VMEM((rows, ff), f32),
            pltpu.VMEM((2, rows // 2, width), low),
            pltpu.VMEM(packed.shape, low),
            pltpu.VMEM(packed.shape, low),
            pltpu.VMEM((rows, width), f32),
            pltpu.SemaphoreType.DMA((4,)),
            pltpu.SemaphoreType.DMA((2, GROUP)),
            pltpu.SemaphoreType.DMA((2, GROUP)),
        ]
        + gather_scratch(),
        compiler_params=comm_params(1),
        name="middle_block",
    )(
        packed,
        hidden,
        cot,
        w_out,
        w_up,
        w_gate,
        w_down,
        s_up[None],
        s_gate[None],
        alpha_attn[None],
        alpha_mlp[None],
    )


SMEM_SPEC = pl.BlockSpec(memory_space=pltpu.SMEM)


def own_head(pair, core):
    shifted = jnp.where(core == 1, pltpu.roll(pair, HEAD_DIM, 1), pair)
    return jnp.where(half_lanes(pair.shape), shifted, 0.0)


def minus_ones(matrix):
    lane = lax.broadcasted_iota(jnp.int32, matrix.shape, 1)
    extra = jnp.where(lane < HEAD_DIM + 3, -1.0, 0.0)
    return jnp.where(lane < HEAD_DIM, matrix, extra).astype(jnp.bfloat16)


def project_kernel(
    own,
    w_query_hbm,
    w_key_hbm,
    w_value_hbm,
    s_qk_ref,
    out,
    qa_ref,
    ka_ref,
    va_ref,
    q_raw_ref,
    k_raw_ref,
    gain_ref,
    w_head,
    load_sem,
    send,
    recv,
):
    gather = Gather(own, out, send, recv)
    window = pl.ds(pl.multiple_of(gather.b // 2 * 128, 128), 128)
    loads = [
        pltpu.make_async_copy(
            source.at[:, window], w_head.at[:, pl.ds(128 * i, 128)], load_sem.at[i]
        )
        for i, source in enumerate((w_query_hbm, w_key_hbm, w_value_hbm))
    ]
    for load in loads:
        load.start()
    greet(gather.partners())
    gather.start()
    gain = own_head(jnp.broadcast_to(s_qk_ref[:, window], (8, 128)), gather.c)[:1]
    gain_ref[...] = gain
    for load in loads:
        load.wait()
    slots = 2 * GROUP // 8
    half = out.shape[1]

    def project(first_slot):
        hidden = out[pl.ds(first_slot, slots)].reshape(slots * half, out.shape[2])
        raw = dot_nn(hidden, w_head[...])
        rows = pl.ds(pl.multiple_of(first_slot * half, half), slots * half)
        query, key, value = (
            own_head(raw[:, 128 * i : 128 * (i + 1)], gather.c) for i in range(3)
        )
        q_raw_ref[rows, :] = query
        k_raw_ref[rows, :] = key
        count = float(HEAD_DIM)
        query_scale = lax.rsqrt(jnp.sum(query * query, axis=1, keepdims=True) / count + 1e-06)
        key_scale = lax.rsqrt(jnp.sum(key * key, axis=1, keepdims=True) / count + 1e-06)
        query = (query * query_scale * gain).astype(jnp.bfloat16).astype(jnp.float32)
        qa_ref[rows, :] = (query * (1.0 / math.sqrt(HEAD_DIM))).astype(jnp.bfloat16)
        ka_ref[rows, :] = minus_ones(key * key_scale * gain)
        va_ref[rows, :] = minus_ones(value)

    def project_line(distance):
        def both(z):
            project(slots * z)
            project(2 * GROUP - slots - slots * z)

        if distance == 0:
            both(gather.z)
        else:

            @pl.when(gather.z - distance >= 0)
            def _():
                both(gather.z - distance)

            @pl.when(gather.z + distance <= 3)
            def _():
                both(gather.z + distance)

    gather.line(1)
    gather.sides(0)
    gather.from_sib(0)
    project_line(0)
    gather.line(2)
    gather.sides(1)
    gather.from_sib(1)
    project_line(1)
    gather.line(3)
    gather.sides(2)
    gather.from_sib(2)
    project_line(2)
    gather.sides(3)
    gather.from_sib(3)
    project_line(3)
    gather.drain()


def project_block(hidden, w_query, w_key, w_value, s_qk):
    rows, width = hidden.shape
    length = GROUP * rows
    low, f32 = jnp.bfloat16, jnp.float32
    shape = jax.ShapeDtypeStruct
    return pl.pallas_call(
        project_kernel,
        out_shape=[
            shape((2 * GROUP, rows // 2, width), low),
            shape((length, 128), low),
            shape((length, 128), low),
            shape((length, 128), low),
            shape((length, 128), f32),
            shape((length, 128), f32),
            shape((1, 128), f32),
        ],
        in_specs=[VMEM_SPEC] + [ANY_SPEC] * 3 + [VMEM_SPEC],
        out_specs=[VMEM_SPEC] * 7,
        scratch_shapes=[pltpu.VMEM((width, 384), low), pltpu.SemaphoreType.DMA((3,))]
        + gather_scratch(),
        compiler_params=comm_params(0),
        name="project_block",
    )(hidden.reshape(2, rows // 2, width), w_query, w_key, w_value, s_qk[None])


def doc_start_of(positions, lengths_ref):
    start = jnp.zeros_like(positions)
    end = jnp.int32(0)
    for doc in range(lengths_ref.shape[1]):
        end = end + lengths_ref[0, doc]
        start = start + jnp.where(positions >= end, lengths_ref[0, doc], 0)
    return start


def split_lanes(column, shape):
    lane = lax.broadcasted_iota(jnp.int32, shape, 1)
    high = column.astype(jnp.bfloat16).astype(jnp.float32)
    rest = column - high
    mid = rest.astype(jnp.bfloat16).astype(jnp.float32)
    last = rest - mid
    return jnp.where(
        lane == HEAD_DIM,
        high,
        jnp.where(lane == HEAD_DIM + 1, mid, jnp.where(lane == HEAD_DIM + 2, last, 0.0)),
    )


ATT = 512


def attend_kernel(lengths_ref, qa_ref, ka_ref, va_ref, o_ref, ql_ref, packed_ref):
    length = qa_ref.shape[0]
    half = packed_ref.shape[1]
    for query_block in range(length // ATT):
        rows = pl.ds(query_block * ATT, ATT)
        queries = qa_ref[rows, :]
        column = query_block * ATT + lax.broadcasted_iota(jnp.int32, (ATT, 1), 0)
        doc_start = doc_start_of(column, lengths_ref)
        first_start = doc_start_of(jnp.int32(query_block * ATT), lengths_ref)
        query_pos = query_block * ATT + lax.broadcasted_iota(jnp.int32, (ATT, ATT), 0)
        key_lane = lax.broadcasted_iota(jnp.int32, (ATT, ATT), 1)

        def step(key_block, total):
            base = pl.multiple_of(key_block * ATT, ATT)
            keys = ka_ref[pl.ds(base, ATT), :]
            values = va_ref[pl.ds(base, ATT), :]
            key_pos = base + key_lane
            allowed = (key_pos <= query_pos) & (key_pos >= doc_start)
            weights = jnp.where(allowed, jnp.exp(dot_nt(queries, keys)), 0.0)
            return total + dot_nn(weights.astype(jnp.bfloat16), values)

        total = lax.fori_loop(
            first_start // ATT, query_block + 1, step, jnp.zeros((ATT, 128), jnp.float32)
        )
        row_sum = -total[:, HEAD_DIM : HEAD_DIM + 1]
        first = half_lanes(total.shape)
        o_ref[rows, :] = jnp.where(first, total / row_sum, 0.0)
        extra = split_lanes(jnp.log(row_sum), total.shape)
        ql_ref[rows, :] = jnp.where(first, queries.astype(jnp.float32), extra).astype(jnp.bfloat16)
    first = half_lanes((half, 128))
    for j in range(GROUP):
        lower = o_ref[j * half : (j + 1) * half, :]
        upper = o_ref[length - (j + 1) * half : length - j * half, :]
        packed_ref[j] = jnp.where(first, lower, pltpu.roll(upper, HEAD_DIM, 1)).astype(
            packed_ref.dtype
        )


def attend(lengths, qa, ka, va, half_rows):
    length = qa.shape[0]
    shape = jax.ShapeDtypeStruct
    return pl.pallas_call(
        attend_kernel,
        out_shape=[
            shape((length, 128), jnp.float32),
            shape((length, 128), jnp.bfloat16),
            shape((GROUP, half_rows, 128), jnp.bfloat16),
        ],
        in_specs=[SMEM_SPEC] + [VMEM_SPEC] * 3,
        out_specs=[VMEM_SPEC] * 3,
        compiler_params=pltpu.CompilerParams(vmem_limit_bytes=VMEM_LIMIT),
        name="attend",
    )(lengths, qa, ka, va)


def finish_kernel(
    lengths_ref,
    grad_packed,
    o_ref,
    ql_ref,
    ka_ref,
    va_ref,
    q_raw_ref,
    k_raw_ref,
    gain_ref,
    hidden_all,
    mid_all,
    g_mlp_own,
    g_res_ref,
    small_in,
    s_up_ref,
    s_gate_ref,
    w_query_hbm,
    w_key_hbm,
    w_value_hbm,
    w_up_hbm,
    w_gate_hbm,
    w_down_hbm,
    input_grad_ref,
    g_query_ref,
    g_key_ref,
    g_value_ref,
    g_up_ref,
    g_gate_ref,
    g_down_ref,
    g_s_ref,
    small_ref,
    g_mlp_all,
    ga_ref,
    dq_ref,
    dk_ref,
    dv_ref,
    raw_low,
    w_qkv,
    w_up,
    w_gate,
    w_down,
    back_send,
    back_in,
    home,
    g_cat,
    inner,
    wide_own,
    wide_send,
    wide_got,
    wide_blocks,
    wide_in,
    qkv_part,
    down_part,
    down_send,
    down_got,
    small_own,
    small_got,
    small_all,
    s_part,
    s_send,
    s_got,
    load_sem,
    x_sems,
    back_sems,
    wide_sems,
    small_sems,
    ag_send,
    ag_recv,
):
    low, f32 = jnp.bfloat16, jnp.float32
    dp, b = here()
    length = ql_ref.shape[0]
    half = g_mlp_own.shape[1]
    width = hidden_all.shape[2]
    gather = Gather(g_mlp_own, g_mlp_all, ag_send, ag_recv)
    twin = (1 - dp, b)
    part = w_down.shape[0] // 2
    ff_half = w_up_hbm.shape[1] // 2

    def load(index, source, target):
        copy = pltpu.make_async_copy(source, target, load_sem.at[index])
        copy.start()
        return copy

    loads = []
    for p in (0, 1):
        window = pl.ds(pl.multiple_of(p * ff_half + b * part, part), part)
        place = pl.ds(p * part, part)
        loads.append(load(3 * p, w_up_hbm.at[:, window], w_up.at[:, place]))
        loads.append(load(3 * p + 1, w_gate_hbm.at[:, window], w_gate.at[:, place]))
        loads.append(load(3 * p + 2, w_down_hbm.at[window, :], w_down.at[place, :]))
    qkv_loads = [
        load(6 + i, source, w_qkv.at[i])
        for i, source in enumerate((w_query_hbm, w_key_hbm, w_value_hbm))
    ]

    def to_twin(index, source, target):
        copy = remote(source, target, x_sems.at[0, index], x_sems.at[1, index], twin)
        copy.start()
        return copy

    back = Swap(back_send, back_in, back_sems.at[0], back_sems.at[1])
    wide_swap = Swap(wide_blocks, wide_in, wide_sems.at[0], wide_sems.at[1])
    small_swap = Swap(small_own, small_all, small_sems.at[0], small_sems.at[1], own=False)
    greet(back.partners + [twin])
    gather.start()

    first = half_lanes((half, 128))
    for j in range(GROUP):
        block = grad_packed[j].astype(f32)
        for start, grads in (
            (j * half, jnp.where(first, block, 0.0)),
            (length - (j + 1) * half, jnp.where(first, pltpu.roll(block, HEAD_DIM, 1), 0.0)),
        ):
            rows = pl.ds(start, half)
            delta = jnp.sum(grads * o_ref[rows, :], axis=1, keepdims=True)
            ga_ref[rows, :] = (grads + split_lanes(delta, grads.shape)).astype(low)
    dq_ref[...] = jnp.zeros_like(dq_ref)
    key_row = lax.broadcasted_iota(jnp.int32, (ATT, ATT), 0)
    query_lane = lax.broadcasted_iota(jnp.int32, (ATT, ATT), 1)
    query_row = lax.broadcasted_iota(jnp.int32, (1, ATT), 1)
    blocks = length // ATT
    for key_block in range(blocks):
        rows = pl.ds(key_block * ATT, ATT)
        keys = ka_ref[rows, :]
        values = va_ref[rows, :]
        key_pos = key_block * ATT + key_row
        dk_ref[rows, :] = jnp.zeros((ATT, 128), f32)
        dv_ref[rows, :] = jnp.zeros((ATT, 128), f32)

        def step(query_block, carry):
            base = pl.multiple_of(query_block * ATT, ATT)
            span = pl.ds(base, ATT)
            queries = ql_ref[span, :]
            grads = ga_ref[span, :]
            doc_start = doc_start_of(base + query_row, lengths_ref)
            allowed = (key_pos <= base + query_lane) & (key_pos >= doc_start)
            weights = jnp.where(allowed, jnp.exp(dot_nt(keys, queries)), 0.0)
            slopes = (weights * dot_nt(values, grads)).astype(low)
            dv_ref[rows, :] += dot_nn(weights.astype(low), grads)
            dk_ref[rows, :] += dot_nn(slopes, queries)
            dq_ref[span, :] += dot_tn(slopes, keys)
            return carry

        lax.fori_loop(key_block, blocks, step, 0)
        if key_block == 0:
            gather.line(1)
            gather.sides(0)
        if key_block == 2:
            gather.line(2)
            gather.sides(1)

    gain = gain_ref[...]
    count = float(HEAD_DIM)
    score_scale = 1.0 / math.sqrt(HEAD_DIM)

    def norm_pull(raw, grad):
        scale = lax.rsqrt(jnp.sum(raw * raw, axis=1, keepdims=True) / count + 1e-06)
        normed = raw * scale
        g_gain = jnp.sum(grad * normed, axis=0, keepdims=True)
        inside = grad * gain
        mean = jnp.sum(inside * normed, axis=1, keepdims=True) / count
        return scale * (inside - normed * mean), g_gain

    g_gain = jnp.zeros((1, 128), f32)
    wide_first = half_lanes((ATT, 128))
    for block in range(blocks):
        rows = pl.ds(block * ATT, ATT)
        dq = jnp.where(wide_first, dq_ref[rows, :] * score_scale, 0.0)
        dk = jnp.where(wide_first, dk_ref[rows, :], 0.0)
        dv = jnp.where(wide_first, dv_ref[rows, :], 0.0)
        g_query, gain_first = norm_pull(q_raw_ref[rows, :], dq)
        g_key, gain_second = norm_pull(k_raw_ref[rows, :], dk)
        g_gain = g_gain + gain_first + gain_second
        for i, grads in enumerate((g_query, g_key, dv)):
            raw_low[rows, 128 * i : 128 * (i + 1)] = grads.astype(low)
    for j in range(GROUP):
        for i in range(3):
            lanes = slice(128 * i, 128 * (i + 1))
            lower = raw_low[j * half : (j + 1) * half, lanes].astype(f32)
            upper = raw_low[length - (j + 1) * half : length - j * half, lanes].astype(f32)
            back_send[j, :, lanes] = jnp.where(
                first, lower, pltpu.roll(upper, HEAD_DIM, 1)
            ).astype(low)
    back.start()
    small_own[...] = small_in[...]
    small_own[16:17, :] = g_gain
    small_copy = to_twin(0, small_own, small_got)
    gather.line(3)
    gather.sides(2)

    quarter = width // 4
    for chunk in range(4):
        lanes = pl.ds(chunk * quarter, quarter)
        tokens = hidden_all[:, :, lanes].reshape(length, quarter)
        grads = dot_tn(tokens, raw_low[...])
        query_key = jnp.where(
            half_lanes((quarter, 128)), grads[:, :128], pltpu.roll(grads[:, 128:256], HEAD_DIM, 1)
        )
        qkv_part[chunk, :, :128] = query_key
        qkv_part[chunk, :, 128:] = grads[:, 256:]
    gather.sides(3)
    gather.finish()

    small_copy.wait()
    small_own[...] += small_got[...]
    small_swap.start()

    for copy in loads:
        copy.wait()
    windows = [pl.ds(pl.multiple_of(p * ff_half + b * part, part), part) for p in (0, 1)]
    s_up = jnp.concatenate([s_up_ref[:, window] for window in windows], axis=1)
    s_gate = jnp.concatenate([s_gate_ref[:, window] for window in windows], axis=1)
    slots = ATT // half

    def tokens_of(array, step):
        return array[pl.ds(step * slots, slots)].reshape(ATT, width)

    def recompute(step, sums):
        rows = pl.ds(pl.multiple_of(step * ATT, ATT), ATT)
        middle = tokens_of(mid_all, step)
        up = dot_nn(middle, w_up[...])
        gate = dot_nn(middle, w_gate[...])
        g_inner = dot_nt(tokens_of(g_mlp_all, step), w_down[...])
        scaled = gate * s_gate
        sigmoid = 1.0 / (1.0 + jnp.exp(-scaled))
        silu = scaled / (1.0 + jnp.exp(-scaled))
        up_scaled = up * s_up
        inner[rows, :] = (up_scaled * silu).astype(low)
        g_up_scaled = g_inner * silu
        g_scaled = g_inner * up_scaled * (sigmoid * (1.0 + scaled * (1.0 - sigmoid)))
        g_cat[rows, : 2 * part] = (g_up_scaled * s_up).astype(low)
        g_cat[rows, 2 * part :] = (g_scaled * s_gate).astype(low)
        return (
            sums[0] + jnp.sum(g_up_scaled * up, axis=0, keepdims=True),
            sums[1] + jnp.sum(g_scaled * gate, axis=0, keepdims=True),
        )

    zero_row = jnp.zeros((1, 2 * part), f32)
    g_s_up, g_s_gate = lax.fori_loop(0, blocks, recompute, (zero_row, zero_row))
    for p in (0, 1):
        s_part[p] = jnp.zeros(s_part.shape[1:], f32)
        s_part[p, 0:1, :] = g_s_up[:, p * part : (p + 1) * part]
        s_part[p, 1:2, :] = g_s_gate[:, p * part : (p + 1) * part]
    s_send[...] = s_part[1 - dp]
    s_copy = to_twin(1, s_send, s_got)
    for chunk in range(4):
        lanes = pl.ds(chunk * quarter, quarter)
        down_part[:, lanes] = dot_tn(inner[...], g_mlp_all[:, :, lanes].reshape(length, quarter))
    down_send[...] = down_part[pl.ds(pl.multiple_of((1 - dp) * part, part), part), :].astype(low)
    down_copy = to_twin(2, down_send, down_got)

    def wide_chunk(chunk):
        lanes = pl.ds(pl.multiple_of(chunk * quarter, quarter), quarter)
        return dot_tn(mid_all[:, :, lanes].reshape(length, quarter), g_cat[...])

    wide_copies = []
    for i in (0, 1):
        chunk = 2 * (1 - dp) + i
        wide_send[i, :, : 4 * part] = wide_chunk(chunk).astype(low)
        wide_send[i, :, 4 * part :] = qkv_part[chunk].astype(low)
        wide_copies.append(to_twin(3 + i, wide_send.at[i], wide_got.at[i]))
    for i in (0, 1):
        chunk = 2 * dp + i
        wide_own[i, :, : 4 * part] = wide_chunk(chunk)
        wide_own[i, :, 4 * part :] = qkv_part[chunk]

    back.wait()
    for pair in range(GROUP // 2):
        for i in range(3):
            lanes = slice(128 * i, 128 * (i + 1))
            even = back_in[2 * pair, :, lanes].astype(f32)
            odd = back_in[2 * pair + 1, :, lanes].astype(f32)
            place = slice(128 * pair, 128 * (pair + 1))
            home[i, :half, place] = jnp.where(first, even, pltpu.roll(odd, HEAD_DIM, 1)).astype(low)
            home[i, half:, place] = jnp.where(first, pltpu.roll(even, HEAD_DIM, 1), odd).astype(low)
    for copy in qkv_loads:
        copy.wait()
    input_grad_ref[...] = (
        g_res_ref[...]
        + dot_nt(home[0], w_qkv[0])
        + dot_nt(home[1], w_qkv[1])
        + dot_nt(home[2], w_qkv[2])
    )

    rows_out = width // (2 * GROUP)
    per_chunk = quarter // rows_out
    for i in (0, 1):
        wide_copies[i].wait()
        total = (wide_own[i] + wide_got[i].astype(f32)).astype(low)
        for k in range(per_chunk):
            wide_blocks[i * per_chunk + k] = total[k * rows_out : (k + 1) * rows_out]
    wide_swap.start()
    s_copy.wait()
    g_s_ref[...] = s_part[dp] + s_got[...]
    down_copy.wait()
    g_down_ref[...] = down_part[pl.ds(pl.multiple_of(dp * part, part), part), :] + down_got[
        ...
    ].astype(f32)
    small_swap.wait()
    small_all[b] = small_own[...]
    small_ref[...] = jnp.sum(small_all[...], axis=0)
    jsrc = 8 * dp + b // 2
    small_ref[17:18, :] = small_all[jsrc, 16:17, :]
    wide_swap.wait()
    row_first = half_lanes((rows_out, 128))
    for j in range(GROUP):
        for p in (0, 1):
            place = slice(p * ff_half + j * part, p * ff_half + (j + 1) * part)
            g_up_ref[:, place] = wide_in[j, :, p * part : (p + 1) * part].astype(f32)
            g_gate_ref[:, place] = wide_in[j, :, (2 + p) * part : (3 + p) * part].astype(f32)
    for pair in range(GROUP // 2):
        place = slice(128 * pair, 128 * (pair + 1))
        even = wide_in[2 * pair, :, 4 * part : 4 * part + 128].astype(f32)
        odd = wide_in[2 * pair + 1, :, 4 * part : 4 * part + 128].astype(f32)
        g_query_ref[:, place] = jnp.where(row_first, even, pltpu.roll(odd, HEAD_DIM, 1))
        g_key_ref[:, place] = jnp.where(row_first, pltpu.roll(even, HEAD_DIM, 1), odd)
        even = wide_in[2 * pair, :, 4 * part + 128 :].astype(f32)
        odd = wide_in[2 * pair + 1, :, 4 * part + 128 :].astype(f32)
        g_value_ref[:, place] = jnp.where(row_first, even, pltpu.roll(odd, HEAD_DIM, 1))


def finish_block(inputs, rows, width, ff):
    low, f32 = jnp.bfloat16, jnp.float32
    shape, vmem, sems = jax.ShapeDtypeStruct, pltpu.VMEM, pltpu.SemaphoreType.DMA
    length = GROUP * rows
    half = rows // 2
    rows_out = width // (2 * GROUP)
    part = ff // (2 * GROUP)
    wide = 4 * part + 256
    quarter = width // 4
    return pl.pallas_call(
        finish_kernel,
        out_shape=[
            shape((rows, width), f32),
            shape((rows_out, width), f32),
            shape((rows_out, width), f32),
            shape((rows_out, width), f32),
            shape((rows_out, ff), f32),
            shape((rows_out, ff), f32),
            shape((part, width), f32),
            shape((8, 128), f32),
            shape((24, 128), f32),
        ],
        in_specs=[SMEM_SPEC] + [VMEM_SPEC] * 15 + [ANY_SPEC] * 6,
        out_specs=[VMEM_SPEC] * 9,
        scratch_shapes=[
            vmem((2 * GROUP, half, width), low),
            vmem((length, 128), low),
            vmem((length, 128), f32),
            vmem((length, 128), f32),
            vmem((length, 128), f32),
            vmem((length, 384), low),
            vmem((3, width, width), low),
            vmem((width, 2 * part), low),
            vmem((width, 2 * part), low),
            vmem((2 * part, width), low),
            vmem((GROUP, half, 384), low),
            vmem((GROUP, half, 384), low),
            vmem((3, rows, width), low),
            vmem((length, 4 * part), low),
            vmem((length, 2 * part), low),
            vmem((2, quarter, wide), f32),
            vmem((2, quarter, wide), low),
            vmem((2, quarter, wide), low),
            vmem((GROUP, rows_out, wide), low),
            vmem((GROUP, rows_out, wide), low),
            vmem((4, quarter, 256), f32),
            vmem((2 * part, width), f32),
            vmem((part, width), low),
            vmem((part, width), low),
            vmem((24, 128), f32),
            vmem((24, 128), f32),
            vmem((GROUP, 24, 128), f32),
            vmem((2, 8, 128), f32),
            vmem((8, 128), f32),
            vmem((8, 128), f32),
            sems((9,)),
            sems((2, 8)),
            sems((2, GROUP)),
            sems((2, GROUP)),
            sems((2, GROUP)),
        ]
        + gather_scratch(),
        compiler_params=comm_params(2),
        name="finish_block",
    )(*inputs)


def on_device_heads(
    tokens,
    cotangent,
    lengths,
    w_query,
    w_key,
    w_value,
    w_out,
    w_up,
    w_gate,
    w_down,
    s_qk,
    s_up,
    s_gate,
    alpha_attn,
    alpha_mlp,
):
    model_width = w_query.shape[0]
    tok_rows = tokens.shape[2]
    half_rows = tok_rows // 2
    hidden = tokens[0, 0]
    hidden_all, qa, ka, va, query_raw, key_raw, gain = project_block(
        hidden, w_query, w_key, w_value, s_qk
    )
    attended, ql, packed = attend(lengths, qa, ka, va, half_rows)
    (
        result,
        grad_hidden,
        grad_packed,
        middle_all,
        grad_mlp,
        attended_low,
        branch_low,
        grad_alpha_attn,
        grad_alpha_mlp,
    ) = middle_block(
        packed,
        hidden,
        cotangent[0, 0],
        w_out,
        w_up,
        w_gate,
        w_down,
        s_up,
        s_gate,
        alpha_attn,
        alpha_mlp,
    )
    part_out = dot_tn(attended_low, branch_low)
    grad_out = lax.psum_scatter(part_out, ("dp", "blk"), scatter_dimension=0, tiled=True)
    small = jnp.concatenate(
        [
            grad_alpha_attn.reshape(-1, 128),
            grad_alpha_mlp.reshape(-1, 128),
            jnp.zeros((8, 128), jnp.float32),
        ],
        axis=0,
    )
    (
        input_grad,
        grad_query,
        grad_key,
        grad_value,
        grad_up,
        grad_gate,
        grad_down,
        grad_scales,
        small,
    ) = finish_block(
        (
            lengths,
            grad_packed,
            attended,
            ql,
            ka,
            va,
            query_raw,
            key_raw,
            gain,
            hidden_all,
            middle_all,
            grad_mlp.reshape(2, half_rows, model_width),
            grad_hidden,
            small,
            s_up[None],
            s_gate[None],
            w_query,
            w_key,
            w_value,
            w_up,
            w_gate,
            w_down,
        ),
        tok_rows,
        model_width,
        w_up.shape[1],
    )
    dp, b = here()
    rows_out = model_width // (2 * GROUP)
    first_row = (dp * GROUP + b) * rows_out
    grad_attn, grad_mlp_alpha = (
        lax.dynamic_slice_in_dim(small[8 * i : 8 * (i + 1)].reshape(-1), first_row, rows_out, 0)
        for i in (0, 1)
    )
    grad_gain = lax.dynamic_slice_in_dim(small[17], (b % 2) * rows_out, rows_out, 0)
    mean_alpha = 0.5 * (jnp.mean(alpha_attn) + jnp.mean(alpha_mlp))
    return (
        result[None, None],
        input_grad[None, None],
        grad_query,
        grad_key,
        grad_value,
        grad_out,
        grad_up,
        grad_gate,
        grad_down,
        grad_gain,
        grad_scales[0],
        grad_scales[1],
        grad_attn,
        grad_mlp_alpha,
        mean_alpha,
    )


def on_device(*arrays):
    head_count = arrays[3].shape[0] // HEAD_DIM
    tok_rows = arrays[0].shape[2]
    fits = lax.axis_size("blk") == head_count == 16 and lax.axis_size("dp") == 2
    if fits and tok_rows == 128:
        return on_device_heads(*arrays)
    return on_device_general(*arrays)


def solution(mesh):
    in_specs = (
        P("dp", "blk", None, None),
        P("dp", "blk", None, None),
        P("dp", None),
        P(),
        P(),
        P(),
        P(),
        P(),
        P(),
        P(),
        P(),
        P(),
        P(),
        P(),
        P(),
    )
    out_specs = (
        P("dp", "blk", None, None),
        P("dp", "blk", None, None),
        P(("dp", "blk"), None),
        P(("dp", "blk"), None),
        P(("dp", "blk"), None),
        P(("dp", "blk"), None),
        P(("dp", "blk"), None),
        P(("dp", "blk"), None),
        P(("dp", "blk"), None),
        P(("dp", "blk")),
        P(("dp", "blk")),
        P(("dp", "blk")),
        P(("dp", "blk")),
        P(("dp", "blk")),
        P(),
    )
    return jax.shard_map(
        on_device, mesh=mesh, in_specs=in_specs, out_specs=out_specs, check_vma=False
    )
```

```python
import functools
import math

import jax
import jax.numpy as jnp
from jax import lax
from jax.experimental import pallas as pl
from jax.experimental.pallas import tpu as pltpu
from jax.sharding import PartitionSpec as P

HEAD_DIM = 64


def rms_norm(vector):
    return vector * lax.rsqrt(jnp.mean(vector * vector, axis=-1, keepdims=True) + 1e-06)


def head_norm(vector, head_count):
    shaped = vector.reshape(vector.shape[0], head_count, -1)
    return rms_norm(shaped).reshape(vector.shape)


def silu_smooth(vector):
    return vector / (1.0 + jnp.exp(-vector))


def residual_mix(inputs, branch, alphas):
    return rms_norm(inputs + alphas * (rms_norm(branch) - inputs))


def gated_inner(up_raw, gate_raw, s_up, s_gate):
    return up_raw * s_up * silu_smooth(gate_raw * s_gate)


def stream_positions(row_index, tok_rows, members):
    half_rows = tok_rows // 2
    device = row_index // tok_rows
    within = row_index % tok_rows
    block_id = jnp.where(within < half_rows, device, 2 * members - 1 - device)
    return block_id * half_rows + within % half_rows


def doc_index(positions, doc_ends):
    return jnp.sum(
        (positions[:, None] >= doc_ends[None, :]).astype(jnp.int32), axis=1, dtype=jnp.int32
    )


def allowed_pairs(query_pos, query_doc, key_pos, key_doc):
    return (key_pos[None, :] <= query_pos[:, None]) & (key_doc[None, :] == query_doc[:, None])


def take_rows(matrix, first_row, row_count):
    return lax.dynamic_slice_in_dim(matrix, first_row, row_count, 0)


def fold_half(running, query_heads, key_heads, value_heads, allowed, score_scale):

    def absorb(carried):
        best_score, total_sum, accumulated = carried
        scores = (
            jnp.einsum("qhd,khd->hqk", query_heads, key_heads, preferred_element_type=jnp.float32)
            * score_scale
        )
        scores = jnp.where(allowed[None], scores, -1e30)
        new_best = jnp.maximum(best_score, jnp.max(scores, axis=2))
        weights = jnp.where(allowed[None], jnp.exp(scores - new_best[:, :, None]), 0.0)
        fade_factor = jnp.exp(best_score - new_best)
        total_sum = jnp.sum(weights, axis=2)
        accumulated = accumulated * fade_factor.T[:, :, None] + jnp.einsum(
            "hqk,khd->qhd",
            weights.astype(jnp.bfloat16),
            value_heads,
            preferred_element_type=jnp.float32,
        )
        return (new_best, total_sum, accumulated)

    return lax.cond(jnp.any(allowed), absorb, lambda carried: carried, running)


def pair_terms(query_side, key_heads, value_heads, allowed, score_scale):
    query_heads, grad_heads, log_total, delta_rows = (
        query_side[0],
        query_side[1],
        query_side[2],
        query_side[3],
    )
    scores = (
        jnp.einsum("qhd,khd->hqk", query_heads, key_heads, preferred_element_type=jnp.float32)
        * score_scale
    )
    scores = jnp.where(allowed[None], scores, -1e30)
    weights = jnp.exp(scores - log_total[:, :, None])
    grad_weights = jnp.einsum(
        "qhd,khd->hqk", grad_heads, value_heads, preferred_element_type=jnp.float32
    )
    grad_scores = (weights * (grad_weights - delta_rows[:, :, None])).astype(jnp.bfloat16)
    return (weights.astype(jnp.bfloat16), grad_scores)


def query_term(query_side, key_heads, value_heads, allowed, score_scale):
    weights, grad_scores = pair_terms(query_side, key_heads, value_heads, allowed, score_scale)
    return score_scale * jnp.einsum(
        "hqk,khd->qhd", grad_scores, key_heads, preferred_element_type=jnp.float32
    )


def key_term(query_side, key_heads, value_heads, allowed, score_scale):
    weights, grad_scores = pair_terms(query_side, key_heads, value_heads, allowed, score_scale)
    grad_keys = score_scale * jnp.einsum(
        "hqk,qhd->khd", grad_scores, query_side[0], preferred_element_type=jnp.float32
    )
    grad_values = jnp.einsum(
        "hqk,qhd->khd", weights, query_side[1], preferred_element_type=jnp.float32
    )
    return (grad_keys, grad_values)


def on_device_general(
    tokens,
    cotangent,
    lengths,
    w_query,
    w_key,
    w_value,
    w_out,
    w_up,
    w_gate,
    w_down,
    s_qk,
    s_up,
    s_gate,
    alpha_attn,
    alpha_mlp,
):
    model_width = w_query.shape[0]
    head_count = model_width // HEAD_DIM
    score_scale = 1.0 / math.sqrt(HEAD_DIM)
    tok_rows = tokens.shape[2]
    half_rows = tok_rows // 2
    members = lax.axis_size("blk")
    position = lax.axis_index("blk")
    doc_ends = jnp.cumsum(lengths[0], dtype=jnp.int32)
    hidden = tokens[0, 0]
    hidden_f = hidden.astype(jnp.float32)

    def key_info(first_row, row_count):
        key_pos = stream_positions(
            first_row + jnp.arange(row_count, dtype=jnp.int32), tok_rows, members
        )
        return (key_pos, doc_index(key_pos, doc_ends))

    def heads_of(matrix):
        return matrix.reshape(matrix.shape[0], head_count, HEAD_DIM)

    def scaled_norm(raw_rows, gain_vector):
        return head_norm(raw_rows, head_count) * gain_vector

    own_pos, own_doc = key_info(position * tok_rows, tok_rows)
    query_raw = jnp.dot(hidden, w_query, preferred_element_type=jnp.float32)
    key_raw = jnp.dot(hidden, w_key, preferred_element_type=jnp.float32)
    value_raw = jnp.dot(hidden, w_value, preferred_element_type=jnp.float32)
    queries = scaled_norm(query_raw, s_qk).astype(jnp.bfloat16)
    key_rows = scaled_norm(key_raw, s_qk).astype(jnp.bfloat16)
    value_rows = value_raw.astype(jnp.bfloat16)
    query_heads = heads_of(queries)

    def empty_state():
        return (
            jnp.full((head_count, half_rows), -1e30, jnp.float32),
            jnp.zeros((head_count, half_rows), jnp.float32),
            jnp.zeros((half_rows, head_count, HEAD_DIM), jnp.float32),
        )

    running = (empty_state(), empty_state())
    key_part = lax.all_gather(key_rows, "blk", axis=0, tiled=True)
    value_part = lax.all_gather(value_rows, "blk", axis=0, tiled=True)
    key_pos, key_doc = key_info(jnp.int32(0), key_part.shape[0])
    updated = []
    for part_index in range(2):
        rows_here = slice(part_index * half_rows, (part_index + 1) * half_rows)
        allowed = allowed_pairs(own_pos[rows_here], own_doc[rows_here], key_pos, key_doc)
        updated.append(
            fold_half(
                running[part_index],
                query_heads[rows_here],
                heads_of(key_part),
                heads_of(value_part),
                allowed,
                score_scale,
            )
        )
    folded = (updated[0], updated[1])
    best_score = jnp.concatenate([folded[0][0], folded[1][0]], axis=1)
    total_sum = jnp.concatenate([folded[0][1], folded[1][1]], axis=1)
    accumulated = jnp.concatenate([folded[0][2], folded[1][2]], axis=0)
    attended = accumulated / total_sum.T[:, :, None]
    log_total = best_score + jnp.log(total_sum)
    attended_low = attended.reshape(tok_rows, model_width).astype(jnp.bfloat16)
    branch = jnp.dot(attended_low, w_out, preferred_element_type=jnp.float32)
    middle = residual_mix(hidden_f, branch, alpha_attn)
    middle_low = middle.astype(jnp.bfloat16)
    up_raw = jnp.dot(middle_low, w_up, preferred_element_type=jnp.float32)
    gate_raw = jnp.dot(middle_low, w_gate, preferred_element_type=jnp.float32)
    inner_low = gated_inner(up_raw, gate_raw, s_up, s_gate).astype(jnp.bfloat16)
    mlp_raw = jnp.dot(inner_low, w_down, preferred_element_type=jnp.float32)
    result = residual_mix(middle, mlp_raw, alpha_mlp)
    mixed_out, pull_out = jax.vjp(residual_mix, middle, mlp_raw, alpha_mlp)
    grad_middle, grad_mlp, grad_alpha_mlp = pull_out(cotangent[0, 0].astype(jnp.float32))
    grad_mlp_low = grad_mlp.astype(jnp.bfloat16)
    grad_w_down = jnp.dot(inner_low.T, grad_mlp_low, preferred_element_type=jnp.float32)
    grad_inner = jnp.dot(grad_mlp_low, w_down.T, preferred_element_type=jnp.float32)
    inner_out, pull_inner = jax.vjp(gated_inner, up_raw, gate_raw, s_up, s_gate)
    grad_up_raw, grad_gate_raw, grad_s_up, grad_s_gate = pull_inner(grad_inner)
    up_low = grad_up_raw.astype(jnp.bfloat16)
    gate_low = grad_gate_raw.astype(jnp.bfloat16)
    grad_w_up = jnp.dot(middle_low.T, up_low, preferred_element_type=jnp.float32)
    grad_w_gate = jnp.dot(middle_low.T, gate_low, preferred_element_type=jnp.float32)
    grad_middle = (
        grad_middle
        + jnp.dot(up_low, w_up.T, preferred_element_type=jnp.float32)
        + jnp.dot(gate_low, w_gate.T, preferred_element_type=jnp.float32)
    )
    attn_out, pull_attn = jax.vjp(residual_mix, hidden_f, branch, alpha_attn)
    grad_hidden, grad_branch, grad_alpha_attn = pull_attn(grad_middle)
    branch_low = grad_branch.astype(jnp.bfloat16)
    grad_w_out = jnp.dot(attended_low.T, branch_low, preferred_element_type=jnp.float32)
    grad_att_low = jnp.dot(branch_low, w_out.T, preferred_element_type=jnp.float32).astype(
        jnp.bfloat16
    )
    grad_heads = heads_of(grad_att_low)
    delta_rows = jnp.sum(grad_heads.astype(jnp.float32) * attended, axis=2).T

    def local_side(part_index):
        rows_here = slice(part_index * half_rows, (part_index + 1) * half_rows)
        return (
            query_heads[rows_here],
            grad_heads[rows_here],
            log_total[:, rows_here],
            delta_rows[:, rows_here],
            own_pos[rows_here],
            own_doc[rows_here],
        )

    local_parts = (local_side(0), local_side(1))
    whole_keys, whole_values = (
        lax.all_gather(key_rows, "blk", axis=0, tiled=True),
        lax.all_gather(value_rows, "blk", axis=0, tiled=True),
    )

    def query_step(grad_parts, shard_index):
        first_row = shard_index * tok_rows
        key_part = heads_of(take_rows(whole_keys, first_row, tok_rows))
        value_part = heads_of(take_rows(whole_values, first_row, tok_rows))
        key_pos, key_doc = key_info(first_row, tok_rows)
        updated = []
        for part_index in range(2):
            query_side = local_parts[part_index]
            allowed = allowed_pairs(query_side[4], query_side[5], key_pos, key_doc)

            def add_term(grad_now):
                return grad_now + query_term(query_side, key_part, value_part, allowed, score_scale)

            updated.append(
                lax.cond(
                    jnp.any(allowed), add_term, lambda grad_now: grad_now, grad_parts[part_index]
                )
            )
        return ((updated[0], updated[1]), None)

    zero_part = jnp.zeros((half_rows, head_count, HEAD_DIM), jnp.float32)
    grad_parts, unused_out = lax.scan(
        query_step, (zero_part, zero_part), jnp.arange(members, dtype=jnp.int32)
    )
    grad_queries = jnp.concatenate(grad_parts, axis=0).reshape(tok_rows, model_width)
    first_row = jnp.int32(0)
    row_count = lax.axis_size("blk") * tok_rows
    key_part = heads_of(take_rows(whole_keys, first_row, row_count))
    value_part = heads_of(take_rows(whole_values, first_row, row_count))
    key_pos, key_doc = key_info(first_row, row_count)
    zero_keys = jnp.zeros((row_count, head_count, HEAD_DIM), jnp.float32)
    totals = (zero_keys, zero_keys)
    for part_index in range(2):
        query_side = local_parts[part_index]
        allowed = allowed_pairs(query_side[4], query_side[5], key_pos, key_doc)

        def add_terms(grad_now):
            grad_keys, grad_values = key_term(
                query_side, key_part, value_part, allowed, score_scale
            )
            return (grad_now[0] + grad_keys, grad_now[1] + grad_values)

        totals = lax.cond(jnp.any(allowed), add_terms, lambda grad_now: grad_now, totals)
    key_value_grads = lax.psum_scatter(
        jnp.concatenate(
            [totals[0].reshape(row_count, model_width), totals[1].reshape(row_count, model_width)],
            axis=1,
        ),
        "blk",
        scatter_dimension=0,
        tiled=True,
    )
    grad_keys = key_value_grads[:, :model_width]
    grad_values = key_value_grads[:, model_width:]
    query_out, pull_query = jax.vjp(scaled_norm, query_raw, s_qk)
    grad_query_raw, grad_qk_first = pull_query(grad_queries)
    key_out, pull_key = jax.vjp(scaled_norm, key_raw, s_qk)
    grad_key_raw, grad_qk_second = pull_key(grad_keys)
    grad_s_qk = grad_qk_first + grad_qk_second
    query_low = grad_query_raw.astype(jnp.bfloat16)
    key_low = grad_key_raw.astype(jnp.bfloat16)
    value_low = grad_values.astype(jnp.bfloat16)
    grad_w_query = jnp.dot(hidden.T, query_low, preferred_element_type=jnp.float32)
    grad_w_key = jnp.dot(hidden.T, key_low, preferred_element_type=jnp.float32)
    grad_w_value = jnp.dot(hidden.T, value_low, preferred_element_type=jnp.float32)
    input_grad = (
        grad_hidden
        + jnp.dot(query_low, w_query.T, preferred_element_type=jnp.float32)
        + jnp.dot(key_low, w_key.T, preferred_element_type=jnp.float32)
        + jnp.dot(value_low, w_value.T, preferred_element_type=jnp.float32)
    )
    summed = (
        lax.psum_scatter(grad_w_query, ("dp", "blk"), scatter_dimension=0, tiled=True),
        lax.psum_scatter(grad_w_key, ("dp", "blk"), scatter_dimension=0, tiled=True),
        lax.psum_scatter(grad_w_value, ("dp", "blk"), scatter_dimension=0, tiled=True),
        lax.psum_scatter(grad_w_out, ("dp", "blk"), scatter_dimension=0, tiled=True),
        lax.psum_scatter(grad_w_up, ("dp", "blk"), scatter_dimension=0, tiled=True),
        lax.psum_scatter(grad_w_gate, ("dp", "blk"), scatter_dimension=0, tiled=True),
        lax.psum_scatter(grad_w_down, ("dp", "blk"), scatter_dimension=0, tiled=True),
        lax.psum_scatter(grad_s_qk, ("dp", "blk"), scatter_dimension=0, tiled=True),
        lax.psum_scatter(grad_s_up, ("dp", "blk"), scatter_dimension=0, tiled=True),
        lax.psum_scatter(grad_s_gate, ("dp", "blk"), scatter_dimension=0, tiled=True),
        lax.psum_scatter(grad_alpha_attn, ("dp", "blk"), scatter_dimension=0, tiled=True),
        lax.psum_scatter(grad_alpha_mlp, ("dp", "blk"), scatter_dimension=0, tiled=True),
    )
    mean_alpha = 0.5 * (jnp.mean(alpha_attn) + jnp.mean(alpha_mlp))
    output = result.astype(jnp.bfloat16)[None, None]
    return (
        output,
        input_grad[None, None],
        summed[0],
        summed[1],
        summed[2],
        summed[3],
        summed[4],
        summed[5],
        summed[6],
        summed[7],
        summed[8],
        summed[9],
        summed[10],
        summed[11],
        mean_alpha,
    )


MESH = pl.DeviceIdType.MESH
VMEM_SPEC = pl.BlockSpec(memory_space=pltpu.VMEM)
VMEM_LIMIT = 62 << 20
GROUP = 16


def here():
    return lax.axis_index("dp"), lax.axis_index("blk")


def greet(partners):
    barrier = pltpu.get_barrier_semaphore()
    for partner in partners:
        pl.semaphore_signal(barrier, inc=1, device_id=partner, device_id_type=MESH)
    pl.semaphore_wait(barrier, len(partners))


def remote(src, dst, send_sem, recv_sem, device):
    return pltpu.make_async_remote_copy(
        src_ref=src,
        dst_ref=dst,
        send_sem=send_sem,
        recv_sem=recv_sem,
        device_id=device,
        device_id_type=MESH,
    )


class Gather:
    KINDS = 22

    def __init__(self, own, out, send, recv, pieces):
        self.own, self.out, self.send, self.recv = own, out, send, recv
        self.pieces = pieces
        dp, b = here()
        self.dp, self.b = dp, b
        self.z, self.y, self.c = b // 4, (b // 2) % 2, b % 2
        self.up = (dp, (b + 4) % GROUP)
        self.down = (dp, (b + 12) % GROUP)
        self.side = (dp, b + 2 - 4 * self.y)
        self.sib = (dp, b + 1 - 2 * self.c)
        self.half = self.pieces // 2

    def partners(self):
        return [self.up, self.down, self.side, self.sib]

    def copy(self, z, y, c, kind, piece, device, own=False):
        block = z * 4 + y * 2 + c
        upper = piece // self.half
        place = 2 * GROUP - 1 - block if upper else block
        rows = self.out.shape[1] // self.half
        span = pl.ds(piece % self.half * rows, rows)
        target = self.out.at[place, span]
        source = self.own.at[upper, span] if own else target
        index = self.pieces * kind + piece
        return remote(source, target, self.send.at[index], self.recv.at[index], device)

    def along(self, z, piece, device, own=False, back=False):
        return self.copy(z, self.y, self.c, z + (4 if back else 0), piece, device, own)

    def across(self, z, y, piece, own=False):
        return self.copy(z, y, self.c, 8 + z, piece, self.side, own)

    def over(self, z, piece, device, back=False):
        return self.copy(z, 1 - self.y, self.c, 21 if back else 20, piece, device)

    def to_sib(self, z, y, c, piece, own=False):
        return self.copy(z, y, c, 12 + 2 * z + y, piece, self.sib, own)

    def each_side(self, distance, action):
        if distance == 0:
            action(self.z, None)
            return
        low, high = self.z - distance, self.z + distance

        @pl.when(low >= 0)
        def _():
            action(low, False)

        @pl.when(high <= 3)
        def _():
            action(high, True)

    def start(self):
        for piece in range(self.pieces):

            @pl.when(self.z < 3)
            def _():
                self.along(self.z, piece, self.up, True).start()

            @pl.when(self.z > 0)
            def _():
                self.along(self.z, piece, self.down, True, True).start()

            self.across(self.z, self.y, piece, True).start()
        for piece in range(self.pieces):
            self.to_sib(self.z, self.y, self.c, piece, True).start()
        for upper in (0, 1):
            place = 2 * GROUP - 1 - self.b if upper else self.b
            self.out[place] = self.own[upper]

    def line(self, distance):
        def action(z, above):
            for piece in range(self.pieces):
                self.along(z, piece, self.sib, False, above).wait_recv()
                if above:

                    @pl.when(self.z > 0)
                    def _():
                        self.along(z, piece, self.down, False, True).start()
                else:

                    @pl.when(self.z < 3)
                    def _():
                        self.along(z, piece, self.up).start()

                if distance > 1 or piece < self.half:
                    self.across(z, self.y, piece).start()
                self.to_sib(z, self.y, self.c, piece).start()

        self.each_side(distance, action)

    def sides(self, distance):
        def action(z, above):
            for piece in range(self.pieces):
                if distance == 1 and piece >= self.half:
                    continue
                self.across(z, 1 - self.y, piece).wait_recv()
                self.to_sib(z, 1 - self.y, self.c, piece).start()

        self.each_side(distance, action)

    def hand_over(self):
        for piece in range(self.half, self.pieces):

            @pl.when(self.z < 3)
            def _():
                self.over(self.z, piece, self.up).start()

            @pl.when(self.z > 0)
            def _():
                self.over(self.z, piece, self.down, True).start()

    def handed(self):
        def action(z, above):
            for piece in range(self.half, self.pieces):
                self.over(z, piece, self.sib, above).wait_recv()
                self.to_sib(z, 1 - self.y, self.c, piece).start()

        self.each_side(1, action)

    def from_sib(self, distance):
        def action(z, above):
            for piece in range(self.pieces):
                for y in (0, 1):
                    self.to_sib(z, y, 1 - self.c, piece).wait_recv()

        self.each_side(distance, action)

    def drain(self):
        for piece in range(self.pieces):
            for z in range(4):
                for y in (0, 1):
                    self.to_sib(z, y, self.c, piece).wait_send()
                if piece < self.half:
                    self.across(z, self.y, piece).wait_send()
                else:

                    @pl.when((z > self.z + 1) | (z < self.z - 1) | (z == self.z))
                    def _():
                        self.across(z, self.y, piece).wait_send()

                @pl.when((self.z >= z) & (self.z < 3))
                def _():
                    self.along(z, piece, self.up).wait_send()

                @pl.when((self.z <= z) & (self.z > 0))
                def _():
                    self.along(z, piece, self.down, False, True).wait_send()

            if piece >= self.half:

                @pl.when(self.z < 3)
                def _():
                    self.over(self.z, piece, self.up).wait_send()

                @pl.when(self.z > 0)
                def _():
                    self.over(self.z, piece, self.down, True).wait_send()

    def finish(self):
        for distance in range(4):
            self.from_sib(distance)
        self.drain()


def gather_scratch(pieces):
    return [pltpu.SemaphoreType.DMA((pieces * Gather.KINDS,)) for _ in range(2)]


def comm_params(collective_id):
    return pltpu.CompilerParams(
        collective_id=collective_id, has_side_effects=True, vmem_limit_bytes=VMEM_LIMIT
    )


def dot_nt(left, right):
    return lax.dot_general(left, right, (((1,), (1,)), ((), ())), preferred_element_type=jnp.float32)


def dot_tn(left, right):
    return lax.dot_general(left, right, (((0,), (0,)), ((), ())), preferred_element_type=jnp.float32)


def dot_nn(left, right):
    return jnp.dot(left, right, preferred_element_type=jnp.float32)


FF_STEP = 512


def mean_last(array):
    return jnp.mean(array, axis=-1, keepdims=True)


def rms_scale(array):
    return lax.rsqrt(mean_last(array * array) + 1e-06)


def rms_pull(grad, normed, scale):
    return scale * (grad - normed * mean_last(grad * normed))


def half_lanes(shape):
    return lax.broadcasted_iota(jnp.int32, shape, 1) < HEAD_DIM


class Swap:
    def __init__(self, blocks, out, send, recv, own=True):
        self.blocks, self.out, self.own = blocks, out, own
        dp, self.b = here()
        self.copies = []
        for step in range(1, GROUP):
            target = (self.b + step) % GROUP
            self.copies.append(
                remote(
                    (blocks.block(target) if isinstance(blocks, SendBlocks) else blocks.at[target])
                    if own
                    else blocks,
                    out.at[self.b],
                    send.at[step],
                    recv.at[step],
                    (dp, target),
                )
            )
        self.partners = [(dp, (self.b + step) % GROUP) for step in range(1, GROUP)]

    def start(self):
        for copy in self.copies:
            copy.start()
        if self.own:
            mine = self.blocks
            mine = mine.block(self.b) if isinstance(mine, SendBlocks) else mine.at[self.b]
            self.out[self.b] = mine[...]

    def wait(self):
        for copy in self.copies:
            copy.wait()


ANY_SPEC = pl.BlockSpec(memory_space=pl.ANY)


SMEM_SPEC = pl.BlockSpec(memory_space=pltpu.SMEM)


def own_head(pair, core):
    shifted = jnp.where(core == 1, pltpu.roll(pair, HEAD_DIM, 1), pair)
    return jnp.where(half_lanes(pair.shape), shifted, 0.0)


def minus_ones(matrix):
    lane = lax.broadcasted_iota(jnp.int32, matrix.shape, 1)
    extra = jnp.where(lane < HEAD_DIM + 3, -1.0, 0.0)
    return jnp.where(lane < HEAD_DIM, matrix, extra).astype(jnp.bfloat16)


PROJECT_PIECES = 4


def project_kernel(
    own,
    w_query_hbm,
    w_key_hbm,
    w_value_hbm,
    s_qk_ref,
    out,
    qa_ref,
    ka_ref,
    va_ref,
    q_raw_ref,
    k_raw_ref,
    gain_ref,
    w_head,
    load_sem,
    send,
    recv,
):
    gather = Gather(own, out, send, recv, PROJECT_PIECES)
    window = pl.ds(pl.multiple_of(gather.b // 2 * 128, 128), 128)
    loads = [
        pltpu.make_async_copy(
            source.at[:, window], w_head.at[:, pl.ds(128 * i, 128)], load_sem.at[i]
        )
        for i, source in enumerate((w_query_hbm, w_key_hbm, w_value_hbm))
    ]
    for load in loads:
        load.start()
    greet(gather.partners())
    gather.start()
    gain = own_head(jnp.broadcast_to(s_qk_ref[:, window], (8, 128)), gather.c)[:1]
    gain_ref[...] = gain
    for load in loads:
        load.wait()
    slots = 2 * GROUP // 8
    half = out.shape[1]

    def project(first_slot):
        hidden = out[pl.ds(first_slot, slots)].reshape(slots * half, out.shape[2])
        raw = dot_nn(hidden, w_head[...])
        rows = pl.ds(pl.multiple_of(first_slot * half, half), slots * half)
        query, key, value = (
            own_head(raw[:, 128 * i : 128 * (i + 1)], gather.c) for i in range(3)
        )
        q_raw_ref[rows, :] = query.astype(jnp.bfloat16)
        k_raw_ref[rows, :] = key.astype(jnp.bfloat16)
        count = float(HEAD_DIM)
        query_scale = lax.rsqrt(jnp.sum(query * query, axis=1, keepdims=True) / count + 1e-06)
        key_scale = lax.rsqrt(jnp.sum(key * key, axis=1, keepdims=True) / count + 1e-06)
        query = (query * query_scale * gain).astype(jnp.bfloat16).astype(jnp.float32)
        qa_ref[rows, :] = (query * (1.0 / math.sqrt(HEAD_DIM))).astype(jnp.bfloat16)
        ka_ref[rows, :] = minus_ones(key * key_scale * gain)
        va_ref[rows, :] = minus_ones(value)

    def project_line(distance):
        def both(z):
            project(slots * z)
            project(2 * GROUP - slots - slots * z)

        if distance == 0:
            both(gather.z)
        else:

            @pl.when(gather.z - distance >= 0)
            def _():
                both(gather.z - distance)

            @pl.when(gather.z + distance <= 3)
            def _():
                both(gather.z + distance)

    gather.line(1)
    gather.sides(0)
    gather.from_sib(0)
    project_line(0)
    gather.line(2)
    gather.hand_over()
    gather.sides(1)
    gather.line(3)
    gather.sides(2)
    gather.from_sib(2)
    project_line(2)
    gather.handed()
    gather.from_sib(1)
    project_line(1)
    gather.sides(3)
    gather.from_sib(3)
    project_line(3)
    gather.drain()


def project_block(hidden, w_query, w_key, w_value, s_qk):
    rows, width = hidden.shape
    length = GROUP * rows
    low, f32 = jnp.bfloat16, jnp.float32
    shape = jax.ShapeDtypeStruct
    return pl.pallas_call(
        project_kernel,
        out_shape=[
            shape((2 * GROUP, rows // 2, width), low),
            shape((length, 128), low),
            shape((length, 128), low),
            shape((length, 128), low),
            shape((length, 128), low),
            shape((length, 128), low),
            shape((1, 128), f32),
        ],
        in_specs=[VMEM_SPEC] + [ANY_SPEC] * 3 + [VMEM_SPEC],
        out_specs=[VMEM_SPEC] * 7,
        scratch_shapes=[pltpu.VMEM((width, 384), low), pltpu.SemaphoreType.DMA((3,))]
        + gather_scratch(PROJECT_PIECES),
        compiler_params=comm_params(0),
        name="project_block",
    )(hidden.reshape(2, rows // 2, width), w_query, w_key, w_value, s_qk[None])


def doc_start_of(positions, lengths_ref):
    start = jnp.zeros_like(positions)
    end = jnp.int32(0)
    for doc in range(lengths_ref.shape[1]):
        end = end + lengths_ref[0, doc]
        start = start + jnp.where(positions >= end, lengths_ref[0, doc], 0)
    return start


def split_lanes(column, shape):
    lane = lax.broadcasted_iota(jnp.int32, shape, 1)
    high = column.astype(jnp.bfloat16).astype(jnp.float32)
    rest = column - high
    mid = rest.astype(jnp.bfloat16).astype(jnp.float32)
    last = rest - mid
    return jnp.where(
        lane == HEAD_DIM,
        high,
        jnp.where(lane == HEAD_DIM + 1, mid, jnp.where(lane == HEAD_DIM + 2, last, 0.0)),
    )


ATT = 512


def attend_kernel(lengths_ref, qa_ref, ka_ref, va_ref, o_ref, ql_ref, packed_ref):
    length = qa_ref.shape[0]
    half = packed_ref.shape[1]
    for query_block in range(length // ATT):
        rows = pl.ds(query_block * ATT, ATT)
        queries = qa_ref[rows, :]
        column = query_block * ATT + lax.broadcasted_iota(jnp.int32, (ATT, 1), 0)
        doc_start = doc_start_of(column, lengths_ref)
        first_start = doc_start_of(jnp.int32(query_block * ATT), lengths_ref)
        query_pos = query_block * ATT + lax.broadcasted_iota(jnp.int32, (ATT, ATT), 0)
        key_lane = lax.broadcasted_iota(jnp.int32, (ATT, ATT), 1)

        def step(key_block, total):
            base = pl.multiple_of(key_block * ATT, ATT)
            keys = ka_ref[pl.ds(base, ATT), :]
            values = va_ref[pl.ds(base, ATT), :]
            key_pos = base + key_lane
            allowed = (key_pos <= query_pos) & (key_pos >= doc_start)
            weights = jnp.where(allowed, jnp.exp(dot_nt(queries, keys)), 0.0)
            return total + dot_nn(weights.astype(jnp.bfloat16), values)

        total = lax.fori_loop(
            first_start // ATT, query_block + 1, step, jnp.zeros((ATT, 128), jnp.float32)
        )
        row_sum = -total[:, HEAD_DIM : HEAD_DIM + 1]
        first = half_lanes(total.shape)
        o_ref[rows, :] = jnp.where(first, total / row_sum, 0.0).astype(o_ref.dtype)
        extra = split_lanes(jnp.log(row_sum), total.shape)
        ql_ref[rows, :] = jnp.where(first, queries.astype(jnp.float32), extra).astype(jnp.bfloat16)
    first = half_lanes((half, 128))
    for j in range(GROUP):
        lower = o_ref[j * half : (j + 1) * half, :].astype(jnp.float32)
        upper = o_ref[length - (j + 1) * half : length - j * half, :].astype(jnp.float32)
        packed_ref[j] = jnp.where(first, lower, pltpu.roll(upper, HEAD_DIM, 1)).astype(
            packed_ref.dtype
        )


def attend(lengths, qa, ka, va, half_rows):
    length = qa.shape[0]
    shape = jax.ShapeDtypeStruct
    return pl.pallas_call(
        attend_kernel,
        out_shape=[
            shape((length, 128), jnp.bfloat16),
            shape((length, 128), jnp.bfloat16),
            shape((GROUP, half_rows, 128), jnp.bfloat16),
        ],
        in_specs=[SMEM_SPEC] + [VMEM_SPEC] * 3,
        out_specs=[VMEM_SPEC] * 3,
        compiler_params=pltpu.CompilerParams(vmem_limit_bytes=VMEM_LIMIT),
        name="attend",
    )(lengths, qa, ka, va)


TAIL_PIECES = 2
KEYS = 256


class SendBlocks:
    def __init__(self, ref, first_row, rows, first_lane, lanes):
        self.ref, self.first_row, self.rows = ref, first_row, rows
        self.lanes = pl.ds(first_lane, lanes)

    def block(self, index):
        start = pl.multiple_of(self.first_row + index * self.rows, self.rows)
        return self.ref.at[pl.ds(start, self.rows), self.lanes]


def tail_kernel(
    lengths_ref,
    o_ref,
    hidden_ref,
    cot_ref,
    gain_ref,
    s_up_ref,
    s_gate_ref,
    alpha_attn_ref,
    alpha_mlp_ref,
    w_out_hbm,
    w_up_hbm,
    w_gate_hbm,
    w_down_hbm,
    w_query_hbm,
    w_key_hbm,
    w_value_hbm,
    ql_hbm,
    ka_hbm,
    va_hbm,
    att_hbm,
    q_raw_hbm,
    k_raw_hbm,
    hidden_hbm,
    result_ref,
    input_grad_ref,
    wide_in,
    qkv_in,
    g_down_ref,
    out_in,
    g_s_ref,
    small_ref,
    mid_all,
    g_mlp_all,
    w_out,
    w_up,
    w_gate,
    w_down,
    up_slice,
    gate_slice,
    down_slice,
    up_raw,
    gate_raw,
    mid_own,
    g_mlp_own,
    o_in,
    g_send,
    g_in,
    acc,
    g_res,
    att_pair,
    branch_pair,
    out_got,
    out_side_got,
    ql_ref,
    ka_ref,
    va_ref,
    ga_ref,
    dq_acc,
    dk_acc,
    dv_acc,
    back_in,
    qkv_part,
    qkv_got,
    wide_own,
    wide_got,
    down_got,
    small_own,
    small_got,
    small_all,
    s_part,
    s_send,
    s_got,
    load_sems,
    x_sems,
    pair_sems,
    out_sems,
    swap_sems,
    grad_sems,
    back_sems,
    qkv_sems,
    wide_sems,
    small_sems,
    mid_send,
    mid_recv,
    mlp_send,
    mlp_recv,
):
    low, f32 = jnp.bfloat16, jnp.float32
    dp, b = here()
    z, y, c = b // 4, (b // 2) % 2, b % 2
    twin, sib, side = (1 - dp, b), (dp, b + 1 - 2 * c), (dp, b + 2 - 4 * y)
    rows, width = hidden_ref.shape
    half = rows // 2
    length = GROUP * rows
    ff = w_up.shape[1]
    ff_half = ff // 2
    part = ff // (2 * GROUP)
    quarter = width // 4
    rows_out = width // (2 * GROUP)
    blocks = length // ATT
    loaded = []

    def load(source, target):
        copy = pltpu.make_async_copy(source, target, load_sems.at[len(loaded)])
        copy.start()
        loaded.append(copy)
        return copy

    def to(device, sems, index, source, target):
        copy = remote(source, target, sems.at[0, index], sems.at[1, index], device)
        copy.start()
        return copy

    load_out = load(w_out_hbm, w_out)
    load_mlp = [load(w_up_hbm, w_up), load(w_gate_hbm, w_gate), load(w_down_hbm, w_down)]
    load_slices = []
    windows = [pl.ds(pl.multiple_of(p * ff_half + b * part, part), part) for p in (0, 1)]
    for p in (0, 1):
        place = pl.ds(p * part, part)
        load_slices.append(load(w_up_hbm.at[:, windows[p]], up_slice.at[:, place]))
        load_slices.append(load(w_gate_hbm.at[:, windows[p]], gate_slice.at[:, place]))
        load_slices.append(load(w_down_hbm.at[windows[p], :], down_slice.at[place, :]))

    swap = Swap(o_ref, o_in, swap_sems.at[0], swap_sems.at[1])
    grad_swap = Swap(g_send, g_in, grad_sems.at[0], grad_sems.at[1])
    small_swap = Swap(small_own, small_all, small_sems.at[0], small_sems.at[1], own=False)
    gather_mid = Gather(mid_own, mid_all, mid_send, mid_recv, TAIL_PIECES)
    gather_mlp = Gather(g_mlp_own, g_mlp_all, mlp_send, mlp_recv, TAIL_PIECES)
    greet(swap.partners + [twin])
    swap.start()
    swap.wait()

    first = half_lanes((half, 128))
    for pair in range(GROUP // 2):
        even = o_in[2 * pair].astype(f32)
        odd = o_in[2 * pair + 1].astype(f32)
        lanes = slice(pair * 128, (pair + 1) * 128)
        att_pair[c, :half, lanes] = jnp.where(first, even, pltpu.roll(odd, HEAD_DIM, 1)).astype(low)
        att_pair[c, half:, lanes] = jnp.where(first, pltpu.roll(even, HEAD_DIM, 1), odd).astype(low)
    att_copy = to(sib, pair_sems, 0, att_pair.at[c], att_pair.at[c])
    hidden = hidden_ref[...].astype(f32)
    alpha_attn = alpha_attn_ref[...]
    alpha_mlp = alpha_mlp_ref[...]
    load_out.wait()
    branch = dot_nn(att_pair[c], w_out[...])
    branch_scale = rms_scale(branch)
    branch_normed = branch * branch_scale
    mixed = hidden + alpha_attn * (branch_normed - hidden)
    middle_scale = rms_scale(mixed)
    middle = mixed * middle_scale
    middle_low = middle.astype(low)
    mid_own[0] = middle_low[:half]
    mid_own[1] = middle_low[half:]
    gather_mid.start()
    for copy in load_mlp:
        copy.wait()
    steps = ff // FF_STEP
    acc[...] = jnp.zeros_like(acc)

    def forward(step, carry):
        cols = pl.ds(pl.multiple_of(step * FF_STEP, FF_STEP), FF_STEP)
        up = dot_nn(middle_low, w_up[:, cols])
        gate = dot_nn(middle_low, w_gate[:, cols])
        up_raw[:, cols] = up
        gate_raw[:, cols] = gate
        scaled = gate * s_gate_ref[:, cols]
        inner = up * s_up_ref[:, cols] * (scaled / (1.0 + jnp.exp(-scaled)))
        acc[...] += dot_nn(inner.astype(low), w_down[cols, :])
        return carry

    lax.fori_loop(0, steps, forward, 0)
    gather_mid.line(1)
    gather_mid.sides(0)
    mlp = acc[...]
    mlp_scale = rms_scale(mlp)
    mlp_normed = mlp * mlp_scale
    mixed_out = middle + alpha_mlp * (mlp_normed - middle)
    out_scale = rms_scale(mixed_out)
    result = mixed_out * out_scale
    result_ref[...] = result.astype(low)

    g_mixed = rms_pull(cot_ref[...].astype(f32), result, out_scale)
    g_alpha_mlp = jnp.sum(g_mixed * (mlp_normed - middle), axis=0, keepdims=True)
    small_own[...] = jnp.zeros_like(small_own)
    for i in range(width // 128):
        small_own[8 + i : 9 + i, :] = g_alpha_mlp[:, 128 * i : 128 * (i + 1)]
    g_mlp = rms_pull(g_mixed * alpha_mlp, mlp_normed, mlp_scale).astype(low)
    g_mlp_own[0] = g_mlp[:half]
    g_mlp_own[1] = g_mlp[half:]
    gather_mlp.start()
    acc[...] = g_mixed * (1.0 - alpha_mlp)

    def backward(step, carry):
        cols = pl.ds(pl.multiple_of(step * FF_STEP, FF_STEP), FF_STEP)
        g_inner = dot_nt(g_mlp, w_down[cols, :])
        s_up = s_up_ref[:, cols]
        s_gate = s_gate_ref[:, cols]
        scaled = gate_raw[:, cols] * s_gate
        sigmoid = 1.0 / (1.0 + jnp.exp(-scaled))
        g_up = g_inner * (scaled / (1.0 + jnp.exp(-scaled))) * s_up
        slope = sigmoid * (1.0 + scaled * (1.0 - sigmoid))
        g_gate = g_inner * (up_raw[:, cols] * s_up) * slope * s_gate
        acc[...] += dot_nt(g_up.astype(low), w_up[:, cols]) + dot_nt(
            g_gate.astype(low), w_gate[:, cols]
        )
        return carry

    lax.fori_loop(0, steps // 2, backward, 0)
    gather_mid.line(2)
    gather_mid.hand_over()
    gather_mid.sides(1)
    lax.fori_loop(steps // 2, steps, backward, 0)
    g_pre = rms_pull(acc[...], middle, middle_scale)
    g_res[...] = g_pre * (1.0 - alpha_attn)
    g_alpha_attn = jnp.sum(g_pre * (branch_normed - hidden), axis=0, keepdims=True)
    for i in range(width // 128):
        small_own[i : i + 1, :] = g_alpha_attn[:, 128 * i : 128 * (i + 1)]
    branch_pair[c] = rms_pull(g_pre * alpha_attn, branch_normed, branch_scale).astype(low)
    g_att = dot_nt(branch_pair[c], w_out[...]).astype(low).astype(f32)
    for pair in range(GROUP // 2):
        lower = g_att[:half, pair * 128 : (pair + 1) * 128]
        upper = g_att[half:, pair * 128 : (pair + 1) * 128]
        g_send[2 * pair] = jnp.where(first, lower, pltpu.roll(upper, HEAD_DIM, 1)).astype(low)
        g_send[2 * pair + 1] = jnp.where(first, pltpu.roll(lower, HEAD_DIM, 1), upper).astype(low)
    grad_swap.start()
    branch_copy = to(sib, pair_sems, 1, branch_pair.at[c], branch_pair.at[c])

    g_cat = w_down.at[pl.ds(0, length), pl.ds(0, 4 * part)]
    inner_all = w_down.at[pl.ds(0, length), pl.ds(512, 2 * part)]
    raw_low = w_down.at[pl.ds(length, length), pl.ds(0, 384)]
    att_ref = w_down.at[pl.ds(length, length), pl.ds(640, 128)]
    q_raw_ref = w_down.at[pl.ds(length, length), pl.ds(768, 128)]
    k_raw_ref = w_down.at[pl.ds(length, length), pl.ds(896, 128)]
    w_qkv = [w_up.at[:, pl.ds(i * width, width)] for i in range(3)]
    home = [w_up.at[pl.ds(i * rows, rows), pl.ds(3 * width, width)] for i in range(3)]
    out_send = w_out.at[pl.ds(0, quarter), :]
    out_side_send = [w_out.at[pl.ds(quarter + half * k, half), :] for k in (0, 1)]
    out_line = w_out.at[pl.ds(2 * quarter, 4 * rows_out), :]
    down_send = w_out.at[pl.ds(3 * quarter, part), :]
    out_own = [up_raw.at[:, pl.ds((2 + k) * width, width)] for k in (0, 1)]
    wide_send = [w_gate.at[pl.ds(quarter * i, quarter), pl.ds(2048, 512)] for i in (0, 1)]
    qkv_send = w_gate.at[pl.ds(0, 2 * quarter), pl.ds(2560, 256)]
    back_send = SendBlocks(w_gate, 0, half, 2816, 384)
    qkv_blocks = SendBlocks(w_gate, 2 * quarter, rows_out, 2560, 256)
    wide_blocks = SendBlocks(w_gate, 2 * quarter, rows_out, 2048, 512)
    back_swap = Swap(back_send, back_in, back_sems.at[0], back_sems.at[1])
    qkv_swap = Swap(qkv_blocks, qkv_in, qkv_sems.at[0], qkv_sems.at[1])
    tokens_of_half = [w_gate.at[:, pl.ds(i * width, width)] for i in (0, 1)]
    load_heads = [
        load(source, target)
        for source, target in (
            (att_hbm, att_ref),
            (ql_hbm, ql_ref),
            (ka_hbm, ka_ref),
            (va_hbm, va_ref),
            (q_raw_hbm, q_raw_ref),
            (k_raw_hbm, k_raw_ref),
        )
    ]
    load_hidden = [
        load(hidden_hbm.at[pl.ds(i * width, width), :], tokens_of_half[i]) for i in (0, 1)
    ]
    load_qkv = [
        load(source, w_qkv[i]) for i, source in enumerate((w_query_hbm, w_key_hbm, w_value_hbm))
    ]
    gather_mid.line(3)
    gather_mid.sides(2)
    gather_mlp.line(1)
    gather_mlp.sides(0)

    att_copy.wait()
    branch_copy.wait()
    both_branch = branch_pair[...].reshape(2 * rows, width)

    def out_rows(owner):
        lanes = pl.ds(pl.multiple_of(owner * 2 * quarter + c * quarter, quarter), quarter)
        return dot_tn(att_pair[:, :, lanes].reshape(2 * rows, quarter), both_branch)

    out_send[...] = out_rows(1 - dp).astype(low)
    out_copy = to(twin, x_sems, 0, out_send, out_got)
    out_mine = out_rows(dp)
    for k in (0, 1):
        out_own[k][...] = out_mine[2 * half * k : 2 * half * (k + 1)]
    gather_mid.handed()
    gather_mid.sides(3)

    for copy in load_heads:
        copy.wait()
    grad_swap.wait()
    for j in range(GROUP):
        block = g_in[j].astype(f32)
        for start, grads in (
            (j * half, jnp.where(first, block, 0.0)),
            (length - (j + 1) * half, jnp.where(first, pltpu.roll(block, HEAD_DIM, 1), 0.0)),
        ):
            span = pl.ds(start, half)
            delta = jnp.sum(grads * att_ref[span, :].astype(f32), axis=1, keepdims=True)
            ga_ref[span, :] = (grads + split_lanes(delta, grads.shape)).astype(low)
    dq_acc[...] = jnp.zeros_like(dq_acc)
    key_row = lax.broadcasted_iota(jnp.int32, (KEYS, ATT), 0)
    query_lane = lax.broadcasted_iota(jnp.int32, (KEYS, ATT), 1)
    query_row = lax.broadcasted_iota(jnp.int32, (1, ATT), 1)
    gain = gain_ref[...]
    count = float(HEAD_DIM)
    score_scale = 1.0 / math.sqrt(HEAD_DIM)
    wide_first = half_lanes((ATT, 128))

    def norm_pull(raw, grad):
        raw = raw.astype(f32)
        scale = lax.rsqrt(jnp.sum(raw * raw, axis=1, keepdims=True) / count + 1e-06)
        normed = raw * scale
        g_gain = jnp.sum(grad * normed, axis=0, keepdims=True)
        inside = grad * gain
        mean = jnp.sum(inside * normed, axis=1, keepdims=True) / count
        return scale * (inside - normed * mean), g_gain

    key_first = half_lanes((KEYS, 128))

    def key_step(key_block, g_gain):
        span = pl.ds(pl.multiple_of(key_block * KEYS, KEYS), KEYS)
        keys = ka_ref[span, :]
        values = va_ref[span, :]
        key_pos = key_block * KEYS + key_row
        dk_acc[...] = jnp.zeros_like(dk_acc)
        dv_acc[...] = jnp.zeros_like(dv_acc)

        def step(query_block, carry):
            base = pl.multiple_of(query_block * ATT, ATT)
            queries = ql_ref[pl.ds(base, ATT), :]
            grads = ga_ref[pl.ds(base, ATT), :]
            doc_start = doc_start_of(base + query_row, lengths_ref)
            allowed = (key_pos <= base + query_lane) & (key_pos >= doc_start)
            weights = jnp.where(allowed, jnp.exp(dot_nt(keys, queries)), 0.0)
            slopes = (weights * dot_nt(values, grads)).astype(low)
            dv_acc[...] += dot_nn(weights.astype(low), grads)
            dk_acc[...] += dot_nn(slopes, queries)
            dq_acc[pl.ds(base, ATT), :] += dot_tn(slopes, keys)
            return carry

        lax.fori_loop(key_block * KEYS // ATT, blocks, step, 0)
        dk = jnp.where(key_first, dk_acc[...], 0.0)
        g_key, key_gain = norm_pull(k_raw_ref[span, :], dk)
        raw_low[span, 128:256] = g_key.astype(low)
        raw_low[span, 256:384] = jnp.where(key_first, dv_acc[...], 0.0).astype(low)
        return g_gain + key_gain

    g_gain = lax.fori_loop(0, 2, key_step, jnp.zeros((1, 128), f32))
    gather_mlp.line(2)
    gather_mlp.hand_over()
    gather_mlp.sides(1)
    g_gain = lax.fori_loop(2, length // KEYS, key_step, g_gain)
    for block in range(blocks):
        span = pl.ds(block * ATT, ATT)
        dq = jnp.where(wide_first, dq_acc[span, :] * score_scale, 0.0)
        g_query, query_gain = norm_pull(q_raw_ref[span, :], dq)
        g_gain = g_gain + query_gain
        raw_low[span, 0:128] = g_query.astype(low)
    for j in range(GROUP):
        for i in range(3):
            lanes = slice(128 * i, 128 * (i + 1))
            lower = raw_low[j * half : (j + 1) * half, lanes].astype(f32)
            upper = raw_low[length - (j + 1) * half : length - j * half, lanes].astype(f32)
            back_send.block(j)[:, lanes] = jnp.where(
                first, lower, pltpu.roll(upper, HEAD_DIM, 1)
            ).astype(low)
    gather_mlp.line(3)
    gather_mlp.sides(2)
    back_swap.start()

    small_own[16:17, :] = g_gain
    small_copy = to(twin, x_sems, 1, small_own, small_got)

    for copy in load_hidden:
        copy.wait()

    def qkv_chunk(chunk):
        lanes = pl.ds(pl.multiple_of(chunk * quarter, quarter), quarter)
        grads = sum(
            dot_tn(tokens_of_half[i][:, lanes], raw_low[pl.ds(i * width, width), :]) for i in (0, 1)
        )
        query_key = jnp.where(
            half_lanes((quarter, 128)), grads[:, :128], pltpu.roll(grads[:, 128:256], HEAD_DIM, 1)
        )
        return query_key, grads[:, 256:]

    for i in (0, 1):
        query_key, value = qkv_chunk(2 * (1 - dp) + i)
        span = slice(quarter * i, quarter * (i + 1))
        qkv_send[span, :128] = query_key.astype(low)
        qkv_send[span, 128:] = value.astype(low)
    qkv_copy = to(twin, x_sems, 2, qkv_send, qkv_got)
    for i in (0, 1):
        query_key, value = qkv_chunk(2 * dp + i)
        span = slice(quarter * i, quarter * (i + 1))
        qkv_part[span, :128] = query_key
        qkv_part[span, 128:] = value

    out_copy.wait()
    side_copies = []
    for k in (0, 1):
        out_own[k][...] += out_got[2 * half * k : 2 * half * (k + 1)].astype(f32)
        other = pl.ds(pl.multiple_of((1 - y) * half, half), half)
        out_side_send[k][...] = out_own[k][other, :].astype(low)
        side_copies.append(to(side, pair_sems, 2 + k, out_side_send[k], out_side_got.at[k]))
    small_copy.wait()
    small_own[...] += small_got[...]
    small_swap.start()
    gather_mlp.sides(3)
    gather_mlp.handed()
    gather_mid.finish()
    gather_mlp.finish()

    for copy in load_slices:
        copy.wait()
    s_up = jnp.concatenate([s_up_ref[:, window] for window in windows], axis=1)
    s_gate = jnp.concatenate([s_gate_ref[:, window] for window in windows], axis=1)
    slots = KEYS // half

    def tokens_of(array, step):
        return array[pl.ds(step * slots, slots)].reshape(KEYS, width)

    def recompute(step, sums):
        span = pl.ds(pl.multiple_of(step * KEYS, KEYS), KEYS)
        some = tokens_of(mid_all, step)
        up = dot_nn(some, up_slice[...])
        gate = dot_nn(some, gate_slice[...])
        g_inner = dot_nt(tokens_of(g_mlp_all, step), down_slice[...])
        scaled = gate * s_gate
        sigmoid = 1.0 / (1.0 + jnp.exp(-scaled))
        silu = scaled / (1.0 + jnp.exp(-scaled))
        up_scaled = up * s_up
        inner_all[span, :] = (up_scaled * silu).astype(low)
        g_up_scaled = g_inner * silu
        g_scaled = g_inner * up_scaled * (sigmoid * (1.0 + scaled * (1.0 - sigmoid)))
        g_cat[span, : 2 * part] = (g_up_scaled * s_up).astype(low)
        g_cat[span, 2 * part :] = (g_scaled * s_gate).astype(low)
        return (
            sums[0] + jnp.sum(g_up_scaled * up, axis=0, keepdims=True),
            sums[1] + jnp.sum(g_scaled * gate, axis=0, keepdims=True),
        )

    zero_row = jnp.zeros((1, 2 * part), f32)
    g_s_up, g_s_gate = lax.fori_loop(0, length // KEYS, recompute, (zero_row, zero_row))

    def wide_chunk(chunk):
        lanes = pl.ds(pl.multiple_of(chunk * quarter, quarter), quarter)
        return dot_tn(mid_all[:, :, lanes].reshape(length, quarter), g_cat[...])

    wide_copies = []
    for i in (0, 1):
        wide_send[i][...] = wide_chunk(2 * (1 - dp) + i).astype(low)
        wide_copies.append(to(twin, x_sems, 3 + i, wide_send[i], wide_got.at[i]))
    for p in (0, 1):
        s_part[p] = jnp.zeros(s_part.shape[1:], f32)
        s_part[p, 0:1, :] = g_s_up[:, p * part : (p + 1) * part]
        s_part[p, 1:2, :] = g_s_gate[:, p * part : (p + 1) * part]
    s_send[...] = s_part[1 - dp]
    s_copy = to(twin, x_sems, 5, s_send, s_got)
    for chunk in range(4):
        lanes = pl.ds(chunk * quarter, quarter)
        grads = dot_tn(inner_all[...], g_mlp_all[:, :, lanes].reshape(length, quarter))
        for p in (0, 1):
            place = slice(p * width + chunk * quarter, p * width + (chunk + 1) * quarter)
            up_raw[:, place] = grads[p * part : (p + 1) * part]
    down_other = pl.ds(pl.multiple_of((1 - dp) * width, width), width)
    down_mine = pl.ds(pl.multiple_of(dp * width, width), width)
    down_send[...] = up_raw[:, down_other].astype(low)
    down_copy = to(twin, x_sems, 6, down_send, down_got)

    qkv_copy.wait()
    per_chunk = quarter // rows_out
    total = (qkv_part[...] + qkv_got[...].astype(f32)).astype(low)
    for k in range(GROUP):
        qkv_blocks.block(k)[...] = total[k * rows_out : (k + 1) * rows_out]
    qkv_swap.start()
    for copy in side_copies:
        copy.wait()
    out_copies = []
    for k in (0, 1):
        mine = pl.ds(pl.multiple_of(y * half, half), half)
        total = (out_own[k][mine, :] + out_side_got[k].astype(f32)).astype(low)
        out_line[2 * rows_out * k : 2 * rows_out * (k + 1), :] = total
        for core in (0, 1):
            line_rows = pl.ds((2 * k + core) * rows_out, rows_out)
            target = (2 * c + k) * 4 + 2 * y + core
            index = 2 * k + core
            copy = remote(
                out_line.at[line_rows],
                out_in.at[z],
                out_sems.at[0, index],
                out_sems.at[1, z],
                (dp, target),
            )
            out_copies.append((target, copy))

            @pl.when(target != b)
            def _():
                copy.start()

            @pl.when(target == b)
            def _():
                out_in[z] = out_line[line_rows, :]

    def wide_copy(target):
        return remote(
            wide_blocks.block(target),
            wide_in.at[b],
            wide_sems.at[0, target],
            wide_sems.at[1, b],
            (dp, target),
        )

    for i in (0, 1):
        wide_own[...] = wide_chunk(2 * dp + i)
        wide_copies[i].wait()
        total = (wide_own[...] + wide_got[i].astype(f32)).astype(low)
        for k in range(per_chunk):
            target = i * per_chunk + k
            wide_blocks.block(target)[...] = total[k * rows_out : (k + 1) * rows_out]

            @pl.when(target != b)
            def _():
                wide_copy(target).start()

            @pl.when(target == b)
            def _():
                wide_in[b] = wide_blocks.block(target)[...]

    for copy in load_qkv:
        copy.wait()
    back_swap.wait()
    for pair in range(GROUP // 2):
        for i in range(3):
            lanes = slice(128 * i, 128 * (i + 1))
            even = back_in[2 * pair, :, lanes].astype(f32)
            odd = back_in[2 * pair + 1, :, lanes].astype(f32)
            place = slice(128 * pair, 128 * (pair + 1))
            home[i][:half, place] = jnp.where(first, even, pltpu.roll(odd, HEAD_DIM, 1)).astype(low)
            home[i][half:, place] = jnp.where(first, pltpu.roll(even, HEAD_DIM, 1), odd).astype(low)
    input_grad_ref[...] = (
        g_res[...]
        + dot_nt(home[0][...], w_qkv[0][...])
        + dot_nt(home[1][...], w_qkv[1][...])
        + dot_nt(home[2][...], w_qkv[2][...])
    )
    s_copy.wait()
    g_s_ref[...] = s_part[dp] + s_got[...]
    down_copy.wait()
    g_down_ref[...] = up_raw[:, down_mine] + down_got[...].astype(f32)
    small_swap.wait()
    small_all[b] = small_own[...]
    small_ref[...] = jnp.sum(small_all[...], axis=0)
    small_ref[17:18, :] = small_all[8 * dp + b // 2, 16:17, :]
    qkv_swap.wait()
    for target, copy in out_copies:

        @pl.when(target != b)
        def _():
            copy.wait_send()

    for source_z in range(4):
        source = source_z * 4 + 2 * y + z // 2

        @pl.when(source != b)
        def _():
            remote(
                out_line.at[pl.ds(0, rows_out)],
                out_in.at[source_z],
                out_sems.at[0, 0],
                out_sems.at[1, source_z],
                sib,
            ).wait_recv()

    for other in range(GROUP):

        @pl.when(other != b)
        def _():
            copy = remote(
                wide_blocks.block(other),
                wide_in.at[other],
                wide_sems.at[0, other],
                wide_sems.at[1, other],
                sib,
            )
            copy.wait_send()
            copy.wait_recv()


def tail_block(vmem_inputs, hbm_inputs):
    low, f32 = jnp.bfloat16, jnp.float32
    shape, vmem, sems = jax.ShapeDtypeStruct, pltpu.VMEM, pltpu.SemaphoreType.DMA
    packed, hidden = vmem_inputs[1], vmem_inputs[2]
    w_out, w_up, w_gate, w_down = hbm_inputs[:4]
    rows, width = hidden.shape
    half = rows // 2
    ff = w_up.shape[1]
    length = GROUP * rows
    rows_out = width // (2 * GROUP)
    part = ff // (2 * GROUP)
    quarter = width // 4
    return pl.pallas_call(
        tail_kernel,
        out_shape=[
            shape((rows, width), low),
            shape((rows, width), f32),
            shape((GROUP, rows_out, 4 * part), low),
            shape((GROUP, rows_out, 256), low),
            shape((part, width), f32),
            shape((4, rows_out, width), low),
            shape((8, 128), f32),
            shape((24, 128), f32),
        ],
        in_specs=[SMEM_SPEC]
        + [VMEM_SPEC] * (len(vmem_inputs) - 1)
        + [ANY_SPEC] * len(hbm_inputs),
        out_specs=[VMEM_SPEC] * 8,
        scratch_shapes=[
            vmem((2 * GROUP, half, width), low),
            vmem((2 * GROUP, half, width), low),
            vmem(w_out.shape, low),
            vmem(w_up.shape, low),
            vmem(w_gate.shape, low),
            vmem(w_down.shape, low),
            vmem((width, 2 * part), low),
            vmem((width, 2 * part), low),
            vmem((2 * part, width), low),
            vmem((rows, ff), f32),
            vmem((rows, ff), f32),
            vmem((2, half, width), low),
            vmem((2, half, width), low),
            vmem(packed.shape, low),
            vmem(packed.shape, low),
            vmem(packed.shape, low),
            vmem((rows, width), f32),
            vmem((rows, width), f32),
            vmem((2, rows, width), low),
            vmem((2, rows, width), low),
            vmem((quarter, width), low),
            vmem((2, half, width), low),
            vmem((length, 128), low),
            vmem((length, 128), low),
            vmem((length, 128), low),
            vmem((length, 128), low),
            vmem((length, 128), f32),
            vmem((KEYS, 128), f32),
            vmem((KEYS, 128), f32),
            vmem((GROUP, half, 384), low),
            vmem((2 * quarter, 256), f32),
            vmem((2 * quarter, 256), low),
            vmem((quarter, 4 * part), f32),
            vmem((2, quarter, 4 * part), low),
            vmem((part, width), low),
            vmem((24, 128), f32),
            vmem((24, 128), f32),
            vmem((GROUP, 24, 128), f32),
            vmem((2, 8, 128), f32),
            vmem((8, 128), f32),
            vmem((8, 128), f32),
            sems((24,)),
            sems((2, 8)),
            sems((2, 4)),
            sems((2, 4)),
            sems((2, GROUP)),
            sems((2, GROUP)),
            sems((2, GROUP)),
            sems((2, GROUP)),
            sems((2, GROUP)),
            sems((2, GROUP)),
        ]
        + gather_scratch(TAIL_PIECES)
        + gather_scratch(TAIL_PIECES),
        compiler_params=comm_params(1),
        name="tail_block",
    )(*vmem_inputs, *hbm_inputs)


def assemble_kernel(
    result,
    input_grad,
    wide_in,
    qkv_in,
    down,
    out_in,
    small,
    output_ref,
    input_grad_ref,
    g_query_ref,
    g_key_ref,
    g_value_ref,
    g_out_ref,
    g_up_ref,
    g_gate_ref,
    g_down_ref,
    small_ref,
):
    f32 = jnp.float32
    output_ref[...] = result[...]
    input_grad_ref[...] = input_grad[...]
    g_down_ref[...] = down[...]
    small_ref[...] = small[...]
    g_out_ref[...] = sum(out_in[i].astype(f32) for i in range(4))
    part = wide_in.shape[2] // 4
    ff_half = g_up_ref.shape[1] // 2
    for j in range(GROUP):
        for p in (0, 1):
            place = slice(p * ff_half + j * part, p * ff_half + (j + 1) * part)
            g_up_ref[:, place] = wide_in[j, :, p * part : (p + 1) * part].astype(f32)
            g_gate_ref[:, place] = wide_in[j, :, (2 + p) * part : (3 + p) * part].astype(f32)
    first = half_lanes((g_query_ref.shape[0], 128))
    for pair in range(GROUP // 2):
        place = slice(128 * pair, 128 * (pair + 1))
        even, odd = qkv_in[2 * pair].astype(f32), qkv_in[2 * pair + 1].astype(f32)
        even_qk, odd_qk = even[:, :128], odd[:, :128]
        g_query_ref[:, place] = jnp.where(first, even_qk, pltpu.roll(odd_qk, HEAD_DIM, 1))
        g_key_ref[:, place] = jnp.where(first, pltpu.roll(even_qk, HEAD_DIM, 1), odd_qk)
        g_value_ref[:, place] = jnp.where(
            first, even[:, 128:], pltpu.roll(odd[:, 128:], HEAD_DIM, 1)
        )


def assemble_block(inputs, ff):
    result, input_grad, wide_in, qkv_in, down, out_in, small = inputs
    f32 = jnp.float32
    shape = jax.ShapeDtypeStruct
    width = result.shape[1]
    rows_out = wide_in.shape[1]
    return pl.pallas_call(
        assemble_kernel,
        out_shape=[
            shape(result.shape, result.dtype),
            shape(input_grad.shape, f32),
            shape((rows_out, width), f32),
            shape((rows_out, width), f32),
            shape((rows_out, width), f32),
            shape((rows_out, width), f32),
            shape((rows_out, ff), f32),
            shape((rows_out, ff), f32),
            shape(down.shape, f32),
            shape(small.shape, f32),
        ],
        in_specs=[VMEM_SPEC] * 7,
        out_specs=[VMEM_SPEC] * 10,
        compiler_params=pltpu.CompilerParams(vmem_limit_bytes=VMEM_LIMIT),
        name="assemble_block",
    )(*inputs)


def on_device_heads(
    tokens,
    cotangent,
    lengths,
    w_query,
    w_key,
    w_value,
    w_out,
    w_up,
    w_gate,
    w_down,
    s_qk,
    s_up,
    s_gate,
    alpha_attn,
    alpha_mlp,
):
    model_width = w_query.shape[0]
    tok_rows = tokens.shape[2]
    half_rows = tok_rows // 2
    hidden = tokens[0, 0]
    hidden_all, qa, ka, va, query_raw, key_raw, gain = project_block(
        hidden, w_query, w_key, w_value, s_qk
    )
    attended, ql, packed = attend(lengths, qa, ka, va, half_rows)
    (result, input_grad, wide_in, qkv_in, grad_down, out_in, grad_scales, small) = tail_block(
        (
            lengths,
            packed,
            hidden,
            cotangent[0, 0],
            gain,
            s_up[None],
            s_gate[None],
            alpha_attn[None],
            alpha_mlp[None],
        ),
        (
            w_out,
            w_up,
            w_gate,
            w_down,
            w_query,
            w_key,
            w_value,
            ql,
            ka,
            va,
            attended,
            query_raw,
            key_raw,
            hidden_all.reshape(GROUP * tok_rows, model_width),
        ),
    )
    (
        output,
        input_grad,
        grad_query,
        grad_key,
        grad_value,
        grad_out,
        grad_up,
        grad_gate,
        grad_down,
        small,
    ) = assemble_block(
        (result, input_grad, wide_in, qkv_in, grad_down, out_in, small), w_up.shape[1]
    )
    dp, b = here()
    rows_out = model_width // (2 * GROUP)
    first_row = (dp * GROUP + b) * rows_out
    grad_attn, grad_mlp_alpha = (
        lax.dynamic_slice_in_dim(small[8 * i : 8 * (i + 1)].reshape(-1), first_row, rows_out, 0)
        for i in (0, 1)
    )
    grad_gain = lax.dynamic_slice_in_dim(small[17], (b % 2) * rows_out, rows_out, 0)
    mean_alpha = 0.5 * (jnp.mean(alpha_attn) + jnp.mean(alpha_mlp))
    return (
        output[None, None],
        input_grad[None, None],
        grad_query,
        grad_key,
        grad_value,
        grad_out,
        grad_up,
        grad_gate,
        grad_down,
        grad_gain,
        grad_scales[0],
        grad_scales[1],
        grad_attn,
        grad_mlp_alpha,
        mean_alpha,
    )


def on_device(*arrays):
    head_count = arrays[3].shape[0] // HEAD_DIM
    tok_rows = arrays[0].shape[2]
    fits = lax.axis_size("blk") == head_count == 16 and lax.axis_size("dp") == 2
    if fits and tok_rows == 128:
        return on_device_heads(*arrays)
    return on_device_general(*arrays)


def solution(mesh):
    in_specs = (
        P("dp", "blk", None, None),
        P("dp", "blk", None, None),
        P("dp", None),
        P(),
        P(),
        P(),
        P(),
        P(),
        P(),
        P(),
        P(),
        P(),
        P(),
        P(),
        P(),
    )
    out_specs = (
        P("dp", "blk", None, None),
        P("dp", "blk", None, None),
        P(("dp", "blk"), None),
        P(("dp", "blk"), None),
        P(("dp", "blk"), None),
        P(("dp", "blk"), None),
        P(("dp", "blk"), None),
        P(("dp", "blk"), None),
        P(("dp", "blk"), None),
        P(("dp", "blk")),
        P(("dp", "blk")),
        P(("dp", "blk")),
        P(("dp", "blk")),
        P(("dp", "blk")),
        P(),
    )
    return jax.shard_map(
        on_device, mesh=mesh, in_specs=in_specs, out_specs=out_specs, check_vma=False
    )
```

```python
import functools
import math

import jax
import jax.numpy as jnp
from jax import lax
from jax.experimental import pallas as pl
from jax.experimental.pallas import tpu as pltpu
from jax.sharding import PartitionSpec as P

HEAD_DIM = 64


def rms_norm(vector):
    return vector * lax.rsqrt(jnp.mean(vector * vector, axis=-1, keepdims=True) + 1e-06)


def head_norm(vector, head_count):
    shaped = vector.reshape(vector.shape[0], head_count, -1)
    return rms_norm(shaped).reshape(vector.shape)


def silu_smooth(vector):
    return vector / (1.0 + jnp.exp(-vector))


def residual_mix(inputs, branch, alphas):
    return rms_norm(inputs + alphas * (rms_norm(branch) - inputs))


def gated_inner(up_raw, gate_raw, s_up, s_gate):
    return up_raw * s_up * silu_smooth(gate_raw * s_gate)


def stream_positions(row_index, tok_rows, members):
    half_rows = tok_rows // 2
    device = row_index // tok_rows
    within = row_index % tok_rows
    block_id = jnp.where(within < half_rows, device, 2 * members - 1 - device)
    return block_id * half_rows + within % half_rows


def doc_index(positions, doc_ends):
    return jnp.sum(
        (positions[:, None] >= doc_ends[None, :]).astype(jnp.int32), axis=1, dtype=jnp.int32
    )


def allowed_pairs(query_pos, query_doc, key_pos, key_doc):
    return (key_pos[None, :] <= query_pos[:, None]) & (key_doc[None, :] == query_doc[:, None])


def take_rows(matrix, first_row, row_count):
    return lax.dynamic_slice_in_dim(matrix, first_row, row_count, 0)


def fold_half(running, query_heads, key_heads, value_heads, allowed, score_scale):

    def absorb(carried):
        best_score, total_sum, accumulated = carried
        scores = (
            jnp.einsum("qhd,khd->hqk", query_heads, key_heads, preferred_element_type=jnp.float32)
            * score_scale
        )
        scores = jnp.where(allowed[None], scores, -1e30)
        new_best = jnp.maximum(best_score, jnp.max(scores, axis=2))
        weights = jnp.where(allowed[None], jnp.exp(scores - new_best[:, :, None]), 0.0)
        fade_factor = jnp.exp(best_score - new_best)
        total_sum = jnp.sum(weights, axis=2)
        accumulated = accumulated * fade_factor.T[:, :, None] + jnp.einsum(
            "hqk,khd->qhd",
            weights.astype(jnp.bfloat16),
            value_heads,
            preferred_element_type=jnp.float32,
        )
        return (new_best, total_sum, accumulated)

    return lax.cond(jnp.any(allowed), absorb, lambda carried: carried, running)


def pair_terms(query_side, key_heads, value_heads, allowed, score_scale):
    query_heads, grad_heads, log_total, delta_rows = (
        query_side[0],
        query_side[1],
        query_side[2],
        query_side[3],
    )
    scores = (
        jnp.einsum("qhd,khd->hqk", query_heads, key_heads, preferred_element_type=jnp.float32)
        * score_scale
    )
    scores = jnp.where(allowed[None], scores, -1e30)
    weights = jnp.exp(scores - log_total[:, :, None])
    grad_weights = jnp.einsum(
        "qhd,khd->hqk", grad_heads, value_heads, preferred_element_type=jnp.float32
    )
    grad_scores = (weights * (grad_weights - delta_rows[:, :, None])).astype(jnp.bfloat16)
    return (weights.astype(jnp.bfloat16), grad_scores)


def query_term(query_side, key_heads, value_heads, allowed, score_scale):
    weights, grad_scores = pair_terms(query_side, key_heads, value_heads, allowed, score_scale)
    return score_scale * jnp.einsum(
        "hqk,khd->qhd", grad_scores, key_heads, preferred_element_type=jnp.float32
    )


def key_term(query_side, key_heads, value_heads, allowed, score_scale):
    weights, grad_scores = pair_terms(query_side, key_heads, value_heads, allowed, score_scale)
    grad_keys = score_scale * jnp.einsum(
        "hqk,qhd->khd", grad_scores, query_side[0], preferred_element_type=jnp.float32
    )
    grad_values = jnp.einsum(
        "hqk,qhd->khd", weights, query_side[1], preferred_element_type=jnp.float32
    )
    return (grad_keys, grad_values)


def on_device_general(
    tokens,
    cotangent,
    lengths,
    w_query,
    w_key,
    w_value,
    w_out,
    w_up,
    w_gate,
    w_down,
    s_qk,
    s_up,
    s_gate,
    alpha_attn,
    alpha_mlp,
):
    model_width = w_query.shape[0]
    head_count = model_width // HEAD_DIM
    score_scale = 1.0 / math.sqrt(HEAD_DIM)
    tok_rows = tokens.shape[2]
    half_rows = tok_rows // 2
    members = lax.axis_size("blk")
    position = lax.axis_index("blk")
    doc_ends = jnp.cumsum(lengths[0], dtype=jnp.int32)
    hidden = tokens[0, 0]
    hidden_f = hidden.astype(jnp.float32)

    def key_info(first_row, row_count):
        key_pos = stream_positions(
            first_row + jnp.arange(row_count, dtype=jnp.int32), tok_rows, members
        )
        return (key_pos, doc_index(key_pos, doc_ends))

    def heads_of(matrix):
        return matrix.reshape(matrix.shape[0], head_count, HEAD_DIM)

    def scaled_norm(raw_rows, gain_vector):
        return head_norm(raw_rows, head_count) * gain_vector

    own_pos, own_doc = key_info(position * tok_rows, tok_rows)
    query_raw = jnp.dot(hidden, w_query, preferred_element_type=jnp.float32)
    key_raw = jnp.dot(hidden, w_key, preferred_element_type=jnp.float32)
    value_raw = jnp.dot(hidden, w_value, preferred_element_type=jnp.float32)
    queries = scaled_norm(query_raw, s_qk).astype(jnp.bfloat16)
    key_rows = scaled_norm(key_raw, s_qk).astype(jnp.bfloat16)
    value_rows = value_raw.astype(jnp.bfloat16)
    query_heads = heads_of(queries)

    def empty_state():
        return (
            jnp.full((head_count, half_rows), -1e30, jnp.float32),
            jnp.zeros((head_count, half_rows), jnp.float32),
            jnp.zeros((half_rows, head_count, HEAD_DIM), jnp.float32),
        )

    running = (empty_state(), empty_state())
    key_part = lax.all_gather(key_rows, "blk", axis=0, tiled=True)
    value_part = lax.all_gather(value_rows, "blk", axis=0, tiled=True)
    key_pos, key_doc = key_info(jnp.int32(0), key_part.shape[0])
    updated = []
    for part_index in range(2):
        rows_here = slice(part_index * half_rows, (part_index + 1) * half_rows)
        allowed = allowed_pairs(own_pos[rows_here], own_doc[rows_here], key_pos, key_doc)
        updated.append(
            fold_half(
                running[part_index],
                query_heads[rows_here],
                heads_of(key_part),
                heads_of(value_part),
                allowed,
                score_scale,
            )
        )
    folded = (updated[0], updated[1])
    best_score = jnp.concatenate([folded[0][0], folded[1][0]], axis=1)
    total_sum = jnp.concatenate([folded[0][1], folded[1][1]], axis=1)
    accumulated = jnp.concatenate([folded[0][2], folded[1][2]], axis=0)
    attended = accumulated / total_sum.T[:, :, None]
    log_total = best_score + jnp.log(total_sum)
    attended_low = attended.reshape(tok_rows, model_width).astype(jnp.bfloat16)
    branch = jnp.dot(attended_low, w_out, preferred_element_type=jnp.float32)
    middle = residual_mix(hidden_f, branch, alpha_attn)
    middle_low = middle.astype(jnp.bfloat16)
    up_raw = jnp.dot(middle_low, w_up, preferred_element_type=jnp.float32)
    gate_raw = jnp.dot(middle_low, w_gate, preferred_element_type=jnp.float32)
    inner_low = gated_inner(up_raw, gate_raw, s_up, s_gate).astype(jnp.bfloat16)
    mlp_raw = jnp.dot(inner_low, w_down, preferred_element_type=jnp.float32)
    result = residual_mix(middle, mlp_raw, alpha_mlp)
    mixed_out, pull_out = jax.vjp(residual_mix, middle, mlp_raw, alpha_mlp)
    grad_middle, grad_mlp, grad_alpha_mlp = pull_out(cotangent[0, 0].astype(jnp.float32))
    grad_mlp_low = grad_mlp.astype(jnp.bfloat16)
    grad_w_down = jnp.dot(inner_low.T, grad_mlp_low, preferred_element_type=jnp.float32)
    grad_inner = jnp.dot(grad_mlp_low, w_down.T, preferred_element_type=jnp.float32)
    inner_out, pull_inner = jax.vjp(gated_inner, up_raw, gate_raw, s_up, s_gate)
    grad_up_raw, grad_gate_raw, grad_s_up, grad_s_gate = pull_inner(grad_inner)
    up_low = grad_up_raw.astype(jnp.bfloat16)
    gate_low = grad_gate_raw.astype(jnp.bfloat16)
    grad_w_up = jnp.dot(middle_low.T, up_low, preferred_element_type=jnp.float32)
    grad_w_gate = jnp.dot(middle_low.T, gate_low, preferred_element_type=jnp.float32)
    grad_middle = (
        grad_middle
        + jnp.dot(up_low, w_up.T, preferred_element_type=jnp.float32)
        + jnp.dot(gate_low, w_gate.T, preferred_element_type=jnp.float32)
    )
    attn_out, pull_attn = jax.vjp(residual_mix, hidden_f, branch, alpha_attn)
    grad_hidden, grad_branch, grad_alpha_attn = pull_attn(grad_middle)
    branch_low = grad_branch.astype(jnp.bfloat16)
    grad_w_out = jnp.dot(attended_low.T, branch_low, preferred_element_type=jnp.float32)
    grad_att_low = jnp.dot(branch_low, w_out.T, preferred_element_type=jnp.float32).astype(
        jnp.bfloat16
    )
    grad_heads = heads_of(grad_att_low)
    delta_rows = jnp.sum(grad_heads.astype(jnp.float32) * attended, axis=2).T

    def local_side(part_index):
        rows_here = slice(part_index * half_rows, (part_index + 1) * half_rows)
        return (
            query_heads[rows_here],
            grad_heads[rows_here],
            log_total[:, rows_here],
            delta_rows[:, rows_here],
            own_pos[rows_here],
            own_doc[rows_here],
        )

    local_parts = (local_side(0), local_side(1))
    whole_keys, whole_values = (
        lax.all_gather(key_rows, "blk", axis=0, tiled=True),
        lax.all_gather(value_rows, "blk", axis=0, tiled=True),
    )

    def query_step(grad_parts, shard_index):
        first_row = shard_index * tok_rows
        key_part = heads_of(take_rows(whole_keys, first_row, tok_rows))
        value_part = heads_of(take_rows(whole_values, first_row, tok_rows))
        key_pos, key_doc = key_info(first_row, tok_rows)
        updated = []
        for part_index in range(2):
            query_side = local_parts[part_index]
            allowed = allowed_pairs(query_side[4], query_side[5], key_pos, key_doc)

            def add_term(grad_now):
                return grad_now + query_term(query_side, key_part, value_part, allowed, score_scale)

            updated.append(
                lax.cond(
                    jnp.any(allowed), add_term, lambda grad_now: grad_now, grad_parts[part_index]
                )
            )
        return ((updated[0], updated[1]), None)

    zero_part = jnp.zeros((half_rows, head_count, HEAD_DIM), jnp.float32)
    grad_parts, unused_out = lax.scan(
        query_step, (zero_part, zero_part), jnp.arange(members, dtype=jnp.int32)
    )
    grad_queries = jnp.concatenate(grad_parts, axis=0).reshape(tok_rows, model_width)
    first_row = jnp.int32(0)
    row_count = lax.axis_size("blk") * tok_rows
    key_part = heads_of(take_rows(whole_keys, first_row, row_count))
    value_part = heads_of(take_rows(whole_values, first_row, row_count))
    key_pos, key_doc = key_info(first_row, row_count)
    zero_keys = jnp.zeros((row_count, head_count, HEAD_DIM), jnp.float32)
    totals = (zero_keys, zero_keys)
    for part_index in range(2):
        query_side = local_parts[part_index]
        allowed = allowed_pairs(query_side[4], query_side[5], key_pos, key_doc)

        def add_terms(grad_now):
            grad_keys, grad_values = key_term(
                query_side, key_part, value_part, allowed, score_scale
            )
            return (grad_now[0] + grad_keys, grad_now[1] + grad_values)

        totals = lax.cond(jnp.any(allowed), add_terms, lambda grad_now: grad_now, totals)
    key_value_grads = lax.psum_scatter(
        jnp.concatenate(
            [totals[0].reshape(row_count, model_width), totals[1].reshape(row_count, model_width)],
            axis=1,
        ),
        "blk",
        scatter_dimension=0,
        tiled=True,
    )
    grad_keys = key_value_grads[:, :model_width]
    grad_values = key_value_grads[:, model_width:]
    query_out, pull_query = jax.vjp(scaled_norm, query_raw, s_qk)
    grad_query_raw, grad_qk_first = pull_query(grad_queries)
    key_out, pull_key = jax.vjp(scaled_norm, key_raw, s_qk)
    grad_key_raw, grad_qk_second = pull_key(grad_keys)
    grad_s_qk = grad_qk_first + grad_qk_second
    query_low = grad_query_raw.astype(jnp.bfloat16)
    key_low = grad_key_raw.astype(jnp.bfloat16)
    value_low = grad_values.astype(jnp.bfloat16)
    grad_w_query = jnp.dot(hidden.T, query_low, preferred_element_type=jnp.float32)
    grad_w_key = jnp.dot(hidden.T, key_low, preferred_element_type=jnp.float32)
    grad_w_value = jnp.dot(hidden.T, value_low, preferred_element_type=jnp.float32)
    input_grad = (
        grad_hidden
        + jnp.dot(query_low, w_query.T, preferred_element_type=jnp.float32)
        + jnp.dot(key_low, w_key.T, preferred_element_type=jnp.float32)
        + jnp.dot(value_low, w_value.T, preferred_element_type=jnp.float32)
    )
    summed = (
        lax.psum_scatter(grad_w_query, ("dp", "blk"), scatter_dimension=0, tiled=True),
        lax.psum_scatter(grad_w_key, ("dp", "blk"), scatter_dimension=0, tiled=True),
        lax.psum_scatter(grad_w_value, ("dp", "blk"), scatter_dimension=0, tiled=True),
        lax.psum_scatter(grad_w_out, ("dp", "blk"), scatter_dimension=0, tiled=True),
        lax.psum_scatter(grad_w_up, ("dp", "blk"), scatter_dimension=0, tiled=True),
        lax.psum_scatter(grad_w_gate, ("dp", "blk"), scatter_dimension=0, tiled=True),
        lax.psum_scatter(grad_w_down, ("dp", "blk"), scatter_dimension=0, tiled=True),
        lax.psum_scatter(grad_s_qk, ("dp", "blk"), scatter_dimension=0, tiled=True),
        lax.psum_scatter(grad_s_up, ("dp", "blk"), scatter_dimension=0, tiled=True),
        lax.psum_scatter(grad_s_gate, ("dp", "blk"), scatter_dimension=0, tiled=True),
        lax.psum_scatter(grad_alpha_attn, ("dp", "blk"), scatter_dimension=0, tiled=True),
        lax.psum_scatter(grad_alpha_mlp, ("dp", "blk"), scatter_dimension=0, tiled=True),
    )
    mean_alpha = 0.5 * (jnp.mean(alpha_attn) + jnp.mean(alpha_mlp))
    output = result.astype(jnp.bfloat16)[None, None]
    return (
        output,
        input_grad[None, None],
        summed[0],
        summed[1],
        summed[2],
        summed[3],
        summed[4],
        summed[5],
        summed[6],
        summed[7],
        summed[8],
        summed[9],
        summed[10],
        summed[11],
        mean_alpha,
    )


MESH = pl.DeviceIdType.MESH
VMEM_SPEC = pl.BlockSpec(memory_space=pltpu.VMEM)
VMEM_LIMIT = 62 << 20
GROUP = 16


def here():
    return lax.axis_index("dp"), lax.axis_index("blk")


def greet(partners):
    barrier = pltpu.get_barrier_semaphore()
    for partner in partners:
        pl.semaphore_signal(barrier, inc=1, device_id=partner, device_id_type=MESH)
    pl.semaphore_wait(barrier, len(partners))


def remote(src, dst, send_sem, recv_sem, device):
    return pltpu.make_async_remote_copy(
        src_ref=src,
        dst_ref=dst,
        send_sem=send_sem,
        recv_sem=recv_sem,
        device_id=device,
        device_id_type=MESH,
    )


class Gather:
    KINDS = 22

    def __init__(self, own, out, send, recv, pieces):
        self.own, self.out, self.send, self.recv = own, out, send, recv
        self.pieces = pieces
        dp, b = here()
        self.dp, self.b = dp, b
        self.z, self.y, self.c = b // 4, (b // 2) % 2, b % 2
        self.up = (dp, (b + 4) % GROUP)
        self.down = (dp, (b + 12) % GROUP)
        self.side = (dp, b + 2 - 4 * self.y)
        self.sib = (dp, b + 1 - 2 * self.c)
        self.half = self.pieces // 2

    def partners(self):
        return [self.up, self.down, self.side, self.sib]

    def copy(self, z, y, c, kind, piece, device, own=False):
        block = z * 4 + y * 2 + c
        upper = piece // self.half
        place = 2 * GROUP - 1 - block if upper else block
        rows = self.out.shape[1] // self.half
        span = pl.ds(piece % self.half * rows, rows)
        target = self.out.at[place, span]
        source = self.own.at[upper, span] if own else target
        index = self.pieces * kind + piece
        return remote(source, target, self.send.at[index], self.recv.at[index], device)

    def along(self, z, piece, device, own=False, back=False):
        return self.copy(z, self.y, self.c, z + (4 if back else 0), piece, device, own)

    def across(self, z, y, piece, own=False):
        return self.copy(z, y, self.c, 8 + z, piece, self.side, own)

    def over(self, z, piece, device, back=False):
        return self.copy(z, 1 - self.y, self.c, 21 if back else 20, piece, device)

    def to_sib(self, z, y, c, piece, own=False):
        return self.copy(z, y, c, 12 + 2 * z + y, piece, self.sib, own)

    def each_side(self, distance, action):
        if distance == 0:
            action(self.z, None)
            return
        low, high = self.z - distance, self.z + distance

        @pl.when(low >= 0)
        def _():
            action(low, False)

        @pl.when(high <= 3)
        def _():
            action(high, True)

    def start(self):
        for piece in range(self.pieces):

            @pl.when(self.z < 3)
            def _():
                self.along(self.z, piece, self.up, True).start()

            @pl.when(self.z > 0)
            def _():
                self.along(self.z, piece, self.down, True, True).start()

            self.across(self.z, self.y, piece, True).start()
        for piece in range(self.pieces):
            self.to_sib(self.z, self.y, self.c, piece, True).start()
        for upper in (0, 1):
            place = 2 * GROUP - 1 - self.b if upper else self.b
            self.out[place] = self.own[upper]

    def line(self, distance):
        def action(z, above):
            for piece in range(self.pieces):
                self.along(z, piece, self.sib, False, above).wait_recv()
                if above:

                    @pl.when(self.z > 0)
                    def _():
                        self.along(z, piece, self.down, False, True).start()
                else:

                    @pl.when(self.z < 3)
                    def _():
                        self.along(z, piece, self.up).start()

                if distance > 1 or piece < self.half:
                    self.across(z, self.y, piece).start()
                self.to_sib(z, self.y, self.c, piece).start()

        self.each_side(distance, action)

    def sides(self, distance):
        def action(z, above):
            for piece in range(self.pieces):
                if distance == 1 and piece >= self.half:
                    continue
                self.across(z, 1 - self.y, piece).wait_recv()
                self.to_sib(z, 1 - self.y, self.c, piece).start()

        self.each_side(distance, action)

    def hand_over(self):
        for piece in range(self.half, self.pieces):

            @pl.when(self.z < 3)
            def _():
                self.over(self.z, piece, self.up).start()

            @pl.when(self.z > 0)
            def _():
                self.over(self.z, piece, self.down, True).start()

    def handed(self):
        def action(z, above):
            for piece in range(self.half, self.pieces):
                self.over(z, piece, self.sib, above).wait_recv()
                self.to_sib(z, 1 - self.y, self.c, piece).start()

        self.each_side(1, action)

    def from_sib(self, distance):
        def action(z, above):
            for piece in range(self.pieces):
                for y in (0, 1):
                    self.to_sib(z, y, 1 - self.c, piece).wait_recv()

        self.each_side(distance, action)

    def drain(self):
        for piece in range(self.pieces):
            for z in range(4):
                for y in (0, 1):
                    self.to_sib(z, y, self.c, piece).wait_send()
                if piece < self.half:
                    self.across(z, self.y, piece).wait_send()
                else:

                    @pl.when((z > self.z + 1) | (z < self.z - 1) | (z == self.z))
                    def _():
                        self.across(z, self.y, piece).wait_send()

                @pl.when((self.z >= z) & (self.z < 3))
                def _():
                    self.along(z, piece, self.up).wait_send()

                @pl.when((self.z <= z) & (self.z > 0))
                def _():
                    self.along(z, piece, self.down, False, True).wait_send()

            if piece >= self.half:

                @pl.when(self.z < 3)
                def _():
                    self.over(self.z, piece, self.up).wait_send()

                @pl.when(self.z > 0)
                def _():
                    self.over(self.z, piece, self.down, True).wait_send()

    def finish(self):
        for distance in range(4):
            self.from_sib(distance)
        self.drain()


def gather_scratch(pieces):
    return [pltpu.SemaphoreType.DMA((pieces * Gather.KINDS,)) for _ in range(2)]


def comm_params(collective_id):
    return pltpu.CompilerParams(
        collective_id=collective_id, has_side_effects=True, vmem_limit_bytes=VMEM_LIMIT
    )


def dot_nt(left, right):
    return lax.dot_general(left, right, (((1,), (1,)), ((), ())), preferred_element_type=jnp.float32)


def dot_tn(left, right):
    return lax.dot_general(left, right, (((0,), (0,)), ((), ())), preferred_element_type=jnp.float32)


def dot_nn(left, right):
    return jnp.dot(left, right, preferred_element_type=jnp.float32)


FF_STEP = 1024


def mean_last(array):
    return jnp.mean(array, axis=-1, keepdims=True)


def rms_scale(array):
    return lax.rsqrt(mean_last(array * array) + 1e-06)


def rms_pull(grad, normed, scale):
    return scale * (grad - normed * mean_last(grad * normed))


def half_lanes(shape):
    return lax.broadcasted_iota(jnp.int32, shape, 1) < HEAD_DIM


class Swap:
    def __init__(self, blocks, out, send, recv, own=True):
        self.blocks, self.out, self.own = blocks, out, own
        dp, self.b = here()
        self.copies = []
        for step in range(1, GROUP):
            target = (self.b + step) % GROUP
            self.copies.append(
                remote(
                    (blocks.block(target) if isinstance(blocks, SendBlocks) else blocks.at[target])
                    if own
                    else blocks,
                    out.at[self.b],
                    send.at[step],
                    recv.at[step],
                    (dp, target),
                )
            )
        self.partners = [(dp, (self.b + step) % GROUP) for step in range(1, GROUP)]

    def start(self):
        for copy in self.copies:
            copy.start()
        if self.own:
            mine = self.blocks
            mine = mine.block(self.b) if isinstance(mine, SendBlocks) else mine.at[self.b]
            self.out[self.b] = mine[...]

    def wait(self):
        for copy in self.copies:
            copy.wait()


ANY_SPEC = pl.BlockSpec(memory_space=pl.ANY)


SMEM_SPEC = pl.BlockSpec(memory_space=pltpu.SMEM)


def own_head(pair, core):
    shifted = jnp.where(core == 1, pltpu.roll(pair, HEAD_DIM, 1), pair)
    return jnp.where(half_lanes(pair.shape), shifted, 0.0)


def minus_ones(matrix):
    lane = lax.broadcasted_iota(jnp.int32, matrix.shape, 1)
    extra = jnp.where(lane < HEAD_DIM + 3, -1.0, 0.0)
    return jnp.where(lane < HEAD_DIM, matrix, extra).astype(jnp.bfloat16)


PROJECT_PIECES = 4


def project_kernel(
    own,
    w_query_hbm,
    w_key_hbm,
    w_value_hbm,
    s_qk_ref,
    out,
    qa_ref,
    ka_ref,
    va_ref,
    q_raw_ref,
    k_raw_ref,
    gain_ref,
    w_head,
    load_sem,
    send,
    recv,
):
    gather = Gather(own, out, send, recv, PROJECT_PIECES)
    window = pl.ds(pl.multiple_of(gather.b // 2 * 128, 128), 128)
    loads = [
        pltpu.make_async_copy(
            source.at[:, window], w_head.at[:, pl.ds(128 * i, 128)], load_sem.at[i]
        )
        for i, source in enumerate((w_query_hbm, w_key_hbm, w_value_hbm))
    ]
    for load in loads:
        load.start()
    greet(gather.partners())
    gather.start()
    gain = own_head(jnp.broadcast_to(s_qk_ref[:, window], (8, 128)), gather.c)[:1]
    gain_ref[...] = gain
    for load in loads:
        load.wait()
    slots = 2 * GROUP // 8
    half = out.shape[1]

    def project(first_slot):
        hidden = out[pl.ds(first_slot, slots)].reshape(slots * half, out.shape[2])
        raw = dot_nn(hidden, w_head[...])
        rows = pl.ds(pl.multiple_of(first_slot * half, half), slots * half)
        query, key, value = (
            own_head(raw[:, 128 * i : 128 * (i + 1)], gather.c) for i in range(3)
        )
        q_raw_ref[rows, :] = query.astype(jnp.bfloat16)
        k_raw_ref[rows, :] = key.astype(jnp.bfloat16)
        count = float(HEAD_DIM)
        query_scale = lax.rsqrt(jnp.sum(query * query, axis=1, keepdims=True) / count + 1e-06)
        key_scale = lax.rsqrt(jnp.sum(key * key, axis=1, keepdims=True) / count + 1e-06)
        query = (query * query_scale * gain).astype(jnp.bfloat16).astype(jnp.float32)
        qa_ref[rows, :] = (query * (1.0 / math.sqrt(HEAD_DIM))).astype(jnp.bfloat16)
        ka_ref[rows, :] = minus_ones(key * key_scale * gain)
        va_ref[rows, :] = minus_ones(value)

    def project_line(distance):
        def both(z):
            project(slots * z)
            project(2 * GROUP - slots - slots * z)

        if distance == 0:
            both(gather.z)
        else:

            @pl.when(gather.z - distance >= 0)
            def _():
                both(gather.z - distance)

            @pl.when(gather.z + distance <= 3)
            def _():
                both(gather.z + distance)

    gather.line(1)
    gather.sides(0)
    gather.from_sib(0)
    project_line(0)
    gather.line(2)
    gather.hand_over()
    gather.sides(1)
    gather.line(3)
    gather.sides(2)
    gather.from_sib(2)
    project_line(2)
    gather.handed()
    gather.from_sib(1)
    project_line(1)
    gather.sides(3)
    gather.from_sib(3)
    project_line(3)
    gather.drain()


def project_block(hidden, w_query, w_key, w_value, s_qk):
    rows, width = hidden.shape
    length = GROUP * rows
    low, f32 = jnp.bfloat16, jnp.float32
    shape = jax.ShapeDtypeStruct
    return pl.pallas_call(
        project_kernel,
        out_shape=[
            shape((2 * GROUP, rows // 2, width), low),
            shape((length, 128), low),
            shape((length, 128), low),
            shape((length, 128), low),
            shape((length, 128), low),
            shape((length, 128), low),
            shape((1, 128), f32),
        ],
        in_specs=[VMEM_SPEC] + [ANY_SPEC] * 3 + [VMEM_SPEC],
        out_specs=[VMEM_SPEC] * 7,
        scratch_shapes=[pltpu.VMEM((width, 384), low), pltpu.SemaphoreType.DMA((3,))]
        + gather_scratch(PROJECT_PIECES),
        compiler_params=comm_params(0),
        name="project_block",
    )(hidden.reshape(2, rows // 2, width), w_query, w_key, w_value, s_qk[None])


def doc_start_of(positions, lengths_ref):
    start = jnp.zeros_like(positions)
    end = jnp.int32(0)
    for doc in range(lengths_ref.shape[1]):
        end = end + lengths_ref[0, doc]
        start = start + jnp.where(positions >= end, lengths_ref[0, doc], 0)
    return start


def split_lanes(column, shape):
    lane = lax.broadcasted_iota(jnp.int32, shape, 1)
    high = column.astype(jnp.bfloat16).astype(jnp.float32)
    rest = column - high
    mid = rest.astype(jnp.bfloat16).astype(jnp.float32)
    last = rest - mid
    return jnp.where(
        lane == HEAD_DIM,
        high,
        jnp.where(lane == HEAD_DIM + 1, mid, jnp.where(lane == HEAD_DIM + 2, last, 0.0)),
    )


ATT = 512


def attend_kernel(lengths_ref, qa_ref, ka_ref, va_ref, o_ref, ql_ref, packed_ref):
    length = qa_ref.shape[0]
    half = packed_ref.shape[1]
    for query_block in range(length // ATT):
        rows = pl.ds(query_block * ATT, ATT)
        queries = qa_ref[rows, :]
        column = query_block * ATT + lax.broadcasted_iota(jnp.int32, (ATT, 1), 0)
        doc_start = doc_start_of(column, lengths_ref)
        query_pos = query_block * ATT + lax.broadcasted_iota(jnp.int32, (ATT, ATT), 0)
        key_lane = lax.broadcasted_iota(jnp.int32, (ATT, ATT), 1)

        def step(key_block, total):
            base = key_block * ATT
            keys = ka_ref[pl.ds(base, ATT), :]
            values = va_ref[pl.ds(base, ATT), :]
            key_pos = base + key_lane
            allowed = key_pos >= doc_start
            if key_block == query_block:
                allowed = allowed & (key_pos <= query_pos)
            weights = jnp.where(allowed, jnp.exp(dot_nt(queries, keys)), 0.0)
            return total + dot_nn(weights.astype(jnp.bfloat16), values)

        total = jnp.zeros((ATT, 128), jnp.float32)
        for key_block in range(query_block + 1):
            total = step(key_block, total)
        row_sum = -total[:, HEAD_DIM : HEAD_DIM + 1]
        first = half_lanes(total.shape)
        o_ref[rows, :] = jnp.where(first, total / row_sum, 0.0).astype(o_ref.dtype)
        extra = split_lanes(jnp.log(row_sum), total.shape)
        ql_ref[rows, :] = jnp.where(first, queries.astype(jnp.float32), extra).astype(jnp.bfloat16)
    first = half_lanes((half, 128))
    for j in range(GROUP):
        lower = o_ref[j * half : (j + 1) * half, :].astype(jnp.float32)
        upper = o_ref[length - (j + 1) * half : length - j * half, :].astype(jnp.float32)
        packed_ref[j] = jnp.where(first, lower, pltpu.roll(upper, HEAD_DIM, 1)).astype(
            packed_ref.dtype
        )


def attend(lengths, qa, ka, va, half_rows):
    length = qa.shape[0]
    shape = jax.ShapeDtypeStruct
    return pl.pallas_call(
        attend_kernel,
        out_shape=[
            shape((length, 128), jnp.bfloat16),
            shape((length, 128), jnp.bfloat16),
            shape((GROUP, half_rows, 128), jnp.bfloat16),
        ],
        in_specs=[SMEM_SPEC] + [VMEM_SPEC] * 3,
        out_specs=[VMEM_SPEC] * 3,
        compiler_params=pltpu.CompilerParams(vmem_limit_bytes=VMEM_LIMIT),
        name="attend",
    )(lengths, qa, ka, va)


TAIL_PIECES = 2
KEYS = 512
PART = 512


class SendBlocks:
    def __init__(self, ref, first_row, rows, first_lane, lanes):
        self.ref, self.first_row, self.rows = ref, first_row, rows
        self.lanes = pl.ds(first_lane, lanes)

    def block(self, index):
        start = pl.multiple_of(self.first_row + index * self.rows, self.rows)
        return self.ref.at[pl.ds(start, self.rows), self.lanes]


def tail_kernel(
    lengths_ref,
    o_ref,
    hidden_ref,
    cot_ref,
    gain_ref,
    s_up_ref,
    s_gate_ref,
    alpha_attn_ref,
    alpha_mlp_ref,
    w_out_hbm,
    w_up_hbm,
    w_gate_hbm,
    w_down_hbm,
    w_query_hbm,
    w_key_hbm,
    w_value_hbm,
    ql_hbm,
    ka_hbm,
    va_hbm,
    att_hbm,
    q_raw_hbm,
    k_raw_hbm,
    hidden_hbm,
    result_ref,
    input_grad_ref,
    wide_in,
    qkv_in,
    g_down_ref,
    out_in,
    g_s_ref,
    small_ref,
    mid_all,
    g_mlp_all,
    w_out,
    w_up,
    w_gate,
    w_down,
    up_slice,
    gate_slice,
    down_slice,
    up_raw,
    gate_raw,
    mid_own,
    g_mlp_own,
    o_in,
    g_send,
    g_in,
    acc,
    g_res,
    att_pair,
    branch_pair,
    out_got,
    out_side_got,
    ql_ref,
    ka_ref,
    va_ref,
    ga_ref,
    dq_acc,
    back_in,
    qkv_part,
    qkv_got,
    wide_own,
    wide_got,
    down_got,
    small_own,
    small_got,
    small_all,
    s_part,
    s_send,
    s_got,
    load_sems,
    x_sems,
    pair_sems,
    out_sems,
    swap_sems,
    grad_sems,
    back_sems,
    qkv_sems,
    wide_sems,
    small_sems,
    mid_send,
    mid_recv,
    mlp_send,
    mlp_recv,
):
    low, f32 = jnp.bfloat16, jnp.float32
    dp, b = here()
    z, y, c = b // 4, (b // 2) % 2, b % 2
    twin, sib, side = (1 - dp, b), (dp, b + 1 - 2 * c), (dp, b + 2 - 4 * y)
    rows, width = hidden_ref.shape
    half = rows // 2
    length = GROUP * rows
    ff = w_up.shape[1]
    ff_half = ff // 2
    part = ff // (2 * GROUP)
    quarter = width // 4
    rows_out = width // (2 * GROUP)
    blocks = length // ATT
    loaded = []

    def load(source, target):
        copy = pltpu.make_async_copy(source, target, load_sems.at[len(loaded)])
        copy.start()
        loaded.append(copy)
        return copy

    def to(device, sems, index, source, target):
        copy = remote(source, target, sems.at[0, index], sems.at[1, index], device)
        copy.start()
        return copy

    load_out = load(w_out_hbm, w_out)
    load_mlp = [load(w_up_hbm, w_up), load(w_gate_hbm, w_gate), load(w_down_hbm, w_down)]
    load_slices = []
    windows = [pl.ds(pl.multiple_of(p * ff_half + b * part, part), part) for p in (0, 1)]
    for p in (0, 1):
        place = pl.ds(p * part, part)
        load_slices.append(load(w_up_hbm.at[:, windows[p]], up_slice.at[:, place]))
        load_slices.append(load(w_gate_hbm.at[:, windows[p]], gate_slice.at[:, place]))
        load_slices.append(load(w_down_hbm.at[windows[p], :], down_slice.at[place, :]))

    swap = Swap(o_ref, o_in, swap_sems.at[0], swap_sems.at[1])
    grad_swap = Swap(g_send, g_in, grad_sems.at[0], grad_sems.at[1])
    small_swap = Swap(small_own, small_all, small_sems.at[0], small_sems.at[1], own=False)
    gather_mid = Gather(mid_own, mid_all, mid_send, mid_recv, TAIL_PIECES)
    gather_mlp = Gather(g_mlp_own, g_mlp_all, mlp_send, mlp_recv, TAIL_PIECES)
    greet(swap.partners + [twin])
    swap.start()
    swap.wait()

    first = half_lanes((half, 128))
    for pair in range(GROUP // 2):
        even = o_in[2 * pair].astype(f32)
        odd = o_in[2 * pair + 1].astype(f32)
        lanes = slice(pair * 128, (pair + 1) * 128)
        att_pair[c, :half, lanes] = jnp.where(first, even, pltpu.roll(odd, HEAD_DIM, 1)).astype(low)
        att_pair[c, half:, lanes] = jnp.where(first, pltpu.roll(even, HEAD_DIM, 1), odd).astype(low)
    att_copy = to(sib, pair_sems, 0, att_pair.at[c], att_pair.at[c])
    hidden = hidden_ref[...].astype(f32)
    alpha_attn = alpha_attn_ref[...]
    alpha_mlp = alpha_mlp_ref[...]
    load_out.wait()
    branch = dot_nn(att_pair[c], w_out[...])
    branch_scale = rms_scale(branch)
    branch_normed = branch * branch_scale
    mixed = hidden + alpha_attn * (branch_normed - hidden)
    middle_scale = rms_scale(mixed)
    middle = mixed * middle_scale
    middle_low = middle.astype(low)
    mid_own[0] = middle_low[:half]
    mid_own[1] = middle_low[half:]
    gather_mid.start()
    for copy in load_mlp:
        copy.wait()
    steps = ff // FF_STEP
    acc[...] = jnp.zeros_like(acc)

    def forward(step):
        cols = pl.ds(step * FF_STEP, FF_STEP)
        up = dot_nn(middle_low, w_up[:, cols])
        gate = dot_nn(middle_low, w_gate[:, cols])
        up_raw[:, cols] = up
        gate_raw[:, cols] = gate
        scaled = gate * s_gate_ref[:, cols]
        inner = up * s_up_ref[:, cols] * (scaled / (1.0 + jnp.exp(-scaled)))
        acc[...] += dot_nn(inner.astype(low), w_down[cols, :])

    for step in range(steps):
        forward(step)
    gather_mid.line(1)
    gather_mid.sides(0)
    mlp = acc[...]
    mlp_scale = rms_scale(mlp)
    mlp_normed = mlp * mlp_scale
    mixed_out = middle + alpha_mlp * (mlp_normed - middle)
    out_scale = rms_scale(mixed_out)
    result = mixed_out * out_scale
    result_ref[...] = result.astype(low)

    g_mixed = rms_pull(cot_ref[...].astype(f32), result, out_scale)
    g_alpha_mlp = jnp.sum(g_mixed * (mlp_normed - middle), axis=0, keepdims=True)
    small_own[...] = jnp.zeros_like(small_own)
    for i in range(width // 128):
        small_own[8 + i : 9 + i, :] = g_alpha_mlp[:, 128 * i : 128 * (i + 1)]
    g_mlp = rms_pull(g_mixed * alpha_mlp, mlp_normed, mlp_scale).astype(low)
    g_mlp_own[0] = g_mlp[:half]
    g_mlp_own[1] = g_mlp[half:]
    gather_mlp.start()
    acc[...] = g_mixed * (1.0 - alpha_mlp)

    def backward(step):
        cols = pl.ds(step * FF_STEP, FF_STEP)
        g_inner = dot_nt(g_mlp, w_down[cols, :])
        s_up = s_up_ref[:, cols]
        s_gate = s_gate_ref[:, cols]
        scaled = gate_raw[:, cols] * s_gate
        sigmoid = 1.0 / (1.0 + jnp.exp(-scaled))
        g_up = g_inner * (scaled / (1.0 + jnp.exp(-scaled))) * s_up
        slope = sigmoid * (1.0 + scaled * (1.0 - sigmoid))
        g_gate = g_inner * (up_raw[:, cols] * s_up) * slope * s_gate
        acc[...] += dot_nt(g_up.astype(low), w_up[:, cols]) + dot_nt(
            g_gate.astype(low), w_gate[:, cols]
        )

    for step in range(steps // 2):
        backward(step)
    gather_mid.line(2)
    gather_mid.hand_over()
    gather_mid.sides(1)
    for step in range(steps // 2, steps):
        backward(step)
    g_pre = rms_pull(acc[...], middle, middle_scale)
    g_res[...] = g_pre * (1.0 - alpha_attn)
    g_alpha_attn = jnp.sum(g_pre * (branch_normed - hidden), axis=0, keepdims=True)
    for i in range(width // 128):
        small_own[i : i + 1, :] = g_alpha_attn[:, 128 * i : 128 * (i + 1)]
    branch_pair[c] = rms_pull(g_pre * alpha_attn, branch_normed, branch_scale).astype(low)
    g_att = dot_nt(branch_pair[c], w_out[...]).astype(low).astype(f32)
    for pair in range(GROUP // 2):
        lower = g_att[:half, pair * 128 : (pair + 1) * 128]
        upper = g_att[half:, pair * 128 : (pair + 1) * 128]
        g_send[2 * pair] = jnp.where(first, lower, pltpu.roll(upper, HEAD_DIM, 1)).astype(low)
        g_send[2 * pair + 1] = jnp.where(first, pltpu.roll(lower, HEAD_DIM, 1), upper).astype(low)
    grad_swap.start()
    branch_copy = to(sib, pair_sems, 1, branch_pair.at[c], branch_pair.at[c])

    g_cat = w_down.at[pl.ds(0, length), pl.ds(0, 4 * part)]
    inner_all = w_down.at[pl.ds(0, length), pl.ds(512, 2 * part)]
    raw_low = w_down.at[pl.ds(length, length), pl.ds(0, 384)]
    att_ref = w_down.at[pl.ds(length, length), pl.ds(640, 128)]
    q_raw_ref = w_down.at[pl.ds(length, length), pl.ds(768, 128)]
    k_raw_ref = w_down.at[pl.ds(length, length), pl.ds(896, 128)]
    w_qkv = [w_up.at[:, pl.ds(i * width, width)] for i in range(3)]
    home = [w_up.at[pl.ds(i * rows, rows), pl.ds(3 * width, width)] for i in range(3)]
    out_send = w_out.at[pl.ds(0, quarter), :]
    out_side_send = [w_out.at[pl.ds(quarter + half * k, half), :] for k in (0, 1)]
    out_line = w_out.at[pl.ds(2 * quarter, 4 * rows_out), :]
    down_send = w_out.at[pl.ds(3 * quarter, part), :]
    out_own = [up_raw.at[:, pl.ds((2 + k) * width, width)] for k in (0, 1)]
    wide_send = [w_gate.at[pl.ds(quarter * i, quarter), pl.ds(2048, 512)] for i in (0, 1)]
    qkv_send = w_gate.at[pl.ds(0, 2 * quarter), pl.ds(2560, 256)]
    back_send = SendBlocks(w_gate, 0, half, 2816, 384)
    qkv_blocks = SendBlocks(w_gate, 2 * quarter, rows_out, 2560, 256)
    wide_blocks = SendBlocks(w_gate, 2 * quarter, rows_out, 2048, 512)
    back_swap = Swap(back_send, back_in, back_sems.at[0], back_sems.at[1])
    qkv_swap = Swap(qkv_blocks, qkv_in, qkv_sems.at[0], qkv_sems.at[1])
    tokens_of_half = [w_gate.at[:, pl.ds(i * width, width)] for i in (0, 1)]
    load_heads = [
        load(source, target)
        for source, target in (
            (att_hbm, att_ref),
            (ql_hbm, ql_ref),
            (ka_hbm, ka_ref),
            (va_hbm, va_ref),
            (q_raw_hbm, q_raw_ref),
            (k_raw_hbm, k_raw_ref),
        )
    ]
    load_hidden = [
        load(hidden_hbm.at[pl.ds(i * width, width), :], tokens_of_half[i]) for i in (0, 1)
    ]
    load_qkv = [
        load(source, w_qkv[i]) for i, source in enumerate((w_query_hbm, w_key_hbm, w_value_hbm))
    ]
    gather_mid.line(3)
    gather_mid.sides(2)
    gather_mlp.line(1)
    gather_mlp.sides(0)

    att_copy.wait()
    branch_copy.wait()
    both_branch = branch_pair[...].reshape(2 * rows, width)

    def out_rows(owner):
        lanes = pl.ds(pl.multiple_of(owner * 2 * quarter + c * quarter, quarter), quarter)
        return dot_tn(att_pair[:, :, lanes].reshape(2 * rows, quarter), both_branch)

    out_send[...] = out_rows(1 - dp).astype(low)
    out_copy = to(twin, x_sems, 0, out_send, out_got)
    out_mine = out_rows(dp)
    for k in (0, 1):
        out_own[k][...] = out_mine[2 * half * k : 2 * half * (k + 1)]
    gather_mid.handed()
    gather_mid.sides(3)
    gather_mlp.line(2)
    gather_mlp.hand_over()
    gather_mlp.sides(1)

    for copy in load_heads:
        copy.wait()
    grad_swap.wait()
    for j in range(GROUP):
        block = g_in[j].astype(f32)
        for start, grads in (
            (j * half, jnp.where(first, block, 0.0)),
            (length - (j + 1) * half, jnp.where(first, pltpu.roll(block, HEAD_DIM, 1), 0.0)),
        ):
            span = pl.ds(start, half)
            delta = jnp.sum(grads * att_ref[span, :].astype(f32), axis=1, keepdims=True)
            ga_ref[span, :] = (grads + split_lanes(delta, grads.shape)).astype(low)
    dq_acc[...] = jnp.zeros_like(dq_acc)
    key_row = lax.broadcasted_iota(jnp.int32, (KEYS, ATT), 0)
    query_lane = lax.broadcasted_iota(jnp.int32, (KEYS, ATT), 1)
    query_row = lax.broadcasted_iota(jnp.int32, (1, ATT), 1)
    gain = gain_ref[...]
    count = float(HEAD_DIM)
    score_scale = 1.0 / math.sqrt(HEAD_DIM)
    wide_first = half_lanes((ATT, 128))

    def norm_pull(raw, grad):
        raw = raw.astype(f32)
        scale = lax.rsqrt(jnp.sum(raw * raw, axis=1, keepdims=True) / count + 1e-06)
        normed = raw * scale
        g_gain = jnp.sum(grad * normed, axis=0, keepdims=True)
        inside = grad * gain
        mean = jnp.sum(inside * normed, axis=1, keepdims=True) / count
        return scale * (inside - normed * mean), g_gain

    key_first = half_lanes((KEYS, 128))

    def pair_grads(keys, values, key_block, query_block):
        base = query_block * ATT
        queries = ql_ref[pl.ds(base, ATT), :]
        grads = ga_ref[pl.ds(base, ATT), :]
        key_pos = key_block * KEYS + key_row
        allowed = key_pos >= doc_start_of(base + query_row, lengths_ref)
        if key_block * KEYS + KEYS > base:
            allowed = allowed & (key_pos <= base + query_lane)
        weights = jnp.where(allowed, jnp.exp(dot_nt(keys, queries)), 0.0)
        slopes = (weights * dot_nt(values, grads)).astype(low)
        dq_acc[pl.ds(base, ATT), :] += dot_tn(slopes, keys)
        return dot_nn(slopes, queries), dot_nn(weights.astype(low), grads)

    g_gain = jnp.zeros((1, 128), f32)
    for key_block in range(length // KEYS):
        span = pl.ds(key_block * KEYS, KEYS)
        keys = ka_ref[span, :]
        values = va_ref[span, :]
        dk, dv = 0.0, 0.0
        for query_block in range(key_block * KEYS // ATT, blocks):
            more_k, more_v = pair_grads(keys, values, key_block, query_block)
            dk, dv = dk + more_k, dv + more_v
        g_key, key_gain = norm_pull(k_raw_ref[span, :], jnp.where(key_first, dk, 0.0))
        g_gain = g_gain + key_gain
        raw_low[span, 128:256] = g_key.astype(low)
        raw_low[span, 256:384] = jnp.where(key_first, dv, 0.0).astype(low)
        if key_block == 0:
            gather_mlp.line(3)
            gather_mlp.sides(2)
        if key_block == 1:
            gather_mlp.handed()
            gather_mlp.sides(3)
    for block in range(blocks):
        span = pl.ds(block * ATT, ATT)
        dq = jnp.where(wide_first, dq_acc[span, :] * score_scale, 0.0)
        g_query, query_gain = norm_pull(q_raw_ref[span, :], dq)
        g_gain = g_gain + query_gain
        raw_low[span, 0:128] = g_query.astype(low)
    for j in range(GROUP):
        for i in range(3):
            lanes = slice(128 * i, 128 * (i + 1))
            lower = raw_low[j * half : (j + 1) * half, lanes].astype(f32)
            upper = raw_low[length - (j + 1) * half : length - j * half, lanes].astype(f32)
            back_send.block(j)[:, lanes] = jnp.where(
                first, lower, pltpu.roll(upper, HEAD_DIM, 1)
            ).astype(low)
    back_swap.start()

    small_own[16:17, :] = g_gain
    small_copy = to(twin, x_sems, 1, small_own, small_got)

    for copy in load_hidden:
        copy.wait()

    def qkv_chunk(chunk):
        lanes = pl.ds(pl.multiple_of(chunk * quarter, quarter), quarter)
        grads = sum(
            dot_tn(tokens_of_half[i][:, lanes], raw_low[pl.ds(i * width, width), :]) for i in (0, 1)
        )
        query_key = jnp.where(
            half_lanes((quarter, 128)), grads[:, :128], pltpu.roll(grads[:, 128:256], HEAD_DIM, 1)
        )
        return query_key, grads[:, 256:]

    for i in (0, 1):
        query_key, value = qkv_chunk(2 * (1 - dp) + i)
        span = slice(quarter * i, quarter * (i + 1))
        qkv_send[span, :128] = query_key.astype(low)
        qkv_send[span, 128:] = value.astype(low)
    qkv_copy = to(twin, x_sems, 2, qkv_send, qkv_got)
    for i in (0, 1):
        query_key, value = qkv_chunk(2 * dp + i)
        span = slice(quarter * i, quarter * (i + 1))
        qkv_part[span, :128] = query_key
        qkv_part[span, 128:] = value

    out_copy.wait()
    side_copies = []
    for k in (0, 1):
        out_own[k][...] += out_got[2 * half * k : 2 * half * (k + 1)].astype(f32)
        other = pl.ds(pl.multiple_of((1 - y) * half, half), half)
        out_side_send[k][...] = out_own[k][other, :].astype(low)
        side_copies.append(to(side, pair_sems, 2 + k, out_side_send[k], out_side_got.at[k]))
    small_copy.wait()
    small_own[...] += small_got[...]
    small_swap.start()
    gather_mid.finish()
    gather_mlp.finish()

    for copy in load_slices:
        copy.wait()
    s_up = jnp.concatenate([s_up_ref[:, window] for window in windows], axis=1)
    s_gate = jnp.concatenate([s_gate_ref[:, window] for window in windows], axis=1)
    slots = PART // half

    def tokens_of(array, step):
        return array[pl.ds(step * slots, slots)].reshape(PART, width)

    def recompute(step, sums):
        span = pl.ds(pl.multiple_of(step * PART, PART), PART)
        some = tokens_of(mid_all, step)
        up = dot_nn(some, up_slice[...])
        gate = dot_nn(some, gate_slice[...])
        g_inner = dot_nt(tokens_of(g_mlp_all, step), down_slice[...])
        scaled = gate * s_gate
        sigmoid = 1.0 / (1.0 + jnp.exp(-scaled))
        silu = scaled / (1.0 + jnp.exp(-scaled))
        up_scaled = up * s_up
        inner_all[span, :] = (up_scaled * silu).astype(low)
        g_up_scaled = g_inner * silu
        g_scaled = g_inner * up_scaled * (sigmoid * (1.0 + scaled * (1.0 - sigmoid)))
        g_cat[span, : 2 * part] = (g_up_scaled * s_up).astype(low)
        g_cat[span, 2 * part :] = (g_scaled * s_gate).astype(low)
        return (
            sums[0] + jnp.sum(g_up_scaled * up, axis=0, keepdims=True),
            sums[1] + jnp.sum(g_scaled * gate, axis=0, keepdims=True),
        )

    zero_row = jnp.zeros((1, 2 * part), f32)
    g_s_up, g_s_gate = lax.fori_loop(0, length // PART, recompute, (zero_row, zero_row))

    line_rows_of = 4 * rows_out
    turns = ((0, 3), (1, 2))

    def wide_chunk(owner, turn):
        tokens = [
            mid_all[
                :,
                :,
                pl.ds(
                    pl.multiple_of(owner * 2 * quarter + line * line_rows_of, line_rows_of),
                    line_rows_of,
                ),
            ].reshape(length, line_rows_of)
            for line in turns[turn]
        ]
        return dot_tn(jnp.concatenate(tokens, axis=1), g_cat[...])

    wide_copies = []
    for i in (0, 1):
        wide_send[i][...] = wide_chunk(1 - dp, i).astype(low)
        wide_copies.append(to(twin, x_sems, 3 + i, wide_send[i], wide_got.at[i]))
    for p in (0, 1):
        s_part[p] = jnp.zeros(s_part.shape[1:], f32)
        s_part[p, 0:1, :] = g_s_up[:, p * part : (p + 1) * part]
        s_part[p, 1:2, :] = g_s_gate[:, p * part : (p + 1) * part]
    s_send[...] = s_part[1 - dp]
    s_copy = to(twin, x_sems, 5, s_send, s_got)
    for chunk in range(4):
        lanes = pl.ds(chunk * quarter, quarter)
        grads = dot_tn(inner_all[...], g_mlp_all[:, :, lanes].reshape(length, quarter))
        for p in (0, 1):
            place = slice(p * width + chunk * quarter, p * width + (chunk + 1) * quarter)
            up_raw[:, place] = grads[p * part : (p + 1) * part]
    down_other = pl.ds(pl.multiple_of((1 - dp) * width, width), width)
    down_mine = pl.ds(pl.multiple_of(dp * width, width), width)
    down_send[...] = up_raw[:, down_other].astype(low)
    down_copy = to(twin, x_sems, 6, down_send, down_got)

    qkv_copy.wait()
    per_chunk = quarter // rows_out
    total = (qkv_part[...] + qkv_got[...].astype(f32)).astype(low)
    for k in range(GROUP):
        qkv_blocks.block(k)[...] = total[k * rows_out : (k + 1) * rows_out]
    qkv_swap.start()
    for copy in side_copies:
        copy.wait()
    out_copies = []
    for k in (0, 1):
        mine = pl.ds(pl.multiple_of(y * half, half), half)
        total = (out_own[k][mine, :] + out_side_got[k].astype(f32)).astype(low)
        out_line[2 * rows_out * k : 2 * rows_out * (k + 1), :] = total
        for core in (0, 1):
            line_rows = pl.ds((2 * k + core) * rows_out, rows_out)
            target = (2 * c + k) * 4 + 2 * y + core
            index = 2 * k + core
            copy = remote(
                out_line.at[line_rows],
                out_in.at[z],
                out_sems.at[0, index],
                out_sems.at[1, z],
                (dp, target),
            )
            out_copies.append((target, copy))

            @pl.when(target != b)
            def _():
                copy.start()

            @pl.when(target == b)
            def _():
                out_in[z] = out_line[line_rows, :]

    def wide_copy(target):
        return remote(
            wide_blocks.block(target),
            wide_in.at[b],
            wide_sems.at[0, target],
            wide_sems.at[1, b],
            (dp, target),
        )

    for i in (0, 1):
        wide_own[...] = wide_chunk(dp, i)
        wide_copies[i].wait()
        total = (wide_own[...] + wide_got[i].astype(f32)).astype(low)
        for k in range(per_chunk):
            target = 4 * turns[i][k // 4] + k % 4
            wide_blocks.block(target)[...] = total[k * rows_out : (k + 1) * rows_out]

            @pl.when(target != b)
            def _():
                wide_copy(target).start()

            @pl.when(target == b)
            def _():
                wide_in[b] = wide_blocks.block(target)[...]

    for copy in load_qkv:
        copy.wait()
    back_swap.wait()
    for pair in range(GROUP // 2):
        for i in range(3):
            lanes = slice(128 * i, 128 * (i + 1))
            even = back_in[2 * pair, :, lanes].astype(f32)
            odd = back_in[2 * pair + 1, :, lanes].astype(f32)
            place = slice(128 * pair, 128 * (pair + 1))
            home[i][:half, place] = jnp.where(first, even, pltpu.roll(odd, HEAD_DIM, 1)).astype(low)
            home[i][half:, place] = jnp.where(first, pltpu.roll(even, HEAD_DIM, 1), odd).astype(low)
    input_grad_ref[...] = (
        g_res[...]
        + dot_nt(home[0][...], w_qkv[0][...])
        + dot_nt(home[1][...], w_qkv[1][...])
        + dot_nt(home[2][...], w_qkv[2][...])
    )
    s_copy.wait()
    g_s_ref[...] = s_part[dp] + s_got[...]
    down_copy.wait()
    g_down_ref[...] = up_raw[:, down_mine] + down_got[...].astype(f32)
    small_swap.wait()
    small_all[b] = small_own[...]
    small_ref[...] = jnp.sum(small_all[...], axis=0)
    small_ref[17:18, :] = small_all[8 * dp + b // 2, 16:17, :]
    qkv_swap.wait()
    for target, copy in out_copies:

        @pl.when(target != b)
        def _():
            copy.wait_send()

    for source_z in range(4):
        source = source_z * 4 + 2 * y + z // 2

        @pl.when(source != b)
        def _():
            remote(
                out_line.at[pl.ds(0, rows_out)],
                out_in.at[source_z],
                out_sems.at[0, 0],
                out_sems.at[1, source_z],
                sib,
            ).wait_recv()

    for other in range(GROUP):

        @pl.when(other != b)
        def _():
            copy = remote(
                wide_blocks.block(other),
                wide_in.at[other],
                wide_sems.at[0, other],
                wide_sems.at[1, other],
                sib,
            )
            copy.wait_send()
            copy.wait_recv()


def tail_block(vmem_inputs, hbm_inputs):
    low, f32 = jnp.bfloat16, jnp.float32
    shape, vmem, sems = jax.ShapeDtypeStruct, pltpu.VMEM, pltpu.SemaphoreType.DMA
    packed, hidden = vmem_inputs[1], vmem_inputs[2]
    w_out, w_up, w_gate, w_down = hbm_inputs[:4]
    rows, width = hidden.shape
    half = rows // 2
    ff = w_up.shape[1]
    length = GROUP * rows
    rows_out = width // (2 * GROUP)
    part = ff // (2 * GROUP)
    quarter = width // 4
    return pl.pallas_call(
        tail_kernel,
        out_shape=[
            shape((rows, width), low),
            shape((rows, width), f32),
            shape((GROUP, rows_out, 4 * part), low),
            shape((GROUP, rows_out, 256), low),
            shape((part, width), f32),
            shape((4, rows_out, width), low),
            shape((8, 128), f32),
            shape((24, 128), f32),
        ],
        in_specs=[SMEM_SPEC]
        + [VMEM_SPEC] * (len(vmem_inputs) - 1)
        + [ANY_SPEC] * len(hbm_inputs),
        out_specs=[VMEM_SPEC] * 8,
        scratch_shapes=[
            vmem((2 * GROUP, half, width), low),
            vmem((2 * GROUP, half, width), low),
            vmem(w_out.shape, low),
            vmem(w_up.shape, low),
            vmem(w_gate.shape, low),
            vmem(w_down.shape, low),
            vmem((width, 2 * part), low),
            vmem((width, 2 * part), low),
            vmem((2 * part, width), low),
            vmem((rows, ff), f32),
            vmem((rows, ff), f32),
            vmem((2, half, width), low),
            vmem((2, half, width), low),
            vmem(packed.shape, low),
            vmem(packed.shape, low),
            vmem(packed.shape, low),
            vmem((rows, width), f32),
            vmem((rows, width), f32),
            vmem((2, rows, width), low),
            vmem((2, rows, width), low),
            vmem((quarter, width), low),
            vmem((2, half, width), low),
            vmem((length, 128), low),
            vmem((length, 128), low),
            vmem((length, 128), low),
            vmem((length, 128), low),
            vmem((length, 128), f32),
            vmem((GROUP, half, 384), low),
            vmem((2 * quarter, 256), f32),
            vmem((2 * quarter, 256), low),
            vmem((quarter, 4 * part), f32),
            vmem((2, quarter, 4 * part), low),
            vmem((part, width), low),
            vmem((24, 128), f32),
            vmem((24, 128), f32),
            vmem((GROUP, 24, 128), f32),
            vmem((2, 8, 128), f32),
            vmem((8, 128), f32),
            vmem((8, 128), f32),
            sems((24,)),
            sems((2, 8)),
            sems((2, 4)),
            sems((2, 4)),
            sems((2, GROUP)),
            sems((2, GROUP)),
            sems((2, GROUP)),
            sems((2, GROUP)),
            sems((2, GROUP)),
            sems((2, GROUP)),
        ]
        + gather_scratch(TAIL_PIECES)
        + gather_scratch(TAIL_PIECES),
        compiler_params=comm_params(1),
        name="tail_block",
    )(*vmem_inputs, *hbm_inputs)


def assemble_kernel(
    result,
    input_grad,
    wide_in,
    qkv_in,
    down,
    out_in,
    scales,
    small,
    alpha_attn,
    alpha_mlp,
    output_ref,
    input_grad_ref,
    g_query_ref,
    g_key_ref,
    g_value_ref,
    g_out_ref,
    g_up_ref,
    g_gate_ref,
    g_down_ref,
    gain_ref,
    s_up_ref,
    s_gate_ref,
    g_alpha_attn_ref,
    g_alpha_mlp_ref,
    mean_ref,
):
    f32 = jnp.float32
    dp, b = here()
    output_ref[...] = result[...]
    input_grad_ref[...] = input_grad[...]
    g_down_ref[...] = down[...]
    s_up_ref[...] = scales[0:1, :]
    s_gate_ref[...] = scales[1:2, :]
    rows_out = g_out_ref.shape[0]
    per_row = 128 // rows_out
    device = dp * GROUP + b

    def own_lanes(row, place):
        start = (128 - rows_out * place) % 128
        return pltpu.roll(jnp.broadcast_to(row, (8, 128)), start, 1)[:1, :rows_out]

    place = device % per_row
    g_alpha_attn_ref[...] = own_lanes(small[pl.ds(device // per_row, 1), :], place)
    g_alpha_mlp_ref[...] = own_lanes(small[pl.ds(8 + device // per_row, 1), :], place)
    gain_ref[...] = own_lanes(small[17:18, :], b % 2)
    mean_ref[...] = 0.5 * (mean_last(alpha_attn[...]) + mean_last(alpha_mlp[...]))
    g_out_ref[...] = sum(out_in[i].astype(f32) for i in range(4))
    part = wide_in.shape[2] // 4
    ff_half = g_up_ref.shape[1] // 2
    for j in range(GROUP):
        for p in (0, 1):
            place = slice(p * ff_half + j * part, p * ff_half + (j + 1) * part)
            g_up_ref[:, place] = wide_in[j, :, p * part : (p + 1) * part].astype(f32)
            g_gate_ref[:, place] = wide_in[j, :, (2 + p) * part : (3 + p) * part].astype(f32)
    first = half_lanes((g_query_ref.shape[0], 128))
    for pair in range(GROUP // 2):
        place = slice(128 * pair, 128 * (pair + 1))
        even, odd = qkv_in[2 * pair].astype(f32), qkv_in[2 * pair + 1].astype(f32)
        even_qk, odd_qk = even[:, :128], odd[:, :128]
        g_query_ref[:, place] = jnp.where(first, even_qk, pltpu.roll(odd_qk, HEAD_DIM, 1))
        g_key_ref[:, place] = jnp.where(first, pltpu.roll(even_qk, HEAD_DIM, 1), odd_qk)
        g_value_ref[:, place] = jnp.where(
            first, even[:, 128:], pltpu.roll(odd[:, 128:], HEAD_DIM, 1)
        )


def assemble_block(inputs, ff):
    result, input_grad, wide_in, qkv_in, down, out_in = inputs[:6]
    f32 = jnp.float32
    shape = jax.ShapeDtypeStruct
    width = result.shape[1]
    rows_out = wide_in.shape[1]
    return pl.pallas_call(
        assemble_kernel,
        out_shape=[
            shape(result.shape, result.dtype),
            shape(input_grad.shape, f32),
            shape((rows_out, width), f32),
            shape((rows_out, width), f32),
            shape((rows_out, width), f32),
            shape((rows_out, width), f32),
            shape((rows_out, ff), f32),
            shape((rows_out, ff), f32),
            shape(down.shape, f32),
            shape((1, rows_out), f32),
            shape((1, 128), f32),
            shape((1, 128), f32),
            shape((1, rows_out), f32),
            shape((1, rows_out), f32),
            shape((1, 1), f32),
        ],
        in_specs=[VMEM_SPEC] * len(inputs),
        out_specs=[VMEM_SPEC] * 15,
        compiler_params=pltpu.CompilerParams(vmem_limit_bytes=VMEM_LIMIT),
        name="assemble_block",
    )(*inputs)


def on_device_heads(
    tokens,
    cotangent,
    lengths,
    w_query,
    w_key,
    w_value,
    w_out,
    w_up,
    w_gate,
    w_down,
    s_qk,
    s_up,
    s_gate,
    alpha_attn,
    alpha_mlp,
):
    model_width = w_query.shape[0]
    tok_rows = tokens.shape[2]
    half_rows = tok_rows // 2
    hidden = tokens[0, 0]
    hidden_all, qa, ka, va, query_raw, key_raw, gain = project_block(
        hidden, w_query, w_key, w_value, s_qk
    )
    attended, ql, packed = attend(lengths, qa, ka, va, half_rows)
    (result, input_grad, wide_in, qkv_in, grad_down, out_in, grad_scales, small) = tail_block(
        (
            lengths,
            packed,
            hidden,
            cotangent[0, 0],
            gain,
            s_up[None],
            s_gate[None],
            alpha_attn[None],
            alpha_mlp[None],
        ),
        (
            w_out,
            w_up,
            w_gate,
            w_down,
            w_query,
            w_key,
            w_value,
            ql,
            ka,
            va,
            attended,
            query_raw,
            key_raw,
            hidden_all.reshape(GROUP * tok_rows, model_width),
        ),
    )
    (
        output,
        input_grad,
        grad_query,
        grad_key,
        grad_value,
        grad_out,
        grad_up,
        grad_gate,
        grad_down,
        grad_gain,
        grad_up_scale,
        grad_gate_scale,
        grad_attn,
        grad_mlp_alpha,
        mean_alpha,
    ) = assemble_block(
        (
            result,
            input_grad,
            wide_in,
            qkv_in,
            grad_down,
            out_in,
            grad_scales,
            small,
            alpha_attn[None],
            alpha_mlp[None],
        ),
        w_up.shape[1],
    )
    return (
        output[None, None],
        input_grad[None, None],
        grad_query,
        grad_key,
        grad_value,
        grad_out,
        grad_up,
        grad_gate,
        grad_down,
        grad_gain[0],
        grad_up_scale[0],
        grad_gate_scale[0],
        grad_attn[0],
        grad_mlp_alpha[0],
        mean_alpha[0, 0],
    )


def on_device(*arrays):
    head_count = arrays[3].shape[0] // HEAD_DIM
    tok_rows = arrays[0].shape[2]
    fits = lax.axis_size("blk") == head_count == 16 and lax.axis_size("dp") == 2
    if fits and tok_rows == 128:
        return on_device_heads(*arrays)
    return on_device_general(*arrays)


def solution(mesh):
    in_specs = (
        P("dp", "blk", None, None),
        P("dp", "blk", None, None),
        P("dp", None),
        P(),
        P(),
        P(),
        P(),
        P(),
        P(),
        P(),
        P(),
        P(),
        P(),
        P(),
        P(),
    )
    out_specs = (
        P("dp", "blk", None, None),
        P("dp", "blk", None, None),
        P(("dp", "blk"), None),
        P(("dp", "blk"), None),
        P(("dp", "blk"), None),
        P(("dp", "blk"), None),
        P(("dp", "blk"), None),
        P(("dp", "blk"), None),
        P(("dp", "blk"), None),
        P(("dp", "blk")),
        P(("dp", "blk")),
        P(("dp", "blk")),
        P(("dp", "blk")),
        P(("dp", "blk")),
        P(),
    )
    return jax.shard_map(
        on_device, mesh=mesh, in_specs=in_specs, out_specs=out_specs, check_vma=False
    )
```

```python
import functools
import math

import jax
import jax.numpy as jnp
from jax import lax
from jax.experimental import pallas as pl
from jax.experimental.pallas import tpu as pltpu
from jax.sharding import PartitionSpec as P

HEAD_DIM = 64


def rms_norm(vector):
    return vector * lax.rsqrt(jnp.mean(vector * vector, axis=-1, keepdims=True) + 1e-06)


def head_norm(vector, head_count):
    shaped = vector.reshape(vector.shape[0], head_count, -1)
    return rms_norm(shaped).reshape(vector.shape)


def silu_smooth(vector):
    return vector / (1.0 + jnp.exp(-vector))


def residual_mix(inputs, branch, alphas):
    return rms_norm(inputs + alphas * (rms_norm(branch) - inputs))


def gated_inner(up_raw, gate_raw, s_up, s_gate):
    return up_raw * s_up * silu_smooth(gate_raw * s_gate)


def stream_positions(row_index, tok_rows, members):
    half_rows = tok_rows // 2
    device = row_index // tok_rows
    within = row_index % tok_rows
    block_id = jnp.where(within < half_rows, device, 2 * members - 1 - device)
    return block_id * half_rows + within % half_rows


def doc_index(positions, doc_ends):
    return jnp.sum(
        (positions[:, None] >= doc_ends[None, :]).astype(jnp.int32), axis=1, dtype=jnp.int32
    )


def allowed_pairs(query_pos, query_doc, key_pos, key_doc):
    return (key_pos[None, :] <= query_pos[:, None]) & (key_doc[None, :] == query_doc[:, None])


def take_rows(matrix, first_row, row_count):
    return lax.dynamic_slice_in_dim(matrix, first_row, row_count, 0)


def fold_half(running, query_heads, key_heads, value_heads, allowed, score_scale):

    def absorb(carried):
        best_score, total_sum, accumulated = carried
        scores = (
            jnp.einsum("qhd,khd->hqk", query_heads, key_heads, preferred_element_type=jnp.float32)
            * score_scale
        )
        scores = jnp.where(allowed[None], scores, -1e30)
        new_best = jnp.maximum(best_score, jnp.max(scores, axis=2))
        weights = jnp.where(allowed[None], jnp.exp(scores - new_best[:, :, None]), 0.0)
        fade_factor = jnp.exp(best_score - new_best)
        total_sum = jnp.sum(weights, axis=2)
        accumulated = accumulated * fade_factor.T[:, :, None] + jnp.einsum(
            "hqk,khd->qhd",
            weights.astype(jnp.bfloat16),
            value_heads,
            preferred_element_type=jnp.float32,
        )
        return (new_best, total_sum, accumulated)

    return lax.cond(jnp.any(allowed), absorb, lambda carried: carried, running)


def pair_terms(query_side, key_heads, value_heads, allowed, score_scale):
    query_heads, grad_heads, log_total, delta_rows = (
        query_side[0],
        query_side[1],
        query_side[2],
        query_side[3],
    )
    scores = (
        jnp.einsum("qhd,khd->hqk", query_heads, key_heads, preferred_element_type=jnp.float32)
        * score_scale
    )
    scores = jnp.where(allowed[None], scores, -1e30)
    weights = jnp.exp(scores - log_total[:, :, None])
    grad_weights = jnp.einsum(
        "qhd,khd->hqk", grad_heads, value_heads, preferred_element_type=jnp.float32
    )
    grad_scores = (weights * (grad_weights - delta_rows[:, :, None])).astype(jnp.bfloat16)
    return (weights.astype(jnp.bfloat16), grad_scores)


def query_term(query_side, key_heads, value_heads, allowed, score_scale):
    weights, grad_scores = pair_terms(query_side, key_heads, value_heads, allowed, score_scale)
    return score_scale * jnp.einsum(
        "hqk,khd->qhd", grad_scores, key_heads, preferred_element_type=jnp.float32
    )


def key_term(query_side, key_heads, value_heads, allowed, score_scale):
    weights, grad_scores = pair_terms(query_side, key_heads, value_heads, allowed, score_scale)
    grad_keys = score_scale * jnp.einsum(
        "hqk,qhd->khd", grad_scores, query_side[0], preferred_element_type=jnp.float32
    )
    grad_values = jnp.einsum(
        "hqk,qhd->khd", weights, query_side[1], preferred_element_type=jnp.float32
    )
    return (grad_keys, grad_values)


def on_device_general(
    tokens,
    cotangent,
    lengths,
    w_query,
    w_key,
    w_value,
    w_out,
    w_up,
    w_gate,
    w_down,
    s_qk,
    s_up,
    s_gate,
    alpha_attn,
    alpha_mlp,
):
    model_width = w_query.shape[0]
    head_count = model_width // HEAD_DIM
    score_scale = 1.0 / math.sqrt(HEAD_DIM)
    tok_rows = tokens.shape[2]
    half_rows = tok_rows // 2
    members = lax.axis_size("blk")
    position = lax.axis_index("blk")
    doc_ends = jnp.cumsum(lengths[0], dtype=jnp.int32)
    hidden = tokens[0, 0]
    hidden_f = hidden.astype(jnp.float32)

    def key_info(first_row, row_count):
        key_pos = stream_positions(
            first_row + jnp.arange(row_count, dtype=jnp.int32), tok_rows, members
        )
        return (key_pos, doc_index(key_pos, doc_ends))

    def heads_of(matrix):
        return matrix.reshape(matrix.shape[0], head_count, HEAD_DIM)

    def scaled_norm(raw_rows, gain_vector):
        return head_norm(raw_rows, head_count) * gain_vector

    own_pos, own_doc = key_info(position * tok_rows, tok_rows)
    query_raw = jnp.dot(hidden, w_query, preferred_element_type=jnp.float32)
    key_raw = jnp.dot(hidden, w_key, preferred_element_type=jnp.float32)
    value_raw = jnp.dot(hidden, w_value, preferred_element_type=jnp.float32)
    queries = scaled_norm(query_raw, s_qk).astype(jnp.bfloat16)
    key_rows = scaled_norm(key_raw, s_qk).astype(jnp.bfloat16)
    value_rows = value_raw.astype(jnp.bfloat16)
    query_heads = heads_of(queries)

    def empty_state():
        return (
            jnp.full((head_count, half_rows), -1e30, jnp.float32),
            jnp.zeros((head_count, half_rows), jnp.float32),
            jnp.zeros((half_rows, head_count, HEAD_DIM), jnp.float32),
        )

    running = (empty_state(), empty_state())
    key_part = lax.all_gather(key_rows, "blk", axis=0, tiled=True)
    value_part = lax.all_gather(value_rows, "blk", axis=0, tiled=True)
    key_pos, key_doc = key_info(jnp.int32(0), key_part.shape[0])
    updated = []
    for part_index in range(2):
        rows_here = slice(part_index * half_rows, (part_index + 1) * half_rows)
        allowed = allowed_pairs(own_pos[rows_here], own_doc[rows_here], key_pos, key_doc)
        updated.append(
            fold_half(
                running[part_index],
                query_heads[rows_here],
                heads_of(key_part),
                heads_of(value_part),
                allowed,
                score_scale,
            )
        )
    folded = (updated[0], updated[1])
    best_score = jnp.concatenate([folded[0][0], folded[1][0]], axis=1)
    total_sum = jnp.concatenate([folded[0][1], folded[1][1]], axis=1)
    accumulated = jnp.concatenate([folded[0][2], folded[1][2]], axis=0)
    attended = accumulated / total_sum.T[:, :, None]
    log_total = best_score + jnp.log(total_sum)
    attended_low = attended.reshape(tok_rows, model_width).astype(jnp.bfloat16)
    branch = jnp.dot(attended_low, w_out, preferred_element_type=jnp.float32)
    middle = residual_mix(hidden_f, branch, alpha_attn)
    middle_low = middle.astype(jnp.bfloat16)
    up_raw = jnp.dot(middle_low, w_up, preferred_element_type=jnp.float32)
    gate_raw = jnp.dot(middle_low, w_gate, preferred_element_type=jnp.float32)
    inner_low = gated_inner(up_raw, gate_raw, s_up, s_gate).astype(jnp.bfloat16)
    mlp_raw = jnp.dot(inner_low, w_down, preferred_element_type=jnp.float32)
    result = residual_mix(middle, mlp_raw, alpha_mlp)
    mixed_out, pull_out = jax.vjp(residual_mix, middle, mlp_raw, alpha_mlp)
    grad_middle, grad_mlp, grad_alpha_mlp = pull_out(cotangent[0, 0].astype(jnp.float32))
    grad_mlp_low = grad_mlp.astype(jnp.bfloat16)
    grad_w_down = jnp.dot(inner_low.T, grad_mlp_low, preferred_element_type=jnp.float32)
    grad_inner = jnp.dot(grad_mlp_low, w_down.T, preferred_element_type=jnp.float32)
    inner_out, pull_inner = jax.vjp(gated_inner, up_raw, gate_raw, s_up, s_gate)
    grad_up_raw, grad_gate_raw, grad_s_up, grad_s_gate = pull_inner(grad_inner)
    up_low = grad_up_raw.astype(jnp.bfloat16)
    gate_low = grad_gate_raw.astype(jnp.bfloat16)
    grad_w_up = jnp.dot(middle_low.T, up_low, preferred_element_type=jnp.float32)
    grad_w_gate = jnp.dot(middle_low.T, gate_low, preferred_element_type=jnp.float32)
    grad_middle = (
        grad_middle
        + jnp.dot(up_low, w_up.T, preferred_element_type=jnp.float32)
        + jnp.dot(gate_low, w_gate.T, preferred_element_type=jnp.float32)
    )
    attn_out, pull_attn = jax.vjp(residual_mix, hidden_f, branch, alpha_attn)
    grad_hidden, grad_branch, grad_alpha_attn = pull_attn(grad_middle)
    branch_low = grad_branch.astype(jnp.bfloat16)
    grad_w_out = jnp.dot(attended_low.T, branch_low, preferred_element_type=jnp.float32)
    grad_att_low = jnp.dot(branch_low, w_out.T, preferred_element_type=jnp.float32).astype(
        jnp.bfloat16
    )
    grad_heads = heads_of(grad_att_low)
    delta_rows = jnp.sum(grad_heads.astype(jnp.float32) * attended, axis=2).T

    def local_side(part_index):
        rows_here = slice(part_index * half_rows, (part_index + 1) * half_rows)
        return (
            query_heads[rows_here],
            grad_heads[rows_here],
            log_total[:, rows_here],
            delta_rows[:, rows_here],
            own_pos[rows_here],
            own_doc[rows_here],
        )

    local_parts = (local_side(0), local_side(1))
    whole_keys, whole_values = (
        lax.all_gather(key_rows, "blk", axis=0, tiled=True),
        lax.all_gather(value_rows, "blk", axis=0, tiled=True),
    )

    def query_step(grad_parts, shard_index):
        first_row = shard_index * tok_rows
        key_part = heads_of(take_rows(whole_keys, first_row, tok_rows))
        value_part = heads_of(take_rows(whole_values, first_row, tok_rows))
        key_pos, key_doc = key_info(first_row, tok_rows)
        updated = []
        for part_index in range(2):
            query_side = local_parts[part_index]
            allowed = allowed_pairs(query_side[4], query_side[5], key_pos, key_doc)

            def add_term(grad_now):
                return grad_now + query_term(query_side, key_part, value_part, allowed, score_scale)

            updated.append(
                lax.cond(
                    jnp.any(allowed), add_term, lambda grad_now: grad_now, grad_parts[part_index]
                )
            )
        return ((updated[0], updated[1]), None)

    zero_part = jnp.zeros((half_rows, head_count, HEAD_DIM), jnp.float32)
    grad_parts, unused_out = lax.scan(
        query_step, (zero_part, zero_part), jnp.arange(members, dtype=jnp.int32)
    )
    grad_queries = jnp.concatenate(grad_parts, axis=0).reshape(tok_rows, model_width)
    first_row = jnp.int32(0)
    row_count = lax.axis_size("blk") * tok_rows
    key_part = heads_of(take_rows(whole_keys, first_row, row_count))
    value_part = heads_of(take_rows(whole_values, first_row, row_count))
    key_pos, key_doc = key_info(first_row, row_count)
    zero_keys = jnp.zeros((row_count, head_count, HEAD_DIM), jnp.float32)
    totals = (zero_keys, zero_keys)
    for part_index in range(2):
        query_side = local_parts[part_index]
        allowed = allowed_pairs(query_side[4], query_side[5], key_pos, key_doc)

        def add_terms(grad_now):
            grad_keys, grad_values = key_term(
                query_side, key_part, value_part, allowed, score_scale
            )
            return (grad_now[0] + grad_keys, grad_now[1] + grad_values)

        totals = lax.cond(jnp.any(allowed), add_terms, lambda grad_now: grad_now, totals)
    key_value_grads = lax.psum_scatter(
        jnp.concatenate(
            [totals[0].reshape(row_count, model_width), totals[1].reshape(row_count, model_width)],
            axis=1,
        ),
        "blk",
        scatter_dimension=0,
        tiled=True,
    )
    grad_keys = key_value_grads[:, :model_width]
    grad_values = key_value_grads[:, model_width:]
    query_out, pull_query = jax.vjp(scaled_norm, query_raw, s_qk)
    grad_query_raw, grad_qk_first = pull_query(grad_queries)
    key_out, pull_key = jax.vjp(scaled_norm, key_raw, s_qk)
    grad_key_raw, grad_qk_second = pull_key(grad_keys)
    grad_s_qk = grad_qk_first + grad_qk_second
    query_low = grad_query_raw.astype(jnp.bfloat16)
    key_low = grad_key_raw.astype(jnp.bfloat16)
    value_low = grad_values.astype(jnp.bfloat16)
    grad_w_query = jnp.dot(hidden.T, query_low, preferred_element_type=jnp.float32)
    grad_w_key = jnp.dot(hidden.T, key_low, preferred_element_type=jnp.float32)
    grad_w_value = jnp.dot(hidden.T, value_low, preferred_element_type=jnp.float32)
    input_grad = (
        grad_hidden
        + jnp.dot(query_low, w_query.T, preferred_element_type=jnp.float32)
        + jnp.dot(key_low, w_key.T, preferred_element_type=jnp.float32)
        + jnp.dot(value_low, w_value.T, preferred_element_type=jnp.float32)
    )
    summed = (
        lax.psum_scatter(grad_w_query, ("dp", "blk"), scatter_dimension=0, tiled=True),
        lax.psum_scatter(grad_w_key, ("dp", "blk"), scatter_dimension=0, tiled=True),
        lax.psum_scatter(grad_w_value, ("dp", "blk"), scatter_dimension=0, tiled=True),
        lax.psum_scatter(grad_w_out, ("dp", "blk"), scatter_dimension=0, tiled=True),
        lax.psum_scatter(grad_w_up, ("dp", "blk"), scatter_dimension=0, tiled=True),
        lax.psum_scatter(grad_w_gate, ("dp", "blk"), scatter_dimension=0, tiled=True),
        lax.psum_scatter(grad_w_down, ("dp", "blk"), scatter_dimension=0, tiled=True),
        lax.psum_scatter(grad_s_qk, ("dp", "blk"), scatter_dimension=0, tiled=True),
        lax.psum_scatter(grad_s_up, ("dp", "blk"), scatter_dimension=0, tiled=True),
        lax.psum_scatter(grad_s_gate, ("dp", "blk"), scatter_dimension=0, tiled=True),
        lax.psum_scatter(grad_alpha_attn, ("dp", "blk"), scatter_dimension=0, tiled=True),
        lax.psum_scatter(grad_alpha_mlp, ("dp", "blk"), scatter_dimension=0, tiled=True),
    )
    mean_alpha = 0.5 * (jnp.mean(alpha_attn) + jnp.mean(alpha_mlp))
    output = result.astype(jnp.bfloat16)[None, None]
    return (
        output,
        input_grad[None, None],
        summed[0],
        summed[1],
        summed[2],
        summed[3],
        summed[4],
        summed[5],
        summed[6],
        summed[7],
        summed[8],
        summed[9],
        summed[10],
        summed[11],
        mean_alpha,
    )


MESH = pl.DeviceIdType.MESH
VMEM_SPEC = pl.BlockSpec(memory_space=pltpu.VMEM)
VMEM_LIMIT = 62 << 20
GROUP = 16


def here():
    return lax.axis_index("dp"), lax.axis_index("blk")


def greet(partners):
    barrier = pltpu.get_barrier_semaphore()
    for partner in partners:
        pl.semaphore_signal(barrier, inc=1, device_id=partner, device_id_type=MESH)
    pl.semaphore_wait(barrier, len(partners))


def remote(src, dst, send_sem, recv_sem, device):
    return pltpu.make_async_remote_copy(
        src_ref=src,
        dst_ref=dst,
        send_sem=send_sem,
        recv_sem=recv_sem,
        device_id=device,
        device_id_type=MESH,
    )


class Gather:
    KINDS = 22

    def __init__(self, own, out, send, recv, pieces):
        self.own, self.out, self.send, self.recv = own, out, send, recv
        self.pieces = pieces
        dp, b = here()
        self.dp, self.b = dp, b
        self.z, self.y, self.c = b // 4, (b // 2) % 2, b % 2
        self.up = (dp, (b + 4) % GROUP)
        self.down = (dp, (b + 12) % GROUP)
        self.side = (dp, b + 2 - 4 * self.y)
        self.sib = (dp, b + 1 - 2 * self.c)
        self.half = self.pieces // 2

    def partners(self):
        return [self.up, self.down, self.side, self.sib]

    def copy(self, z, y, c, kind, piece, device, own=False):
        block = z * 4 + y * 2 + c
        upper = piece // self.half
        place = 2 * GROUP - 1 - block if upper else block
        rows = self.out.shape[1] // self.half
        span = pl.ds(piece % self.half * rows, rows)
        target = self.out.at[place, span]
        source = self.own.at[upper, span] if own else target
        index = self.pieces * kind + piece
        return remote(source, target, self.send.at[index], self.recv.at[index], device)

    def along(self, z, piece, device, own=False, back=False):
        return self.copy(z, self.y, self.c, z + (4 if back else 0), piece, device, own)

    def across(self, z, y, piece, own=False):
        return self.copy(z, y, self.c, 8 + z, piece, self.side, own)

    def over(self, z, piece, device, back=False):
        return self.copy(z, 1 - self.y, self.c, 21 if back else 20, piece, device)

    def to_sib(self, z, y, c, piece, own=False):
        return self.copy(z, y, c, 12 + 2 * z + y, piece, self.sib, own)

    def each_side(self, distance, action):
        if distance == 0:
            action(self.z, None)
            return
        low, high = self.z - distance, self.z + distance

        @pl.when(low >= 0)
        def _():
            action(low, False)

        @pl.when(high <= 3)
        def _():
            action(high, True)

    def start(self):
        for piece in range(self.pieces):

            @pl.when(self.z < 3)
            def _():
                self.along(self.z, piece, self.up, True).start()

            @pl.when(self.z > 0)
            def _():
                self.along(self.z, piece, self.down, True, True).start()

            self.across(self.z, self.y, piece, True).start()
        for piece in range(self.pieces):
            self.to_sib(self.z, self.y, self.c, piece, True).start()
        for upper in (0, 1):
            place = 2 * GROUP - 1 - self.b if upper else self.b
            self.out[place] = self.own[upper]

    def line(self, distance):
        def action(z, above):
            for piece in range(self.pieces):
                self.along(z, piece, self.sib, False, above).wait_recv()
                if above:

                    @pl.when(self.z > 0)
                    def _():
                        self.along(z, piece, self.down, False, True).start()
                else:

                    @pl.when(self.z < 3)
                    def _():
                        self.along(z, piece, self.up).start()

                if distance > 1 or piece < self.half:
                    self.across(z, self.y, piece).start()
                self.to_sib(z, self.y, self.c, piece).start()

        self.each_side(distance, action)

    def sides(self, distance):
        def action(z, above):
            for piece in range(self.pieces):
                if distance == 1 and piece >= self.half:
                    continue
                self.across(z, 1 - self.y, piece).wait_recv()
                self.to_sib(z, 1 - self.y, self.c, piece).start()

        self.each_side(distance, action)

    def hand_over(self):
        for piece in range(self.half, self.pieces):

            @pl.when(self.z < 3)
            def _():
                self.over(self.z, piece, self.up).start()

            @pl.when(self.z > 0)
            def _():
                self.over(self.z, piece, self.down, True).start()

    def handed(self):
        def action(z, above):
            for piece in range(self.half, self.pieces):
                self.over(z, piece, self.sib, above).wait_recv()
                self.to_sib(z, 1 - self.y, self.c, piece).start()

        self.each_side(1, action)

    def from_sib(self, distance):
        def action(z, above):
            for piece in range(self.pieces):
                for y in (0, 1):
                    self.to_sib(z, y, 1 - self.c, piece).wait_recv()

        self.each_side(distance, action)

    def drain(self):
        for piece in range(self.pieces):
            for z in range(4):
                for y in (0, 1):
                    self.to_sib(z, y, self.c, piece).wait_send()
                if piece < self.half:
                    self.across(z, self.y, piece).wait_send()
                else:

                    @pl.when((z > self.z + 1) | (z < self.z - 1) | (z == self.z))
                    def _():
                        self.across(z, self.y, piece).wait_send()

                @pl.when((self.z >= z) & (self.z < 3))
                def _():
                    self.along(z, piece, self.up).wait_send()

                @pl.when((self.z <= z) & (self.z > 0))
                def _():
                    self.along(z, piece, self.down, False, True).wait_send()

            if piece >= self.half:

                @pl.when(self.z < 3)
                def _():
                    self.over(self.z, piece, self.up).wait_send()

                @pl.when(self.z > 0)
                def _():
                    self.over(self.z, piece, self.down, True).wait_send()

    def finish(self):
        for distance in range(4):
            self.from_sib(distance)
        self.drain()


def gather_scratch(pieces):
    return [pltpu.SemaphoreType.DMA((pieces * Gather.KINDS,)) for _ in range(2)]


def comm_params(collective_id):
    return pltpu.CompilerParams(
        collective_id=collective_id, has_side_effects=True, vmem_limit_bytes=VMEM_LIMIT
    )


def dot_nt(left, right):
    return lax.dot_general(left, right, (((1,), (1,)), ((), ())), preferred_element_type=jnp.float32)


def dot_tn(left, right):
    return lax.dot_general(left, right, (((0,), (0,)), ((), ())), preferred_element_type=jnp.float32)


def dot_nn(left, right):
    return jnp.dot(left, right, preferred_element_type=jnp.float32)


FF_STEP = 1024


def mean_last(array):
    return jnp.mean(array, axis=-1, keepdims=True)


def rms_scale(array):
    return lax.rsqrt(mean_last(array * array) + 1e-06)


def rms_pull(grad, normed, scale):
    return scale * (grad - normed * mean_last(grad * normed))


def half_lanes(shape):
    return lax.broadcasted_iota(jnp.int32, shape, 1) < HEAD_DIM


class Swap:
    def __init__(self, blocks, out, send, recv, own=True):
        self.blocks, self.out, self.own = blocks, out, own
        dp, self.b = here()
        self.copies = []
        for step in range(1, GROUP):
            target = (self.b + step) % GROUP
            self.copies.append(
                remote(
                    (blocks.block(target) if isinstance(blocks, SendBlocks) else blocks.at[target])
                    if own
                    else blocks,
                    out.at[self.b],
                    send.at[step],
                    recv.at[step],
                    (dp, target),
                )
            )
        self.partners = [(dp, (self.b + step) % GROUP) for step in range(1, GROUP)]

    def start(self):
        for copy in self.copies:
            copy.start()
        if self.own:
            mine = self.blocks
            mine = mine.block(self.b) if isinstance(mine, SendBlocks) else mine.at[self.b]
            self.out[self.b] = mine[...]

    def wait(self):
        for copy in self.copies:
            copy.wait()


ANY_SPEC = pl.BlockSpec(memory_space=pl.ANY)


SMEM_SPEC = pl.BlockSpec(memory_space=pltpu.SMEM)


def own_head(pair, core):
    shifted = jnp.where(core == 1, pltpu.roll(pair, HEAD_DIM, 1), pair)
    return jnp.where(half_lanes(pair.shape), shifted, 0.0)


def minus_ones(matrix):
    lane = lax.broadcasted_iota(jnp.int32, matrix.shape, 1)
    extra = jnp.where(lane < HEAD_DIM + 3, -1.0, 0.0)
    return jnp.where(lane < HEAD_DIM, matrix, extra).astype(jnp.bfloat16)


PROJECT_PIECES = 4


def doc_start_of(positions, lengths_ref):
    start = jnp.zeros_like(positions)
    end = jnp.int32(0)
    for doc in range(lengths_ref.shape[1]):
        end = end + lengths_ref[0, doc]
        start = start + jnp.where(positions >= end, lengths_ref[0, doc], 0)
    return start


def split_lanes(column, shape):
    lane = lax.broadcasted_iota(jnp.int32, shape, 1)
    high = column.astype(jnp.bfloat16).astype(jnp.float32)
    rest = column - high
    mid = rest.astype(jnp.bfloat16).astype(jnp.float32)
    last = rest - mid
    return jnp.where(
        lane == HEAD_DIM,
        high,
        jnp.where(lane == HEAD_DIM + 1, mid, jnp.where(lane == HEAD_DIM + 2, last, 0.0)),
    )


ATT = 512


TAIL_PIECES = 2
KEYS = 512
PART = 512


class SendBlocks:
    def __init__(self, ref, first_row, rows, first_lane, lanes):
        self.ref, self.first_row, self.rows = ref, first_row, rows
        self.lanes = pl.ds(first_lane, lanes)

    def block(self, index):
        start = pl.multiple_of(self.first_row + index * self.rows, self.rows)
        return self.ref.at[pl.ds(start, self.rows), self.lanes]


def layer_kernel(
    lengths_ref,
    hidden_own,
    cot_ref,
    s_qk_ref,
    s_up_ref,
    s_gate_ref,
    alpha_attn_ref,
    alpha_mlp_ref,
    w_out_hbm,
    w_up_hbm,
    w_gate_hbm,
    w_down_hbm,
    w_query_hbm,
    w_key_hbm,
    w_value_hbm,
    result_ref,
    input_grad_ref,
    wide_in,
    qkv_in,
    g_down_ref,
    out_in,
    g_s_ref,
    small_ref,
    hidden_hbm,
    mid_all,
    g_mlp_all,
    w_out,
    w_up,
    w_gate,
    w_down,
    up_slice,
    gate_slice,
    down_slice,
    up_raw,
    gate_raw,
    mid_own,
    g_mlp_own,
    o_in,
    g_send,
    g_in,
    acc,
    g_res,
    att_pair,
    branch_pair,
    out_got,
    out_side_got,
    ql_ref,
    ka_ref,
    va_ref,
    ga_ref,
    q_raw_ref,
    k_raw_ref,
    att_ref,
    o_ref,
    dq_acc,
    back_in,
    qkv_part,
    qkv_got,
    wide_own,
    wide_got,
    down_got,
    small_own,
    small_got,
    small_all,
    s_part,
    s_send,
    s_got,
    load_sems,
    x_sems,
    pair_sems,
    out_sems,
    swap_sems,
    grad_sems,
    back_sems,
    qkv_sems,
    wide_sems,
    small_sems,
    hid_send,
    hid_recv,
    mid_send,
    mid_recv,
    mlp_send,
    mlp_recv,
):
    low, f32 = jnp.bfloat16, jnp.float32
    dp, b = here()
    z, y, c = b // 4, (b // 2) % 2, b % 2
    twin, sib, side = (1 - dp, b), (dp, b + 1 - 2 * c), (dp, b + 2 - 4 * y)
    half, width = hidden_own.shape[1:]
    rows = 2 * half
    length = GROUP * rows
    ff = w_up.shape[1]
    ff_half = ff // 2
    part = ff // (2 * GROUP)
    quarter = width // 4
    rows_out = width // (2 * GROUP)
    blocks = length // ATT
    loaded = []

    def load(source, target):
        copy = pltpu.make_async_copy(source, target, load_sems.at[len(loaded)])
        copy.start()
        loaded.append(copy)
        return copy

    def to(device, sems, index, source, target):
        copy = remote(source, target, sems.at[0, index], sems.at[1, index], device)
        copy.start()
        return copy

    swap = Swap(o_ref, o_in, swap_sems.at[0], swap_sems.at[1])
    grad_swap = Swap(g_send, g_in, grad_sems.at[0], grad_sems.at[1])
    small_swap = Swap(small_own, small_all, small_sems.at[0], small_sems.at[1], own=False)
    gather_mid = Gather(mid_own, mid_all, mid_send, mid_recv, TAIL_PIECES)
    gather_mlp = Gather(g_mlp_own, g_mlp_all, mlp_send, mlp_recv, TAIL_PIECES)
    gather_hid = Gather(hidden_own, g_mlp_all, hid_send, hid_recv, PROJECT_PIECES)
    window = pl.ds(pl.multiple_of(b // 2 * 128, 128), 128)
    load_head = [
        load(w_query_hbm.at[:, window], up_slice.at[:, pl.ds(0, 128)]),
        load(w_key_hbm.at[:, window], up_slice.at[:, pl.ds(128, 128)]),
        load(w_value_hbm.at[:, window], gate_slice.at[:, pl.ds(0, 128)]),
    ]
    greet(swap.partners + [twin])
    gather_hid.start()
    load_out = load(w_out_hbm, w_out)
    load_mlp = [load(w_up_hbm, w_up), load(w_gate_hbm, w_gate), load(w_down_hbm, w_down)]

    gain = own_head(jnp.broadcast_to(s_qk_ref[:, window], (8, 128)), c)[:1]
    count = float(HEAD_DIM)
    score_scale = 1.0 / math.sqrt(HEAD_DIM)
    line_slots = 2 * GROUP // 8
    for copy in load_head:
        copy.wait()

    def project(first_slot):
        some = g_mlp_all[pl.ds(first_slot, line_slots)].reshape(line_slots * half, width)
        span = pl.ds(pl.multiple_of(first_slot * half, half), line_slots * half)
        query_key = dot_nn(some, up_slice[...])
        query = own_head(query_key[:, :128], c)
        key = own_head(query_key[:, 128:], c)
        value = own_head(dot_nn(some, gate_slice[:, :128]), c)
        q_raw_ref[span, :] = query.astype(low)
        k_raw_ref[span, :] = key.astype(low)
        query_scale = lax.rsqrt(jnp.sum(query * query, axis=1, keepdims=True) / count + 1e-06)
        key_scale = lax.rsqrt(jnp.sum(key * key, axis=1, keepdims=True) / count + 1e-06)
        query = (query * query_scale * gain).astype(low).astype(f32)
        ql_ref[span, :] = (query * score_scale).astype(low)
        ka_ref[span, :] = minus_ones(key * key_scale * gain)
        va_ref[span, :] = minus_ones(value)

    def project_line(distance):
        def both(line, above):
            project(line_slots * line)
            project(2 * GROUP - line_slots - line_slots * line)

        gather_hid.each_side(distance, both)

    gather_hid.line(1)
    gather_hid.sides(0)
    gather_hid.from_sib(0)
    project_line(0)
    gather_hid.line(2)
    gather_hid.hand_over()
    gather_hid.sides(1)
    gather_hid.line(3)
    gather_hid.sides(2)
    gather_hid.from_sib(2)
    project_line(2)
    gather_hid.handed()
    gather_hid.from_sib(1)
    project_line(1)
    gather_hid.sides(3)
    gather_hid.from_sib(3)
    project_line(3)
    gather_hid.drain()
    store_hidden = [
        load(g_mlp_all.at[slot], hidden_hbm.at[pl.ds(slot * half, half), :])
        for slot in range(2 * GROUP)
    ]
    load_slices = []
    windows = [pl.ds(pl.multiple_of(p * ff_half + b * part, part), part) for p in (0, 1)]
    for p in (0, 1):
        place = pl.ds(p * part, part)
        load_slices.append(load(w_up_hbm.at[:, windows[p]], up_slice.at[:, place]))
        load_slices.append(load(w_gate_hbm.at[:, windows[p]], gate_slice.at[:, place]))
        load_slices.append(load(w_down_hbm.at[windows[p], :], down_slice.at[place, :]))

    query_row_pos = lax.broadcasted_iota(jnp.int32, (ATT, ATT), 0)
    key_lane = lax.broadcasted_iota(jnp.int32, (ATT, ATT), 1)
    wide_first = half_lanes((ATT, 128))
    for query_block in range(blocks):
        span = pl.ds(query_block * ATT, ATT)
        queries = ql_ref[span, :]
        column = query_block * ATT + lax.broadcasted_iota(jnp.int32, (ATT, 1), 0)
        doc_start = doc_start_of(column, lengths_ref)
        total = jnp.zeros((ATT, 128), f32)
        for key_block in range(query_block + 1):
            base = key_block * ATT
            keys = ka_ref[pl.ds(base, ATT), :]
            values = va_ref[pl.ds(base, ATT), :]
            allowed = base + key_lane >= doc_start
            if key_block == query_block:
                allowed = allowed & (key_lane <= query_row_pos)
            weights = jnp.where(allowed, jnp.exp(dot_nt(queries, keys)), 0.0)
            total = total + dot_nn(weights.astype(low), values)
        row_sum = -total[:, HEAD_DIM : HEAD_DIM + 1]
        att_ref[span, :] = jnp.where(wide_first, total / row_sum, 0.0).astype(low)
        extra = split_lanes(jnp.log(row_sum), total.shape)
        ql_ref[span, :] = jnp.where(wide_first, queries.astype(f32), extra).astype(low)
    first = half_lanes((half, 128))
    for j in range(GROUP):
        lower = att_ref[j * half : (j + 1) * half, :].astype(f32)
        upper = att_ref[length - (j + 1) * half : length - j * half, :].astype(f32)
        o_ref[j] = jnp.where(first, lower, pltpu.roll(upper, HEAD_DIM, 1)).astype(low)
    for copy in store_hidden:
        copy.wait()
    swap.start()
    swap.wait()

    for pair in range(GROUP // 2):
        even = o_in[2 * pair].astype(f32)
        odd = o_in[2 * pair + 1].astype(f32)
        lanes = slice(pair * 128, (pair + 1) * 128)
        att_pair[c, :half, lanes] = jnp.where(first, even, pltpu.roll(odd, HEAD_DIM, 1)).astype(low)
        att_pair[c, half:, lanes] = jnp.where(first, pltpu.roll(even, HEAD_DIM, 1), odd).astype(low)
    att_copy = to(sib, pair_sems, 0, att_pair.at[c], att_pair.at[c])
    hidden = hidden_own[...].reshape(rows, width).astype(f32)
    alpha_attn = alpha_attn_ref[...]
    alpha_mlp = alpha_mlp_ref[...]
    load_out.wait()
    branch = dot_nn(att_pair[c], w_out[...])
    branch_scale = rms_scale(branch)
    branch_normed = branch * branch_scale
    mixed = hidden + alpha_attn * (branch_normed - hidden)
    middle_scale = rms_scale(mixed)
    middle = mixed * middle_scale
    middle_low = middle.astype(low)
    mid_own[0] = middle_low[:half]
    mid_own[1] = middle_low[half:]
    gather_mid.start()
    for copy in load_mlp:
        copy.wait()
    steps = ff // FF_STEP
    acc[...] = jnp.zeros_like(acc)

    def forward(step):
        cols = pl.ds(step * FF_STEP, FF_STEP)
        up = dot_nn(middle_low, w_up[:, cols])
        gate = dot_nn(middle_low, w_gate[:, cols])
        up_raw[:, cols] = up
        gate_raw[:, cols] = gate
        scaled = gate * s_gate_ref[:, cols]
        inner = up * s_up_ref[:, cols] * (scaled / (1.0 + jnp.exp(-scaled)))
        acc[...] += dot_nn(inner.astype(low), w_down[cols, :])

    for step in range(steps):
        forward(step)
    gather_mid.line(1)
    gather_mid.sides(0)
    mlp = acc[...]
    mlp_scale = rms_scale(mlp)
    mlp_normed = mlp * mlp_scale
    mixed_out = middle + alpha_mlp * (mlp_normed - middle)
    out_scale = rms_scale(mixed_out)
    result = mixed_out * out_scale
    result_ref[...] = result.astype(low)

    g_mixed = rms_pull(cot_ref[...].astype(f32), result, out_scale)
    g_alpha_mlp = jnp.sum(g_mixed * (mlp_normed - middle), axis=0, keepdims=True)
    small_own[...] = jnp.zeros_like(small_own)
    for i in range(width // 128):
        small_own[8 + i : 9 + i, :] = g_alpha_mlp[:, 128 * i : 128 * (i + 1)]
    g_mlp = rms_pull(g_mixed * alpha_mlp, mlp_normed, mlp_scale).astype(low)
    g_mlp_own[0] = g_mlp[:half]
    g_mlp_own[1] = g_mlp[half:]
    gather_mlp.start()
    acc[...] = g_mixed * (1.0 - alpha_mlp)

    def backward(step):
        cols = pl.ds(step * FF_STEP, FF_STEP)
        g_inner = dot_nt(g_mlp, w_down[cols, :])
        s_up = s_up_ref[:, cols]
        s_gate = s_gate_ref[:, cols]
        scaled = gate_raw[:, cols] * s_gate
        sigmoid = 1.0 / (1.0 + jnp.exp(-scaled))
        g_up = g_inner * (scaled / (1.0 + jnp.exp(-scaled))) * s_up
        slope = sigmoid * (1.0 + scaled * (1.0 - sigmoid))
        g_gate = g_inner * (up_raw[:, cols] * s_up) * slope * s_gate
        acc[...] += dot_nt(g_up.astype(low), w_up[:, cols]) + dot_nt(
            g_gate.astype(low), w_gate[:, cols]
        )

    for step in range(steps // 2):
        backward(step)
    gather_mid.line(2)
    gather_mid.hand_over()
    gather_mid.sides(1)
    for step in range(steps // 2, steps):
        backward(step)
    g_pre = rms_pull(acc[...], middle, middle_scale)
    g_res[...] = g_pre * (1.0 - alpha_attn)
    g_alpha_attn = jnp.sum(g_pre * (branch_normed - hidden), axis=0, keepdims=True)
    for i in range(width // 128):
        small_own[i : i + 1, :] = g_alpha_attn[:, 128 * i : 128 * (i + 1)]
    branch_pair[c] = rms_pull(g_pre * alpha_attn, branch_normed, branch_scale).astype(low)
    g_att = dot_nt(branch_pair[c], w_out[...]).astype(low).astype(f32)
    for pair in range(GROUP // 2):
        lower = g_att[:half, pair * 128 : (pair + 1) * 128]
        upper = g_att[half:, pair * 128 : (pair + 1) * 128]
        g_send[2 * pair] = jnp.where(first, lower, pltpu.roll(upper, HEAD_DIM, 1)).astype(low)
        g_send[2 * pair + 1] = jnp.where(first, pltpu.roll(lower, HEAD_DIM, 1), upper).astype(low)
    grad_swap.start()
    branch_copy = to(sib, pair_sems, 1, branch_pair.at[c], branch_pair.at[c])

    g_cat = w_down.at[pl.ds(0, length), pl.ds(0, 4 * part)]
    inner_all = w_down.at[pl.ds(0, length), pl.ds(512, 2 * part)]
    raw_low = w_down.at[pl.ds(length, length), pl.ds(0, 384)]
    w_qkv = [w_up.at[:, pl.ds(i * width, width)] for i in range(3)]
    home = [w_up.at[pl.ds(i * rows, rows), pl.ds(3 * width, width)] for i in range(3)]
    out_send = w_out.at[pl.ds(0, quarter), :]
    out_side_send = [w_out.at[pl.ds(quarter + half * k, half), :] for k in (0, 1)]
    out_line = w_out.at[pl.ds(2 * quarter, 4 * rows_out), :]
    down_send = w_out.at[pl.ds(3 * quarter, part), :]
    out_own = [up_raw.at[:, pl.ds((2 + k) * width, width)] for k in (0, 1)]
    wide_send = [w_gate.at[pl.ds(quarter * i, quarter), pl.ds(2048, 512)] for i in (0, 1)]
    qkv_send = w_gate.at[pl.ds(0, 2 * quarter), pl.ds(2560, 256)]
    back_send = SendBlocks(w_gate, 0, half, 2816, 384)
    qkv_blocks = SendBlocks(w_gate, 2 * quarter, rows_out, 2560, 256)
    wide_blocks = SendBlocks(w_gate, 2 * quarter, rows_out, 2048, 512)
    back_swap = Swap(back_send, back_in, back_sems.at[0], back_sems.at[1])
    qkv_swap = Swap(qkv_blocks, qkv_in, qkv_sems.at[0], qkv_sems.at[1])
    tokens_of_half = [w_gate.at[:, pl.ds(i * width, width)] for i in (0, 1)]
    load_hidden = [
        load(hidden_hbm.at[pl.ds(i * width, width), :], tokens_of_half[i]) for i in (0, 1)
    ]
    load_qkv = [
        load(source, w_qkv[i]) for i, source in enumerate((w_query_hbm, w_key_hbm, w_value_hbm))
    ]
    gather_mid.line(3)
    gather_mid.sides(2)
    gather_mlp.line(1)
    gather_mlp.sides(0)

    att_copy.wait()
    branch_copy.wait()
    both_branch = branch_pair[...].reshape(2 * rows, width)

    def out_rows(owner):
        lanes = pl.ds(pl.multiple_of(owner * 2 * quarter + c * quarter, quarter), quarter)
        return dot_tn(att_pair[:, :, lanes].reshape(2 * rows, quarter), both_branch)

    out_send[...] = out_rows(1 - dp).astype(low)
    out_copy = to(twin, x_sems, 0, out_send, out_got)
    out_mine = out_rows(dp)
    for k in (0, 1):
        out_own[k][...] = out_mine[2 * half * k : 2 * half * (k + 1)]
    gather_mid.handed()
    gather_mid.sides(3)
    gather_mlp.line(2)
    gather_mlp.hand_over()
    gather_mlp.sides(1)

    grad_swap.wait()
    for j in range(GROUP):
        block = g_in[j].astype(f32)
        for start, grads in (
            (j * half, jnp.where(first, block, 0.0)),
            (length - (j + 1) * half, jnp.where(first, pltpu.roll(block, HEAD_DIM, 1), 0.0)),
        ):
            span = pl.ds(start, half)
            delta = jnp.sum(grads * att_ref[span, :].astype(f32), axis=1, keepdims=True)
            ga_ref[span, :] = (grads + split_lanes(delta, grads.shape)).astype(low)
    dq_acc[...] = jnp.zeros_like(dq_acc)
    key_row = lax.broadcasted_iota(jnp.int32, (KEYS, ATT), 0)
    query_lane = lax.broadcasted_iota(jnp.int32, (KEYS, ATT), 1)
    query_row = lax.broadcasted_iota(jnp.int32, (1, ATT), 1)

    def norm_pull(raw, grad):
        raw = raw.astype(f32)
        scale = lax.rsqrt(jnp.sum(raw * raw, axis=1, keepdims=True) / count + 1e-06)
        normed = raw * scale
        g_gain = jnp.sum(grad * normed, axis=0, keepdims=True)
        inside = grad * gain
        mean = jnp.sum(inside * normed, axis=1, keepdims=True) / count
        return scale * (inside - normed * mean), g_gain

    key_first = half_lanes((KEYS, 128))

    def pair_grads(keys, values, key_block, query_block):
        base = query_block * ATT
        queries = ql_ref[pl.ds(base, ATT), :]
        grads = ga_ref[pl.ds(base, ATT), :]
        key_pos = key_block * KEYS + key_row
        allowed = key_pos >= doc_start_of(base + query_row, lengths_ref)
        if key_block * KEYS + KEYS > base:
            allowed = allowed & (key_pos <= base + query_lane)
        weights = jnp.where(allowed, jnp.exp(dot_nt(keys, queries)), 0.0)
        slopes = (weights * dot_nt(values, grads)).astype(low)
        dq_acc[pl.ds(base, ATT), :] += dot_tn(slopes, keys)
        return dot_nn(slopes, queries), dot_nn(weights.astype(low), grads)

    g_gain = jnp.zeros((1, 128), f32)
    for key_block in range(length // KEYS):
        span = pl.ds(key_block * KEYS, KEYS)
        keys = ka_ref[span, :]
        values = va_ref[span, :]
        dk, dv = 0.0, 0.0
        for query_block in range(key_block * KEYS // ATT, blocks):
            more_k, more_v = pair_grads(keys, values, key_block, query_block)
            dk, dv = dk + more_k, dv + more_v
        g_key, key_gain = norm_pull(k_raw_ref[span, :], jnp.where(key_first, dk, 0.0))
        g_gain = g_gain + key_gain
        raw_low[span, 128:256] = g_key.astype(low)
        raw_low[span, 256:384] = jnp.where(key_first, dv, 0.0).astype(low)
        if key_block == 0:
            gather_mlp.line(3)
            gather_mlp.sides(2)
        if key_block == 1:
            gather_mlp.handed()
            gather_mlp.sides(3)
    for block in range(blocks):
        span = pl.ds(block * ATT, ATT)
        dq = jnp.where(wide_first, dq_acc[span, :] * score_scale, 0.0)
        g_query, query_gain = norm_pull(q_raw_ref[span, :], dq)
        g_gain = g_gain + query_gain
        raw_low[span, 0:128] = g_query.astype(low)
    for j in range(GROUP):
        for i in range(3):
            lanes = slice(128 * i, 128 * (i + 1))
            lower = raw_low[j * half : (j + 1) * half, lanes].astype(f32)
            upper = raw_low[length - (j + 1) * half : length - j * half, lanes].astype(f32)
            back_send.block(j)[:, lanes] = jnp.where(
                first, lower, pltpu.roll(upper, HEAD_DIM, 1)
            ).astype(low)
    back_swap.start()

    small_own[16:17, :] = g_gain
    small_copy = to(twin, x_sems, 1, small_own, small_got)

    for copy in load_hidden:
        copy.wait()

    def qkv_chunk(chunk):
        lanes = pl.ds(pl.multiple_of(chunk * quarter, quarter), quarter)
        grads = sum(
            dot_tn(tokens_of_half[i][:, lanes], raw_low[pl.ds(i * width, width), :]) for i in (0, 1)
        )
        query_key = jnp.where(
            half_lanes((quarter, 128)), grads[:, :128], pltpu.roll(grads[:, 128:256], HEAD_DIM, 1)
        )
        return query_key, grads[:, 256:]

    for i in (0, 1):
        query_key, value = qkv_chunk(2 * (1 - dp) + i)
        span = slice(quarter * i, quarter * (i + 1))
        qkv_send[span, :128] = query_key.astype(low)
        qkv_send[span, 128:] = value.astype(low)
    qkv_copy = to(twin, x_sems, 2, qkv_send, qkv_got)
    for i in (0, 1):
        query_key, value = qkv_chunk(2 * dp + i)
        span = slice(quarter * i, quarter * (i + 1))
        qkv_part[span, :128] = query_key
        qkv_part[span, 128:] = value

    out_copy.wait()
    side_copies = []
    for k in (0, 1):
        out_own[k][...] += out_got[2 * half * k : 2 * half * (k + 1)].astype(f32)
        other = pl.ds(pl.multiple_of((1 - y) * half, half), half)
        out_side_send[k][...] = out_own[k][other, :].astype(low)
        side_copies.append(to(side, pair_sems, 2 + k, out_side_send[k], out_side_got.at[k]))
    small_copy.wait()
    small_own[...] += small_got[...]
    small_swap.start()
    gather_mid.finish()
    gather_mlp.finish()

    for copy in load_slices:
        copy.wait()
    s_up = jnp.concatenate([s_up_ref[:, window] for window in windows], axis=1)
    s_gate = jnp.concatenate([s_gate_ref[:, window] for window in windows], axis=1)
    slots = PART // half

    def tokens_of(array, step):
        return array[pl.ds(step * slots, slots)].reshape(PART, width)

    def recompute(step, sums):
        span = pl.ds(pl.multiple_of(step * PART, PART), PART)
        some = tokens_of(mid_all, step)
        up = dot_nn(some, up_slice[...])
        gate = dot_nn(some, gate_slice[...])
        g_inner = dot_nt(tokens_of(g_mlp_all, step), down_slice[...])
        scaled = gate * s_gate
        sigmoid = 1.0 / (1.0 + jnp.exp(-scaled))
        silu = scaled / (1.0 + jnp.exp(-scaled))
        up_scaled = up * s_up
        inner_all[span, :] = (up_scaled * silu).astype(low)
        g_up_scaled = g_inner * silu
        g_scaled = g_inner * up_scaled * (sigmoid * (1.0 + scaled * (1.0 - sigmoid)))
        g_cat[span, : 2 * part] = (g_up_scaled * s_up).astype(low)
        g_cat[span, 2 * part :] = (g_scaled * s_gate).astype(low)
        return (
            sums[0] + jnp.sum(g_up_scaled * up, axis=0, keepdims=True),
            sums[1] + jnp.sum(g_scaled * gate, axis=0, keepdims=True),
        )

    zero_row = jnp.zeros((1, 2 * part), f32)
    g_s_up, g_s_gate = lax.fori_loop(0, length // PART, recompute, (zero_row, zero_row))

    line_rows_of = 4 * rows_out
    turns = ((0, 3), (1, 2))

    def wide_chunk(owner, turn):
        tokens = [
            mid_all[
                :,
                :,
                pl.ds(
                    pl.multiple_of(owner * 2 * quarter + line * line_rows_of, line_rows_of),
                    line_rows_of,
                ),
            ].reshape(length, line_rows_of)
            for line in turns[turn]
        ]
        return dot_tn(jnp.concatenate(tokens, axis=1), g_cat[...])

    wide_copies = []
    for i in (0, 1):
        wide_send[i][...] = wide_chunk(1 - dp, i).astype(low)
        wide_copies.append(to(twin, x_sems, 3 + i, wide_send[i], wide_got.at[i]))
    for p in (0, 1):
        s_part[p] = jnp.zeros(s_part.shape[1:], f32)
        s_part[p, 0:1, :] = g_s_up[:, p * part : (p + 1) * part]
        s_part[p, 1:2, :] = g_s_gate[:, p * part : (p + 1) * part]
    s_send[...] = s_part[1 - dp]
    s_copy = to(twin, x_sems, 5, s_send, s_got)
    for chunk in range(4):
        lanes = pl.ds(chunk * quarter, quarter)
        grads = dot_tn(inner_all[...], g_mlp_all[:, :, lanes].reshape(length, quarter))
        for p in (0, 1):
            place = slice(p * width + chunk * quarter, p * width + (chunk + 1) * quarter)
            up_raw[:, place] = grads[p * part : (p + 1) * part]
    down_other = pl.ds(pl.multiple_of((1 - dp) * width, width), width)
    down_mine = pl.ds(pl.multiple_of(dp * width, width), width)
    down_send[...] = up_raw[:, down_other].astype(low)
    down_copy = to(twin, x_sems, 6, down_send, down_got)

    qkv_copy.wait()
    per_chunk = quarter // rows_out
    total = (qkv_part[...] + qkv_got[...].astype(f32)).astype(low)
    for k in range(GROUP):
        qkv_blocks.block(k)[...] = total[k * rows_out : (k + 1) * rows_out]
    qkv_swap.start()
    for copy in side_copies:
        copy.wait()
    out_copies = []
    for k in (0, 1):
        mine = pl.ds(pl.multiple_of(y * half, half), half)
        total = (out_own[k][mine, :] + out_side_got[k].astype(f32)).astype(low)
        out_line[2 * rows_out * k : 2 * rows_out * (k + 1), :] = total
        for core in (0, 1):
            line_rows = pl.ds((2 * k + core) * rows_out, rows_out)
            target = (2 * c + k) * 4 + 2 * y + core
            index = 2 * k + core
            copy = remote(
                out_line.at[line_rows],
                out_in.at[z],
                out_sems.at[0, index],
                out_sems.at[1, z],
                (dp, target),
            )
            out_copies.append((target, copy))

            @pl.when(target != b)
            def _():
                copy.start()

            @pl.when(target == b)
            def _():
                out_in[z] = out_line[line_rows, :]

    def wide_copy(target):
        return remote(
            wide_blocks.block(target),
            wide_in.at[b],
            wide_sems.at[0, target],
            wide_sems.at[1, b],
            (dp, target),
        )

    for i in (0, 1):
        wide_own[...] = wide_chunk(dp, i)
        wide_copies[i].wait()
        total = (wide_own[...] + wide_got[i].astype(f32)).astype(low)
        for k in range(per_chunk):
            target = 4 * turns[i][k // 4] + k % 4
            wide_blocks.block(target)[...] = total[k * rows_out : (k + 1) * rows_out]

            @pl.when(target != b)
            def _():
                wide_copy(target).start()

            @pl.when(target == b)
            def _():
                wide_in[b] = wide_blocks.block(target)[...]

    for copy in load_qkv:
        copy.wait()
    back_swap.wait()
    for pair in range(GROUP // 2):
        for i in range(3):
            lanes = slice(128 * i, 128 * (i + 1))
            even = back_in[2 * pair, :, lanes].astype(f32)
            odd = back_in[2 * pair + 1, :, lanes].astype(f32)
            place = slice(128 * pair, 128 * (pair + 1))
            home[i][:half, place] = jnp.where(first, even, pltpu.roll(odd, HEAD_DIM, 1)).astype(low)
            home[i][half:, place] = jnp.where(first, pltpu.roll(even, HEAD_DIM, 1), odd).astype(low)
    input_grad_ref[...] = (
        g_res[...]
        + dot_nt(home[0][...], w_qkv[0][...])
        + dot_nt(home[1][...], w_qkv[1][...])
        + dot_nt(home[2][...], w_qkv[2][...])
    )
    s_copy.wait()
    g_s_ref[...] = s_part[dp] + s_got[...]
    down_copy.wait()
    g_down_ref[...] = up_raw[:, down_mine] + down_got[...].astype(f32)
    small_swap.wait()
    small_all[b] = small_own[...]
    small_ref[...] = jnp.sum(small_all[...], axis=0)
    small_ref[17:18, :] = small_all[8 * dp + b // 2, 16:17, :]
    qkv_swap.wait()
    for target, copy in out_copies:

        @pl.when(target != b)
        def _():
            copy.wait_send()

    for source_z in range(4):
        source = source_z * 4 + 2 * y + z // 2

        @pl.when(source != b)
        def _():
            remote(
                out_line.at[pl.ds(0, rows_out)],
                out_in.at[source_z],
                out_sems.at[0, 0],
                out_sems.at[1, source_z],
                sib,
            ).wait_recv()

    for other in range(GROUP):

        @pl.when(other != b)
        def _():
            copy = remote(
                wide_blocks.block(other),
                wide_in.at[other],
                wide_sems.at[0, other],
                wide_sems.at[1, other],
                sib,
            )
            copy.wait_send()
            copy.wait_recv()


def layer_block(vmem_inputs, hbm_inputs):
    low, f32 = jnp.bfloat16, jnp.float32
    shape, vmem, sems = jax.ShapeDtypeStruct, pltpu.VMEM, pltpu.SemaphoreType.DMA
    hidden = vmem_inputs[1]
    w_out, w_up, w_gate, w_down = hbm_inputs[:4]
    half, width = hidden.shape[1:]
    rows = 2 * half
    ff = w_up.shape[1]
    length = GROUP * rows
    rows_out = width // (2 * GROUP)
    part = ff // (2 * GROUP)
    quarter = width // 4
    packed = (GROUP, half, 128)
    return pl.pallas_call(
        layer_kernel,
        out_shape=[
            shape((rows, width), low),
            shape((rows, width), f32),
            shape((GROUP, rows_out, 4 * part), low),
            shape((GROUP, rows_out, 256), low),
            shape((part, width), f32),
            shape((4, rows_out, width), low),
            shape((8, 128), f32),
            shape((24, 128), f32),
            shape((length, width), low),
        ],
        in_specs=[SMEM_SPEC]
        + [VMEM_SPEC] * (len(vmem_inputs) - 1)
        + [ANY_SPEC] * len(hbm_inputs),
        out_specs=[VMEM_SPEC] * 8 + [ANY_SPEC],
        scratch_shapes=[
            vmem((2 * GROUP, half, width), low),
            vmem((2 * GROUP, half, width), low),
            vmem(w_out.shape, low),
            vmem(w_up.shape, low),
            vmem(w_gate.shape, low),
            vmem(w_down.shape, low),
            vmem((width, 2 * part), low),
            vmem((width, 2 * part), low),
            vmem((2 * part, width), low),
            vmem((rows, ff), f32),
            vmem((rows, ff), f32),
            vmem((2, half, width), low),
            vmem((2, half, width), low),
            vmem(packed, low),
            vmem(packed, low),
            vmem(packed, low),
            vmem((rows, width), f32),
            vmem((rows, width), f32),
            vmem((2, rows, width), low),
            vmem((2, rows, width), low),
            vmem((quarter, width), low),
            vmem((2, half, width), low),
            vmem((length, 128), low),
            vmem((length, 128), low),
            vmem((length, 128), low),
            vmem((length, 128), low),
            vmem((length, 128), low),
            vmem((length, 128), low),
            vmem((length, 128), low),
            vmem(packed, low),
            vmem((length, 128), f32),
            vmem((GROUP, half, 384), low),
            vmem((2 * quarter, 256), f32),
            vmem((2 * quarter, 256), low),
            vmem((quarter, 4 * part), f32),
            vmem((2, quarter, 4 * part), low),
            vmem((part, width), low),
            vmem((24, 128), f32),
            vmem((24, 128), f32),
            vmem((GROUP, 24, 128), f32),
            vmem((2, 8, 128), f32),
            vmem((8, 128), f32),
            vmem((8, 128), f32),
            sems((64,)),
            sems((2, 8)),
            sems((2, 4)),
            sems((2, 4)),
            sems((2, GROUP)),
            sems((2, GROUP)),
            sems((2, GROUP)),
            sems((2, GROUP)),
            sems((2, GROUP)),
            sems((2, GROUP)),
        ]
        + gather_scratch(PROJECT_PIECES)
        + gather_scratch(TAIL_PIECES)
        + gather_scratch(TAIL_PIECES),
        compiler_params=comm_params(1),
        name="layer_block",
    )(*vmem_inputs, *hbm_inputs)


def assemble_kernel(
    result,
    input_grad,
    wide_in,
    qkv_in,
    down,
    out_in,
    scales,
    small,
    alpha_attn,
    alpha_mlp,
    output_ref,
    input_grad_ref,
    g_query_ref,
    g_key_ref,
    g_value_ref,
    g_out_ref,
    g_up_ref,
    g_gate_ref,
    g_down_ref,
    gain_ref,
    s_up_ref,
    s_gate_ref,
    g_alpha_attn_ref,
    g_alpha_mlp_ref,
    mean_ref,
):
    f32 = jnp.float32
    dp, b = here()
    output_ref[...] = result[...]
    input_grad_ref[...] = input_grad[...]
    g_down_ref[...] = down[...]
    s_up_ref[...] = scales[0:1, :]
    s_gate_ref[...] = scales[1:2, :]
    rows_out = g_out_ref.shape[0]
    per_row = 128 // rows_out
    device = dp * GROUP + b

    def own_lanes(row, place):
        start = (128 - rows_out * place) % 128
        return pltpu.roll(jnp.broadcast_to(row, (8, 128)), start, 1)[:1, :rows_out]

    place = device % per_row
    g_alpha_attn_ref[...] = own_lanes(small[pl.ds(device // per_row, 1), :], place)
    g_alpha_mlp_ref[...] = own_lanes(small[pl.ds(8 + device // per_row, 1), :], place)
    gain_ref[...] = own_lanes(small[17:18, :], b % 2)
    mean_ref[...] = 0.5 * (mean_last(alpha_attn[...]) + mean_last(alpha_mlp[...]))
    g_out_ref[...] = sum(out_in[i].astype(f32) for i in range(4))
    part = wide_in.shape[2] // 4
    ff_half = g_up_ref.shape[1] // 2
    for j in range(GROUP):
        for p in (0, 1):
            place = slice(p * ff_half + j * part, p * ff_half + (j + 1) * part)
            g_up_ref[:, place] = wide_in[j, :, p * part : (p + 1) * part].astype(f32)
            g_gate_ref[:, place] = wide_in[j, :, (2 + p) * part : (3 + p) * part].astype(f32)
    first = half_lanes((g_query_ref.shape[0], 128))
    for pair in range(GROUP // 2):
        place = slice(128 * pair, 128 * (pair + 1))
        even, odd = qkv_in[2 * pair].astype(f32), qkv_in[2 * pair + 1].astype(f32)
        even_qk, odd_qk = even[:, :128], odd[:, :128]
        g_query_ref[:, place] = jnp.where(first, even_qk, pltpu.roll(odd_qk, HEAD_DIM, 1))
        g_key_ref[:, place] = jnp.where(first, pltpu.roll(even_qk, HEAD_DIM, 1), odd_qk)
        g_value_ref[:, place] = jnp.where(
            first, even[:, 128:], pltpu.roll(odd[:, 128:], HEAD_DIM, 1)
        )


def assemble_block(inputs, ff):
    result, input_grad, wide_in, qkv_in, down, out_in = inputs[:6]
    f32 = jnp.float32
    shape = jax.ShapeDtypeStruct
    width = result.shape[1]
    rows_out = wide_in.shape[1]
    return pl.pallas_call(
        assemble_kernel,
        out_shape=[
            shape(result.shape, result.dtype),
            shape(input_grad.shape, f32),
            shape((rows_out, width), f32),
            shape((rows_out, width), f32),
            shape((rows_out, width), f32),
            shape((rows_out, width), f32),
            shape((rows_out, ff), f32),
            shape((rows_out, ff), f32),
            shape(down.shape, f32),
            shape((1, rows_out), f32),
            shape((1, 128), f32),
            shape((1, 128), f32),
            shape((1, rows_out), f32),
            shape((1, rows_out), f32),
            shape((1, 1), f32),
        ],
        in_specs=[VMEM_SPEC] * len(inputs),
        out_specs=[VMEM_SPEC] * 15,
        compiler_params=pltpu.CompilerParams(vmem_limit_bytes=VMEM_LIMIT),
        name="assemble_block",
    )(*inputs)


def on_device_heads(
    tokens,
    cotangent,
    lengths,
    w_query,
    w_key,
    w_value,
    w_out,
    w_up,
    w_gate,
    w_down,
    s_qk,
    s_up,
    s_gate,
    alpha_attn,
    alpha_mlp,
):
    model_width = w_query.shape[0]
    tok_rows = tokens.shape[2]
    half_rows = tok_rows // 2
    hidden = tokens[0, 0]
    (result, input_grad, wide_in, qkv_in, grad_down, out_in, grad_scales, small, _) = layer_block(
        (
            lengths,
            hidden.reshape(2, half_rows, model_width),
            cotangent[0, 0],
            s_qk[None],
            s_up[None],
            s_gate[None],
            alpha_attn[None],
            alpha_mlp[None],
        ),
        (w_out, w_up, w_gate, w_down, w_query, w_key, w_value),
    )
    (
        output,
        input_grad,
        grad_query,
        grad_key,
        grad_value,
        grad_out,
        grad_up,
        grad_gate,
        grad_down,
        grad_gain,
        grad_up_scale,
        grad_gate_scale,
        grad_attn,
        grad_mlp_alpha,
        mean_alpha,
    ) = assemble_block(
        (
            result,
            input_grad,
            wide_in,
            qkv_in,
            grad_down,
            out_in,
            grad_scales,
            small,
            alpha_attn[None],
            alpha_mlp[None],
        ),
        w_up.shape[1],
    )
    return (
        output[None, None],
        input_grad[None, None],
        grad_query,
        grad_key,
        grad_value,
        grad_out,
        grad_up,
        grad_gate,
        grad_down,
        grad_gain[0],
        grad_up_scale[0],
        grad_gate_scale[0],
        grad_attn[0],
        grad_mlp_alpha[0],
        mean_alpha[0, 0],
    )


def on_device(*arrays):
    head_count = arrays[3].shape[0] // HEAD_DIM
    tok_rows = arrays[0].shape[2]
    fits = lax.axis_size("blk") == head_count == 16 and lax.axis_size("dp") == 2
    if fits and tok_rows == 128:
        return on_device_heads(*arrays)
    return on_device_general(*arrays)


def solution(mesh):
    in_specs = (
        P("dp", "blk", None, None),
        P("dp", "blk", None, None),
        P("dp", None),
        P(),
        P(),
        P(),
        P(),
        P(),
        P(),
        P(),
        P(),
        P(),
        P(),
        P(),
        P(),
    )
    out_specs = (
        P("dp", "blk", None, None),
        P("dp", "blk", None, None),
        P(("dp", "blk"), None),
        P(("dp", "blk"), None),
        P(("dp", "blk"), None),
        P(("dp", "blk"), None),
        P(("dp", "blk"), None),
        P(("dp", "blk"), None),
        P(("dp", "blk"), None),
        P(("dp", "blk")),
        P(("dp", "blk")),
        P(("dp", "blk")),
        P(("dp", "blk")),
        P(("dp", "blk")),
        P(),
    )
    return jax.shard_map(
        on_device, mesh=mesh, in_specs=in_specs, out_specs=out_specs, check_vma=False
    )
```

```python
import functools
import math

import jax
import jax.numpy as jnp
from jax import lax
from jax.experimental import pallas as pl
from jax.experimental.pallas import tpu as pltpu
from jax.sharding import PartitionSpec as P

HEAD_DIM = 64


def rms_norm(vector):
    return vector * lax.rsqrt(jnp.mean(vector * vector, axis=-1, keepdims=True) + 1e-06)


def head_norm(vector, head_count):
    shaped = vector.reshape(vector.shape[0], head_count, -1)
    return rms_norm(shaped).reshape(vector.shape)


def silu_smooth(vector):
    return vector / (1.0 + jnp.exp(-vector))


def residual_mix(inputs, branch, alphas):
    return rms_norm(inputs + alphas * (rms_norm(branch) - inputs))


def gated_inner(up_raw, gate_raw, s_up, s_gate):
    return up_raw * s_up * silu_smooth(gate_raw * s_gate)


def stream_positions(row_index, tok_rows, members):
    half_rows = tok_rows // 2
    device = row_index // tok_rows
    within = row_index % tok_rows
    block_id = jnp.where(within < half_rows, device, 2 * members - 1 - device)
    return block_id * half_rows + within % half_rows


def doc_index(positions, doc_ends):
    return jnp.sum(
        (positions[:, None] >= doc_ends[None, :]).astype(jnp.int32), axis=1, dtype=jnp.int32
    )


def allowed_pairs(query_pos, query_doc, key_pos, key_doc):
    return (key_pos[None, :] <= query_pos[:, None]) & (key_doc[None, :] == query_doc[:, None])


def take_rows(matrix, first_row, row_count):
    return lax.dynamic_slice_in_dim(matrix, first_row, row_count, 0)


def fold_half(running, query_heads, key_heads, value_heads, allowed, score_scale):

    def absorb(carried):
        best_score, total_sum, accumulated = carried
        scores = (
            jnp.einsum("qhd,khd->hqk", query_heads, key_heads, preferred_element_type=jnp.float32)
            * score_scale
        )
        scores = jnp.where(allowed[None], scores, -1e30)
        new_best = jnp.maximum(best_score, jnp.max(scores, axis=2))
        weights = jnp.where(allowed[None], jnp.exp(scores - new_best[:, :, None]), 0.0)
        fade_factor = jnp.exp(best_score - new_best)
        total_sum = jnp.sum(weights, axis=2)
        accumulated = accumulated * fade_factor.T[:, :, None] + jnp.einsum(
            "hqk,khd->qhd",
            weights.astype(jnp.bfloat16),
            value_heads,
            preferred_element_type=jnp.float32,
        )
        return (new_best, total_sum, accumulated)

    return lax.cond(jnp.any(allowed), absorb, lambda carried: carried, running)


def pair_terms(query_side, key_heads, value_heads, allowed, score_scale):
    query_heads, grad_heads, log_total, delta_rows = (
        query_side[0],
        query_side[1],
        query_side[2],
        query_side[3],
    )
    scores = (
        jnp.einsum("qhd,khd->hqk", query_heads, key_heads, preferred_element_type=jnp.float32)
        * score_scale
    )
    scores = jnp.where(allowed[None], scores, -1e30)
    weights = jnp.exp(scores - log_total[:, :, None])
    grad_weights = jnp.einsum(
        "qhd,khd->hqk", grad_heads, value_heads, preferred_element_type=jnp.float32
    )
    grad_scores = (weights * (grad_weights - delta_rows[:, :, None])).astype(jnp.bfloat16)
    return (weights.astype(jnp.bfloat16), grad_scores)


def query_term(query_side, key_heads, value_heads, allowed, score_scale):
    weights, grad_scores = pair_terms(query_side, key_heads, value_heads, allowed, score_scale)
    return score_scale * jnp.einsum(
        "hqk,khd->qhd", grad_scores, key_heads, preferred_element_type=jnp.float32
    )


def key_term(query_side, key_heads, value_heads, allowed, score_scale):
    weights, grad_scores = pair_terms(query_side, key_heads, value_heads, allowed, score_scale)
    grad_keys = score_scale * jnp.einsum(
        "hqk,qhd->khd", grad_scores, query_side[0], preferred_element_type=jnp.float32
    )
    grad_values = jnp.einsum(
        "hqk,qhd->khd", weights, query_side[1], preferred_element_type=jnp.float32
    )
    return (grad_keys, grad_values)


def on_device_general(
    tokens,
    cotangent,
    lengths,
    w_query,
    w_key,
    w_value,
    w_out,
    w_up,
    w_gate,
    w_down,
    s_qk,
    s_up,
    s_gate,
    alpha_attn,
    alpha_mlp,
):
    model_width = w_query.shape[0]
    head_count = model_width // HEAD_DIM
    score_scale = 1.0 / math.sqrt(HEAD_DIM)
    tok_rows = tokens.shape[2]
    half_rows = tok_rows // 2
    members = lax.axis_size("blk")
    position = lax.axis_index("blk")
    doc_ends = jnp.cumsum(lengths[0], dtype=jnp.int32)
    hidden = tokens[0, 0]
    hidden_f = hidden.astype(jnp.float32)

    def key_info(first_row, row_count):
        key_pos = stream_positions(
            first_row + jnp.arange(row_count, dtype=jnp.int32), tok_rows, members
        )
        return (key_pos, doc_index(key_pos, doc_ends))

    def heads_of(matrix):
        return matrix.reshape(matrix.shape[0], head_count, HEAD_DIM)

    def scaled_norm(raw_rows, gain_vector):
        return head_norm(raw_rows, head_count) * gain_vector

    own_pos, own_doc = key_info(position * tok_rows, tok_rows)
    query_raw = jnp.dot(hidden, w_query, preferred_element_type=jnp.float32)
    key_raw = jnp.dot(hidden, w_key, preferred_element_type=jnp.float32)
    value_raw = jnp.dot(hidden, w_value, preferred_element_type=jnp.float32)
    queries = scaled_norm(query_raw, s_qk).astype(jnp.bfloat16)
    key_rows = scaled_norm(key_raw, s_qk).astype(jnp.bfloat16)
    value_rows = value_raw.astype(jnp.bfloat16)
    query_heads = heads_of(queries)

    def empty_state():
        return (
            jnp.full((head_count, half_rows), -1e30, jnp.float32),
            jnp.zeros((head_count, half_rows), jnp.float32),
            jnp.zeros((half_rows, head_count, HEAD_DIM), jnp.float32),
        )

    running = (empty_state(), empty_state())
    key_part = lax.all_gather(key_rows, "blk", axis=0, tiled=True)
    value_part = lax.all_gather(value_rows, "blk", axis=0, tiled=True)
    key_pos, key_doc = key_info(jnp.int32(0), key_part.shape[0])
    updated = []
    for part_index in range(2):
        rows_here = slice(part_index * half_rows, (part_index + 1) * half_rows)
        allowed = allowed_pairs(own_pos[rows_here], own_doc[rows_here], key_pos, key_doc)
        updated.append(
            fold_half(
                running[part_index],
                query_heads[rows_here],
                heads_of(key_part),
                heads_of(value_part),
                allowed,
                score_scale,
            )
        )
    folded = (updated[0], updated[1])
    best_score = jnp.concatenate([folded[0][0], folded[1][0]], axis=1)
    total_sum = jnp.concatenate([folded[0][1], folded[1][1]], axis=1)
    accumulated = jnp.concatenate([folded[0][2], folded[1][2]], axis=0)
    attended = accumulated / total_sum.T[:, :, None]
    log_total = best_score + jnp.log(total_sum)
    attended_low = attended.reshape(tok_rows, model_width).astype(jnp.bfloat16)
    branch = jnp.dot(attended_low, w_out, preferred_element_type=jnp.float32)
    middle = residual_mix(hidden_f, branch, alpha_attn)
    middle_low = middle.astype(jnp.bfloat16)
    up_raw = jnp.dot(middle_low, w_up, preferred_element_type=jnp.float32)
    gate_raw = jnp.dot(middle_low, w_gate, preferred_element_type=jnp.float32)
    inner_low = gated_inner(up_raw, gate_raw, s_up, s_gate).astype(jnp.bfloat16)
    mlp_raw = jnp.dot(inner_low, w_down, preferred_element_type=jnp.float32)
    result = residual_mix(middle, mlp_raw, alpha_mlp)
    mixed_out, pull_out = jax.vjp(residual_mix, middle, mlp_raw, alpha_mlp)
    grad_middle, grad_mlp, grad_alpha_mlp = pull_out(cotangent[0, 0].astype(jnp.float32))
    grad_mlp_low = grad_mlp.astype(jnp.bfloat16)
    grad_w_down = jnp.dot(inner_low.T, grad_mlp_low, preferred_element_type=jnp.float32)
    grad_inner = jnp.dot(grad_mlp_low, w_down.T, preferred_element_type=jnp.float32)
    inner_out, pull_inner = jax.vjp(gated_inner, up_raw, gate_raw, s_up, s_gate)
    grad_up_raw, grad_gate_raw, grad_s_up, grad_s_gate = pull_inner(grad_inner)
    up_low = grad_up_raw.astype(jnp.bfloat16)
    gate_low = grad_gate_raw.astype(jnp.bfloat16)
    grad_w_up = jnp.dot(middle_low.T, up_low, preferred_element_type=jnp.float32)
    grad_w_gate = jnp.dot(middle_low.T, gate_low, preferred_element_type=jnp.float32)
    grad_middle = (
        grad_middle
        + jnp.dot(up_low, w_up.T, preferred_element_type=jnp.float32)
        + jnp.dot(gate_low, w_gate.T, preferred_element_type=jnp.float32)
    )
    attn_out, pull_attn = jax.vjp(residual_mix, hidden_f, branch, alpha_attn)
    grad_hidden, grad_branch, grad_alpha_attn = pull_attn(grad_middle)
    branch_low = grad_branch.astype(jnp.bfloat16)
    grad_w_out = jnp.dot(attended_low.T, branch_low, preferred_element_type=jnp.float32)
    grad_att_low = jnp.dot(branch_low, w_out.T, preferred_element_type=jnp.float32).astype(
        jnp.bfloat16
    )
    grad_heads = heads_of(grad_att_low)
    delta_rows = jnp.sum(grad_heads.astype(jnp.float32) * attended, axis=2).T

    def local_side(part_index):
        rows_here = slice(part_index * half_rows, (part_index + 1) * half_rows)
        return (
            query_heads[rows_here],
            grad_heads[rows_here],
            log_total[:, rows_here],
            delta_rows[:, rows_here],
            own_pos[rows_here],
            own_doc[rows_here],
        )

    local_parts = (local_side(0), local_side(1))
    whole_keys, whole_values = (
        lax.all_gather(key_rows, "blk", axis=0, tiled=True),
        lax.all_gather(value_rows, "blk", axis=0, tiled=True),
    )

    def query_step(grad_parts, shard_index):
        first_row = shard_index * tok_rows
        key_part = heads_of(take_rows(whole_keys, first_row, tok_rows))
        value_part = heads_of(take_rows(whole_values, first_row, tok_rows))
        key_pos, key_doc = key_info(first_row, tok_rows)
        updated = []
        for part_index in range(2):
            query_side = local_parts[part_index]
            allowed = allowed_pairs(query_side[4], query_side[5], key_pos, key_doc)

            def add_term(grad_now):
                return grad_now + query_term(query_side, key_part, value_part, allowed, score_scale)

            updated.append(
                lax.cond(
                    jnp.any(allowed), add_term, lambda grad_now: grad_now, grad_parts[part_index]
                )
            )
        return ((updated[0], updated[1]), None)

    zero_part = jnp.zeros((half_rows, head_count, HEAD_DIM), jnp.float32)
    grad_parts, unused_out = lax.scan(
        query_step, (zero_part, zero_part), jnp.arange(members, dtype=jnp.int32)
    )
    grad_queries = jnp.concatenate(grad_parts, axis=0).reshape(tok_rows, model_width)
    first_row = jnp.int32(0)
    row_count = lax.axis_size("blk") * tok_rows
    key_part = heads_of(take_rows(whole_keys, first_row, row_count))
    value_part = heads_of(take_rows(whole_values, first_row, row_count))
    key_pos, key_doc = key_info(first_row, row_count)
    zero_keys = jnp.zeros((row_count, head_count, HEAD_DIM), jnp.float32)
    totals = (zero_keys, zero_keys)
    for part_index in range(2):
        query_side = local_parts[part_index]
        allowed = allowed_pairs(query_side[4], query_side[5], key_pos, key_doc)

        def add_terms(grad_now):
            grad_keys, grad_values = key_term(
                query_side, key_part, value_part, allowed, score_scale
            )
            return (grad_now[0] + grad_keys, grad_now[1] + grad_values)

        totals = lax.cond(jnp.any(allowed), add_terms, lambda grad_now: grad_now, totals)
    key_value_grads = lax.psum_scatter(
        jnp.concatenate(
            [totals[0].reshape(row_count, model_width), totals[1].reshape(row_count, model_width)],
            axis=1,
        ),
        "blk",
        scatter_dimension=0,
        tiled=True,
    )
    grad_keys = key_value_grads[:, :model_width]
    grad_values = key_value_grads[:, model_width:]
    query_out, pull_query = jax.vjp(scaled_norm, query_raw, s_qk)
    grad_query_raw, grad_qk_first = pull_query(grad_queries)
    key_out, pull_key = jax.vjp(scaled_norm, key_raw, s_qk)
    grad_key_raw, grad_qk_second = pull_key(grad_keys)
    grad_s_qk = grad_qk_first + grad_qk_second
    query_low = grad_query_raw.astype(jnp.bfloat16)
    key_low = grad_key_raw.astype(jnp.bfloat16)
    value_low = grad_values.astype(jnp.bfloat16)
    grad_w_query = jnp.dot(hidden.T, query_low, preferred_element_type=jnp.float32)
    grad_w_key = jnp.dot(hidden.T, key_low, preferred_element_type=jnp.float32)
    grad_w_value = jnp.dot(hidden.T, value_low, preferred_element_type=jnp.float32)
    input_grad = (
        grad_hidden
        + jnp.dot(query_low, w_query.T, preferred_element_type=jnp.float32)
        + jnp.dot(key_low, w_key.T, preferred_element_type=jnp.float32)
        + jnp.dot(value_low, w_value.T, preferred_element_type=jnp.float32)
    )
    summed = (
        lax.psum_scatter(grad_w_query, ("dp", "blk"), scatter_dimension=0, tiled=True),
        lax.psum_scatter(grad_w_key, ("dp", "blk"), scatter_dimension=0, tiled=True),
        lax.psum_scatter(grad_w_value, ("dp", "blk"), scatter_dimension=0, tiled=True),
        lax.psum_scatter(grad_w_out, ("dp", "blk"), scatter_dimension=0, tiled=True),
        lax.psum_scatter(grad_w_up, ("dp", "blk"), scatter_dimension=0, tiled=True),
        lax.psum_scatter(grad_w_gate, ("dp", "blk"), scatter_dimension=0, tiled=True),
        lax.psum_scatter(grad_w_down, ("dp", "blk"), scatter_dimension=0, tiled=True),
        lax.psum_scatter(grad_s_qk, ("dp", "blk"), scatter_dimension=0, tiled=True),
        lax.psum_scatter(grad_s_up, ("dp", "blk"), scatter_dimension=0, tiled=True),
        lax.psum_scatter(grad_s_gate, ("dp", "blk"), scatter_dimension=0, tiled=True),
        lax.psum_scatter(grad_alpha_attn, ("dp", "blk"), scatter_dimension=0, tiled=True),
        lax.psum_scatter(grad_alpha_mlp, ("dp", "blk"), scatter_dimension=0, tiled=True),
    )
    mean_alpha = 0.5 * (jnp.mean(alpha_attn) + jnp.mean(alpha_mlp))
    output = result.astype(jnp.bfloat16)[None, None]
    return (
        output,
        input_grad[None, None],
        summed[0],
        summed[1],
        summed[2],
        summed[3],
        summed[4],
        summed[5],
        summed[6],
        summed[7],
        summed[8],
        summed[9],
        summed[10],
        summed[11],
        mean_alpha,
    )


MESH = pl.DeviceIdType.MESH
VMEM_SPEC = pl.BlockSpec(memory_space=pltpu.VMEM)
VMEM_LIMIT = 62 << 20
GROUP = 16


def here():
    return lax.axis_index("dp"), lax.axis_index("blk")


def greet(partners):
    barrier = pltpu.get_barrier_semaphore()
    for partner in partners:
        pl.semaphore_signal(barrier, inc=1, device_id=partner, device_id_type=MESH)
    pl.semaphore_wait(barrier, len(partners))


def remote(src, dst, send_sem, recv_sem, device):
    return pltpu.make_async_remote_copy(
        src_ref=src,
        dst_ref=dst,
        send_sem=send_sem,
        recv_sem=recv_sem,
        device_id=device,
        device_id_type=MESH,
    )


class Gather:
    KINDS = 22

    def __init__(self, own, out, send, recv, pieces):
        self.own, self.out, self.send, self.recv = own, out, send, recv
        self.pieces = pieces
        dp, b = here()
        self.dp, self.b = dp, b
        self.z, self.y, self.c = b // 4, (b // 2) % 2, b % 2
        self.up = (dp, (b + 4) % GROUP)
        self.down = (dp, (b + 12) % GROUP)
        self.side = (dp, b + 2 - 4 * self.y)
        self.sib = (dp, b + 1 - 2 * self.c)
        self.half = self.pieces // 2

    def partners(self):
        return [self.up, self.down, self.side, self.sib]

    def copy(self, z, y, c, kind, piece, device, own=False):
        block = z * 4 + y * 2 + c
        upper = piece // self.half
        place = 2 * GROUP - 1 - block if upper else block
        rows = self.out.shape[1] // self.half
        span = pl.ds(piece % self.half * rows, rows)
        target = self.out.at[place, span]
        source = self.own.at[upper, span] if own else target
        index = self.pieces * kind + piece
        return remote(source, target, self.send.at[index], self.recv.at[index], device)

    def along(self, z, piece, device, own=False, back=False):
        return self.copy(z, self.y, self.c, z + (4 if back else 0), piece, device, own)

    def across(self, z, y, piece, own=False):
        return self.copy(z, y, self.c, 8 + z, piece, self.side, own)

    def over(self, z, piece, device, back=False):
        return self.copy(z, 1 - self.y, self.c, 21 if back else 20, piece, device)

    def to_sib(self, z, y, c, piece, own=False):
        return self.copy(z, y, c, 12 + 2 * z + y, piece, self.sib, own)

    def each_side(self, distance, action):
        if distance == 0:
            action(self.z, None)
            return
        low, high = self.z - distance, self.z + distance

        @pl.when(low >= 0)
        def _():
            action(low, False)

        @pl.when(high <= 3)
        def _():
            action(high, True)

    def start(self):
        for piece in range(self.pieces):

            @pl.when(self.z < 3)
            def _():
                self.along(self.z, piece, self.up, True).start()

            @pl.when(self.z > 0)
            def _():
                self.along(self.z, piece, self.down, True, True).start()

            self.across(self.z, self.y, piece, True).start()
        for piece in range(self.pieces):
            self.to_sib(self.z, self.y, self.c, piece, True).start()
        for upper in (0, 1):
            place = 2 * GROUP - 1 - self.b if upper else self.b
            self.out[place] = self.own[upper]

    def line(self, distance):
        def action(z, above):
            for piece in range(self.pieces):
                self.along(z, piece, self.sib, False, above).wait_recv()
                if above:

                    @pl.when(self.z > 0)
                    def _():
                        self.along(z, piece, self.down, False, True).start()
                else:

                    @pl.when(self.z < 3)
                    def _():
                        self.along(z, piece, self.up).start()

                if distance > 1 or piece < self.half:
                    self.across(z, self.y, piece).start()
                self.to_sib(z, self.y, self.c, piece).start()

        self.each_side(distance, action)

    def sides(self, distance):
        def action(z, above):
            for piece in range(self.pieces):
                if distance == 1 and piece >= self.half:
                    continue
                self.across(z, 1 - self.y, piece).wait_recv()
                self.to_sib(z, 1 - self.y, self.c, piece).start()

        self.each_side(distance, action)

    def hand_over(self):
        for piece in range(self.half, self.pieces):

            @pl.when(self.z < 3)
            def _():
                self.over(self.z, piece, self.up).start()

            @pl.when(self.z > 0)
            def _():
                self.over(self.z, piece, self.down, True).start()

    def handed(self):
        def action(z, above):
            for piece in range(self.half, self.pieces):
                self.over(z, piece, self.sib, above).wait_recv()
                self.to_sib(z, 1 - self.y, self.c, piece).start()

        self.each_side(1, action)

    def from_sib(self, distance):
        def action(z, above):
            for piece in range(self.pieces):
                for y in (0, 1):
                    self.to_sib(z, y, 1 - self.c, piece).wait_recv()

        self.each_side(distance, action)

    def drain(self):
        for piece in range(self.pieces):
            for z in range(4):
                for y in (0, 1):
                    self.to_sib(z, y, self.c, piece).wait_send()
                if piece < self.half:
                    self.across(z, self.y, piece).wait_send()
                else:

                    @pl.when((z > self.z + 1) | (z < self.z - 1) | (z == self.z))
                    def _():
                        self.across(z, self.y, piece).wait_send()

                @pl.when((self.z >= z) & (self.z < 3))
                def _():
                    self.along(z, piece, self.up).wait_send()

                @pl.when((self.z <= z) & (self.z > 0))
                def _():
                    self.along(z, piece, self.down, False, True).wait_send()

            if piece >= self.half:

                @pl.when(self.z < 3)
                def _():
                    self.over(self.z, piece, self.up).wait_send()

                @pl.when(self.z > 0)
                def _():
                    self.over(self.z, piece, self.down, True).wait_send()

    def finish(self):
        for distance in range(4):
            self.from_sib(distance)
        self.drain()


def gather_scratch(pieces):
    return [pltpu.SemaphoreType.DMA((pieces * Gather.KINDS,)) for _ in range(2)]


def comm_params(collective_id):
    return pltpu.CompilerParams(
        collective_id=collective_id, has_side_effects=True, vmem_limit_bytes=VMEM_LIMIT
    )


def dot_nt(left, right):
    return lax.dot_general(left, right, (((1,), (1,)), ((), ())), preferred_element_type=jnp.float32)


def dot_tn(left, right):
    return lax.dot_general(left, right, (((0,), (0,)), ((), ())), preferred_element_type=jnp.float32)


def dot_nn(left, right):
    return jnp.dot(left, right, preferred_element_type=jnp.float32)


FF_STEP = 1024


def mean_last(array):
    return jnp.mean(array, axis=-1, keepdims=True)


def rms_scale(array):
    return lax.rsqrt(mean_last(array * array) + 1e-06)


def rms_pull(grad, normed, scale):
    return scale * (grad - normed * mean_last(grad * normed))


def half_lanes(shape):
    return lax.broadcasted_iota(jnp.int32, shape, 1) < HEAD_DIM


FAR_FIRST = sorted(range(1, GROUP), key=lambda step: abs(step - GROUP // 2))


class Swap:
    def __init__(self, blocks, out, send, recv, own=True):
        self.blocks, self.out, self.own = blocks, out, own
        dp, self.b = here()
        self.copies = []
        for step in FAR_FIRST:
            target = (self.b + step) % GROUP
            self.copies.append(
                remote(
                    (blocks.block(target) if isinstance(blocks, SendBlocks) else blocks.at[target])
                    if own
                    else blocks,
                    out.at[self.b],
                    send.at[step],
                    recv.at[step],
                    (dp, target),
                )
            )
        self.partners = [(dp, (self.b + step) % GROUP) for step in range(1, GROUP)]

    def start(self):
        for copy in self.copies:
            copy.start()
        if self.own:
            mine = self.blocks
            mine = mine.block(self.b) if isinstance(mine, SendBlocks) else mine.at[self.b]
            self.out[self.b] = mine[...]

    def wait(self):
        for copy in self.copies:
            copy.wait()


ANY_SPEC = pl.BlockSpec(memory_space=pl.ANY)


SMEM_SPEC = pl.BlockSpec(memory_space=pltpu.SMEM)


def own_head(pair, core):
    shifted = jnp.where(core == 1, pltpu.roll(pair, HEAD_DIM, 1), pair)
    return jnp.where(half_lanes(pair.shape), shifted, 0.0)


def minus_ones(matrix):
    lane = lax.broadcasted_iota(jnp.int32, matrix.shape, 1)
    extra = jnp.where(lane < HEAD_DIM + 3, -1.0, 0.0)
    return jnp.where(lane < HEAD_DIM, matrix, extra).astype(jnp.bfloat16)


PROJECT_PIECES = 4


def doc_start_of(positions, lengths_ref):
    start = jnp.zeros_like(positions)
    end = jnp.int32(0)
    for doc in range(lengths_ref.shape[1]):
        end = end + lengths_ref[0, doc]
        start = start + jnp.where(positions >= end, lengths_ref[0, doc], 0)
    return start


def split_lanes(column, shape):
    lane = lax.broadcasted_iota(jnp.int32, shape, 1)
    high = column.astype(jnp.bfloat16).astype(jnp.float32)
    rest = column - high
    mid = rest.astype(jnp.bfloat16).astype(jnp.float32)
    last = rest - mid
    return jnp.where(
        lane == HEAD_DIM,
        high,
        jnp.where(lane == HEAD_DIM + 1, mid, jnp.where(lane == HEAD_DIM + 2, last, 0.0)),
    )


ATT = 512


TAIL_PIECES = 2
KEYS = 512
PART = 512


class SendBlocks:
    def __init__(self, ref, first_row, rows, first_lane, lanes):
        self.ref, self.first_row, self.rows = ref, first_row, rows
        self.lanes = pl.ds(first_lane, lanes)

    def block(self, index):
        start = pl.multiple_of(self.first_row + index * self.rows, self.rows)
        return self.ref.at[pl.ds(start, self.rows), self.lanes]


def layer_kernel(
    lengths_ref,
    hidden_own,
    cot_ref,
    s_qk_ref,
    s_up_ref,
    s_gate_ref,
    alpha_attn_ref,
    alpha_mlp_ref,
    w_out_hbm,
    w_up_hbm,
    w_gate_hbm,
    w_down_hbm,
    w_query_hbm,
    w_key_hbm,
    w_value_hbm,
    result_ref,
    input_grad_ref,
    wide_in,
    qkv_in,
    g_down_ref,
    out_in,
    g_s_ref,
    small_ref,
    hidden_hbm,
    mid_all,
    g_mlp_all,
    w_out,
    w_up,
    w_gate,
    w_down,
    up_slice,
    gate_slice,
    down_slice,
    up_raw,
    gate_raw,
    mid_own,
    g_mlp_own,
    o_in,
    g_send,
    g_in,
    acc,
    g_res,
    att_pair,
    branch_pair,
    out_got,
    out_side_got,
    ql_ref,
    ka_ref,
    va_ref,
    ga_ref,
    q_raw_ref,
    k_raw_ref,
    att_ref,
    o_ref,
    dq_acc,
    back_in,
    qkv_part,
    qkv_got,
    wide_own,
    wide_got,
    down_got,
    small_own,
    small_got,
    small_all,
    s_part,
    s_send,
    s_got,
    load_sems,
    x_sems,
    pair_sems,
    out_sems,
    swap_sems,
    grad_sems,
    back_sems,
    qkv_sems,
    wide_sems,
    small_sems,
    hid_send,
    hid_recv,
    mid_send,
    mid_recv,
    mlp_send,
    mlp_recv,
):
    low, f32 = jnp.bfloat16, jnp.float32
    dp, b = here()
    z, y, c = b // 4, (b // 2) % 2, b % 2
    twin, sib, side = (1 - dp, b), (dp, b + 1 - 2 * c), (dp, b + 2 - 4 * y)
    half, width = hidden_own.shape[1:]
    rows = 2 * half
    length = GROUP * rows
    ff = w_up.shape[1]
    ff_half = ff // 2
    part = ff // (2 * GROUP)
    quarter = width // 4
    rows_out = width // (2 * GROUP)
    blocks = length // ATT
    loaded = []

    def load(source, target):
        copy = pltpu.make_async_copy(source, target, load_sems.at[len(loaded)])
        copy.start()
        loaded.append(copy)
        return copy

    def to(device, sems, index, source, target):
        copy = remote(source, target, sems.at[0, index], sems.at[1, index], device)
        copy.start()
        return copy

    grad_swap = Swap(g_send, g_in, grad_sems.at[0], grad_sems.at[1])
    small_swap = Swap(small_own, small_all, small_sems.at[0], small_sems.at[1], own=False)
    gather_mid = Gather(mid_own, mid_all, mid_send, mid_recv, TAIL_PIECES)
    gather_mlp = Gather(g_mlp_own, g_mlp_all, mlp_send, mlp_recv, TAIL_PIECES)
    gather_hid = Gather(hidden_own, g_mlp_all, hid_send, hid_recv, PROJECT_PIECES)
    window = pl.ds(pl.multiple_of(b // 2 * 128, 128), 128)
    load_head = [
        load(w_query_hbm.at[:, window], up_slice.at[:, pl.ds(0, 128)]),
        load(w_key_hbm.at[:, window], up_slice.at[:, pl.ds(128, 128)]),
        load(w_value_hbm.at[:, window], gate_slice.at[:, pl.ds(0, 128)]),
    ]
    greet(grad_swap.partners + [twin])
    gather_hid.start()
    load_out = load(w_out_hbm, w_out)
    load_mlp = [load(w_up_hbm, w_up), load(w_gate_hbm, w_gate), load(w_down_hbm, w_down)]

    gain = own_head(jnp.broadcast_to(s_qk_ref[:, window], (8, 128)), c)[:1]
    count = float(HEAD_DIM)
    score_scale = 1.0 / math.sqrt(HEAD_DIM)
    line_slots = 2 * GROUP // 8
    for copy in load_head:
        copy.wait()

    def project(first_slot):
        some = g_mlp_all[pl.ds(first_slot, line_slots)].reshape(line_slots * half, width)
        span = pl.ds(pl.multiple_of(first_slot * half, half), line_slots * half)
        query_key = dot_nn(some, up_slice[...])
        query = own_head(query_key[:, :128], c)
        key = own_head(query_key[:, 128:], c)
        value = own_head(dot_nn(some, gate_slice[:, :128]), c)
        q_raw_ref[span, :] = query.astype(low)
        k_raw_ref[span, :] = key.astype(low)
        query_scale = lax.rsqrt(jnp.sum(query * query, axis=1, keepdims=True) / count + 1e-06)
        key_scale = lax.rsqrt(jnp.sum(key * key, axis=1, keepdims=True) / count + 1e-06)
        query = (query * query_scale * gain).astype(low).astype(f32)
        ql_ref[span, :] = (query * score_scale).astype(low)
        ka_ref[span, :] = minus_ones(key * key_scale * gain)
        va_ref[span, :] = minus_ones(value)

    def project_line(distance):
        def both(line, above):
            project(line_slots * line)
            project(2 * GROUP - line_slots - line_slots * line)

        gather_hid.each_side(distance, both)

    gather_hid.line(1)
    gather_hid.sides(0)
    gather_hid.from_sib(0)
    project_line(0)
    gather_hid.line(2)
    gather_hid.hand_over()
    gather_hid.sides(1)
    gather_hid.line(3)
    gather_hid.sides(2)
    gather_hid.from_sib(2)
    project_line(2)
    gather_hid.handed()
    gather_hid.from_sib(1)
    project_line(1)
    gather_hid.sides(3)
    gather_hid.from_sib(3)
    project_line(3)
    gather_hid.drain()
    store_hidden = [
        load(g_mlp_all.at[slot], hidden_hbm.at[pl.ds(slot * half, half), :])
        for slot in range(2 * GROUP)
    ]
    load_slices = []
    windows = [pl.ds(pl.multiple_of(p * ff_half + b * part, part), part) for p in (0, 1)]
    for p in (0, 1):
        place = pl.ds(p * part, part)
        load_slices.append(load(w_up_hbm.at[:, windows[p]], up_slice.at[:, place]))
        load_slices.append(load(w_gate_hbm.at[:, windows[p]], gate_slice.at[:, place]))
        load_slices.append(load(w_down_hbm.at[windows[p], :], down_slice.at[place, :]))

    query_row_pos = lax.broadcasted_iota(jnp.int32, (ATT, ATT), 0)
    key_lane = lax.broadcasted_iota(jnp.int32, (ATT, ATT), 1)
    wide_first = half_lanes((ATT, 128))
    def o_copy(target):
        return remote(
            o_ref.at[target],
            o_in.at[b],
            swap_sems.at[0, target],
            swap_sems.at[1, b],
            (dp, target),
        )

    first = half_lanes((half, 128))
    for query_block in (1, 2, 0, 3):
        span = pl.ds(query_block * ATT, ATT)
        queries = ql_ref[span, :]
        column = query_block * ATT + lax.broadcasted_iota(jnp.int32, (ATT, 1), 0)
        doc_start = doc_start_of(column, lengths_ref)
        total = jnp.zeros((ATT, 128), f32)
        for key_block in range(query_block + 1):
            base = key_block * ATT
            keys = ka_ref[pl.ds(base, ATT), :]
            values = va_ref[pl.ds(base, ATT), :]
            allowed = base + key_lane >= doc_start
            if key_block == query_block:
                allowed = allowed & (key_lane <= query_row_pos)
            weights = jnp.where(allowed, jnp.exp(dot_nt(queries, keys)), 0.0)
            total = total + dot_nn(weights.astype(low), values)
        row_sum = -total[:, HEAD_DIM : HEAD_DIM + 1]
        att_ref[span, :] = jnp.where(wide_first, total / row_sum, 0.0).astype(low)
        extra = split_lanes(jnp.log(row_sum), total.shape)
        ql_ref[span, :] = jnp.where(wide_first, queries.astype(f32), extra).astype(low)
        if query_block not in (2, 3):
            continue
        if query_block == 2:
            for copy in store_hidden:
                copy.wait()
        for j in range(GROUP // 2, GROUP) if query_block == 2 else range(GROUP // 2):
            lower = att_ref[j * half : (j + 1) * half, :].astype(f32)
            upper = att_ref[length - (j + 1) * half : length - j * half, :].astype(f32)
            o_ref[j] = jnp.where(first, lower, pltpu.roll(upper, HEAD_DIM, 1)).astype(low)

            @pl.when(j != b)
            def _():
                o_copy(j).start()

            @pl.when(j == b)
            def _():
                o_in[b] = o_ref[b]

    for other in range(GROUP):

        @pl.when(other != b)
        def _():
            copy = remote(
                o_ref.at[other],
                o_in.at[other],
                swap_sems.at[0, other],
                swap_sems.at[1, other],
                sib,
            )
            copy.wait_send()
            copy.wait_recv()

    for pair in range(GROUP // 2):
        even = o_in[2 * pair].astype(f32)
        odd = o_in[2 * pair + 1].astype(f32)
        lanes = slice(pair * 128, (pair + 1) * 128)
        att_pair[c, :half, lanes] = jnp.where(first, even, pltpu.roll(odd, HEAD_DIM, 1)).astype(low)
        att_pair[c, half:, lanes] = jnp.where(first, pltpu.roll(even, HEAD_DIM, 1), odd).astype(low)
    att_copy = to(sib, pair_sems, 0, att_pair.at[c], att_pair.at[c])
    hidden = hidden_own[...].reshape(rows, width).astype(f32)
    alpha_attn = alpha_attn_ref[...]
    alpha_mlp = alpha_mlp_ref[...]
    load_out.wait()
    branch = dot_nn(att_pair[c], w_out[...])
    branch_scale = rms_scale(branch)
    branch_normed = branch * branch_scale
    mixed = hidden + alpha_attn * (branch_normed - hidden)
    middle_scale = rms_scale(mixed)
    middle = mixed * middle_scale
    middle_low = middle.astype(low)
    mid_own[0] = middle_low[:half]
    mid_own[1] = middle_low[half:]
    gather_mid.start()
    for copy in load_mlp:
        copy.wait()
    steps = ff // FF_STEP
    acc[...] = jnp.zeros_like(acc)

    def forward(step):
        cols = pl.ds(step * FF_STEP, FF_STEP)
        up = dot_nn(middle_low, w_up[:, cols])
        gate = dot_nn(middle_low, w_gate[:, cols])
        up_raw[:, cols] = up
        gate_raw[:, cols] = gate
        scaled = gate * s_gate_ref[:, cols]
        inner = up * s_up_ref[:, cols] * (scaled / (1.0 + jnp.exp(-scaled)))
        acc[...] += dot_nn(inner.astype(low), w_down[cols, :])

    for step in range(steps):
        forward(step)
    gather_mid.line(1)
    gather_mid.sides(0)
    mlp = acc[...]
    mlp_scale = rms_scale(mlp)
    mlp_normed = mlp * mlp_scale
    mixed_out = middle + alpha_mlp * (mlp_normed - middle)
    out_scale = rms_scale(mixed_out)
    result = mixed_out * out_scale
    result_ref[...] = result.astype(low)

    g_mixed = rms_pull(cot_ref[...].astype(f32), result, out_scale)
    g_alpha_mlp = jnp.sum(g_mixed * (mlp_normed - middle), axis=0, keepdims=True)
    small_own[...] = jnp.zeros_like(small_own)
    for i in range(width // 128):
        small_own[8 + i : 9 + i, :] = g_alpha_mlp[:, 128 * i : 128 * (i + 1)]
    g_mlp = rms_pull(g_mixed * alpha_mlp, mlp_normed, mlp_scale).astype(low)
    g_mlp_own[0] = g_mlp[:half]
    g_mlp_own[1] = g_mlp[half:]
    gather_mlp.start()
    acc[...] = g_mixed * (1.0 - alpha_mlp)

    def backward(step):
        cols = pl.ds(step * FF_STEP, FF_STEP)
        g_inner = dot_nt(g_mlp, w_down[cols, :])
        s_up = s_up_ref[:, cols]
        s_gate = s_gate_ref[:, cols]
        scaled = gate_raw[:, cols] * s_gate
        sigmoid = 1.0 / (1.0 + jnp.exp(-scaled))
        g_up = g_inner * (scaled / (1.0 + jnp.exp(-scaled))) * s_up
        slope = sigmoid * (1.0 + scaled * (1.0 - sigmoid))
        g_gate = g_inner * (up_raw[:, cols] * s_up) * slope * s_gate
        acc[...] += dot_nt(g_up.astype(low), w_up[:, cols]) + dot_nt(
            g_gate.astype(low), w_gate[:, cols]
        )

    for step in range(steps // 2):
        backward(step)
    gather_mid.line(2)
    gather_mid.hand_over()
    gather_mid.sides(1)
    for step in range(steps // 2, steps):
        backward(step)
    g_pre = rms_pull(acc[...], middle, middle_scale)
    g_res[...] = g_pre * (1.0 - alpha_attn)
    g_alpha_attn = jnp.sum(g_pre * (branch_normed - hidden), axis=0, keepdims=True)
    for i in range(width // 128):
        small_own[i : i + 1, :] = g_alpha_attn[:, 128 * i : 128 * (i + 1)]
    branch_pair[c] = rms_pull(g_pre * alpha_attn, branch_normed, branch_scale).astype(low)
    g_att = dot_nt(branch_pair[c], w_out[...]).astype(low).astype(f32)
    for pair in range(GROUP // 2):
        lower = g_att[:half, pair * 128 : (pair + 1) * 128]
        upper = g_att[half:, pair * 128 : (pair + 1) * 128]
        g_send[2 * pair] = jnp.where(first, lower, pltpu.roll(upper, HEAD_DIM, 1)).astype(low)
        g_send[2 * pair + 1] = jnp.where(first, pltpu.roll(lower, HEAD_DIM, 1), upper).astype(low)
    grad_swap.start()
    branch_copy = to(sib, pair_sems, 1, branch_pair.at[c], branch_pair.at[c])

    g_cat = w_down.at[pl.ds(0, length), pl.ds(0, 4 * part)]
    inner_all = w_down.at[pl.ds(0, length), pl.ds(512, 2 * part)]
    raw_low = w_down.at[pl.ds(length, length), pl.ds(0, 384)]
    w_qkv = [w_up.at[:, pl.ds(i * width, width)] for i in range(3)]
    home = [w_up.at[pl.ds(i * rows, rows), pl.ds(3 * width, width)] for i in range(3)]
    out_send = w_out.at[pl.ds(0, quarter), :]
    out_side_send = [w_out.at[pl.ds(quarter + half * k, half), :] for k in (0, 1)]
    out_line = w_out.at[pl.ds(2 * quarter, 4 * rows_out), :]
    down_send = w_out.at[pl.ds(3 * quarter, part), :]
    out_own = [up_raw.at[:, pl.ds((2 + k) * width, width)] for k in (0, 1)]
    wide_send = [w_gate.at[pl.ds(quarter * i, quarter), pl.ds(2048, 512)] for i in (0, 1)]
    qkv_send = w_gate.at[pl.ds(0, 2 * quarter), pl.ds(2560, 256)]
    back_send = SendBlocks(w_gate, 0, half, 2816, 384)
    qkv_blocks = SendBlocks(w_gate, 2 * quarter, rows_out, 2560, 256)
    wide_blocks = SendBlocks(w_gate, 2 * quarter, rows_out, 2048, 512)
    back_swap = Swap(back_send, back_in, back_sems.at[0], back_sems.at[1])
    qkv_swap = Swap(qkv_blocks, qkv_in, qkv_sems.at[0], qkv_sems.at[1])
    tokens_of_half = [w_gate.at[:, pl.ds(i * width, width)] for i in (0, 1)]
    load_hidden = [
        load(hidden_hbm.at[pl.ds(i * width, width), :], tokens_of_half[i]) for i in (0, 1)
    ]
    load_qkv = [
        load(source, w_qkv[i]) for i, source in enumerate((w_query_hbm, w_key_hbm, w_value_hbm))
    ]
    gather_mid.line(3)
    gather_mid.sides(2)
    gather_mlp.line(1)
    gather_mlp.sides(0)

    att_copy.wait()
    branch_copy.wait()
    both_branch = branch_pair[...].reshape(2 * rows, width)

    def out_rows(owner):
        lanes = pl.ds(pl.multiple_of(owner * 2 * quarter + c * quarter, quarter), quarter)
        return dot_tn(att_pair[:, :, lanes].reshape(2 * rows, quarter), both_branch)

    out_send[...] = out_rows(1 - dp).astype(low)
    out_copy = to(twin, x_sems, 0, out_send, out_got)
    out_mine = out_rows(dp)
    for k in (0, 1):
        out_own[k][...] = out_mine[2 * half * k : 2 * half * (k + 1)]
    gather_mid.handed()
    gather_mid.sides(3)

    grad_swap.wait()
    for j in range(GROUP):
        block = g_in[j].astype(f32)
        for start, grads in (
            (j * half, jnp.where(first, block, 0.0)),
            (length - (j + 1) * half, jnp.where(first, pltpu.roll(block, HEAD_DIM, 1), 0.0)),
        ):
            span = pl.ds(start, half)
            delta = jnp.sum(grads * att_ref[span, :].astype(f32), axis=1, keepdims=True)
            ga_ref[span, :] = (grads + split_lanes(delta, grads.shape)).astype(low)
    dq_acc[...] = jnp.zeros_like(dq_acc)
    key_row = lax.broadcasted_iota(jnp.int32, (KEYS, ATT), 0)
    query_lane = lax.broadcasted_iota(jnp.int32, (KEYS, ATT), 1)
    query_row = lax.broadcasted_iota(jnp.int32, (1, ATT), 1)

    def norm_pull(raw, grad):
        raw = raw.astype(f32)
        scale = lax.rsqrt(jnp.sum(raw * raw, axis=1, keepdims=True) / count + 1e-06)
        normed = raw * scale
        g_gain = jnp.sum(grad * normed, axis=0, keepdims=True)
        inside = grad * gain
        mean = jnp.sum(inside * normed, axis=1, keepdims=True) / count
        return scale * (inside - normed * mean), g_gain

    key_first = half_lanes((KEYS, 128))

    def pair_grads(keys, values, key_block, query_block):
        base = query_block * ATT
        queries = ql_ref[pl.ds(base, ATT), :]
        grads = ga_ref[pl.ds(base, ATT), :]
        key_pos = key_block * KEYS + key_row
        allowed = key_pos >= doc_start_of(base + query_row, lengths_ref)
        if key_block * KEYS + KEYS > base:
            allowed = allowed & (key_pos <= base + query_lane)
        weights = jnp.where(allowed, jnp.exp(dot_nt(keys, queries)), 0.0)
        slopes = (weights * dot_nt(values, grads)).astype(low)
        dq_acc[pl.ds(base, ATT), :] += dot_tn(slopes, keys)
        return dot_nn(slopes, queries), dot_nn(weights.astype(low), grads)

    g_gain = jnp.zeros((1, 128), f32)
    for key_block in range(length // KEYS):
        span = pl.ds(key_block * KEYS, KEYS)
        keys = ka_ref[span, :]
        values = va_ref[span, :]
        dk, dv = 0.0, 0.0
        for query_block in range(key_block * KEYS // ATT, blocks):
            more_k, more_v = pair_grads(keys, values, key_block, query_block)
            dk, dv = dk + more_k, dv + more_v
        g_key, key_gain = norm_pull(k_raw_ref[span, :], jnp.where(key_first, dk, 0.0))
        g_gain = g_gain + key_gain
        raw_low[span, 128:256] = g_key.astype(low)
        raw_low[span, 256:384] = jnp.where(key_first, dv, 0.0).astype(low)
        if key_block == 0:
            gather_mlp.line(2)
            gather_mlp.hand_over()
            gather_mlp.sides(1)
        if key_block == 2:
            gather_mlp.line(3)
            gather_mlp.sides(2)
    for block in range(blocks):
        span = pl.ds(block * ATT, ATT)
        dq = jnp.where(wide_first, dq_acc[span, :] * score_scale, 0.0)
        g_query, query_gain = norm_pull(q_raw_ref[span, :], dq)
        g_gain = g_gain + query_gain
        raw_low[span, 0:128] = g_query.astype(low)
    for j in range(GROUP):
        for i in range(3):
            lanes = slice(128 * i, 128 * (i + 1))
            lower = raw_low[j * half : (j + 1) * half, lanes].astype(f32)
            upper = raw_low[length - (j + 1) * half : length - j * half, lanes].astype(f32)
            back_send.block(j)[:, lanes] = jnp.where(
                first, lower, pltpu.roll(upper, HEAD_DIM, 1)
            ).astype(low)
    back_swap.start()

    small_own[16:17, :] = g_gain
    small_copy = to(twin, x_sems, 1, small_own, small_got)

    for copy in load_hidden:
        copy.wait()

    def qkv_chunk(chunk):
        lanes = pl.ds(pl.multiple_of(chunk * quarter, quarter), quarter)
        grads = sum(
            dot_tn(tokens_of_half[i][:, lanes], raw_low[pl.ds(i * width, width), :]) for i in (0, 1)
        )
        query_key = jnp.where(
            half_lanes((quarter, 128)), grads[:, :128], pltpu.roll(grads[:, 128:256], HEAD_DIM, 1)
        )
        return query_key, grads[:, 256:]

    for i in (0, 1):
        query_key, value = qkv_chunk(2 * (1 - dp) + i)
        span = slice(quarter * i, quarter * (i + 1))
        qkv_send[span, :128] = query_key.astype(low)
        qkv_send[span, 128:] = value.astype(low)
    qkv_copy = to(twin, x_sems, 2, qkv_send, qkv_got)
    for i in (0, 1):
        query_key, value = qkv_chunk(2 * dp + i)
        span = slice(quarter * i, quarter * (i + 1))
        qkv_part[span, :128] = query_key
        qkv_part[span, 128:] = value

    out_copy.wait()
    side_copies = []
    for k in (0, 1):
        out_own[k][...] += out_got[2 * half * k : 2 * half * (k + 1)].astype(f32)
        other = pl.ds(pl.multiple_of((1 - y) * half, half), half)
        out_side_send[k][...] = out_own[k][other, :].astype(low)
        side_copies.append(to(side, pair_sems, 2 + k, out_side_send[k], out_side_got.at[k]))
    small_copy.wait()
    small_own[...] += small_got[...]
    small_swap.start()
    gather_mid.finish()
    gather_mlp.handed()
    gather_mlp.sides(3)
    gather_mlp.finish()

    for copy in load_slices:
        copy.wait()
    s_up = jnp.concatenate([s_up_ref[:, window] for window in windows], axis=1)
    s_gate = jnp.concatenate([s_gate_ref[:, window] for window in windows], axis=1)
    slots = PART // half

    def tokens_of(array, step):
        return array[pl.ds(step * slots, slots)].reshape(PART, width)

    def recompute(step, sums):
        span = pl.ds(pl.multiple_of(step * PART, PART), PART)
        some = tokens_of(mid_all, step)
        up = dot_nn(some, up_slice[...])
        gate = dot_nn(some, gate_slice[...])
        g_inner = dot_nt(tokens_of(g_mlp_all, step), down_slice[...])
        scaled = gate * s_gate
        sigmoid = 1.0 / (1.0 + jnp.exp(-scaled))
        silu = scaled / (1.0 + jnp.exp(-scaled))
        up_scaled = up * s_up
        inner_all[span, :] = (up_scaled * silu).astype(low)
        g_up_scaled = g_inner * silu
        g_scaled = g_inner * up_scaled * (sigmoid * (1.0 + scaled * (1.0 - sigmoid)))
        g_cat[span, : 2 * part] = (g_up_scaled * s_up).astype(low)
        g_cat[span, 2 * part :] = (g_scaled * s_gate).astype(low)
        return (
            sums[0] + jnp.sum(g_up_scaled * up, axis=0, keepdims=True),
            sums[1] + jnp.sum(g_scaled * gate, axis=0, keepdims=True),
        )

    zero_row = jnp.zeros((1, 2 * part), f32)
    g_s_up, g_s_gate = lax.fori_loop(0, length // PART, recompute, (zero_row, zero_row))

    line_rows_of = 4 * rows_out
    turns = ((0, 3), (1, 2))

    def wide_chunk(owner, turn):
        tokens = [
            mid_all[
                :,
                :,
                pl.ds(
                    pl.multiple_of(owner * 2 * quarter + line * line_rows_of, line_rows_of),
                    line_rows_of,
                ),
            ].reshape(length, line_rows_of)
            for line in turns[turn]
        ]
        return dot_tn(jnp.concatenate(tokens, axis=1), g_cat[...])

    wide_copies = []
    for i in (0, 1):
        wide_send[i][...] = wide_chunk(1 - dp, i).astype(low)
        wide_copies.append(to(twin, x_sems, 3 + i, wide_send[i], wide_got.at[i]))
    for p in (0, 1):
        s_part[p] = jnp.zeros(s_part.shape[1:], f32)
        s_part[p, 0:1, :] = g_s_up[:, p * part : (p + 1) * part]
        s_part[p, 1:2, :] = g_s_gate[:, p * part : (p + 1) * part]
    s_send[...] = s_part[1 - dp]
    s_copy = to(twin, x_sems, 5, s_send, s_got)
    for chunk in range(4):
        lanes = pl.ds(chunk * quarter, quarter)
        grads = dot_tn(inner_all[...], g_mlp_all[:, :, lanes].reshape(length, quarter))
        for p in (0, 1):
            place = slice(p * width + chunk * quarter, p * width + (chunk + 1) * quarter)
            up_raw[:, place] = grads[p * part : (p + 1) * part]
    down_other = pl.ds(pl.multiple_of((1 - dp) * width, width), width)
    down_mine = pl.ds(pl.multiple_of(dp * width, width), width)
    down_send[...] = up_raw[:, down_other].astype(low)
    down_copy = to(twin, x_sems, 6, down_send, down_got)

    qkv_copy.wait()
    per_chunk = quarter // rows_out
    total = (qkv_part[...] + qkv_got[...].astype(f32)).astype(low)
    for k in range(GROUP):
        qkv_blocks.block(k)[...] = total[k * rows_out : (k + 1) * rows_out]
    qkv_swap.start()
    for copy in side_copies:
        copy.wait()
    out_copies = []
    for k in (0, 1):
        mine = pl.ds(pl.multiple_of(y * half, half), half)
        total = (out_own[k][mine, :] + out_side_got[k].astype(f32)).astype(low)
        out_line[2 * rows_out * k : 2 * rows_out * (k + 1), :] = total
        for core in (0, 1):
            line_rows = pl.ds((2 * k + core) * rows_out, rows_out)
            target = (2 * c + k) * 4 + 2 * y + core
            index = 2 * k + core
            copy = remote(
                out_line.at[line_rows],
                out_in.at[z],
                out_sems.at[0, index],
                out_sems.at[1, z],
                (dp, target),
            )
            out_copies.append((target, copy))

            @pl.when(target != b)
            def _():
                copy.start()

            @pl.when(target == b)
            def _():
                out_in[z] = out_line[line_rows, :]

    def wide_copy(target):
        return remote(
            wide_blocks.block(target),
            wide_in.at[b],
            wide_sems.at[0, target],
            wide_sems.at[1, b],
            (dp, target),
        )

    for i in (0, 1):
        wide_own[...] = wide_chunk(dp, i)
        wide_copies[i].wait()
        total = (wide_own[...] + wide_got[i].astype(f32)).astype(low)
        for k in range(per_chunk):
            target = 4 * turns[i][k // 4] + k % 4
            wide_blocks.block(target)[...] = total[k * rows_out : (k + 1) * rows_out]

            @pl.when(target != b)
            def _():
                wide_copy(target).start()

            @pl.when(target == b)
            def _():
                wide_in[b] = wide_blocks.block(target)[...]

    for copy in load_qkv:
        copy.wait()
    back_swap.wait()
    for pair in range(GROUP // 2):
        for i in range(3):
            lanes = slice(128 * i, 128 * (i + 1))
            even = back_in[2 * pair, :, lanes].astype(f32)
            odd = back_in[2 * pair + 1, :, lanes].astype(f32)
            place = slice(128 * pair, 128 * (pair + 1))
            home[i][:half, place] = jnp.where(first, even, pltpu.roll(odd, HEAD_DIM, 1)).astype(low)
            home[i][half:, place] = jnp.where(first, pltpu.roll(even, HEAD_DIM, 1), odd).astype(low)
    input_grad_ref[...] = (
        g_res[...]
        + dot_nt(home[0][...], w_qkv[0][...])
        + dot_nt(home[1][...], w_qkv[1][...])
        + dot_nt(home[2][...], w_qkv[2][...])
    )
    s_copy.wait()
    g_s_ref[...] = s_part[dp] + s_got[...]
    down_copy.wait()
    g_down_ref[...] = up_raw[:, down_mine] + down_got[...].astype(f32)
    small_swap.wait()
    small_all[b] = small_own[...]
    small_ref[...] = jnp.sum(small_all[...], axis=0)
    small_ref[17:18, :] = small_all[8 * dp + b // 2, 16:17, :]
    qkv_swap.wait()
    for target, copy in out_copies:

        @pl.when(target != b)
        def _():
            copy.wait_send()

    for source_z in range(4):
        source = source_z * 4 + 2 * y + z // 2

        @pl.when(source != b)
        def _():
            remote(
                out_line.at[pl.ds(0, rows_out)],
                out_in.at[source_z],
                out_sems.at[0, 0],
                out_sems.at[1, source_z],
                sib,
            ).wait_recv()

    for other in range(GROUP):

        @pl.when(other != b)
        def _():
            copy = remote(
                wide_blocks.block(other),
                wide_in.at[other],
                wide_sems.at[0, other],
                wide_sems.at[1, other],
                sib,
            )
            copy.wait_send()
            copy.wait_recv()


def layer_block(vmem_inputs, hbm_inputs):
    low, f32 = jnp.bfloat16, jnp.float32
    shape, vmem, sems = jax.ShapeDtypeStruct, pltpu.VMEM, pltpu.SemaphoreType.DMA
    hidden = vmem_inputs[1]
    w_out, w_up, w_gate, w_down = hbm_inputs[:4]
    half, width = hidden.shape[1:]
    rows = 2 * half
    ff = w_up.shape[1]
    length = GROUP * rows
    rows_out = width // (2 * GROUP)
    part = ff // (2 * GROUP)
    quarter = width // 4
    packed = (GROUP, half, 128)
    return pl.pallas_call(
        layer_kernel,
        out_shape=[
            shape((rows, width), low),
            shape((rows, width), f32),
            shape((GROUP, rows_out, 4 * part), low),
            shape((GROUP, rows_out, 256), low),
            shape((part, width), f32),
            shape((4, rows_out, width), low),
            shape((8, 128), f32),
            shape((24, 128), f32),
            shape((length, width), low),
        ],
        in_specs=[SMEM_SPEC]
        + [VMEM_SPEC] * (len(vmem_inputs) - 1)
        + [ANY_SPEC] * len(hbm_inputs),
        out_specs=[VMEM_SPEC] * 8 + [ANY_SPEC],
        scratch_shapes=[
            vmem((2 * GROUP, half, width), low),
            vmem((2 * GROUP, half, width), low),
            vmem(w_out.shape, low),
            vmem(w_up.shape, low),
            vmem(w_gate.shape, low),
            vmem(w_down.shape, low),
            vmem((width, 2 * part), low),
            vmem((width, 2 * part), low),
            vmem((2 * part, width), low),
            vmem((rows, ff), f32),
            vmem((rows, ff), f32),
            vmem((2, half, width), low),
            vmem((2, half, width), low),
            vmem(packed, low),
            vmem(packed, low),
            vmem(packed, low),
            vmem((rows, width), f32),
            vmem((rows, width), f32),
            vmem((2, rows, width), low),
            vmem((2, rows, width), low),
            vmem((quarter, width), low),
            vmem((2, half, width), low),
            vmem((length, 128), low),
            vmem((length, 128), low),
            vmem((length, 128), low),
            vmem((length, 128), low),
            vmem((length, 128), low),
            vmem((length, 128), low),
            vmem((length, 128), low),
            vmem(packed, low),
            vmem((length, 128), f32),
            vmem((GROUP, half, 384), low),
            vmem((2 * quarter, 256), f32),
            vmem((2 * quarter, 256), low),
            vmem((quarter, 4 * part), f32),
            vmem((2, quarter, 4 * part), low),
            vmem((part, width), low),
            vmem((24, 128), f32),
            vmem((24, 128), f32),
            vmem((GROUP, 24, 128), f32),
            vmem((2, 8, 128), f32),
            vmem((8, 128), f32),
            vmem((8, 128), f32),
            sems((64,)),
            sems((2, 8)),
            sems((2, 4)),
            sems((2, 4)),
            sems((2, GROUP)),
            sems((2, GROUP)),
            sems((2, GROUP)),
            sems((2, GROUP)),
            sems((2, GROUP)),
            sems((2, GROUP)),
        ]
        + gather_scratch(PROJECT_PIECES)
        + gather_scratch(TAIL_PIECES)
        + gather_scratch(TAIL_PIECES),
        compiler_params=comm_params(1),
        name="layer_block",
    )(*vmem_inputs, *hbm_inputs)


def assemble_kernel(
    result,
    input_grad,
    wide_in,
    qkv_in,
    down,
    out_in,
    scales,
    small,
    alpha_attn,
    alpha_mlp,
    output_ref,
    input_grad_ref,
    g_query_ref,
    g_key_ref,
    g_value_ref,
    g_out_ref,
    g_up_ref,
    g_gate_ref,
    g_down_ref,
    gain_ref,
    s_up_ref,
    s_gate_ref,
    g_alpha_attn_ref,
    g_alpha_mlp_ref,
    mean_ref,
):
    f32 = jnp.float32
    dp, b = here()
    output_ref[...] = result[...]
    input_grad_ref[...] = input_grad[...]
    g_down_ref[...] = down[...]
    s_up_ref[...] = scales[0:1, :]
    s_gate_ref[...] = scales[1:2, :]
    rows_out = g_out_ref.shape[0]
    per_row = 128 // rows_out
    device = dp * GROUP + b

    def own_lanes(row, place):
        start = (128 - rows_out * place) % 128
        return pltpu.roll(jnp.broadcast_to(row, (8, 128)), start, 1)[:1, :rows_out]

    place = device % per_row
    g_alpha_attn_ref[...] = own_lanes(small[pl.ds(device // per_row, 1), :], place)
    g_alpha_mlp_ref[...] = own_lanes(small[pl.ds(8 + device // per_row, 1), :], place)
    gain_ref[...] = own_lanes(small[17:18, :], b % 2)
    mean_ref[...] = 0.5 * (mean_last(alpha_attn[...]) + mean_last(alpha_mlp[...]))
    g_out_ref[...] = sum(out_in[i].astype(f32) for i in range(4))
    part = wide_in.shape[2] // 4
    ff_half = g_up_ref.shape[1] // 2
    for j in range(GROUP):
        for p in (0, 1):
            place = slice(p * ff_half + j * part, p * ff_half + (j + 1) * part)
            g_up_ref[:, place] = wide_in[j, :, p * part : (p + 1) * part].astype(f32)
            g_gate_ref[:, place] = wide_in[j, :, (2 + p) * part : (3 + p) * part].astype(f32)
    first = half_lanes((g_query_ref.shape[0], 128))
    for pair in range(GROUP // 2):
        place = slice(128 * pair, 128 * (pair + 1))
        even, odd = qkv_in[2 * pair].astype(f32), qkv_in[2 * pair + 1].astype(f32)
        even_qk, odd_qk = even[:, :128], odd[:, :128]
        g_query_ref[:, place] = jnp.where(first, even_qk, pltpu.roll(odd_qk, HEAD_DIM, 1))
        g_key_ref[:, place] = jnp.where(first, pltpu.roll(even_qk, HEAD_DIM, 1), odd_qk)
        g_value_ref[:, place] = jnp.where(
            first, even[:, 128:], pltpu.roll(odd[:, 128:], HEAD_DIM, 1)
        )


def assemble_block(inputs, ff):
    result, input_grad, wide_in, qkv_in, down, out_in = inputs[:6]
    f32 = jnp.float32
    shape = jax.ShapeDtypeStruct
    width = result.shape[1]
    rows_out = wide_in.shape[1]
    return pl.pallas_call(
        assemble_kernel,
        out_shape=[
            shape(result.shape, result.dtype),
            shape(input_grad.shape, f32),
            shape((rows_out, width), f32),
            shape((rows_out, width), f32),
            shape((rows_out, width), f32),
            shape((rows_out, width), f32),
            shape((rows_out, ff), f32),
            shape((rows_out, ff), f32),
            shape(down.shape, f32),
            shape((1, rows_out), f32),
            shape((1, 128), f32),
            shape((1, 128), f32),
            shape((1, rows_out), f32),
            shape((1, rows_out), f32),
            shape((1, 1), f32),
        ],
        in_specs=[VMEM_SPEC] * len(inputs),
        out_specs=[VMEM_SPEC] * 15,
        compiler_params=pltpu.CompilerParams(vmem_limit_bytes=VMEM_LIMIT),
        name="assemble_block",
    )(*inputs)


def on_device_heads(
    tokens,
    cotangent,
    lengths,
    w_query,
    w_key,
    w_value,
    w_out,
    w_up,
    w_gate,
    w_down,
    s_qk,
    s_up,
    s_gate,
    alpha_attn,
    alpha_mlp,
):
    model_width = w_query.shape[0]
    tok_rows = tokens.shape[2]
    half_rows = tok_rows // 2
    hidden = tokens[0, 0]
    (result, input_grad, wide_in, qkv_in, grad_down, out_in, grad_scales, small, _) = layer_block(
        (
            lengths,
            hidden.reshape(2, half_rows, model_width),
            cotangent[0, 0],
            s_qk[None],
            s_up[None],
            s_gate[None],
            alpha_attn[None],
            alpha_mlp[None],
        ),
        (w_out, w_up, w_gate, w_down, w_query, w_key, w_value),
    )
    (
        output,
        input_grad,
        grad_query,
        grad_key,
        grad_value,
        grad_out,
        grad_up,
        grad_gate,
        grad_down,
        grad_gain,
        grad_up_scale,
        grad_gate_scale,
        grad_attn,
        grad_mlp_alpha,
        mean_alpha,
    ) = assemble_block(
        (
            result,
            input_grad,
            wide_in,
            qkv_in,
            grad_down,
            out_in,
            grad_scales,
            small,
            alpha_attn[None],
            alpha_mlp[None],
        ),
        w_up.shape[1],
    )
    return (
        output[None, None],
        input_grad[None, None],
        grad_query,
        grad_key,
        grad_value,
        grad_out,
        grad_up,
        grad_gate,
        grad_down,
        grad_gain[0],
        grad_up_scale[0],
        grad_gate_scale[0],
        grad_attn[0],
        grad_mlp_alpha[0],
        mean_alpha[0, 0],
    )


def on_device(*arrays):
    head_count = arrays[3].shape[0] // HEAD_DIM
    tok_rows = arrays[0].shape[2]
    fits = lax.axis_size("blk") == head_count == 16 and lax.axis_size("dp") == 2
    if fits and tok_rows == 128:
        return on_device_heads(*arrays)
    return on_device_general(*arrays)


def solution(mesh):
    in_specs = (
        P("dp", "blk", None, None),
        P("dp", "blk", None, None),
        P("dp", None),
        P(),
        P(),
        P(),
        P(),
        P(),
        P(),
        P(),
        P(),
        P(),
        P(),
        P(),
        P(),
    )
    out_specs = (
        P("dp", "blk", None, None),
        P("dp", "blk", None, None),
        P(("dp", "blk"), None),
        P(("dp", "blk"), None),
        P(("dp", "blk"), None),
        P(("dp", "blk"), None),
        P(("dp", "blk"), None),
        P(("dp", "blk"), None),
        P(("dp", "blk"), None),
        P(("dp", "blk")),
        P(("dp", "blk")),
        P(("dp", "blk")),
        P(("dp", "blk")),
        P(("dp", "blk")),
        P(),
    )
    return jax.shard_map(
        on_device, mesh=mesh, in_specs=in_specs, out_specs=out_specs, check_vma=False
    )
```

```python
import functools
import math

import jax
import jax.numpy as jnp
from jax import lax
from jax.experimental import pallas as pl
from jax.experimental.pallas import tpu as pltpu
from jax.sharding import PartitionSpec as P

HEAD_DIM = 64


def rms_norm(vector):
    return vector * lax.rsqrt(jnp.mean(vector * vector, axis=-1, keepdims=True) + 1e-06)


def head_norm(vector, head_count):
    shaped = vector.reshape(vector.shape[0], head_count, -1)
    return rms_norm(shaped).reshape(vector.shape)


def silu_smooth(vector):
    return vector / (1.0 + jnp.exp(-vector))


def residual_mix(inputs, branch, alphas):
    return rms_norm(inputs + alphas * (rms_norm(branch) - inputs))


def gated_inner(up_raw, gate_raw, s_up, s_gate):
    return up_raw * s_up * silu_smooth(gate_raw * s_gate)


def stream_positions(row_index, tok_rows, members):
    half_rows = tok_rows // 2
    device = row_index // tok_rows
    within = row_index % tok_rows
    block_id = jnp.where(within < half_rows, device, 2 * members - 1 - device)
    return block_id * half_rows + within % half_rows


def doc_index(positions, doc_ends):
    return jnp.sum(
        (positions[:, None] >= doc_ends[None, :]).astype(jnp.int32), axis=1, dtype=jnp.int32
    )


def allowed_pairs(query_pos, query_doc, key_pos, key_doc):
    return (key_pos[None, :] <= query_pos[:, None]) & (key_doc[None, :] == query_doc[:, None])


def take_rows(matrix, first_row, row_count):
    return lax.dynamic_slice_in_dim(matrix, first_row, row_count, 0)


def fold_half(running, query_heads, key_heads, value_heads, allowed, score_scale):

    def absorb(carried):
        best_score, total_sum, accumulated = carried
        scores = (
            jnp.einsum("qhd,khd->hqk", query_heads, key_heads, preferred_element_type=jnp.float32)
            * score_scale
        )
        scores = jnp.where(allowed[None], scores, -1e30)
        new_best = jnp.maximum(best_score, jnp.max(scores, axis=2))
        weights = jnp.where(allowed[None], jnp.exp(scores - new_best[:, :, None]), 0.0)
        fade_factor = jnp.exp(best_score - new_best)
        total_sum = jnp.sum(weights, axis=2)
        accumulated = accumulated * fade_factor.T[:, :, None] + jnp.einsum(
            "hqk,khd->qhd",
            weights.astype(jnp.bfloat16),
            value_heads,
            preferred_element_type=jnp.float32,
        )
        return (new_best, total_sum, accumulated)

    return lax.cond(jnp.any(allowed), absorb, lambda carried: carried, running)


def pair_terms(query_side, key_heads, value_heads, allowed, score_scale):
    query_heads, grad_heads, log_total, delta_rows = (
        query_side[0],
        query_side[1],
        query_side[2],
        query_side[3],
    )
    scores = (
        jnp.einsum("qhd,khd->hqk", query_heads, key_heads, preferred_element_type=jnp.float32)
        * score_scale
    )
    scores = jnp.where(allowed[None], scores, -1e30)
    weights = jnp.exp(scores - log_total[:, :, None])
    grad_weights = jnp.einsum(
        "qhd,khd->hqk", grad_heads, value_heads, preferred_element_type=jnp.float32
    )
    grad_scores = (weights * (grad_weights - delta_rows[:, :, None])).astype(jnp.bfloat16)
    return (weights.astype(jnp.bfloat16), grad_scores)


def query_term(query_side, key_heads, value_heads, allowed, score_scale):
    weights, grad_scores = pair_terms(query_side, key_heads, value_heads, allowed, score_scale)
    return score_scale * jnp.einsum(
        "hqk,khd->qhd", grad_scores, key_heads, preferred_element_type=jnp.float32
    )


def key_term(query_side, key_heads, value_heads, allowed, score_scale):
    weights, grad_scores = pair_terms(query_side, key_heads, value_heads, allowed, score_scale)
    grad_keys = score_scale * jnp.einsum(
        "hqk,qhd->khd", grad_scores, query_side[0], preferred_element_type=jnp.float32
    )
    grad_values = jnp.einsum(
        "hqk,qhd->khd", weights, query_side[1], preferred_element_type=jnp.float32
    )
    return (grad_keys, grad_values)


def on_device_general(
    tokens,
    cotangent,
    lengths,
    w_query,
    w_key,
    w_value,
    w_out,
    w_up,
    w_gate,
    w_down,
    s_qk,
    s_up,
    s_gate,
    alpha_attn,
    alpha_mlp,
):
    model_width = w_query.shape[0]
    head_count = model_width // HEAD_DIM
    score_scale = 1.0 / math.sqrt(HEAD_DIM)
    tok_rows = tokens.shape[2]
    half_rows = tok_rows // 2
    members = lax.axis_size("blk")
    position = lax.axis_index("blk")
    doc_ends = jnp.cumsum(lengths[0], dtype=jnp.int32)
    hidden = tokens[0, 0]
    hidden_f = hidden.astype(jnp.float32)

    def key_info(first_row, row_count):
        key_pos = stream_positions(
            first_row + jnp.arange(row_count, dtype=jnp.int32), tok_rows, members
        )
        return (key_pos, doc_index(key_pos, doc_ends))

    def heads_of(matrix):
        return matrix.reshape(matrix.shape[0], head_count, HEAD_DIM)

    def scaled_norm(raw_rows, gain_vector):
        return head_norm(raw_rows, head_count) * gain_vector

    own_pos, own_doc = key_info(position * tok_rows, tok_rows)
    query_raw = jnp.dot(hidden, w_query, preferred_element_type=jnp.float32)
    key_raw = jnp.dot(hidden, w_key, preferred_element_type=jnp.float32)
    value_raw = jnp.dot(hidden, w_value, preferred_element_type=jnp.float32)
    queries = scaled_norm(query_raw, s_qk).astype(jnp.bfloat16)
    key_rows = scaled_norm(key_raw, s_qk).astype(jnp.bfloat16)
    value_rows = value_raw.astype(jnp.bfloat16)
    query_heads = heads_of(queries)

    def empty_state():
        return (
            jnp.full((head_count, half_rows), -1e30, jnp.float32),
            jnp.zeros((head_count, half_rows), jnp.float32),
            jnp.zeros((half_rows, head_count, HEAD_DIM), jnp.float32),
        )

    running = (empty_state(), empty_state())
    key_part = lax.all_gather(key_rows, "blk", axis=0, tiled=True)
    value_part = lax.all_gather(value_rows, "blk", axis=0, tiled=True)
    key_pos, key_doc = key_info(jnp.int32(0), key_part.shape[0])
    updated = []
    for part_index in range(2):
        rows_here = slice(part_index * half_rows, (part_index + 1) * half_rows)
        allowed = allowed_pairs(own_pos[rows_here], own_doc[rows_here], key_pos, key_doc)
        updated.append(
            fold_half(
                running[part_index],
                query_heads[rows_here],
                heads_of(key_part),
                heads_of(value_part),
                allowed,
                score_scale,
            )
        )
    folded = (updated[0], updated[1])
    best_score = jnp.concatenate([folded[0][0], folded[1][0]], axis=1)
    total_sum = jnp.concatenate([folded[0][1], folded[1][1]], axis=1)
    accumulated = jnp.concatenate([folded[0][2], folded[1][2]], axis=0)
    attended = accumulated / total_sum.T[:, :, None]
    log_total = best_score + jnp.log(total_sum)
    attended_low = attended.reshape(tok_rows, model_width).astype(jnp.bfloat16)
    branch = jnp.dot(attended_low, w_out, preferred_element_type=jnp.float32)
    middle = residual_mix(hidden_f, branch, alpha_attn)
    middle_low = middle.astype(jnp.bfloat16)
    up_raw = jnp.dot(middle_low, w_up, preferred_element_type=jnp.float32)
    gate_raw = jnp.dot(middle_low, w_gate, preferred_element_type=jnp.float32)
    inner_low = gated_inner(up_raw, gate_raw, s_up, s_gate).astype(jnp.bfloat16)
    mlp_raw = jnp.dot(inner_low, w_down, preferred_element_type=jnp.float32)
    result = residual_mix(middle, mlp_raw, alpha_mlp)
    mixed_out, pull_out = jax.vjp(residual_mix, middle, mlp_raw, alpha_mlp)
    grad_middle, grad_mlp, grad_alpha_mlp = pull_out(cotangent[0, 0].astype(jnp.float32))
    grad_mlp_low = grad_mlp.astype(jnp.bfloat16)
    grad_w_down = jnp.dot(inner_low.T, grad_mlp_low, preferred_element_type=jnp.float32)
    grad_inner = jnp.dot(grad_mlp_low, w_down.T, preferred_element_type=jnp.float32)
    inner_out, pull_inner = jax.vjp(gated_inner, up_raw, gate_raw, s_up, s_gate)
    grad_up_raw, grad_gate_raw, grad_s_up, grad_s_gate = pull_inner(grad_inner)
    up_low = grad_up_raw.astype(jnp.bfloat16)
    gate_low = grad_gate_raw.astype(jnp.bfloat16)
    grad_w_up = jnp.dot(middle_low.T, up_low, preferred_element_type=jnp.float32)
    grad_w_gate = jnp.dot(middle_low.T, gate_low, preferred_element_type=jnp.float32)
    grad_middle = (
        grad_middle
        + jnp.dot(up_low, w_up.T, preferred_element_type=jnp.float32)
        + jnp.dot(gate_low, w_gate.T, preferred_element_type=jnp.float32)
    )
    attn_out, pull_attn = jax.vjp(residual_mix, hidden_f, branch, alpha_attn)
    grad_hidden, grad_branch, grad_alpha_attn = pull_attn(grad_middle)
    branch_low = grad_branch.astype(jnp.bfloat16)
    grad_w_out = jnp.dot(attended_low.T, branch_low, preferred_element_type=jnp.float32)
    grad_att_low = jnp.dot(branch_low, w_out.T, preferred_element_type=jnp.float32).astype(
        jnp.bfloat16
    )
    grad_heads = heads_of(grad_att_low)
    delta_rows = jnp.sum(grad_heads.astype(jnp.float32) * attended, axis=2).T

    def local_side(part_index):
        rows_here = slice(part_index * half_rows, (part_index + 1) * half_rows)
        return (
            query_heads[rows_here],
            grad_heads[rows_here],
            log_total[:, rows_here],
            delta_rows[:, rows_here],
            own_pos[rows_here],
            own_doc[rows_here],
        )

    local_parts = (local_side(0), local_side(1))
    whole_keys, whole_values = (
        lax.all_gather(key_rows, "blk", axis=0, tiled=True),
        lax.all_gather(value_rows, "blk", axis=0, tiled=True),
    )

    def query_step(grad_parts, shard_index):
        first_row = shard_index * tok_rows
        key_part = heads_of(take_rows(whole_keys, first_row, tok_rows))
        value_part = heads_of(take_rows(whole_values, first_row, tok_rows))
        key_pos, key_doc = key_info(first_row, tok_rows)
        updated = []
        for part_index in range(2):
            query_side = local_parts[part_index]
            allowed = allowed_pairs(query_side[4], query_side[5], key_pos, key_doc)

            def add_term(grad_now):
                return grad_now + query_term(query_side, key_part, value_part, allowed, score_scale)

            updated.append(
                lax.cond(
                    jnp.any(allowed), add_term, lambda grad_now: grad_now, grad_parts[part_index]
                )
            )
        return ((updated[0], updated[1]), None)

    zero_part = jnp.zeros((half_rows, head_count, HEAD_DIM), jnp.float32)
    grad_parts, unused_out = lax.scan(
        query_step, (zero_part, zero_part), jnp.arange(members, dtype=jnp.int32)
    )
    grad_queries = jnp.concatenate(grad_parts, axis=0).reshape(tok_rows, model_width)
    first_row = jnp.int32(0)
    row_count = lax.axis_size("blk") * tok_rows
    key_part = heads_of(take_rows(whole_keys, first_row, row_count))
    value_part = heads_of(take_rows(whole_values, first_row, row_count))
    key_pos, key_doc = key_info(first_row, row_count)
    zero_keys = jnp.zeros((row_count, head_count, HEAD_DIM), jnp.float32)
    totals = (zero_keys, zero_keys)
    for part_index in range(2):
        query_side = local_parts[part_index]
        allowed = allowed_pairs(query_side[4], query_side[5], key_pos, key_doc)

        def add_terms(grad_now):
            grad_keys, grad_values = key_term(
                query_side, key_part, value_part, allowed, score_scale
            )
            return (grad_now[0] + grad_keys, grad_now[1] + grad_values)

        totals = lax.cond(jnp.any(allowed), add_terms, lambda grad_now: grad_now, totals)
    key_value_grads = lax.psum_scatter(
        jnp.concatenate(
            [totals[0].reshape(row_count, model_width), totals[1].reshape(row_count, model_width)],
            axis=1,
        ),
        "blk",
        scatter_dimension=0,
        tiled=True,
    )
    grad_keys = key_value_grads[:, :model_width]
    grad_values = key_value_grads[:, model_width:]
    query_out, pull_query = jax.vjp(scaled_norm, query_raw, s_qk)
    grad_query_raw, grad_qk_first = pull_query(grad_queries)
    key_out, pull_key = jax.vjp(scaled_norm, key_raw, s_qk)
    grad_key_raw, grad_qk_second = pull_key(grad_keys)
    grad_s_qk = grad_qk_first + grad_qk_second
    query_low = grad_query_raw.astype(jnp.bfloat16)
    key_low = grad_key_raw.astype(jnp.bfloat16)
    value_low = grad_values.astype(jnp.bfloat16)
    grad_w_query = jnp.dot(hidden.T, query_low, preferred_element_type=jnp.float32)
    grad_w_key = jnp.dot(hidden.T, key_low, preferred_element_type=jnp.float32)
    grad_w_value = jnp.dot(hidden.T, value_low, preferred_element_type=jnp.float32)
    input_grad = (
        grad_hidden
        + jnp.dot(query_low, w_query.T, preferred_element_type=jnp.float32)
        + jnp.dot(key_low, w_key.T, preferred_element_type=jnp.float32)
        + jnp.dot(value_low, w_value.T, preferred_element_type=jnp.float32)
    )
    summed = (
        lax.psum_scatter(grad_w_query, ("dp", "blk"), scatter_dimension=0, tiled=True),
        lax.psum_scatter(grad_w_key, ("dp", "blk"), scatter_dimension=0, tiled=True),
        lax.psum_scatter(grad_w_value, ("dp", "blk"), scatter_dimension=0, tiled=True),
        lax.psum_scatter(grad_w_out, ("dp", "blk"), scatter_dimension=0, tiled=True),
        lax.psum_scatter(grad_w_up, ("dp", "blk"), scatter_dimension=0, tiled=True),
        lax.psum_scatter(grad_w_gate, ("dp", "blk"), scatter_dimension=0, tiled=True),
        lax.psum_scatter(grad_w_down, ("dp", "blk"), scatter_dimension=0, tiled=True),
        lax.psum_scatter(grad_s_qk, ("dp", "blk"), scatter_dimension=0, tiled=True),
        lax.psum_scatter(grad_s_up, ("dp", "blk"), scatter_dimension=0, tiled=True),
        lax.psum_scatter(grad_s_gate, ("dp", "blk"), scatter_dimension=0, tiled=True),
        lax.psum_scatter(grad_alpha_attn, ("dp", "blk"), scatter_dimension=0, tiled=True),
        lax.psum_scatter(grad_alpha_mlp, ("dp", "blk"), scatter_dimension=0, tiled=True),
    )
    mean_alpha = 0.5 * (jnp.mean(alpha_attn) + jnp.mean(alpha_mlp))
    output = result.astype(jnp.bfloat16)[None, None]
    return (
        output,
        input_grad[None, None],
        summed[0],
        summed[1],
        summed[2],
        summed[3],
        summed[4],
        summed[5],
        summed[6],
        summed[7],
        summed[8],
        summed[9],
        summed[10],
        summed[11],
        mean_alpha,
    )


MESH = pl.DeviceIdType.MESH
VMEM_SPEC = pl.BlockSpec(memory_space=pltpu.VMEM)
VMEM_LIMIT = 62 << 20
GROUP = 16


def here():
    return lax.axis_index("dp"), lax.axis_index("blk")


def greet(partners):
    barrier = pltpu.get_barrier_semaphore()
    for partner in partners:
        pl.semaphore_signal(barrier, inc=1, device_id=partner, device_id_type=MESH)
    pl.semaphore_wait(barrier, len(partners))


def remote(src, dst, send_sem, recv_sem, device):
    return pltpu.make_async_remote_copy(
        src_ref=src,
        dst_ref=dst,
        send_sem=send_sem,
        recv_sem=recv_sem,
        device_id=device,
        device_id_type=MESH,
    )


class Gather:
    KINDS = 22

    def __init__(self, own, out, send, recv, pieces):
        self.own, self.out, self.send, self.recv = own, out, send, recv
        self.pieces = pieces
        dp, b = here()
        self.dp, self.b = dp, b
        self.z, self.y, self.c = b // 4, (b // 2) % 2, b % 2
        self.up = (dp, (b + 4) % GROUP)
        self.down = (dp, (b + 12) % GROUP)
        self.side = (dp, b + 2 - 4 * self.y)
        self.sib = (dp, b + 1 - 2 * self.c)
        self.half = self.pieces // 2

    def partners(self):
        return [self.up, self.down, self.side, self.sib]

    def copy(self, z, y, c, kind, piece, device, own=False):
        block = z * 4 + y * 2 + c
        upper = piece // self.half
        place = 2 * GROUP - 1 - block if upper else block
        rows = self.out.shape[1] // self.half
        span = pl.ds(piece % self.half * rows, rows)
        target = self.out.at[place, span]
        source = self.own.at[upper, span] if own else target
        index = self.pieces * kind + piece
        return remote(source, target, self.send.at[index], self.recv.at[index], device)

    def along(self, z, piece, device, own=False, back=False):
        return self.copy(z, self.y, self.c, z + (4 if back else 0), piece, device, own)

    def across(self, z, y, piece, own=False):
        return self.copy(z, y, self.c, 8 + z, piece, self.side, own)

    def over(self, z, piece, device, back=False):
        return self.copy(z, 1 - self.y, self.c, 21 if back else 20, piece, device)

    def to_sib(self, z, y, c, piece, own=False):
        return self.copy(z, y, c, 12 + 2 * z + y, piece, self.sib, own)

    def each_side(self, distance, action):
        if distance == 0:
            action(self.z, None)
            return
        low, high = self.z - distance, self.z + distance

        @pl.when(low >= 0)
        def _():
            action(low, False)

        @pl.when(high <= 3)
        def _():
            action(high, True)

    def start(self):
        for piece in range(self.pieces):

            @pl.when(self.z < 3)
            def _():
                self.along(self.z, piece, self.up, True).start()

            @pl.when(self.z > 0)
            def _():
                self.along(self.z, piece, self.down, True, True).start()

            self.across(self.z, self.y, piece, True).start()
        for piece in range(self.pieces):
            self.to_sib(self.z, self.y, self.c, piece, True).start()
        for upper in (0, 1):
            place = 2 * GROUP - 1 - self.b if upper else self.b
            self.out[place] = self.own[upper]

    def line(self, distance):
        def action(z, above):
            for piece in range(self.pieces):
                self.along(z, piece, self.sib, False, above).wait_recv()
                if above:

                    @pl.when(self.z > 0)
                    def _():
                        self.along(z, piece, self.down, False, True).start()
                else:

                    @pl.when(self.z < 3)
                    def _():
                        self.along(z, piece, self.up).start()

                if distance > 1 or piece < self.half:
                    self.across(z, self.y, piece).start()
                self.to_sib(z, self.y, self.c, piece).start()

        self.each_side(distance, action)

    def sides(self, distance):
        def action(z, above):
            for piece in range(self.pieces):
                if distance == 1 and piece >= self.half:
                    continue
                self.across(z, 1 - self.y, piece).wait_recv()
                self.to_sib(z, 1 - self.y, self.c, piece).start()

        self.each_side(distance, action)

    def hand_over(self):
        for piece in range(self.half, self.pieces):

            @pl.when(self.z < 3)
            def _():
                self.over(self.z, piece, self.up).start()

            @pl.when(self.z > 0)
            def _():
                self.over(self.z, piece, self.down, True).start()

    def handed(self):
        def action(z, above):
            for piece in range(self.half, self.pieces):
                self.over(z, piece, self.sib, above).wait_recv()
                self.to_sib(z, 1 - self.y, self.c, piece).start()

        self.each_side(1, action)

    def from_sib(self, distance):
        def action(z, above):
            for piece in range(self.pieces):
                for y in (0, 1):
                    self.to_sib(z, y, 1 - self.c, piece).wait_recv()

        self.each_side(distance, action)

    def drain(self):
        for piece in range(self.pieces):
            for z in range(4):
                for y in (0, 1):
                    self.to_sib(z, y, self.c, piece).wait_send()
                if piece < self.half:
                    self.across(z, self.y, piece).wait_send()
                else:

                    @pl.when((z > self.z + 1) | (z < self.z - 1) | (z == self.z))
                    def _():
                        self.across(z, self.y, piece).wait_send()

                @pl.when((self.z >= z) & (self.z < 3))
                def _():
                    self.along(z, piece, self.up).wait_send()

                @pl.when((self.z <= z) & (self.z > 0))
                def _():
                    self.along(z, piece, self.down, False, True).wait_send()

            if piece >= self.half:

                @pl.when(self.z < 3)
                def _():
                    self.over(self.z, piece, self.up).wait_send()

                @pl.when(self.z > 0)
                def _():
                    self.over(self.z, piece, self.down, True).wait_send()

    def finish(self):
        for distance in range(4):
            self.from_sib(distance)
        self.drain()


def gather_scratch(pieces):
    return [pltpu.SemaphoreType.DMA((pieces * Gather.KINDS,)) for _ in range(2)]


def comm_params(collective_id):
    return pltpu.CompilerParams(
        collective_id=collective_id, has_side_effects=True, vmem_limit_bytes=VMEM_LIMIT
    )


def dot_nt(left, right):
    return lax.dot_general(left, right, (((1,), (1,)), ((), ())), preferred_element_type=jnp.float32)


def dot_tn(left, right):
    return lax.dot_general(left, right, (((0,), (0,)), ((), ())), preferred_element_type=jnp.float32)


def dot_nn(left, right):
    return jnp.dot(left, right, preferred_element_type=jnp.float32)


FF_STEP = 1024


def mean_last(array):
    return jnp.mean(array, axis=-1, keepdims=True)


def rms_scale(array):
    return lax.rsqrt(mean_last(array * array) + 1e-06)


def rms_pull(grad, normed, scale):
    return scale * (grad - normed * mean_last(grad * normed))


def half_lanes(shape):
    return lax.broadcasted_iota(jnp.int32, shape, 1) < HEAD_DIM


FAR_FIRST = sorted(range(1, GROUP), key=lambda step: abs(step - GROUP // 2))


class Swap:
    def __init__(self, blocks, out, send, recv, own=True):
        self.blocks, self.out, self.own = blocks, out, own
        dp, self.b = here()
        self.copies = []
        for step in FAR_FIRST:
            target = (self.b + step) % GROUP
            self.copies.append(
                remote(
                    (blocks.block(target) if isinstance(blocks, SendBlocks) else blocks.at[target])
                    if own
                    else blocks,
                    out.at[self.b],
                    send.at[step],
                    recv.at[step],
                    (dp, target),
                )
            )
        self.partners = [(dp, (self.b + step) % GROUP) for step in range(1, GROUP)]

    def start(self):
        for copy in self.copies:
            copy.start()
        if self.own:
            mine = self.blocks
            mine = mine.block(self.b) if isinstance(mine, SendBlocks) else mine.at[self.b]
            self.out[self.b] = mine[...]

    def wait(self):
        for copy in self.copies:
            copy.wait()


ANY_SPEC = pl.BlockSpec(memory_space=pl.ANY)


SMEM_SPEC = pl.BlockSpec(memory_space=pltpu.SMEM)


def own_head(pair, core):
    shifted = jnp.where(core == 1, pltpu.roll(pair, HEAD_DIM, 1), pair)
    return jnp.where(half_lanes(pair.shape), shifted, 0.0)


def minus_ones(matrix):
    lane = lax.broadcasted_iota(jnp.int32, matrix.shape, 1)
    extra = jnp.where(lane < HEAD_DIM + 3, -1.0, 0.0)
    return jnp.where(lane < HEAD_DIM, matrix, extra).astype(jnp.bfloat16)


PROJECT_PIECES = 4


def doc_start_of(positions, lengths_ref):
    start = jnp.zeros_like(positions)
    end = jnp.int32(0)
    for doc in range(lengths_ref.shape[1]):
        end = end + lengths_ref[0, doc]
        start = start + jnp.where(positions >= end, lengths_ref[0, doc], 0)
    return start


def split_lanes(column, shape):
    lane = lax.broadcasted_iota(jnp.int32, shape, 1)
    high = column.astype(jnp.bfloat16).astype(jnp.float32)
    rest = column - high
    mid = rest.astype(jnp.bfloat16).astype(jnp.float32)
    last = rest - mid
    return jnp.where(
        lane == HEAD_DIM,
        high,
        jnp.where(lane == HEAD_DIM + 1, mid, jnp.where(lane == HEAD_DIM + 2, last, 0.0)),
    )


ATT = 512


TAIL_PIECES = 2
KEYS = 512
PART = 512


class SendBlocks:
    def __init__(self, ref, first_row, rows, first_lane, lanes):
        self.ref, self.first_row, self.rows = ref, first_row, rows
        self.lanes = pl.ds(first_lane, lanes)

    def block(self, index):
        start = pl.multiple_of(self.first_row + index * self.rows, self.rows)
        return self.ref.at[pl.ds(start, self.rows), self.lanes]


def layer_kernel(
    lengths_ref,
    hidden_own,
    cot_ref,
    s_qk_ref,
    s_up_ref,
    s_gate_ref,
    alpha_attn_ref,
    alpha_mlp_ref,
    w_out_hbm,
    w_up_hbm,
    w_gate_hbm,
    w_down_hbm,
    w_query_hbm,
    w_key_hbm,
    w_value_hbm,
    result_ref,
    input_grad_ref,
    wide_in,
    qkv_in,
    g_down_ref,
    out_in,
    g_s_ref,
    small_ref,
    hidden_hbm,
    mid_all,
    g_mlp_all,
    w_out,
    w_up,
    w_gate,
    w_down,
    up_slice,
    gate_slice,
    down_slice,
    up_raw,
    gate_raw,
    mid_own,
    g_mlp_own,
    o_in,
    g_send,
    g_in,
    acc,
    g_res,
    att_pair,
    branch_pair,
    out_got,
    out_side_got,
    ql_ref,
    ka_ref,
    va_ref,
    ga_ref,
    q_raw_ref,
    k_raw_ref,
    att_ref,
    o_ref,
    dq_acc,
    back_in,
    qkv_part,
    qkv_got,
    wide_own,
    wide_got,
    down_got,
    small_own,
    small_got,
    small_all,
    s_part,
    s_send,
    s_got,
    load_sems,
    x_sems,
    pair_sems,
    out_sems,
    swap_sems,
    grad_sems,
    back_sems,
    qkv_sems,
    wide_sems,
    small_sems,
    hid_send,
    hid_recv,
    mid_send,
    mid_recv,
    mlp_send,
    mlp_recv,
):
    low, f32 = jnp.bfloat16, jnp.float32
    dp, b = here()
    z, y, c = b // 4, (b // 2) % 2, b % 2
    twin, sib, side = (1 - dp, b), (dp, b + 1 - 2 * c), (dp, b + 2 - 4 * y)
    half, width = hidden_own.shape[1:]
    rows = 2 * half
    length = GROUP * rows
    ff = w_up.shape[1]
    ff_half = ff // 2
    part = ff // (2 * GROUP)
    quarter = width // 4
    rows_out = width // (2 * GROUP)
    blocks = length // ATT
    loaded = []

    def load(source, target):
        copy = pltpu.make_async_copy(source, target, load_sems.at[len(loaded)])
        copy.start()
        loaded.append(copy)
        return copy

    def to(device, sems, index, source, target):
        copy = remote(source, target, sems.at[0, index], sems.at[1, index], device)
        copy.start()
        return copy

    grad_swap = Swap(g_send, g_in, grad_sems.at[0], grad_sems.at[1])
    small_swap = Swap(small_own, small_all, small_sems.at[0], small_sems.at[1], own=False)
    gather_mid = Gather(mid_own, mid_all, mid_send, mid_recv, TAIL_PIECES)
    gather_mlp = Gather(g_mlp_own, g_mlp_all, mlp_send, mlp_recv, TAIL_PIECES)
    gather_hid = Gather(hidden_own, g_mlp_all, hid_send, hid_recv, PROJECT_PIECES)
    window = pl.ds(pl.multiple_of(b // 2 * 128, 128), 128)
    load_head = [
        load(w_query_hbm.at[:, window], up_slice.at[:, pl.ds(0, 128)]),
        load(w_key_hbm.at[:, window], up_slice.at[:, pl.ds(128, 128)]),
        load(w_value_hbm.at[:, window], gate_slice.at[:, pl.ds(0, 128)]),
    ]
    greet(grad_swap.partners + [twin])
    gather_hid.start()
    load_out = load(w_out_hbm, w_out)
    load_mlp = [load(w_up_hbm, w_up), load(w_gate_hbm, w_gate), load(w_down_hbm, w_down)]

    gain = own_head(jnp.broadcast_to(s_qk_ref[:, window], (8, 128)), c)[:1]
    count = float(HEAD_DIM)
    score_scale = 1.0 / math.sqrt(HEAD_DIM)
    line_slots = 2 * GROUP // 8
    for copy in load_head:
        copy.wait()

    def project(first_slot):
        some = g_mlp_all[pl.ds(first_slot, line_slots)].reshape(line_slots * half, width)
        span = pl.ds(pl.multiple_of(first_slot * half, half), line_slots * half)
        query_key = dot_nn(some, up_slice[...])
        query = own_head(query_key[:, :128], c)
        key = own_head(query_key[:, 128:], c)
        value = own_head(dot_nn(some, gate_slice[:, :128]), c)
        q_raw_ref[span, :] = query.astype(low)
        k_raw_ref[span, :] = key.astype(low)
        query_scale = lax.rsqrt(jnp.sum(query * query, axis=1, keepdims=True) / count + 1e-06)
        key_scale = lax.rsqrt(jnp.sum(key * key, axis=1, keepdims=True) / count + 1e-06)
        query = (query * query_scale * gain).astype(low).astype(f32)
        ql_ref[span, :] = (query * score_scale).astype(low)
        ka_ref[span, :] = minus_ones(key * key_scale * gain)
        va_ref[span, :] = minus_ones(value)

    def project_line(distance):
        def both(line, above):
            project(line_slots * line)
            project(2 * GROUP - line_slots - line_slots * line)

        gather_hid.each_side(distance, both)

    gather_hid.line(1)
    gather_hid.sides(0)
    gather_hid.from_sib(0)
    project_line(0)
    gather_hid.line(2)
    gather_hid.hand_over()
    gather_hid.sides(1)
    gather_hid.line(3)
    gather_hid.sides(2)
    gather_hid.from_sib(2)
    project_line(2)
    gather_hid.handed()
    gather_hid.from_sib(1)
    project_line(1)
    gather_hid.sides(3)
    gather_hid.from_sib(3)
    project_line(3)
    gather_hid.drain()
    store_hidden = [
        load(g_mlp_all.at[slot], hidden_hbm.at[pl.ds(slot * half, half), :])
        for slot in range(2 * GROUP)
    ]
    load_slices = []
    windows = [pl.ds(pl.multiple_of(p * ff_half + b * part, part), part) for p in (0, 1)]
    for p in (0, 1):
        place = pl.ds(p * part, part)
        load_slices.append(load(w_up_hbm.at[:, windows[p]], up_slice.at[:, place]))
        load_slices.append(load(w_gate_hbm.at[:, windows[p]], gate_slice.at[:, place]))
        load_slices.append(load(w_down_hbm.at[windows[p], :], down_slice.at[place, :]))

    query_row_pos = lax.broadcasted_iota(jnp.int32, (ATT, ATT), 0)
    key_lane = lax.broadcasted_iota(jnp.int32, (ATT, ATT), 1)
    wide_first = half_lanes((ATT, 128))
    def o_copy(target):
        return remote(
            o_ref.at[target],
            o_in.at[b],
            swap_sems.at[0, target],
            swap_sems.at[1, b],
            (dp, target),
        )

    first = half_lanes((half, 128))
    for query_block in (1, 2, 0, 3):
        span = pl.ds(query_block * ATT, ATT)
        queries = ql_ref[span, :]
        column = query_block * ATT + lax.broadcasted_iota(jnp.int32, (ATT, 1), 0)
        doc_start = doc_start_of(column, lengths_ref)
        total = jnp.zeros((ATT, 128), f32)
        for key_block in range(query_block + 1):
            base = key_block * ATT
            keys = ka_ref[pl.ds(base, ATT), :]
            values = va_ref[pl.ds(base, ATT), :]
            allowed = base + key_lane >= doc_start
            if key_block == query_block:
                allowed = allowed & (key_lane <= query_row_pos)
            weights = jnp.where(allowed, jnp.exp(dot_nt(queries, keys)), 0.0)
            total = total + dot_nn(weights.astype(low), values)
        row_sum = -total[:, HEAD_DIM : HEAD_DIM + 1]
        att_ref[span, :] = jnp.where(wide_first, total / row_sum, 0.0).astype(low)
        extra = split_lanes(jnp.log(row_sum), total.shape)
        ql_ref[span, :] = jnp.where(wide_first, queries.astype(f32), extra).astype(low)
        if query_block not in (2, 3):
            continue
        if query_block == 2:
            for copy in store_hidden:
                copy.wait()
        for j in range(GROUP // 2, GROUP) if query_block == 2 else range(GROUP // 2):
            lower = att_ref[j * half : (j + 1) * half, :].astype(f32)
            upper = att_ref[length - (j + 1) * half : length - j * half, :].astype(f32)
            o_ref[j] = jnp.where(first, lower, pltpu.roll(upper, HEAD_DIM, 1)).astype(low)

            @pl.when(j != b)
            def _():
                o_copy(j).start()

            @pl.when(j == b)
            def _():
                o_in[b] = o_ref[b]

    for other in range(GROUP):

        @pl.when(other != b)
        def _():
            copy = remote(
                o_ref.at[other],
                o_in.at[other],
                swap_sems.at[0, other],
                swap_sems.at[1, other],
                sib,
            )
            copy.wait_send()
            copy.wait_recv()

    for pair in range(GROUP // 2):
        even = o_in[2 * pair].astype(f32)
        odd = o_in[2 * pair + 1].astype(f32)
        lanes = slice(pair * 128, (pair + 1) * 128)
        att_pair[c, :half, lanes] = jnp.where(first, even, pltpu.roll(odd, HEAD_DIM, 1)).astype(low)
        att_pair[c, half:, lanes] = jnp.where(first, pltpu.roll(even, HEAD_DIM, 1), odd).astype(low)
    att_copy = to(sib, pair_sems, 0, att_pair.at[c], att_pair.at[c])
    hidden = hidden_own[...].reshape(rows, width).astype(f32)
    alpha_attn = alpha_attn_ref[...]
    alpha_mlp = alpha_mlp_ref[...]
    load_out.wait()
    branch = dot_nn(att_pair[c], w_out[...])
    branch_scale = rms_scale(branch)
    branch_normed = branch * branch_scale
    mixed = hidden + alpha_attn * (branch_normed - hidden)
    middle_scale = rms_scale(mixed)
    middle = mixed * middle_scale
    middle_low = middle.astype(low)
    mid_own[0] = middle_low[:half]
    mid_own[1] = middle_low[half:]
    gather_mid.start()
    for copy in load_mlp:
        copy.wait()
    steps = ff // FF_STEP
    acc[...] = jnp.zeros_like(acc)

    def forward(step):
        cols = pl.ds(step * FF_STEP, FF_STEP)
        up = dot_nn(middle_low, w_up[:, cols])
        gate = dot_nn(middle_low, w_gate[:, cols])
        up_raw[:, cols] = up
        gate_raw[:, cols] = gate
        scaled = gate * s_gate_ref[:, cols]
        inner = up * s_up_ref[:, cols] * (scaled / (1.0 + jnp.exp(-scaled)))
        acc[...] += dot_nn(inner.astype(low), w_down[cols, :])

    for step in range(steps):
        forward(step)
    gather_mid.line(1)
    gather_mid.sides(0)
    mlp = acc[...]
    mlp_scale = rms_scale(mlp)
    mlp_normed = mlp * mlp_scale
    mixed_out = middle + alpha_mlp * (mlp_normed - middle)
    out_scale = rms_scale(mixed_out)
    result = mixed_out * out_scale
    result_ref[...] = result.astype(low)

    g_mixed = rms_pull(cot_ref[...].astype(f32), result, out_scale)
    g_alpha_mlp = jnp.sum(g_mixed * (mlp_normed - middle), axis=0, keepdims=True)
    small_own[...] = jnp.zeros_like(small_own)
    for i in range(width // 128):
        small_own[8 + i : 9 + i, :] = g_alpha_mlp[:, 128 * i : 128 * (i + 1)]
    g_mlp = rms_pull(g_mixed * alpha_mlp, mlp_normed, mlp_scale).astype(low)
    g_mlp_own[0] = g_mlp[:half]
    g_mlp_own[1] = g_mlp[half:]
    gather_mlp.start()
    acc[...] = g_mixed * (1.0 - alpha_mlp)

    def backward(step):
        cols = pl.ds(step * FF_STEP, FF_STEP)
        g_inner = dot_nt(g_mlp, w_down[cols, :])
        s_up = s_up_ref[:, cols]
        s_gate = s_gate_ref[:, cols]
        scaled = gate_raw[:, cols] * s_gate
        sigmoid = 1.0 / (1.0 + jnp.exp(-scaled))
        g_up = g_inner * (scaled / (1.0 + jnp.exp(-scaled))) * s_up
        slope = sigmoid * (1.0 + scaled * (1.0 - sigmoid))
        g_gate = g_inner * (up_raw[:, cols] * s_up) * slope * s_gate
        acc[...] += dot_nt(g_up.astype(low), w_up[:, cols]) + dot_nt(
            g_gate.astype(low), w_gate[:, cols]
        )

    for step in range(steps // 2):
        backward(step)
    gather_mid.line(2)
    gather_mid.hand_over()
    gather_mid.sides(1)
    for step in range(steps // 2, steps):
        backward(step)
    g_pre = rms_pull(acc[...], middle, middle_scale)
    g_res[...] = g_pre * (1.0 - alpha_attn)
    g_alpha_attn = jnp.sum(g_pre * (branch_normed - hidden), axis=0, keepdims=True)
    for i in range(width // 128):
        small_own[i : i + 1, :] = g_alpha_attn[:, 128 * i : 128 * (i + 1)]
    branch_pair[c] = rms_pull(g_pre * alpha_attn, branch_normed, branch_scale).astype(low)
    g_att = dot_nt(branch_pair[c], w_out[...]).astype(low).astype(f32)
    for pair in range(GROUP // 2):
        lower = g_att[:half, pair * 128 : (pair + 1) * 128]
        upper = g_att[half:, pair * 128 : (pair + 1) * 128]
        g_send[2 * pair] = jnp.where(first, lower, pltpu.roll(upper, HEAD_DIM, 1)).astype(low)
        g_send[2 * pair + 1] = jnp.where(first, pltpu.roll(lower, HEAD_DIM, 1), upper).astype(low)
    grad_swap.start()
    branch_copy = to(sib, pair_sems, 1, branch_pair.at[c], branch_pair.at[c])

    g_cat = w_down.at[pl.ds(0, length), pl.ds(0, 4 * part)]
    inner_all = w_down.at[pl.ds(0, length), pl.ds(512, 2 * part)]
    raw_low = w_down.at[pl.ds(length, length), pl.ds(0, 384)]
    w_qkv = [w_up.at[:, pl.ds(i * width, width)] for i in range(3)]
    home = [w_up.at[pl.ds(i * rows, rows), pl.ds(3 * width, width)] for i in range(3)]
    out_send = w_out.at[pl.ds(0, quarter), :]
    out_side_send = [w_out.at[pl.ds(quarter + half * k, half), :] for k in (0, 1)]
    out_line = w_out.at[pl.ds(2 * quarter, 4 * rows_out), :]
    down_send = w_out.at[pl.ds(3 * quarter, part), :]
    out_own = [up_raw.at[:, pl.ds((2 + k) * width, width)] for k in (0, 1)]
    wide_send = [w_gate.at[pl.ds(quarter * i, quarter), pl.ds(2048, 512)] for i in (0, 1)]
    qkv_send = w_gate.at[pl.ds(0, 2 * quarter), pl.ds(2560, 256)]
    back_send = SendBlocks(w_gate, 0, half, 2816, 384)
    qkv_blocks = SendBlocks(w_gate, 2 * quarter, rows_out, 2560, 256)
    wide_blocks = SendBlocks(w_gate, 2 * quarter, rows_out, 2048, 512)
    back_swap = Swap(back_send, back_in, back_sems.at[0], back_sems.at[1])
    qkv_swap = Swap(qkv_blocks, qkv_in, qkv_sems.at[0], qkv_sems.at[1])
    tokens_of_half = [w_gate.at[:, pl.ds(i * width, width)] for i in (0, 1)]
    load_hidden = [
        load(hidden_hbm.at[pl.ds(i * width, width), :], tokens_of_half[i]) for i in (0, 1)
    ]
    load_qkv = [
        load(source, w_qkv[i]) for i, source in enumerate((w_query_hbm, w_key_hbm, w_value_hbm))
    ]
    gather_mid.line(3)
    gather_mid.sides(2)
    gather_mlp.line(1)
    gather_mlp.sides(0)

    att_copy.wait()
    branch_copy.wait()
    both_branch = branch_pair[...].reshape(2 * rows, width)

    def out_rows(owner):
        lanes = pl.ds(pl.multiple_of(owner * 2 * quarter + c * quarter, quarter), quarter)
        return dot_tn(att_pair[:, :, lanes].reshape(2 * rows, quarter), both_branch)

    out_send[...] = out_rows(1 - dp).astype(low)
    out_copy = to(twin, x_sems, 0, out_send, out_got)

    grad_swap.wait()
    for j in range(GROUP):
        block = g_in[j].astype(f32)
        for start, grads in (
            (j * half, jnp.where(first, block, 0.0)),
            (length - (j + 1) * half, jnp.where(first, pltpu.roll(block, HEAD_DIM, 1), 0.0)),
        ):
            span = pl.ds(start, half)
            delta = jnp.sum(grads * att_ref[span, :].astype(f32), axis=1, keepdims=True)
            ga_ref[span, :] = (grads + split_lanes(delta, grads.shape)).astype(low)
    dq_acc[...] = jnp.zeros_like(dq_acc)
    key_row = lax.broadcasted_iota(jnp.int32, (KEYS, ATT), 0)
    query_lane = lax.broadcasted_iota(jnp.int32, (KEYS, ATT), 1)
    query_row = lax.broadcasted_iota(jnp.int32, (1, ATT), 1)

    def norm_pull(raw, grad):
        raw = raw.astype(f32)
        scale = lax.rsqrt(jnp.sum(raw * raw, axis=1, keepdims=True) / count + 1e-06)
        normed = raw * scale
        g_gain = jnp.sum(grad * normed, axis=0, keepdims=True)
        inside = grad * gain
        mean = jnp.sum(inside * normed, axis=1, keepdims=True) / count
        return scale * (inside - normed * mean), g_gain

    key_first = half_lanes((KEYS, 128))

    def pair_grads(keys, values, key_block, query_block):
        base = query_block * ATT
        queries = ql_ref[pl.ds(base, ATT), :]
        grads = ga_ref[pl.ds(base, ATT), :]
        key_pos = key_block * KEYS + key_row
        allowed = key_pos >= doc_start_of(base + query_row, lengths_ref)
        if key_block * KEYS + KEYS > base:
            allowed = allowed & (key_pos <= base + query_lane)
        weights = jnp.where(allowed, jnp.exp(dot_nt(keys, queries)), 0.0)
        slopes = (weights * dot_nt(values, grads)).astype(low)
        dq_acc[pl.ds(base, ATT), :] += dot_tn(slopes, keys)
        return dot_nn(slopes, queries), dot_nn(weights.astype(low), grads)

    g_gain = jnp.zeros((1, 128), f32)
    for key_block in range(length // KEYS):
        span = pl.ds(key_block * KEYS, KEYS)
        keys = ka_ref[span, :]
        values = va_ref[span, :]
        dk, dv = 0.0, 0.0
        for query_block in range(key_block * KEYS // ATT, blocks):
            more_k, more_v = pair_grads(keys, values, key_block, query_block)
            dk, dv = dk + more_k, dv + more_v
        g_key, key_gain = norm_pull(k_raw_ref[span, :], jnp.where(key_first, dk, 0.0))
        g_gain = g_gain + key_gain
        raw_low[span, 128:256] = g_key.astype(low)
        raw_low[span, 256:384] = jnp.where(key_first, dv, 0.0).astype(low)
        if key_block == 0:
            gather_mid.handed()
            gather_mid.sides(3)
            gather_mlp.line(2)
            gather_mlp.hand_over()
            gather_mlp.sides(1)
        if key_block == 2:
            gather_mlp.line(3)
            gather_mlp.sides(2)
    for block in range(blocks):
        span = pl.ds(block * ATT, ATT)
        dq = jnp.where(wide_first, dq_acc[span, :] * score_scale, 0.0)
        g_query, query_gain = norm_pull(q_raw_ref[span, :], dq)
        g_gain = g_gain + query_gain
        raw_low[span, 0:128] = g_query.astype(low)
    for j in range(GROUP):
        for i in range(3):
            lanes = slice(128 * i, 128 * (i + 1))
            lower = raw_low[j * half : (j + 1) * half, lanes].astype(f32)
            upper = raw_low[length - (j + 1) * half : length - j * half, lanes].astype(f32)
            back_send.block(j)[:, lanes] = jnp.where(
                first, lower, pltpu.roll(upper, HEAD_DIM, 1)
            ).astype(low)
    back_swap.start()

    small_own[16:17, :] = g_gain
    small_copy = to(twin, x_sems, 1, small_own, small_got)

    for copy in load_hidden:
        copy.wait()

    def qkv_chunk(chunk):
        lanes = pl.ds(pl.multiple_of(chunk * quarter, quarter), quarter)
        grads = sum(
            dot_tn(tokens_of_half[i][:, lanes], raw_low[pl.ds(i * width, width), :]) for i in (0, 1)
        )
        query_key = jnp.where(
            half_lanes((quarter, 128)), grads[:, :128], pltpu.roll(grads[:, 128:256], HEAD_DIM, 1)
        )
        return query_key, grads[:, 256:]

    for i in (0, 1):
        query_key, value = qkv_chunk(2 * (1 - dp) + i)
        span = slice(quarter * i, quarter * (i + 1))
        qkv_send[span, :128] = query_key.astype(low)
        qkv_send[span, 128:] = value.astype(low)
    qkv_copy = to(twin, x_sems, 2, qkv_send, qkv_got)
    for i in (0, 1):
        query_key, value = qkv_chunk(2 * dp + i)
        span = slice(quarter * i, quarter * (i + 1))
        qkv_part[span, :128] = query_key
        qkv_part[span, 128:] = value

    out_mine = out_rows(dp)
    for k in (0, 1):
        out_own[k][...] = out_mine[2 * half * k : 2 * half * (k + 1)]
    out_copy.wait()
    side_copies = []
    for k in (0, 1):
        out_own[k][...] += out_got[2 * half * k : 2 * half * (k + 1)].astype(f32)
        other = pl.ds(pl.multiple_of((1 - y) * half, half), half)
        out_side_send[k][...] = out_own[k][other, :].astype(low)
        side_copies.append(to(side, pair_sems, 2 + k, out_side_send[k], out_side_got.at[k]))
    small_copy.wait()
    small_own[...] += small_got[...]
    small_swap.start()
    gather_mid.finish()
    gather_mlp.handed()
    gather_mlp.sides(3)
    gather_mlp.finish()

    for copy in load_slices:
        copy.wait()
    s_up = jnp.concatenate([s_up_ref[:, window] for window in windows], axis=1)
    s_gate = jnp.concatenate([s_gate_ref[:, window] for window in windows], axis=1)
    slots = PART // half

    def tokens_of(array, step):
        return array[pl.ds(step * slots, slots)].reshape(PART, width)

    def recompute(step, sums):
        span = pl.ds(pl.multiple_of(step * PART, PART), PART)
        some = tokens_of(mid_all, step)
        up = dot_nn(some, up_slice[...])
        gate = dot_nn(some, gate_slice[...])
        g_inner = dot_nt(tokens_of(g_mlp_all, step), down_slice[...])
        scaled = gate * s_gate
        sigmoid = 1.0 / (1.0 + jnp.exp(-scaled))
        silu = scaled / (1.0 + jnp.exp(-scaled))
        up_scaled = up * s_up
        inner_all[span, :] = (up_scaled * silu).astype(low)
        g_up_scaled = g_inner * silu
        g_scaled = g_inner * up_scaled * (sigmoid * (1.0 + scaled * (1.0 - sigmoid)))
        g_cat[span, : 2 * part] = (g_up_scaled * s_up).astype(low)
        g_cat[span, 2 * part :] = (g_scaled * s_gate).astype(low)
        return (
            sums[0] + jnp.sum(g_up_scaled * up, axis=0, keepdims=True),
            sums[1] + jnp.sum(g_scaled * gate, axis=0, keepdims=True),
        )

    zero_row = jnp.zeros((1, 2 * part), f32)
    g_s_up, g_s_gate = lax.fori_loop(0, length // PART, recompute, (zero_row, zero_row))

    line_rows_of = 4 * rows_out
    turns = ((0, 3), (1, 2))

    def wide_chunk(owner, turn):
        tokens = [
            mid_all[
                :,
                :,
                pl.ds(
                    pl.multiple_of(owner * 2 * quarter + line * line_rows_of, line_rows_of),
                    line_rows_of,
                ),
            ].reshape(length, line_rows_of)
            for line in turns[turn]
        ]
        return dot_tn(jnp.concatenate(tokens, axis=1), g_cat[...])

    wide_copies = []
    for i in (0, 1):
        wide_send[i][...] = wide_chunk(1 - dp, i).astype(low)
        wide_copies.append(to(twin, x_sems, 3 + i, wide_send[i], wide_got.at[i]))
    for p in (0, 1):
        s_part[p] = jnp.zeros(s_part.shape[1:], f32)
        s_part[p, 0:1, :] = g_s_up[:, p * part : (p + 1) * part]
        s_part[p, 1:2, :] = g_s_gate[:, p * part : (p + 1) * part]
    s_send[...] = s_part[1 - dp]
    s_copy = to(twin, x_sems, 5, s_send, s_got)
    for chunk in range(4):
        lanes = pl.ds(chunk * quarter, quarter)
        grads = dot_tn(inner_all[...], g_mlp_all[:, :, lanes].reshape(length, quarter))
        for p in (0, 1):
            place = slice(p * width + chunk * quarter, p * width + (chunk + 1) * quarter)
            up_raw[:, place] = grads[p * part : (p + 1) * part]
    down_other = pl.ds(pl.multiple_of((1 - dp) * width, width), width)
    down_mine = pl.ds(pl.multiple_of(dp * width, width), width)
    down_send[...] = up_raw[:, down_other].astype(low)
    down_copy = to(twin, x_sems, 6, down_send, down_got)

    qkv_copy.wait()
    per_chunk = quarter // rows_out
    total = (qkv_part[...] + qkv_got[...].astype(f32)).astype(low)
    for k in range(GROUP):
        qkv_blocks.block(k)[...] = total[k * rows_out : (k + 1) * rows_out]
    qkv_swap.start()
    for copy in side_copies:
        copy.wait()
    out_copies = []
    for k in (0, 1):
        mine = pl.ds(pl.multiple_of(y * half, half), half)
        total = (out_own[k][mine, :] + out_side_got[k].astype(f32)).astype(low)
        out_line[2 * rows_out * k : 2 * rows_out * (k + 1), :] = total
        for core in (0, 1):
            line_rows = pl.ds((2 * k + core) * rows_out, rows_out)
            target = (2 * c + k) * 4 + 2 * y + core
            index = 2 * k + core
            copy = remote(
                out_line.at[line_rows],
                out_in.at[z],
                out_sems.at[0, index],
                out_sems.at[1, z],
                (dp, target),
            )
            out_copies.append((target, copy))

            @pl.when(target != b)
            def _():
                copy.start()

            @pl.when(target == b)
            def _():
                out_in[z] = out_line[line_rows, :]

    def wide_copy(target):
        return remote(
            wide_blocks.block(target),
            wide_in.at[b],
            wide_sems.at[0, target],
            wide_sems.at[1, b],
            (dp, target),
        )

    for i in (0, 1):
        wide_own[...] = wide_chunk(dp, i)
        wide_copies[i].wait()
        total = (wide_own[...] + wide_got[i].astype(f32)).astype(low)
        for k in range(per_chunk):
            target = 4 * turns[i][k // 4] + k % 4
            wide_blocks.block(target)[...] = total[k * rows_out : (k + 1) * rows_out]

            @pl.when(target != b)
            def _():
                wide_copy(target).start()

            @pl.when(target == b)
            def _():
                wide_in[b] = wide_blocks.block(target)[...]

    for copy in load_qkv:
        copy.wait()
    back_swap.wait()
    for pair in range(GROUP // 2):
        for i in range(3):
            lanes = slice(128 * i, 128 * (i + 1))
            even = back_in[2 * pair, :, lanes].astype(f32)
            odd = back_in[2 * pair + 1, :, lanes].astype(f32)
            place = slice(128 * pair, 128 * (pair + 1))
            home[i][:half, place] = jnp.where(first, even, pltpu.roll(odd, HEAD_DIM, 1)).astype(low)
            home[i][half:, place] = jnp.where(first, pltpu.roll(even, HEAD_DIM, 1), odd).astype(low)
    input_grad_ref[...] = (
        g_res[...]
        + dot_nt(home[0][...], w_qkv[0][...])
        + dot_nt(home[1][...], w_qkv[1][...])
        + dot_nt(home[2][...], w_qkv[2][...])
    )
    s_copy.wait()
    g_s_ref[...] = s_part[dp] + s_got[...]
    down_copy.wait()
    g_down_ref[...] = up_raw[:, down_mine] + down_got[...].astype(f32)
    small_swap.wait()
    small_all[b] = small_own[...]
    small_ref[...] = jnp.sum(small_all[...], axis=0)
    small_ref[17:18, :] = small_all[8 * dp + b // 2, 16:17, :]
    qkv_swap.wait()
    for target, copy in out_copies:

        @pl.when(target != b)
        def _():
            copy.wait_send()

    for source_z in range(4):
        source = source_z * 4 + 2 * y + z // 2

        @pl.when(source != b)
        def _():
            remote(
                out_line.at[pl.ds(0, rows_out)],
                out_in.at[source_z],
                out_sems.at[0, 0],
                out_sems.at[1, source_z],
                sib,
            ).wait_recv()

    for other in range(GROUP):

        @pl.when(other != b)
        def _():
            copy = remote(
                wide_blocks.block(other),
                wide_in.at[other],
                wide_sems.at[0, other],
                wide_sems.at[1, other],
                sib,
            )
            copy.wait_send()
            copy.wait_recv()


def layer_block(vmem_inputs, hbm_inputs):
    low, f32 = jnp.bfloat16, jnp.float32
    shape, vmem, sems = jax.ShapeDtypeStruct, pltpu.VMEM, pltpu.SemaphoreType.DMA
    hidden = vmem_inputs[1]
    w_out, w_up, w_gate, w_down = hbm_inputs[:4]
    half, width = hidden.shape[1:]
    rows = 2 * half
    ff = w_up.shape[1]
    length = GROUP * rows
    rows_out = width // (2 * GROUP)
    part = ff // (2 * GROUP)
    quarter = width // 4
    packed = (GROUP, half, 128)
    return pl.pallas_call(
        layer_kernel,
        out_shape=[
            shape((rows, width), low),
            shape((rows, width), f32),
            shape((GROUP, rows_out, 4 * part), low),
            shape((GROUP, rows_out, 256), low),
            shape((part, width), f32),
            shape((4, rows_out, width), low),
            shape((8, 128), f32),
            shape((24, 128), f32),
            shape((length, width), low),
        ],
        in_specs=[SMEM_SPEC]
        + [VMEM_SPEC] * (len(vmem_inputs) - 1)
        + [ANY_SPEC] * len(hbm_inputs),
        out_specs=[VMEM_SPEC] * 8 + [ANY_SPEC],
        scratch_shapes=[
            vmem((2 * GROUP, half, width), low),
            vmem((2 * GROUP, half, width), low),
            vmem(w_out.shape, low),
            vmem(w_up.shape, low),
            vmem(w_gate.shape, low),
            vmem(w_down.shape, low),
            vmem((width, 2 * part), low),
            vmem((width, 2 * part), low),
            vmem((2 * part, width), low),
            vmem((rows, ff), f32),
            vmem((rows, ff), f32),
            vmem((2, half, width), low),
            vmem((2, half, width), low),
            vmem(packed, low),
            vmem(packed, low),
            vmem(packed, low),
            vmem((rows, width), f32),
            vmem((rows, width), f32),
            vmem((2, rows, width), low),
            vmem((2, rows, width), low),
            vmem((quarter, width), low),
            vmem((2, half, width), low),
            vmem((length, 128), low),
            vmem((length, 128), low),
            vmem((length, 128), low),
            vmem((length, 128), low),
            vmem((length, 128), low),
            vmem((length, 128), low),
            vmem((length, 128), low),
            vmem(packed, low),
            vmem((length, 128), f32),
            vmem((GROUP, half, 384), low),
            vmem((2 * quarter, 256), f32),
            vmem((2 * quarter, 256), low),
            vmem((quarter, 4 * part), f32),
            vmem((2, quarter, 4 * part), low),
            vmem((part, width), low),
            vmem((24, 128), f32),
            vmem((24, 128), f32),
            vmem((GROUP, 24, 128), f32),
            vmem((2, 8, 128), f32),
            vmem((8, 128), f32),
            vmem((8, 128), f32),
            sems((64,)),
            sems((2, 8)),
            sems((2, 4)),
            sems((2, 4)),
            sems((2, GROUP)),
            sems((2, GROUP)),
            sems((2, GROUP)),
            sems((2, GROUP)),
            sems((2, GROUP)),
            sems((2, GROUP)),
        ]
        + gather_scratch(PROJECT_PIECES)
        + gather_scratch(TAIL_PIECES)
        + gather_scratch(TAIL_PIECES),
        compiler_params=comm_params(1),
        name="layer_block",
    )(*vmem_inputs, *hbm_inputs)


def assemble_kernel(
    result,
    input_grad,
    wide_in,
    qkv_in,
    down,
    out_in,
    scales,
    small,
    alpha_attn,
    alpha_mlp,
    output_ref,
    input_grad_ref,
    g_query_ref,
    g_key_ref,
    g_value_ref,
    g_out_ref,
    g_up_ref,
    g_gate_ref,
    g_down_ref,
    gain_ref,
    s_up_ref,
    s_gate_ref,
    g_alpha_attn_ref,
    g_alpha_mlp_ref,
    mean_ref,
):
    f32 = jnp.float32
    dp, b = here()
    output_ref[...] = result[...]
    input_grad_ref[...] = input_grad[...]
    g_down_ref[...] = down[...]
    s_up_ref[...] = scales[0:1, :]
    s_gate_ref[...] = scales[1:2, :]
    rows_out = g_out_ref.shape[0]
    per_row = 128 // rows_out
    device = dp * GROUP + b

    def own_lanes(row, place):
        start = (128 - rows_out * place) % 128
        return pltpu.roll(jnp.broadcast_to(row, (8, 128)), start, 1)[:1, :rows_out]

    place = device % per_row
    g_alpha_attn_ref[...] = own_lanes(small[pl.ds(device // per_row, 1), :], place)
    g_alpha_mlp_ref[...] = own_lanes(small[pl.ds(8 + device // per_row, 1), :], place)
    gain_ref[...] = own_lanes(small[17:18, :], b % 2)
    mean_ref[...] = 0.5 * (mean_last(alpha_attn[...]) + mean_last(alpha_mlp[...]))
    g_out_ref[...] = sum(out_in[i].astype(f32) for i in range(4))
    part = wide_in.shape[2] // 4
    ff_half = g_up_ref.shape[1] // 2
    for j in range(GROUP):
        for p in (0, 1):
            place = slice(p * ff_half + j * part, p * ff_half + (j + 1) * part)
            g_up_ref[:, place] = wide_in[j, :, p * part : (p + 1) * part].astype(f32)
            g_gate_ref[:, place] = wide_in[j, :, (2 + p) * part : (3 + p) * part].astype(f32)
    first = half_lanes((g_query_ref.shape[0], 128))
    for pair in range(GROUP // 2):
        place = slice(128 * pair, 128 * (pair + 1))
        even, odd = qkv_in[2 * pair].astype(f32), qkv_in[2 * pair + 1].astype(f32)
        even_qk, odd_qk = even[:, :128], odd[:, :128]
        g_query_ref[:, place] = jnp.where(first, even_qk, pltpu.roll(odd_qk, HEAD_DIM, 1))
        g_key_ref[:, place] = jnp.where(first, pltpu.roll(even_qk, HEAD_DIM, 1), odd_qk)
        g_value_ref[:, place] = jnp.where(
            first, even[:, 128:], pltpu.roll(odd[:, 128:], HEAD_DIM, 1)
        )


def assemble_block(inputs, ff):
    result, input_grad, wide_in, qkv_in, down, out_in = inputs[:6]
    f32 = jnp.float32
    shape = jax.ShapeDtypeStruct
    width = result.shape[1]
    rows_out = wide_in.shape[1]
    return pl.pallas_call(
        assemble_kernel,
        out_shape=[
            shape(result.shape, result.dtype),
            shape(input_grad.shape, f32),
            shape((rows_out, width), f32),
            shape((rows_out, width), f32),
            shape((rows_out, width), f32),
            shape((rows_out, width), f32),
            shape((rows_out, ff), f32),
            shape((rows_out, ff), f32),
            shape(down.shape, f32),
            shape((1, rows_out), f32),
            shape((1, 128), f32),
            shape((1, 128), f32),
            shape((1, rows_out), f32),
            shape((1, rows_out), f32),
            shape((1, 1), f32),
        ],
        in_specs=[VMEM_SPEC] * len(inputs),
        out_specs=[VMEM_SPEC] * 15,
        compiler_params=pltpu.CompilerParams(vmem_limit_bytes=VMEM_LIMIT),
        name="assemble_block",
    )(*inputs)


def on_device_heads(
    tokens,
    cotangent,
    lengths,
    w_query,
    w_key,
    w_value,
    w_out,
    w_up,
    w_gate,
    w_down,
    s_qk,
    s_up,
    s_gate,
    alpha_attn,
    alpha_mlp,
):
    model_width = w_query.shape[0]
    tok_rows = tokens.shape[2]
    half_rows = tok_rows // 2
    hidden = tokens[0, 0]
    (result, input_grad, wide_in, qkv_in, grad_down, out_in, grad_scales, small, _) = layer_block(
        (
            lengths,
            hidden.reshape(2, half_rows, model_width),
            cotangent[0, 0],
            s_qk[None],
            s_up[None],
            s_gate[None],
            alpha_attn[None],
            alpha_mlp[None],
        ),
        (w_out, w_up, w_gate, w_down, w_query, w_key, w_value),
    )
    (
        output,
        input_grad,
        grad_query,
        grad_key,
        grad_value,
        grad_out,
        grad_up,
        grad_gate,
        grad_down,
        grad_gain,
        grad_up_scale,
        grad_gate_scale,
        grad_attn,
        grad_mlp_alpha,
        mean_alpha,
    ) = assemble_block(
        (
            result,
            input_grad,
            wide_in,
            qkv_in,
            grad_down,
            out_in,
            grad_scales,
            small,
            alpha_attn[None],
            alpha_mlp[None],
        ),
        w_up.shape[1],
    )
    return (
        output[None, None],
        input_grad[None, None],
        grad_query,
        grad_key,
        grad_value,
        grad_out,
        grad_up,
        grad_gate,
        grad_down,
        grad_gain[0],
        grad_up_scale[0],
        grad_gate_scale[0],
        grad_attn[0],
        grad_mlp_alpha[0],
        mean_alpha[0, 0],
    )


def on_device(*arrays):
    head_count = arrays[3].shape[0] // HEAD_DIM
    tok_rows = arrays[0].shape[2]
    fits = lax.axis_size("blk") == head_count == 16 and lax.axis_size("dp") == 2
    if fits and tok_rows == 128:
        return on_device_heads(*arrays)
    return on_device_general(*arrays)


def solution(mesh):
    in_specs = (
        P("dp", "blk", None, None),
        P("dp", "blk", None, None),
        P("dp", None),
        P(),
        P(),
        P(),
        P(),
        P(),
        P(),
        P(),
        P(),
        P(),
        P(),
        P(),
        P(),
    )
    out_specs = (
        P("dp", "blk", None, None),
        P("dp", "blk", None, None),
        P(("dp", "blk"), None),
        P(("dp", "blk"), None),
        P(("dp", "blk"), None),
        P(("dp", "blk"), None),
        P(("dp", "blk"), None),
        P(("dp", "blk"), None),
        P(("dp", "blk"), None),
        P(("dp", "blk")),
        P(("dp", "blk")),
        P(("dp", "blk")),
        P(("dp", "blk")),
        P(("dp", "blk")),
        P(),
    )
    return jax.shard_map(
        on_device, mesh=mesh, in_specs=in_specs, out_specs=out_specs, check_vma=False
    )
```
